32 devices in a mesh: seq: 8 (over z, x), tp: 4 (over y, core).
Axes of the slice: x: 2, y: 2, z: 4, core: 2. Of those that a mesh axis runs over, the one named last changes fastest.
Arguments:
- tokens: bfloat16 [4096, 2048], P('seq', 'tp'), may hold values from -6 to 6
- norm_gain: float32 [2048], replicated, may hold values from 0.1 to 1.9
- w_query: bfloat16 [2048, 2048], P(None, 'tp'), may hold values from -0.125 to 0.125
- w_keyval: bfloat16 [2048, 256], replicated, may hold values from -0.125 to 0.125
- w_out: bfloat16 [2048, 2048], P('tp'), may hold values from -0.5 to 0.5
- span_lens: int32 [8], P('seq'), may hold values from 1 to 512, 3072 in all
- cached_lens: int32 [8], P('seq'), may hold values from 1 to 1536, 6144 in all
- old_table: int32 [8, 8], P('seq'), may hold values from 0 to 7, each once within a row
- new_table: int32 [8, 8], P('seq'), may hold values from 0 to 7, each once within a row
- old_cache: bfloat16 [64, 256, 256], P('seq', 'tp'), may hold values from -720 to 720
Outputs:
- mixed: bfloat16 [4096, 2048], P('seq', 'tp')
- new_cache: bfloat16 [64, 256, 256], P('seq', 'tp')
The draws below stay inside these ranges and needn't reach their ends.
Inputs may be any that keep to these rules, and one draw needn't show every extreme that they name: Request r's new tokens are the first span_lens[r] of its 512 rows. `old_table`: each row names every device once: each device holds exactly one block of every request. `new_table`: each row names every device once: each device receives exactly one block of every request.
All inputs are finite; a program needn't handle non-finite values. No bound on the sum of `span_lens` or of `cached_lens` on one device may be relied on, other than what follows from the above.
Results may differ from the reference program's by a relative error of at most 0.012.
The reference program's roundings to bfloat16 on the way count: a program that leaves them out, or rounds other values in their place, can miss the bound.
Values may be sent and summed in bfloat16 or wider, within the bound.
No kernel may reach another device: no remote copies, remote signals or barrier semaphores. Data moves between devices by JAX's collectives and lax.ppermute only.
A program may use at most 128 MiB of HBM per device.

```python
import math
import jax
import jax.numpy as jnp
import numpy as np
from jax import lax

D = 2048
HEADS = 16
HD = 128
TOK_DEV = 512
CAP = 2048
REQS = 8
TOKENS = 4096
BLK = 256
SLOTS = 64
N_SEQ = 8
N_TP = 4


def draw_old_cache(key, part):
    first = jax.random.fold_in(jax.random.fold_in(key, 17), 0)
    base = jnp.clip(jax.random.normal(first, (SLOTS, BLK, 2 * HD), jnp.float32), -6.0, 6.0)
    return base.astype(jnp.bfloat16)


def block_levels(rng, dims, cuts, smallest, high):
    level = 1.0
    for axis_at, parts in cuts:
        steps = jax.random.uniform(jax.random.fold_in(jax.random.fold_in(rng, 6), axis_at), (parts,), jnp.float32, smallest / len(cuts), high / len(cuts))
        level = level * jnp.repeat(jnp.exp(steps), dims[axis_at] // parts).reshape((-1,) + (1,) * (len(dims) - 1 - axis_at))
    return level


def length_profile(amount, total, limit, slope):
    portions = [(1 << 20) // math.isqrt(standing ** slope) + 1 for standing in range(2, amount + 1)]
    surplus, given = total - limit - (amount - 1), [1] * (amount - 1)
    while surplus > 0:
        movable = [i for i in range(amount - 1) if given[i] < limit]
        whole, budget = sum([portions[i] for i in movable]), surplus
        for i in movable:
            more = min(limit - given[i], max(1, budget * portions[i] // whole), surplus)
            given[i] = given[i] + more
            surplus = surplus - more
    return np.array([limit] + given)


def uneven(stream_key, count, total, limit, skew):
    if count == 2:
        one = jax.random.randint(stream_key, (), max(1, total - limit), min(limit, total - 1) + 1)
        return jnp.stack([one, total - one])
    sizes = jnp.asarray(length_profile(count, total, limit, skew), jnp.int32)
    couples = (count - 1) // 2
    source_of, receiver = sizes[1:1 + 2 * couples:2], sizes[2:2 + 2 * couples:2]
    margin = jnp.minimum(source_of - 1, limit - receiver)
    passed = jax.random.randint(jax.random.fold_in(stream_key, 1), (couples,), 0, 1 << 20) % (margin + 1)
    sizes = sizes.at[1:1 + 2 * couples:2].set(source_of - passed).at[2:2 + 2 * couples:2].set(receiver + passed)
    return sizes[jax.random.permutation(jax.random.fold_in(stream_key, 2), count)]


def bell_draw(rng, extent, width, limit, cuts=(), held_as=jnp.bfloat16):
    result = jax.random.normal(rng, extent, jnp.float32) * width
    if len(cuts) > 0:
        result = block_levels(rng, extent, cuts, -0.22, 0.18) * result
    return jnp.clip(result, min=-limit, max=limit).astype(held_as)


def setup_inputs(seed: int = 0) -> dict:
    splits = jax.random.split(jax.random.key(seed), 11)
    tokens = bell_draw(splits[0], (TOKENS, D), 1.0, 6.0, ((0, 8), (1, 4)))
    norm_gain = jnp.clip(1.0 + 0.18 * jax.random.normal(splits[1], (D,), jnp.float32), 0.1, 1.9)
    w_query = bell_draw(splits[2], (D, HEADS * HD), D ** -0.5, 0.125, ((1, 4),))
    w_keyval = bell_draw(splits[3], (D, 2 * HD), D ** -0.5, 0.125)
    w_out = bell_draw(splits[4], (HEADS * HD, D), HD ** -0.5, 0.5, ((0, 4),))
    span_lens = uneven(splits[5], REQS, REQS * TOK_DEV * 3 // 4, TOK_DEV, 1).astype(jnp.int32)
    cached_lens = uneven(splits[6], REQS, REQS * (CAP - TOK_DEV) // 2, CAP - TOK_DEV, 1).astype(jnp.int32)
    old_table = jax.vmap(lambda own: jax.random.permutation(own, N_SEQ))(jax.random.split(splits[7], REQS)).reshape((REQS, N_SEQ)).astype(jnp.int32)
    new_table = jax.vmap(lambda own: jax.random.permutation(own, N_SEQ))(jax.random.split(splits[8], REQS)).reshape((REQS, N_SEQ)).astype(jnp.int32)
    old_cache = draw_old_cache(jax.random.fold_in(splits[10], 71), 0)
    return {"tokens": tokens, "norm_gain": norm_gain, "w_query": w_query, "w_keyval": w_keyval, "w_out": w_out, "span_lens": span_lens, "cached_lens": cached_lens, "old_table": old_table, "new_table": new_table, "old_cache": old_cache}


EPSILON = 1e-05
MASKED = -1e+30

def normalize(rows, norm_gain):
    values = rows.astype(jnp.float32)
    average = lax.optimization_barrier(jnp.mean(values, axis=1, keepdims=True))
    centred = values - average
    spread = lax.optimization_barrier(jnp.mean(centred * centred, axis=1, keepdims=True))
    return (centred * lax.rsqrt(spread + EPSILON) * norm_gain.astype(jnp.float32)).astype(jnp.bfloat16)

def reference(tokens, norm_gain, w_query, w_keyval, w_out, span_lens, cached_lens, old_table, new_table, old_cache):
    normed = normalize(tokens, norm_gain)
    query = jnp.dot(normed, w_query, preferred_element_type=jnp.float32).astype(jnp.bfloat16)
    keyval = jnp.dot(normed, w_keyval, preferred_element_type=jnp.float32).astype(jnp.bfloat16)
    pool = old_cache.reshape(N_SEQ, N_SEQ, BLK, 2 * HD)
    requests = jnp.arange(N_SEQ).astype(jnp.int32)
    cached = pool[old_table, requests[:, None]].reshape(N_SEQ, CAP, 2 * HD)
    group_width = HEADS * HD // N_TP

    def attend(items):
        query_rows, keyval_rows, cache_rows, token_rows, held_len, span_len = items
        placed = lax.dynamic_update_slice(cache_rows, keyval_rows, (held_len.astype(jnp.int32), jnp.int32(0)))
        positions = lax.broadcasted_iota(jnp.int32, (CAP, 1), 0)
        fresh = jnp.where(positions < held_len + span_len, placed, jnp.zeros_like(placed))
        keys = fresh[:, :HD].astype(jnp.float32)
        values = fresh[:, HD:].astype(jnp.float32)
        query3 = query_rows.reshape(TOK_DEV, HEADS, HD).astype(jnp.float32)
        scores = jnp.einsum('thd,kd->htk', query3, keys) * HD ** (-0.5)
        row_pos = lax.broadcasted_iota(jnp.int32, (TOK_DEV, 1), 0)
        key_pos = lax.broadcasted_iota(jnp.int32, (1, CAP), 1)
        allowed = key_pos <= held_len + row_pos
        scores = jnp.where(allowed[None], scores, MASKED)
        top = lax.optimization_barrier(jnp.max(scores, axis=2, keepdims=True))
        weights = jnp.exp(scores - top)
        probs = (weights / lax.optimization_barrier(jnp.sum(weights, axis=2, keepdims=True))).astype(jnp.bfloat16)
        context = jnp.einsum('htk,kd->thd', probs.astype(jnp.float32), values).astype(jnp.bfloat16)
        context = context.reshape(TOK_DEV, HEADS * HD)
        total = token_rows.astype(jnp.float32)
        for group in range(N_TP):
            part = jnp.dot(context[:, group * group_width:(group + 1) * group_width], w_out[group * group_width:(group + 1) * group_width], preferred_element_type=jnp.float32).astype(jnp.bfloat16)
            part = lax.optimization_barrier(part)
            total = total + part.astype(jnp.float32)
        mixed_rows = jnp.where(row_pos < span_len, total, jnp.zeros_like(total)).astype(jnp.bfloat16)
        return (fresh, mixed_rows)
    fresh_all, mixed_all = lax.map(attend, (query.reshape(N_SEQ, TOK_DEV, HEADS * HD), keyval.reshape(N_SEQ, TOK_DEV, 2 * HD), cached, tokens.reshape(N_SEQ, TOK_DEV, D), cached_lens, span_lens))
    layout = jnp.zeros((N_SEQ, N_SEQ, BLK, 2 * HD), jnp.bfloat16)
    layout = layout.at[new_table, requests[:, None]].set(fresh_all.reshape(N_SEQ, N_SEQ, BLK, 2 * HD))
    return (mixed_all.reshape(TOKENS, D), layout.reshape(SLOTS, BLK, 2 * HD))
```

```python
import functools
import math

import jax
import jax.numpy as jnp
from jax import lax
from jax.experimental import pallas as pl
from jax.experimental.pallas import tpu as pltpu
from jax.sharding import PartitionSpec as P

EPSILON = 1e-05
MASKED = -1e30
CHUNKS = 2
ROW_TILE = 128
NORM_ROWS = 64
F32 = jnp.float32
BF16 = jnp.bfloat16

VMEM = pl.BlockSpec(memory_space=pltpu.VMEM)
SMEM = pl.BlockSpec(memory_space=pltpu.SMEM)


def dot(a, b):
    return lax.dot_general(a, b, (((1,), (0,)), ((), ())), preferred_element_type=F32)


def dot_t(a, b):
    return lax.dot_general(a, b, (((1,), (1,)), ((), ())), preferred_element_type=F32)


def order_kernel(share, table_ref, arrived_ref, out_ref):
    rows, count = out_ref.shape[0], arrived_ref.shape[0]
    row = lax.broadcasted_iota(jnp.int32, (rows, 128), 0)
    block = row // share
    holder = jnp.zeros_like(block)
    for b in range(rows // share):
        holder = jnp.where(block == b, table_ref[0, b], holder)
    index = (holder * share + row % share)[:, :1]
    column = lax.broadcasted_iota(jnp.int32, (rows, count), 1)
    pick = jnp.where(column == index, 1.0, 0.0).astype(BF16)
    out_ref[...] = dot(pick, arrived_ref[...]).astype(BF16)


def extend_kernel(share, block_rows, old_ref, new_ref, held_ref, span_ref, arrived_ref, *refs):
    kv_refs, out_ref = refs[:-1], refs[-1]
    rows = arrived_ref.shape[0]
    groups = rows // share
    held, span = held_ref[0], span_ref[0]
    row = lax.broadcasted_iota(jnp.int32, (rows, 128), 0)
    target = row // share
    block, holder = jnp.zeros_like(row), jnp.zeros_like(row)
    for b in range(groups):
        hit = target == new_ref[0, b]
        block = jnp.where(hit, b, block)
        holder = jnp.where(hit, old_ref[0, b], holder)
    position = block * block_rows + lax.axis_index("tp") * share + row % share
    old_row = jnp.where(position < held, holder * share + row % share, -1)[:, :1]
    fresh = position - held
    new_row = jnp.where((fresh >= 0) & (fresh < span), fresh, -1)[:, :1]
    column = lax.broadcasted_iota(jnp.int32, (rows, rows), 1)
    total = dot(jnp.where(column == old_row, 1.0, 0.0).astype(BF16), arrived_ref[...])
    at = 0
    for kv_ref in kv_refs:
        count = kv_ref.shape[0]
        column = lax.broadcasted_iota(jnp.int32, (rows, count), 1) + at
        total += dot(jnp.where(column == new_row, 1.0, 0.0).astype(BF16), kv_ref[...])
        at += count
    out_ref[...] = total.astype(BF16)


def project_kernel(x0, x1, x2, x3, gain_ref, wq_ref, wkv_ref, q_ref, kv_ref, normed):
    pieces = (x0, x1, x2, x3)
    me = lax.axis_index("tp")
    rows, width = x0.shape
    features = width * len(pieces)

    def norm(step, carry):
        at = pl.ds(pl.multiple_of(step * NORM_ROWS, NORM_ROWS), NORM_ROWS)
        values = [piece[at, :].astype(F32) for piece in pieces]
        average = sum(jnp.sum(v, axis=1, keepdims=True) for v in values) / features
        centred = [v - average for v in values]
        spread = sum(jnp.sum(v * v, axis=1, keepdims=True) for v in centred) / features
        scale = lax.rsqrt(spread + EPSILON)
        for j, v in enumerate(centred):
            normed[j, at, :] = (v * scale * gain_ref[me ^ j]).astype(BF16)
        return carry

    lax.fori_loop(0, rows // NORM_ROWS, norm, 0)
    q_ref[...] = sum(dot(normed[j], wq_ref[me ^ j]) for j in range(len(pieces))).astype(BF16)
    kv_ref[...] = sum(dot(normed[j], wkv_ref[me ^ j]) for j in range(len(pieces))).astype(BF16)


def attend_kernel(share, block_rows, held_ref, q_ref, c0, c1, c2, c3, wout_ref, *refs):
    kv_refs, (far_ref, near_ref, keys, values, context) = refs[:-5], refs[-5:]
    pieces = (c0, c1, c2, c3)
    me = lax.axis_index("tp")
    held = held_ref[0]
    rows = q_ref.shape[0]
    piece_rows, width = c0.shape
    hd = width // 2
    heads = q_ref.shape[1] // hd
    cached = piece_rows * len(pieces)
    before = sum(ref.shape[0] for ref in kv_refs) - rows
    ones = jnp.ones((piece_rows, hd), BF16)

    spare = kv_refs[0][0:1, :hd]
    row = lax.broadcasted_iota(jnp.int32, (piece_rows, hd), 0)
    place = row // share * block_rows + row % share
    for j, piece in enumerate(pieces):
        at = pl.ds(j * piece_rows, piece_rows)
        used = place + (me ^ j) * share < held
        keys[at, :] = jnp.where(used, piece[:, :hd].astype(F32), spare.astype(F32)).astype(BF16)
        values[at, hd:] = jnp.where(used, piece[:, hd:].astype(F32), 0.0).astype(BF16)
        values[at, :hd] = jnp.where(used, 1.0, 0.0).astype(BF16)
    top = cached
    for ref in kv_refs:
        at = pl.ds(top, ref.shape[0])
        keys[at, :] = ref[:, :hd]
        values[at, hd:] = ref[:, hd:]
        values[at, :hd] = ones[:1].astype(F32).astype(BF16) * jnp.ones((ref.shape[0], hd), BF16)
        top += ref.shape[0]

    factor = hd ** (-0.5) * math.log2(math.e)
    tile = min(ROW_TILE, rows)
    for start in range(0, rows, tile):
        stop = cached + before + start
        q4 = jnp.concatenate(
            [q_ref[pl.ds(start, tile), h * hd : (h + 1) * hd] for h in range(heads)], axis=0
        )
        done = dot_t(q4, keys[pl.ds(0, stop), :])
        last = dot_t(q4, keys[pl.ds(stop, tile), :])
        own = lax.broadcasted_iota(jnp.int32, (heads * tile, tile), 0) % tile
        other = lax.broadcasted_iota(jnp.int32, (heads * tile, tile), 1)
        last = jnp.where(other <= own, last, MASKED)
        high = jnp.maximum(
            jnp.max(done, axis=1, keepdims=True), jnp.max(last, axis=1, keepdims=True)
        )
        p_done = jnp.exp2((done - high) * factor).astype(BF16)
        p_last = jnp.exp2((last - high) * factor).astype(BF16)
        both = dot(p_done, values[pl.ds(0, stop), :]) + dot(p_last, values[pl.ds(stop, tile), :])
        out = (both[:, hd:] / both[:, :hd]).astype(BF16)
        for h in range(heads):
            context[pl.ds(start, tile), h * hd : (h + 1) * hd] = out[h * tile : (h + 1) * tile]

    share_cols = wout_ref.shape[1] // 4
    for k in range(4):
        columns = pl.ds(pl.multiple_of((me ^ k) * share_cols, share_cols), share_cols)
        part = dot(context[...], wout_ref[:, columns]).astype(BF16)
        if k & 1:
            far_ref[k >> 1] = part
        else:
            near_ref[k >> 1] = part


def call(kernel, out_shape, in_specs, args, flops, scratch=(), exps=0, name=None):
    outs = out_shape if isinstance(out_shape, (list, tuple)) else [out_shape]
    moved = sum(a.size * a.dtype.itemsize for a in list(args) + list(outs))
    return pl.pallas_call(
        kernel,
        out_shape=out_shape,
        in_specs=in_specs,
        out_specs=jax.tree.map(lambda _: VMEM, out_shape),
        scratch_shapes=list(scratch),
        cost_estimate=pl.CostEstimate(flops=flops, bytes_accessed=moved, transcendentals=exps),
        compiler_params=pltpu.CompilerParams(vmem_limit_bytes=32 * 1024 * 1024),
        name=name,
    )(*args)


def body(
    tokens,
    norm_gain,
    w_query,
    w_keyval,
    w_out,
    span_lens,
    cached_lens,
    old_table,
    new_table,
    old_cache,
):
    tp = lax.axis_size("tp")
    groups, share, width = old_cache.shape
    block_rows = share * tp
    capacity = groups * block_rows
    rows, cols = tokens.shape
    q_cols = w_query.shape[1]
    features = w_query.shape[0]
    hd = width // 2
    most_held = capacity - rows
    piece_rows = most_held // tp

    def swap(x, bit):
        return lax.ppermute(x, "tp", [(i, i ^ bit) for i in range(tp)])

    with jax.named_scope("tokens_gather"):
        part = rows // CHUNKS
        own = [tokens[c * part : (c + 1) * part] for c in range(CHUNKS)]
        across = [swap(x, 2) for x in own]
        beside = [swap(x, 1) for x in own]
        corner = [swap(x, 1) for x in across]

    with jax.named_scope("cache_gather"):
        arrived = lax.all_to_all(old_cache, "seq", split_axis=0, concat_axis=0, tiled=True)
        arrived = arrived.reshape(groups * share, width)
        ordered = call(
            functools.partial(order_kernel, share),
            jax.ShapeDtypeStruct((piece_rows, width), BF16),
            [SMEM, VMEM],
            (old_table, arrived),
            flops=2 * piece_rows * groups * share * width,
            name="order",
        )
        c_across = swap(ordered, 2)
        cached = (ordered, swap(ordered, 1), c_across, swap(c_across, 1))

    gain = norm_gain.reshape(tp, 1, cols)
    wq = w_query.reshape(tp, cols, q_cols)
    wkv = w_keyval.reshape(tp, cols, width)
    queries, keyvals = [], []
    with jax.named_scope("project"):
        for c in range(CHUNKS):
            q, kv = call(
                project_kernel,
                [
                    jax.ShapeDtypeStruct((part, q_cols), BF16),
                    jax.ShapeDtypeStruct((part, width), BF16),
                ],
                [VMEM] * 7,
                (own[c], beside[c], across[c], corner[c], gain, wq, wkv),
                flops=2 * part * features * (q_cols + width),
                scratch=[pltpu.VMEM((tp, part, cols), BF16)],
                name="project",
            )
            queries.append(q)
            keyvals.append(kv)

    with jax.named_scope("extend"):
        sent = call(
            functools.partial(extend_kernel, share, block_rows),
            jax.ShapeDtypeStruct((groups * share, width), BF16),
            [SMEM] * 4 + [VMEM] * (1 + CHUNKS),
            (old_table, new_table, cached_lens, span_lens, arrived, *keyvals),
            flops=4 * groups * share * groups * share * width,
            name="extend",
        )
        new_cache = lax.all_to_all(
            sent.reshape(groups, share, width), "seq", split_axis=0, concat_axis=0, tiled=True
        )

    mixed = []
    for c in range(CHUNKS):
        with jax.named_scope("attend"):
            seen = most_held + (c + 1) * part
            far, near = call(
                functools.partial(attend_kernel, share, block_rows),
                [jax.ShapeDtypeStruct((2, part, cols), BF16)] * 2,
                [SMEM] + [VMEM] * (6 + c + 1),
                (cached_lens, queries[c], *cached, w_out, *keyvals[: c + 1]),
                flops=4 * part * seen * q_cols + 2 * part * q_cols * features,
                exps=part * seen * (q_cols // hd),
                scratch=[
                    pltpu.VMEM((seen, hd), BF16),
                    pltpu.VMEM((seen, width), BF16),
                    pltpu.VMEM((part, q_cols), BF16),
                ],
                name="attend",
            )
        with jax.named_scope("reduce"):
            got = swap(far[1], 1)
            pair = (near[1].astype(F32) + got.astype(F32)).astype(BF16)
            crossed = swap(pair, 2)
            kept = near[0].astype(F32) + swap(far[0], 1).astype(F32)
            total = own[c].astype(F32) + (kept + crossed.astype(F32))
            row = lax.broadcasted_iota(jnp.int32, (part, 1), 0) + c * part
            mixed.append(jnp.where(row < span_lens[0], total, 0.0).astype(BF16))
    return (jnp.concatenate(mixed, axis=0), new_cache)


def solution(mesh):
    in_specs = (
        P("seq", "tp"),
        P(),
        P(None, "tp"),
        P(),
        P("tp", None),
        P("seq"),
        P("seq"),
        P("seq", None),
        P("seq", None),
        P("seq", "tp", None),
    )
    out_specs = (P("seq", "tp"), P("seq", "tp", None))
    return jax.shard_map(body, mesh=mesh, in_specs=in_specs, out_specs=out_specs, check_vma=False)
```

```python
import functools
import math

import jax
import jax.numpy as jnp
from jax import lax
from jax.experimental import pallas as pl
from jax.experimental.pallas import tpu as pltpu
from jax.sharding import PartitionSpec as P

EPSILON = 1e-05
MASKED = -1e30
CHUNKS = 2
ROW_TILE = 128
NORM_ROWS = 64
F32 = jnp.float32
BF16 = jnp.bfloat16

VMEM = pl.BlockSpec(memory_space=pltpu.VMEM)
SMEM = pl.BlockSpec(memory_space=pltpu.SMEM)


def dot(a, b):
    return lax.dot_general(a, b, (((1,), (0,)), ((), ())), preferred_element_type=F32)


def dot_t(a, b):
    return lax.dot_general(a, b, (((1,), (1,)), ((), ())), preferred_element_type=F32)


def pack_kernel(cache_ref, *out_refs):
    me = lax.axis_index("seq")
    for k, out_ref in enumerate(out_refs):
        out_ref[...] = cache_ref[me ^ (k + 1)]


def order_kernel(share, swapped, table_ref, cache_ref, *refs):
    arrived, me = gathered(swapped, cache_ref, refs[:-1])
    out_ref = refs[-1]
    rows, count = out_ref.shape[0], arrived.shape[0]
    row = lax.broadcasted_iota(jnp.int32, (rows, 128), 0)
    block = row // share
    holder = jnp.zeros_like(block)
    for b in range(rows // share):
        holder = jnp.where(block == b, table_ref[0, b] ^ me, holder)
    index = (holder * share + row % share)[:, :1]
    column = lax.broadcasted_iota(jnp.int32, (rows, count), 1)
    pick = jnp.where(column == index, 1.0, 0.0).astype(BF16)
    out_ref[...] = dot(pick, arrived).astype(BF16)


def gathered(swapped, cache_ref, refs):
    if swapped:
        me = lax.axis_index("seq")
        return jnp.concatenate([cache_ref[me]] + [ref[...] for ref in refs], axis=0), me
    return refs[0][...], 0


def extend_kernel(
    share, block_rows, swapped, old_ref, new_ref, held_ref, span_ref, kv_ref, cache_ref, *refs
):
    arrived_refs = refs[: len(refs) // 2] if swapped else refs[:1]
    out_refs = refs[len(arrived_refs) :]
    arrived, me = gathered(swapped, cache_ref, arrived_refs)
    rows = arrived.shape[0]
    groups = rows // share
    held, span = held_ref[0], span_ref[0]
    row = lax.broadcasted_iota(jnp.int32, (rows, 128), 0)
    target = row // share
    block, holder = jnp.zeros_like(row), jnp.zeros_like(row)
    for b in range(groups):
        hit = target == new_ref[0, b] ^ me
        block = jnp.where(hit, b, block)
        holder = jnp.where(hit, old_ref[0, b] ^ me, holder)
    position = block * block_rows + lax.axis_index("tp") * share + row % share
    old_row = jnp.where(position < held, holder * share + row % share, -1)[:, :1]
    fresh = position - held
    new_row = jnp.where((fresh >= 0) & (fresh < span), fresh, -1)[:, :1]
    column = lax.broadcasted_iota(jnp.int32, (rows, rows), 1)
    total = dot(jnp.where(column == old_row, 1.0, 0.0).astype(BF16), arrived)
    column = lax.broadcasted_iota(jnp.int32, (rows, kv_ref.shape[0]), 1)
    total += dot(jnp.where(column == new_row, 1.0, 0.0).astype(BF16), kv_ref[...])
    total = total.astype(BF16)
    count = rows // len(out_refs)
    for k, out_ref in enumerate(out_refs):
        out_ref[...] = total[k * count : (k + 1) * count]


def unpack_kernel(*refs):
    me = lax.axis_index("seq")
    for k, ref in enumerate(refs[:-1]):
        refs[-1][me ^ k] = ref[...]


def project_kernel(x0, x1, x2, x3, gain_ref, wq_ref, wkv_ref, q_ref, kv_ref, normed):
    pieces = (x0, x1, x2, x3)
    me = lax.axis_index("tp")
    rows, width = x0.shape
    features = width * len(pieces)

    def norm(step, carry):
        at = pl.ds(pl.multiple_of(step * NORM_ROWS, NORM_ROWS), NORM_ROWS)
        values = [piece[at, :].astype(F32) for piece in pieces]
        average = sum(jnp.sum(v, axis=1, keepdims=True) for v in values) / features
        centred = [v - average for v in values]
        spread = sum(jnp.sum(v * v, axis=1, keepdims=True) for v in centred) / features
        scale = lax.rsqrt(spread + EPSILON)
        for j, v in enumerate(centred):
            normed[j, at, :] = (v * scale * gain_ref[me ^ j]).astype(BF16)
        return carry

    lax.fori_loop(0, rows // NORM_ROWS, norm, 0)
    q_ref[...] = sum(dot(normed[j], wq_ref[me ^ j]) for j in range(len(pieces))).astype(BF16)
    kv_ref[...] = sum(dot(normed[j], wkv_ref[me ^ j]) for j in range(len(pieces))).astype(BF16)


def attend_kernel(share, block_rows, start_row, rows, held_ref, q_ref, kv_ref, c0, c1, c2, c3, *refs):
    wout_ref, far_refs, near_refs, (keys, values, context) = refs[0], refs[1:3], refs[3:5], refs[5:]
    pieces = (c0, c1, c2, c3)
    me = lax.axis_index("tp")
    held = held_ref[0]
    piece_rows, width = c0.shape
    hd = width // 2
    heads = q_ref.shape[1] // hd
    cached = piece_rows * len(pieces)
    known = start_row + rows

    spare = kv_ref[0:1, :hd].astype(F32)
    row = lax.broadcasted_iota(jnp.int32, (piece_rows, hd), 0)
    place = row // share * block_rows + row % share
    for j, piece in enumerate(pieces):
        at = pl.ds(j * piece_rows, piece_rows)
        used = place + (me ^ j) * share < held
        keys[at, :] = jnp.where(used, piece[:, :hd].astype(F32), spare).astype(BF16)
        values[at, hd:] = jnp.where(used, piece[:, hd:].astype(F32), 0.0).astype(BF16)
        values[at, :hd] = jnp.where(used, 1.0, 0.0).astype(BF16)
    at = pl.ds(cached, known)
    keys[at, :] = kv_ref[:known, :hd]
    values[at, hd:] = kv_ref[:known, hd:]
    values[at, :hd] = jnp.ones((known, hd), BF16)

    factor = hd ** (-0.5) * math.log2(math.e)
    tile = min(ROW_TILE, rows)
    for start in range(0, rows, tile):
        stop = cached + start_row + start
        q4 = jnp.concatenate(
            [
                q_ref[pl.ds(start_row + start, tile), h * hd : (h + 1) * hd]
                for h in range(heads)
            ],
            axis=0,
        )
        done = dot_t(q4, keys[pl.ds(0, stop), :])
        last = dot_t(q4, keys[pl.ds(stop, tile), :])
        own = lax.broadcasted_iota(jnp.int32, (heads * tile, tile), 0) % tile
        other = lax.broadcasted_iota(jnp.int32, (heads * tile, tile), 1)
        last = jnp.where(other <= own, last, MASKED)
        high = jnp.maximum(
            jnp.max(done, axis=1, keepdims=True), jnp.max(last, axis=1, keepdims=True)
        )
        p_done = jnp.exp2((done - high) * factor).astype(BF16)
        p_last = jnp.exp2((last - high) * factor).astype(BF16)
        both = dot(p_done, values[pl.ds(0, stop), :]) + dot(p_last, values[pl.ds(stop, tile), :])
        out = (both[:, hd:] / both[:, :hd]).astype(BF16)
        for h in range(heads):
            context[pl.ds(start, tile), h * hd : (h + 1) * hd] = out[h * tile : (h + 1) * tile]

    cols = wout_ref.shape[1] // 4
    for k in (3, 1, 2, 0):
        columns = pl.ds(pl.multiple_of((me ^ k) * cols, cols), cols)
        part = dot(context[...], wout_ref[:, columns]).astype(BF16)
        if k & 1:
            far_refs[k >> 1][...] = part
        else:
            near_refs[k >> 1][...] = part


def finish_kernel(rows, at, span_ref, tokens_ref, near_ref, got_ref, crossed_ref, *refs):
    out_ref = refs[-1]
    kept = near_ref[...].astype(F32) + got_ref[...].astype(F32)
    total = tokens_ref[...].astype(F32) + (kept + crossed_ref[...].astype(F32))
    row = lax.broadcasted_iota(jnp.int32, total.shape, 0) + at
    out_ref[...] = jnp.where(row < span_ref[0], total, 0.0).astype(BF16)


def call(kernel, out_shape, in_specs, args, flops, scratch=(), exps=0, name=None):
    outs = out_shape if isinstance(out_shape, (list, tuple)) else [out_shape]
    moved = sum(a.size * a.dtype.itemsize for a in list(args) + list(outs))
    return pl.pallas_call(
        kernel,
        out_shape=out_shape,
        in_specs=in_specs,
        out_specs=jax.tree.map(lambda _: VMEM, out_shape),
        scratch_shapes=list(scratch),
        cost_estimate=pl.CostEstimate(flops=flops, bytes_accessed=moved, transcendentals=exps),
        compiler_params=pltpu.CompilerParams(vmem_limit_bytes=32 * 1024 * 1024),
        name=name,
    )(*args)


def body(
    tokens,
    norm_gain,
    w_query,
    w_keyval,
    w_out,
    span_lens,
    cached_lens,
    old_table,
    new_table,
    old_cache,
):
    tp = lax.axis_size("tp")
    groups, share, width = old_cache.shape
    block_rows = share * tp
    capacity = groups * block_rows
    rows, cols = tokens.shape
    q_cols = w_query.shape[1]
    features = w_query.shape[0]
    hd = width // 2
    most_held = capacity - rows
    piece_rows = most_held // tp

    def swap(x, bit, axis="tp"):
        size = lax.axis_size(axis)
        return lax.ppermute(x, axis, [(i, i ^ bit) for i in range(size)])

    swapped = groups <= 8 and groups & (groups - 1) == 0
    block = jax.ShapeDtypeStruct((share, width), BF16)

    with jax.named_scope("tokens_gather"):
        across = swap(tokens, 2)
        beside = swap(tokens, 1)
        corner = swap(across, 1)

    with jax.named_scope("cache_gather"):
        if swapped:
            packed = call(
                pack_kernel, [block] * (groups - 1), [VMEM], (old_cache,), flops=0, name="pack"
            )
            arrived = [swap(x, k + 1, "seq") for k, x in enumerate(packed)]
        else:
            arrived = lax.all_to_all(old_cache, "seq", split_axis=0, concat_axis=0, tiled=True)
            arrived = [arrived.reshape(groups * share, width)]
        ordered = call(
            functools.partial(order_kernel, share, swapped),
            jax.ShapeDtypeStruct((piece_rows, width), BF16),
            [SMEM, VMEM] + [VMEM] * len(arrived),
            (old_table, old_cache, *arrived),
            flops=2 * piece_rows * groups * share * width,
            name="order",
        )
        c_across = swap(ordered, 2)
        cached = (ordered, swap(ordered, 1), c_across, swap(c_across, 1))

    with jax.named_scope("project"):
        query, keyval = call(
            project_kernel,
            [
                jax.ShapeDtypeStruct((rows, q_cols), BF16),
                jax.ShapeDtypeStruct((rows, width), BF16),
            ],
            [VMEM] * 7,
            (
                tokens,
                beside,
                across,
                corner,
                norm_gain.reshape(tp, 1, cols),
                w_query.reshape(tp, cols, q_cols),
                w_keyval.reshape(tp, cols, width),
            ),
            flops=2 * rows * features * (q_cols + width),
            scratch=[pltpu.VMEM((tp, rows, cols), BF16)],
            name="project",
        )

    with jax.named_scope("extend"):
        sent = call(
            functools.partial(extend_kernel, share, block_rows, swapped),
            [block] * groups if swapped else [jax.ShapeDtypeStruct((groups * share, width), BF16)],
            [SMEM] * 4 + [VMEM] * (2 + len(arrived)),
            (old_table, new_table, cached_lens, span_lens, keyval, old_cache, *arrived),
            flops=4 * groups * share * groups * share * width,
            name="extend",
        )
        if swapped:
            returned = [swap(x, k, "seq") if k else x for k, x in enumerate(sent)]
            new_cache = call(
                unpack_kernel,
                jax.ShapeDtypeStruct(old_cache.shape, BF16),
                [VMEM] * groups,
                returned,
                flops=0,
                name="unpack",
            )
        else:
            new_cache = lax.all_to_all(
                sent[0].reshape(groups, share, width), "seq", split_axis=0, concat_axis=0, tiled=True
            )

    part = rows // CHUNKS
    mixed = None
    for c in range(CHUNKS):
        with jax.named_scope("attend"):
            seen = most_held + (c + 1) * part
            far0, far1, near0, near1 = call(
                functools.partial(attend_kernel, share, block_rows, c * part, part),
                [jax.ShapeDtypeStruct((part, cols), BF16)] * 4,
                [SMEM] + [VMEM] * 7,
                (cached_lens, query, keyval, *cached, w_out),
                flops=4 * part * seen * q_cols + 2 * part * q_cols * features,
                exps=part * seen * (q_cols // hd),
                scratch=[
                    pltpu.VMEM((seen, hd), BF16),
                    pltpu.VMEM((seen, width), BF16),
                    pltpu.VMEM((part, q_cols), BF16),
                ],
                name="attend",
            )
        with jax.named_scope("reduce"):
            got1 = swap(far1, 1)
            pair = (near1.astype(F32) + got1.astype(F32)).astype(BF16)
            crossed = swap(pair, 2)
            got0 = swap(far0, 1)
            rows_at = pl.BlockSpec((part, cols), lambda i, c=c: (c, 0))
            whole = pl.BlockSpec((part, cols), lambda i: (0, 0))
            mixed = pl.pallas_call(
                functools.partial(finish_kernel, part, c * part),
                grid=(1,),
                out_shape=jax.ShapeDtypeStruct((rows, cols), BF16),
                in_specs=[SMEM, rows_at, whole, whole, whole]
                + [pl.BlockSpec(memory_space=pl.ANY)] * (c > 0),
                out_specs=rows_at,
                input_output_aliases={5: 0} if c else {},
                cost_estimate=pl.CostEstimate(
                    flops=4 * part * cols, bytes_accessed=10 * part * cols, transcendentals=0
                ),
                name="finish",
            )(span_lens, tokens, near0, got0, crossed, *([mixed] if c else []))
    return (mixed, new_cache)


def solution(mesh):
    in_specs = (
        P("seq", "tp"),
        P(),
        P(None, "tp"),
        P(),
        P("tp", None),
        P("seq"),
        P("seq"),
        P("seq", None),
        P("seq", None),
        P("seq", "tp", None),
    )
    out_specs = (P("seq", "tp"), P("seq", "tp", None))
    return jax.shard_map(body, mesh=mesh, in_specs=in_specs, out_specs=out_specs, check_vma=False)
```

```python
import functools
import math

import jax
import jax.numpy as jnp
from jax import lax
from jax.experimental import pallas as pl
from jax.experimental.pallas import tpu as pltpu
from jax.sharding import PartitionSpec as P

EPSILON = 1e-05
MASKED = -1e30
CHUNKS = 2
ROW_TILE = 128
KEY_TILE = 128
NORM_STEPS = 4
F32 = jnp.float32
BF16 = jnp.bfloat16

VMEM = pl.BlockSpec(memory_space=pltpu.VMEM)
SMEM = pl.BlockSpec(memory_space=pltpu.SMEM)
HBM = pl.BlockSpec(memory_space=pltpu.HBM)


def dot(a, b):
    return lax.dot_general(a, b, (((1,), (0,)), ((), ())), preferred_element_type=F32)


def dot_t(a, b):
    return lax.dot_general(a, b, (((1,), (1,)), ((), ())), preferred_element_type=F32)


def order_kernel(share, table_ref, arrived_ref, out_ref):
    rows, count = out_ref.shape[0], arrived_ref.shape[0]
    row = lax.broadcasted_iota(jnp.int32, (rows, 128), 0)
    block = row // share
    holder = jnp.zeros_like(block)
    for b in range(rows // share):
        holder = jnp.where(block == b, table_ref[0, b], holder)
    index = (holder * share + row % share)[:, :1]
    column = lax.broadcasted_iota(jnp.int32, (rows, count), 1)
    pick = jnp.where(column == index, 1.0, 0.0).astype(BF16)
    out_ref[...] = dot(pick, arrived_ref[...]).astype(BF16)


def extend_kernel(
    share, block_rows, old_ref, new_ref, held_ref, span_ref, arrived_ref, kv_ref, out_ref
):
    rows = arrived_ref.shape[0]
    held, span = held_ref[0], span_ref[0]
    row = lax.broadcasted_iota(jnp.int32, (rows, 128), 0)
    target = row // share
    block, holder = jnp.zeros_like(row), jnp.zeros_like(row)
    for b in range(rows // share):
        hit = target == new_ref[0, b]
        block = jnp.where(hit, b, block)
        holder = jnp.where(hit, old_ref[0, b], holder)
    position = block * block_rows + lax.axis_index("tp") * share + row % share
    old_row = jnp.where(position < held, holder * share + row % share, -1)[:, :1]
    fresh = position - held
    new_row = jnp.where((fresh >= 0) & (fresh < span), fresh, -1)[:, :1]
    column = lax.broadcasted_iota(jnp.int32, (rows, rows), 1)
    total = dot(jnp.where(column == old_row, 1.0, 0.0).astype(BF16), arrived_ref[...])
    column = lax.broadcasted_iota(jnp.int32, (rows, kv_ref.shape[0]), 1)
    total += dot(jnp.where(column == new_row, 1.0, 0.0).astype(BF16), kv_ref[...])
    out_ref[...] = total.astype(BF16)


def project_kernel(
    x0, x1, x2, x3, gain_ref, wq_hbm, wkv_hbm, q_ref, kv_ref, normed, wq, wkv, q_acc, kv_acc, sems
):
    pieces = (x0, x1, x2, x3)
    me = lax.axis_index("tp")
    rows, width = x0.shape
    features = width * len(pieces)
    half = rows // 2
    step_rows = half // NORM_STEPS
    loads = [
        pltpu.make_async_copy(wq_hbm, wq, sems.at[0]),
        pltpu.make_async_copy(wkv_hbm, wkv, sems.at[1]),
    ]
    for load in loads:
        load.start()

    def norm(start):
        at = pl.ds(pl.multiple_of(start, step_rows), step_rows)
        values = [piece[at, :].astype(F32) for piece in pieces]
        average = jnp.sum(sum(values), axis=1, keepdims=True) / features
        centred = [v - average for v in values]
        spread = jnp.sum(sum(v * v for v in centred), axis=1, keepdims=True) / features
        scale = lax.rsqrt(spread + EPSILON)
        for j, v in enumerate(centred):
            normed[j, at, :] = (v * scale * gain_ref[me ^ j]).astype(BF16)

    def multiply(j, start):
        left = normed[j, pl.ds(start, half), :]
        q_acc[...] += dot(left, wq[me ^ j])
        kv_acc[...] += dot(left, wkv[me ^ j])

    def first(step, carry):
        norm(step * step_rows)
        return carry

    def both(step, carry):
        norm(half + step * step_rows)
        multiply(step, 0)
        return carry

    def last(step, carry):
        multiply(step, half)
        return carry

    lax.fori_loop(0, NORM_STEPS, first, 0)
    for load in loads:
        load.wait()
    for start, run in ((0, both), (half, last)):
        q_acc[...] = jnp.zeros_like(q_acc)
        kv_acc[...] = jnp.zeros_like(kv_acc)
        lax.fori_loop(0, len(pieces), run, 0)
        q_ref[pl.ds(start, half), :] = q_acc[...].astype(BF16)
        kv_ref[pl.ds(start, half), :] = kv_acc[...].astype(BF16)


def attend_kernel(
    share, block_rows, start_row, rows, held_ref, span_ref, q_ref, kv_ref, c0, c1, c2, c3, *refs
):
    wout_hbm, far_refs, near_refs = refs[0], refs[1:3], refs[3:5]
    keys, values, context, wout, sem = refs[5:]
    pieces = (c0, c1, c2, c3)
    me = lax.axis_index("tp")
    held, span = held_ref[0], span_ref[0]
    piece_rows, width = c0.shape
    hd = width // 2
    heads = q_ref.shape[1] // hd
    cached = piece_rows * len(pieces)
    known = start_row + rows
    load = pltpu.make_async_copy(wout_hbm, wout, sem)
    load.start()

    spare = kv_ref[0:1, :hd].astype(F32)
    row = lax.broadcasted_iota(jnp.int32, (KEY_TILE, hd), 0)
    place = row // share * block_rows + row % share
    group = KEY_TILE * len(pieces)
    for i in range(piece_rows // KEY_TILE):
        for j, piece in enumerate(pieces):
            at = pl.ds(i * group + j * KEY_TILE, KEY_TILE)
            source = pl.ds(i * KEY_TILE, KEY_TILE)
            used = place + (me ^ j) * share + i * group < held
            keys[at, :] = jnp.where(used, piece[source, :hd].astype(F32), spare).astype(BF16)
            values[at, hd:] = jnp.where(used, piece[source, hd:].astype(F32), 0.0).astype(BF16)
            values[at, :hd] = jnp.where(used, 1.0, 0.0).astype(BF16)
    at = pl.ds(cached, known)
    keys[at, :] = kv_ref[:known, :hd]
    values[at, hd:] = kv_ref[:known, hd:]
    values[at, :hd] = jnp.ones((known, hd), BF16)

    factor = hd ** (-0.5) * math.log2(math.e)
    tile = min(ROW_TILE, rows)

    def soften(start, used):
        parts = [pl.ds(0, used)]
        if start_row + start:
            parts.append(pl.ds(cached, start_row + start))
        own = pl.ds(cached + start_row + start, tile)
        q4 = jnp.concatenate(
            [
                q_ref[pl.ds(start_row + start, tile), h * hd : (h + 1) * hd]
                for h in range(heads)
            ],
            axis=0,
        )
        scores = [dot_t(q4, keys[part, :]) for part in parts]
        last = dot_t(q4, keys[own, :])
        to = lax.broadcasted_iota(jnp.int32, (heads * tile, tile), 0) % tile
        by = lax.broadcasted_iota(jnp.int32, (heads * tile, tile), 1)
        scores.append(jnp.where(by <= to, last, MASKED))
        high = functools.reduce(jnp.maximum, [jnp.max(s, axis=1, keepdims=True) for s in scores])
        both = sum(
            dot(jnp.exp2((s - high) * factor).astype(BF16), values[part, :])
            for s, part in zip(scores, parts + [own])
        )
        out = (both[:, hd:] / both[:, :hd]).astype(BF16)
        for h in range(heads):
            context[pl.ds(start, tile), h * hd : (h + 1) * hd] = out[h * tile : (h + 1) * tile]

    context[...] = jnp.zeros_like(context)
    for start in range(0, rows, tile):
        for used in range(group, cached + 1, group):
            fits = held <= used if used < cached else True
            needed = (held > used - group) & fits & (start_row + start < span)
            pl.when(needed)(functools.partial(soften, start, used))

    load.wait()
    cols = wout.shape[1] // 4
    for k in (3, 1, 2, 0):
        columns = pl.ds(pl.multiple_of((me ^ k) * cols, cols), cols)
        part = dot(context[...], wout[:, columns]).astype(BF16)
        if k & 1:
            far_refs[k >> 1][...] = part
        else:
            near_refs[k >> 1][...] = part


def finish_kernel(span_ref, tokens_ref, *refs):
    out_ref = refs[-1]
    part = refs[0].shape[0]
    for c in range(len(refs) // 3):
        near, got, crossed = refs[3 * c : 3 * c + 3]
        at = pl.ds(c * part, part)
        kept = near[...].astype(F32) + got[...].astype(F32)
        total = tokens_ref[at, :].astype(F32) + (kept + crossed[...].astype(F32))
        row = lax.broadcasted_iota(jnp.int32, total.shape, 0) + c * part
        out_ref[at, :] = jnp.where(row < span_ref[0], total, 0.0).astype(BF16)


def call(kernel, out_shape, in_specs, args, mib, scratch=(), name=None):
    return pl.pallas_call(
        kernel,
        out_shape=out_shape,
        in_specs=in_specs,
        out_specs=jax.tree.map(lambda _: VMEM, out_shape),
        scratch_shapes=list(scratch),
        cost_estimate=pl.CostEstimate(flops=1024, bytes_accessed=1024, transcendentals=0),
        compiler_params=pltpu.CompilerParams(vmem_limit_bytes=mib * 1024 * 1024),
        name=name,
    )(*args)


def body(
    tokens,
    norm_gain,
    w_query,
    w_keyval,
    w_out,
    span_lens,
    cached_lens,
    old_table,
    new_table,
    old_cache,
):
    tp = lax.axis_size("tp")
    groups, share, width = old_cache.shape
    block_rows = share * tp
    capacity = groups * block_rows
    rows, cols = tokens.shape
    q_cols = w_query.shape[1]
    features = w_query.shape[0]
    hd = width // 2
    most_held = capacity - rows
    piece_rows = most_held // tp

    def swap(x, bit):
        return lax.ppermute(x, "tp", [(i, i ^ bit) for i in range(tp)])

    def exchange(x):
        return lax.all_to_all(x, "seq", split_axis=0, concat_axis=0, tiled=True)

    with jax.named_scope("tokens_gather"):
        across = swap(tokens, 2)
        beside = swap(tokens, 1)
        corner = swap(across, 1)

    with jax.named_scope("cache_gather"):
        beside, stored = lax.optimization_barrier((beside, old_cache))
        arrived = exchange(stored).reshape(groups * share, width)

    with jax.named_scope("project"):
        query, keyval = call(
            project_kernel,
            [
                jax.ShapeDtypeStruct((rows, q_cols), BF16),
                jax.ShapeDtypeStruct((rows, width), BF16),
            ],
            [VMEM] * 5 + [HBM] * 2,
            (
                tokens,
                beside,
                across,
                corner,
                norm_gain.reshape(tp, 1, cols),
                w_query.reshape(tp, cols, q_cols),
                w_keyval.reshape(tp, cols, width),
            ),
            mib=24,
            scratch=[
                pltpu.VMEM((tp, rows, cols), BF16),
                pltpu.VMEM((tp, cols, q_cols), BF16),
                pltpu.VMEM((tp, cols, width), BF16),
                pltpu.VMEM((rows // 2, q_cols), F32),
                pltpu.VMEM((rows // 2, width), F32),
                pltpu.SemaphoreType.DMA((2,)),
            ],
            name="project",
        )

    with jax.named_scope("cache_gather"):
        keyval, arrived = lax.optimization_barrier((keyval, arrived))
        ordered = call(
            functools.partial(order_kernel, share),
            jax.ShapeDtypeStruct((piece_rows, width), BF16),
            [SMEM, VMEM],
            (old_table, arrived),
            mib=8,
            name="order",
        )
        c_across = swap(ordered, 2)
        c_beside = swap(ordered, 1)

    with jax.named_scope("extend"):
        kv_later, c_beside = lax.optimization_barrier((keyval, c_beside))
        sent = call(
            functools.partial(extend_kernel, share, block_rows),
            jax.ShapeDtypeStruct((groups * share, width), BF16),
            [SMEM] * 4 + [VMEM] * 2,
            (old_table, new_table, cached_lens, span_lens, arrived, kv_later),
            mib=8,
            name="extend",
        )
        sent, c_across = lax.optimization_barrier((sent, c_across))
        new_cache = exchange(sent.reshape(groups, share, width))
        cached = (ordered, c_beside, c_across, swap(c_across, 1))

    part = rows // CHUNKS
    sums = []
    for c in range(CHUNKS):
        with jax.named_scope("attend"):
            seen = most_held + (c + 1) * part
            far0, far1, near0, near1 = call(
                functools.partial(attend_kernel, share, block_rows, c * part, part),
                [jax.ShapeDtypeStruct((part, cols), BF16)] * 4,
                [SMEM] * 2 + [VMEM] * 6 + [HBM],
                (cached_lens, span_lens, query, keyval, *cached, w_out),
                    mib=24,
                scratch=[
                    pltpu.VMEM((seen, hd), BF16),
                    pltpu.VMEM((seen, width), BF16),
                    pltpu.VMEM((part, q_cols), BF16),
                    pltpu.VMEM(w_out.shape, BF16),
                    pltpu.SemaphoreType.DMA,
                ],
                name="attend",
            )
        with jax.named_scope("reduce"):
            got1 = swap(far1, 1)
            pair = (near1.astype(F32) + got1.astype(F32)).astype(BF16)
            query, pair = lax.optimization_barrier((query, pair))
            sums += [near0, swap(far0, 1), swap(pair, 2)]
    with jax.named_scope("finish"):
        mixed = call(
            finish_kernel,
            jax.ShapeDtypeStruct((rows, cols), BF16),
            [SMEM] + [VMEM] * (1 + len(sums)),
            (span_lens, tokens, *sums),
            mib=8,
            name="finish",
        )
    return (mixed, new_cache)


def solution(mesh):
    in_specs = (
        P("seq", "tp"),
        P(),
        P(None, "tp"),
        P(),
        P("tp", None),
        P("seq"),
        P("seq"),
        P("seq", None),
        P("seq", None),
        P("seq", "tp", None),
    )
    out_specs = (P("seq", "tp"), P("seq", "tp", None))
    return jax.shard_map(body, mesh=mesh, in_specs=in_specs, out_specs=out_specs, check_vma=False)
```

```python
import functools
import math

import jax
import jax.numpy as jnp
from jax import lax
from jax.experimental import pallas as pl
from jax.experimental.pallas import tpu as pltpu
from jax.sharding import PartitionSpec as P

EPSILON = 1e-05
MASKED = -1e30
CHUNKS = 2
ROW_TILE = 128
KEY_TILE = 128
NORM_ROWS = 128
SAFE = 60.0
F32 = jnp.float32
BF16 = jnp.bfloat16

VMEM = pl.BlockSpec(memory_space=pltpu.VMEM)
SMEM = pl.BlockSpec(memory_space=pltpu.SMEM)
HBM = pl.BlockSpec(memory_space=pltpu.HBM)


def dot(a, b):
    return lax.dot_general(a, b, (((1,), (0,)), ((), ())), preferred_element_type=F32)


def dot_t(a, b):
    return lax.dot_general(a, b, (((1,), (1,)), ((), ())), preferred_element_type=F32)


def order_kernel(share, table_ref, arrived_ref, out_ref):
    rows, count = out_ref.shape[0], arrived_ref.shape[0]
    row = lax.broadcasted_iota(jnp.int32, (rows, 128), 0)
    block = row // share
    holder = jnp.zeros_like(block)
    for b in range(rows // share):
        holder = jnp.where(block == b, table_ref[0, b], holder)
    index = (holder * share + row % share)[:, :1]
    column = lax.broadcasted_iota(jnp.int32, (rows, count), 1)
    pick = jnp.where(column == index, 1.0, 0.0).astype(BF16)
    out_ref[...] = dot(pick, arrived_ref[...]).astype(BF16)


def extend_kernel(
    share, block_rows, old_ref, new_ref, held_ref, span_ref, arrived_ref, kv_ref, out_ref
):
    rows = arrived_ref.shape[0]
    held, span = held_ref[0], span_ref[0]
    row = lax.broadcasted_iota(jnp.int32, (rows, 128), 0)
    target = row // share
    block, holder = jnp.zeros_like(row), jnp.zeros_like(row)
    for b in range(rows // share):
        hit = target == new_ref[0, b]
        block = jnp.where(hit, b, block)
        holder = jnp.where(hit, old_ref[0, b], holder)
    position = block * block_rows + lax.axis_index("tp") * share + row % share
    old_row = jnp.where(position < held, holder * share + row % share, -1)[:, :1]
    fresh = position - held
    new_row = jnp.where((fresh >= 0) & (fresh < span), fresh, -1)[:, :1]
    column = lax.broadcasted_iota(jnp.int32, (rows, rows), 1)
    total = dot(jnp.where(column == old_row, 1.0, 0.0).astype(BF16), arrived_ref[...])
    column = lax.broadcasted_iota(jnp.int32, (rows, kv_ref.shape[0]), 1)
    total += dot(jnp.where(column == new_row, 1.0, 0.0).astype(BF16), kv_ref[...])
    out_ref[...] = total.astype(BF16)


def project_kernel(
    x0, x1, x2, x3, gain_ref, wq_hbm, wkv_hbm, q_ref, kv_ref, normed, wq, wkv, sems
):
    pieces = (x0, x1, x2, x3)
    me = lax.axis_index("tp")
    rows, width = x0.shape
    features = width * len(pieces)
    loads = [
        pltpu.make_async_copy(wq_hbm, wq, sems.at[0]),
        pltpu.make_async_copy(wkv_hbm, wkv, sems.at[1]),
    ]
    for load in loads:
        load.start()

    def norm(at):
        values = [piece[at, :].astype(F32) for piece in pieces]
        average = jnp.sum(sum(values), axis=1, keepdims=True) / features
        centred = [v - average for v in values]
        spread = jnp.sum(sum(v * v for v in centred), axis=1, keepdims=True) / features
        scale = lax.rsqrt(spread + EPSILON)
        for j, v in enumerate(centred):
            normed[j, at, :] = (v * scale * gain_ref[me ^ j]).astype(BF16)

    half = rows // 2
    for start in range(0, rows, half):
        for step in range(start, start + half, NORM_ROWS):
            norm(pl.ds(step, NORM_ROWS))
        if start == 0:
            for load in loads:
                load.wait()
        at = pl.ds(start, half)
        left = [normed[j, at, :] for j in range(len(pieces))]
        q_ref[at, :] = sum(dot(x, wq[me ^ j]) for j, x in enumerate(left)).astype(BF16)
        kv_ref[at, :] = sum(dot(x, wkv[me ^ j]) for j, x in enumerate(left)).astype(BF16)


def attend_kernel(
    share, block_rows, start_row, rows, held_ref, span_ref, q_ref, kv_ref, c0, c1, c2, c3, *refs
):
    wout_hbm, far_refs, near_refs = refs[0], refs[1:3], refs[3:5]
    keys, values, stacked, total, high, context, wout, sem = refs[5:]
    pieces = (c0, c1, c2, c3)
    me = lax.axis_index("tp")
    held, span = held_ref[0], span_ref[0]
    piece_rows, width = c0.shape
    hd = width // 2
    heads = q_ref.shape[1] // hd
    cached = piece_rows * len(pieces)
    known = start_row + rows
    load = pltpu.make_async_copy(wout_hbm, wout, sem)
    load.start()

    group = KEY_TILE * len(pieces)
    tiles = (held + group - 1) // group
    spare = kv_ref[0:1, :hd].astype(F32)
    row = lax.broadcasted_iota(jnp.int32, (KEY_TILE, hd), 0)
    place = row // share * block_rows + row % share
    longest = jnp.zeros((KEY_TILE, 1), F32)
    for i in range(piece_rows // KEY_TILE):
        for j, piece in enumerate(pieces):
            at = pl.ds(i * group + j * KEY_TILE, KEY_TILE)
            source = pl.ds(i * KEY_TILE, KEY_TILE)
            used = place + (me ^ j) * share + i * group < held
            key = jnp.where(used, piece[source, :hd].astype(F32), spare)
            longest = jnp.maximum(longest, jnp.sum(key * key, axis=1, keepdims=True))
            keys[at, :] = key.astype(BF16)
            values[at, hd:] = jnp.where(used, piece[source, hd:].astype(F32), 0.0).astype(BF16)
            values[at, :hd] = jnp.where(used, 1.0, 0.0).astype(BF16)
    for start in range(0, known, KEY_TILE):
        at = pl.ds(cached + start, KEY_TILE)
        source = pl.ds(start, KEY_TILE)
        key = kv_ref[source, :hd].astype(F32)
        longest = jnp.maximum(longest, jnp.sum(key * key, axis=1, keepdims=True))
        keys[at, :] = kv_ref[source, :hd]
        values[at, hd:] = kv_ref[source, hd:]
        values[at, :hd] = jnp.ones((KEY_TILE, hd), BF16)

    tile = min(ROW_TILE, rows)
    for start in range(0, rows, tile):
        for h in range(heads):
            stacked[pl.ds(start * heads + h * tile, tile), :] = q_ref[
                pl.ds(start_row + start, tile), h * hd : (h + 1) * hd
            ]
    query = stacked[...].astype(F32)
    widest = jnp.max(jnp.sum(query * query, axis=1, keepdims=True))
    factor = hd ** (-0.5) * math.log2(math.e)
    small = widest * jnp.max(longest) * (1.0 / hd) < SAFE * SAFE

    total[...] = jnp.zeros_like(total)
    all_rows = rows * heads

    def weigh(at, part, shifted, mask=None):
        scores = dot_t(stacked[at, :], keys[part, :])
        if mask is not None:
            scores = jnp.where(mask, scores, MASKED)
        if shifted:
            scores = scores - high[at, :1]
        weights = jnp.exp2(scores * factor).astype(BF16)
        total[at, :] += dot(weights, values[part, :])

    def raise_high(at, part, mask=None):
        scores = dot_t(stacked[at, :], keys[part, :])
        if mask is not None:
            scores = jnp.where(mask, scores, MASKED)
        high[at, :] = jnp.maximum(high[at, :], jnp.max(scores, axis=1, keepdims=True))

    def over_keys(use):
        def one(i, carry):
            use(pl.ds(0, all_rows), pl.ds(pl.multiple_of(i * group, group), group))
            return carry

        lax.fori_loop(0, tiles, one, 0)
        if start_row:
            use(pl.ds(0, all_rows), pl.ds(cached, start_row))
        for start in range(0, rows, tile):
            at = pl.ds(start * heads, tile * heads)
            if start:
                use(at, pl.ds(cached + start_row, start))
            to = lax.broadcasted_iota(jnp.int32, (heads * tile, tile), 0) % tile
            by = lax.broadcasted_iota(jnp.int32, (heads * tile, tile), 1)
            use(at, pl.ds(cached + start_row + start, tile), mask=by <= to)

    busy = start_row < span

    @pl.when(busy & small)
    def _():
        over_keys(functools.partial(weigh, shifted=False))

    @pl.when(busy & jnp.logical_not(small))
    def _():
        high[...] = jnp.full_like(high, MASKED)
        over_keys(raise_high)
        over_keys(functools.partial(weigh, shifted=True))

    for start in range(0, rows, tile):
        for h in range(heads):
            both = total[pl.ds(start * heads + h * tile, tile), :]
            out = both[:, hd:] / both[:, :hd]
            context[pl.ds(start, tile), h * hd : (h + 1) * hd] = out.astype(BF16)

    load.wait()
    cols = wout.shape[1] // 4
    for k in (3, 1, 2, 0):
        columns = pl.ds(pl.multiple_of((me ^ k) * cols, cols), cols)
        part = dot(context[...], wout[:, columns]).astype(BF16)
        if k & 1:
            far_refs[k >> 1][...] = part
        else:
            near_refs[k >> 1][...] = part


def finish_kernel(span_ref, tokens_ref, *refs):
    out_ref = refs[-1]
    part = refs[0].shape[0]
    for c in range(len(refs) // 3):
        near, got, crossed = refs[3 * c : 3 * c + 3]
        at = pl.ds(c * part, part)
        kept = near[...].astype(F32) + got[...].astype(F32)
        total = tokens_ref[at, :].astype(F32) + (kept + crossed[...].astype(F32))
        row = lax.broadcasted_iota(jnp.int32, total.shape, 0) + c * part
        out_ref[at, :] = jnp.where(row < span_ref[0], total, 0.0).astype(BF16)


def call(kernel, out_shape, in_specs, args, flops, scratch=(), exps=0, name=None):
    outs = out_shape if isinstance(out_shape, (list, tuple)) else [out_shape]
    moved = sum(a.size * a.dtype.itemsize for a in list(args) + list(outs))
    return pl.pallas_call(
        kernel,
        out_shape=out_shape,
        in_specs=in_specs,
        out_specs=jax.tree.map(lambda _: VMEM, out_shape),
        scratch_shapes=list(scratch),
        cost_estimate=pl.CostEstimate(flops=flops, bytes_accessed=moved, transcendentals=exps),
        compiler_params=pltpu.CompilerParams(vmem_limit_bytes=51 * 1024 * 1024),
        name=name,
    )(*args)


def body(
    tokens,
    norm_gain,
    w_query,
    w_keyval,
    w_out,
    span_lens,
    cached_lens,
    old_table,
    new_table,
    old_cache,
):
    tp = lax.axis_size("tp")
    groups, share, width = old_cache.shape
    block_rows = share * tp
    capacity = groups * block_rows
    rows, cols = tokens.shape
    q_cols = w_query.shape[1]
    features = w_query.shape[0]
    hd = width // 2
    most_held = capacity - rows
    piece_rows = most_held // tp

    def swap(x, bit):
        return lax.ppermute(x, "tp", [(i, i ^ bit) for i in range(tp)])

    def exchange(x):
        return lax.all_to_all(x, "seq", split_axis=0, concat_axis=0, tiled=True)

    with jax.named_scope("tokens_gather"):
        across = swap(tokens, 2)
        beside = swap(tokens, 1)

    with jax.named_scope("cache_gather"):
        beside, stored = lax.optimization_barrier((beside, old_cache))
        arrived = exchange(stored).reshape(groups * share, width)
        arrived, across = lax.optimization_barrier((arrived, across))
        ordered = call(
            functools.partial(order_kernel, share),
            jax.ShapeDtypeStruct((piece_rows, width), BF16),
            [SMEM, VMEM],
            (old_table, arrived),
            flops=2 * piece_rows * groups * share * width,
            name="order",
        )
        c_across = swap(ordered, 2)
        c_beside = swap(ordered, 1)

    with jax.named_scope("project"):
        corner = swap(across, 1)
        query, keyval = call(
            project_kernel,
            [
                jax.ShapeDtypeStruct((rows, q_cols), BF16),
                jax.ShapeDtypeStruct((rows, width), BF16),
            ],
            [VMEM] * 5 + [HBM] * 2,
            (
                tokens,
                beside,
                across,
                corner,
                norm_gain.reshape(tp, 1, cols),
                w_query.reshape(tp, cols, q_cols),
                w_keyval.reshape(tp, cols, width),
            ),
            flops=2 * rows * features * (q_cols + width),
            scratch=[
                pltpu.VMEM((tp, rows, cols), BF16),
                pltpu.VMEM((tp, cols, q_cols), BF16),
                pltpu.VMEM((tp, cols, width), BF16),
                pltpu.SemaphoreType.DMA((2,)),
            ],
            name="project",
        )
        keyval, c_across = lax.optimization_barrier((keyval, c_across))
        cached = (ordered, c_beside, c_across, swap(c_across, 1))

    with jax.named_scope("extend"):
        sent = call(
            functools.partial(extend_kernel, share, block_rows),
            jax.ShapeDtypeStruct((groups * share, width), BF16),
            [SMEM] * 4 + [VMEM] * 2,
            (old_table, new_table, cached_lens, span_lens, arrived, keyval),
            flops=4 * groups * share * groups * share * width,
            name="extend",
        )
        new_cache = exchange(sent.reshape(groups, share, width))

    part = rows // CHUNKS
    sums = []
    for c in range(CHUNKS):
        with jax.named_scope("attend"):
            seen = most_held + (c + 1) * part
            far0, far1, near0, near1 = call(
                functools.partial(attend_kernel, share, block_rows, c * part, part),
                [jax.ShapeDtypeStruct((part, cols), BF16)] * 4,
                [SMEM] * 2 + [VMEM] * 6 + [HBM],
                (cached_lens, span_lens, query, keyval, *cached, w_out),
                flops=4 * part * seen * q_cols + 2 * part * q_cols * features,
                exps=part * seen * (q_cols // hd),
                scratch=[
                    pltpu.VMEM((seen, hd), BF16),
                    pltpu.VMEM((seen, width), BF16),
                    pltpu.VMEM((part * (q_cols // hd), hd), BF16),
                    pltpu.VMEM((part * (q_cols // hd), width), F32),
                    pltpu.VMEM((part * (q_cols // hd), hd), F32),
                    pltpu.VMEM((part, q_cols), BF16),
                    pltpu.VMEM(w_out.shape, BF16),
                    pltpu.SemaphoreType.DMA,
                ],
                name="attend",
            )
        with jax.named_scope("reduce"):
            got1 = swap(far1, 1)
            pair = (near1.astype(F32) + got1.astype(F32)).astype(BF16)
            query, pair = lax.optimization_barrier((query, pair))
            sums += [near0, swap(far0, 1), swap(pair, 2)]
    with jax.named_scope("finish"):
        mixed = call(
            finish_kernel,
            jax.ShapeDtypeStruct((rows, cols), BF16),
            [SMEM] + [VMEM] * (1 + len(sums)),
            (span_lens, tokens, *sums),
            flops=4 * rows * cols,
            name="finish",
        )
    return (mixed, new_cache)


def solution(mesh):
    in_specs = (
        P("seq", "tp"),
        P(),
        P(None, "tp"),
        P(),
        P("tp", None),
        P("seq"),
        P("seq"),
        P("seq", None),
        P("seq", None),
        P("seq", "tp", None),
    )
    out_specs = (P("seq", "tp"), P("seq", "tp", None))
    return jax.shard_map(body, mesh=mesh, in_specs=in_specs, out_specs=out_specs, check_vma=False)
```

```python
import functools
import math

import jax
import jax.numpy as jnp
from jax import lax
from jax.experimental import pallas as pl
from jax.experimental.pallas import tpu as pltpu
from jax.sharding import PartitionSpec as P

EPSILON = 1e-05
MASKED = -1e30
PART_ROWS = 256
ROW_TILE = 128
KEY_TILE = 128
NORM_ROWS = 128
SAFE = 60.0
F32 = jnp.float32
BF16 = jnp.bfloat16

VMEM = pl.BlockSpec(memory_space=pltpu.VMEM)
SMEM = pl.BlockSpec(memory_space=pltpu.SMEM)
HBM = pl.BlockSpec(memory_space=pltpu.HBM)


def dot(a, b):
    return lax.dot_general(a, b, (((1,), (0,)), ((), ())), preferred_element_type=F32)


def dot_t(a, b):
    return lax.dot_general(a, b, (((1,), (1,)), ((), ())), preferred_element_type=F32)


def order_kernel(share, plan_ref, arrived_ref, out_ref):
    rows, count = out_ref.shape[0], arrived_ref.shape[0]
    row = lax.broadcasted_iota(jnp.int32, (rows, 128), 0)
    block = row // share
    holder = jnp.zeros_like(block)
    for b in range(rows // share):
        holder = jnp.where(block == b, plan_ref[2 + b], holder)
    index = (holder * share + row % share)[:, :1]
    column = lax.broadcasted_iota(jnp.int32, (rows, count), 1)
    pick = jnp.where(column == index, 1.0, 0.0).astype(BF16)
    out_ref[...] = dot(pick, arrived_ref[...]).astype(BF16)


def extend_kernel(share, block_rows, plan_ref, arrived_ref, kv_ref, out_ref):
    rows = arrived_ref.shape[0]
    groups = rows // share
    held, span = plan_ref[0], plan_ref[1]
    row = lax.broadcasted_iota(jnp.int32, (rows, 128), 0)
    target = row // share
    block, holder = jnp.zeros_like(row), jnp.zeros_like(row)
    for b in range(groups):
        hit = target == plan_ref[2 + groups + b]
        block = jnp.where(hit, b, block)
        holder = jnp.where(hit, plan_ref[2 + b], holder)
    position = block * block_rows + lax.axis_index("tp") * share + row % share
    old_row = jnp.where(position < held, holder * share + row % share, -1)[:, :1]
    fresh = position - held
    new_row = jnp.where((fresh >= 0) & (fresh < span), fresh, -1)[:, :1]
    column = lax.broadcasted_iota(jnp.int32, (rows, rows), 1)
    total = dot(jnp.where(column == old_row, 1.0, 0.0).astype(BF16), arrived_ref[...])
    column = lax.broadcasted_iota(jnp.int32, (rows, kv_ref.shape[0]), 1)
    total += dot(jnp.where(column == new_row, 1.0, 0.0).astype(BF16), kv_ref[...])
    out_ref[...] = total.astype(BF16)


def project_kernel(
    x0, x1, x2, x3, gain_ref, wq_hbm, wkv_hbm, q_ref, kv_ref, normed, weights, sems
):
    pieces = (x0, x1, x2, x3)
    me = lax.axis_index("tp")
    rows, width = x0.shape
    features = width * len(pieces)
    q_cols = q_ref.shape[1]
    loads = []
    for j in range(len(pieces)):
        at = pl.ds(j * width, width)
        for hbm, to in ((wq_hbm, pl.ds(0, q_cols)), (wkv_hbm, pl.ds(q_cols, kv_ref.shape[1]))):
            loads.append(
                pltpu.make_async_copy(hbm.at[me ^ j], weights.at[at, to], sems.at[len(loads)])
            )
            loads[-1].start()

    for step in range(0, rows, NORM_ROWS):
        at = pl.ds(step, NORM_ROWS)
        values = [piece[at, :].astype(F32) for piece in pieces]
        average = jnp.sum(sum(values), axis=1, keepdims=True) / features
        centred = [v - average for v in values]
        spread = jnp.sum(sum(v * v for v in centred), axis=1, keepdims=True) / features
        scale = lax.rsqrt(spread + EPSILON)
        for j, v in enumerate(centred):
            normed[at, j * width : (j + 1) * width] = (v * scale * gain_ref[j]).astype(BF16)
    for load in loads:
        load.wait()
    q_ref[...] = dot(normed[...], weights[:, :q_cols]).astype(BF16)
    kv_ref[...] = dot(normed[...], weights[:, q_cols:]).astype(BF16)


def attend_kernel(share, block_rows, plan_ref, q_ref, kv_ref, c0, c1, c2, c3, *refs):
    wout_hbm, far_refs, near_refs = refs[0], refs[1:3], refs[3:5]
    keys, values, stacked, total, high, context, wout, sem = refs[5:]
    pieces = (c0, c1, c2, c3)
    me = lax.axis_index("tp")
    held, span = plan_ref[0], plan_ref[1]
    rows = q_ref.shape[0]
    piece_rows, width = c0.shape
    hd = width // 2
    heads = q_ref.shape[1] // hd
    cached = piece_rows * len(pieces)
    load = pltpu.make_async_copy(wout_hbm, wout, sem)
    load.start()

    ones = jnp.ones((hd, hd), BF16)

    def lengths(x):
        return dot((x * x).astype(BF16), ones)

    group = KEY_TILE * len(pieces)
    tiles = (held + group - 1) // group
    spare = kv_ref[0:1, :hd].astype(F32)
    row = lax.broadcasted_iota(jnp.int32, (KEY_TILE, hd), 0)
    place = row // share * block_rows + row % share
    longest = jnp.zeros((KEY_TILE, hd), F32)
    for i in range(piece_rows // KEY_TILE):
        for j, piece in enumerate(pieces):
            at = pl.ds(i * group + j * KEY_TILE, KEY_TILE)
            source = pl.ds(i * KEY_TILE, KEY_TILE)
            used = place + (me ^ j) * share + i * group < held
            key = jnp.where(used, piece[source, :hd].astype(F32), spare)
            longest = jnp.maximum(longest, lengths(key))
            keys[at, :] = key.astype(BF16)
            values[at, hd:] = jnp.where(used, piece[source, hd:].astype(F32), 0.0).astype(BF16)
            values[at, :hd] = jnp.where(used, 1.0, 0.0).astype(BF16)
    for start in range(0, rows, KEY_TILE):
        at = pl.ds(cached + start, KEY_TILE)
        source = pl.ds(start, KEY_TILE)
        longest = jnp.maximum(longest, lengths(kv_ref[source, :hd].astype(F32)))
        keys[at, :] = kv_ref[source, :hd]
        values[at, hd:] = kv_ref[source, hd:]
        values[at, :hd] = jnp.ones((KEY_TILE, hd), BF16)

    tile = min(ROW_TILE, rows)
    widest = jnp.zeros((tile, hd), F32)
    for start in range(0, rows, tile):
        for h in range(heads):
            piece = q_ref[pl.ds(start, tile), h * hd : (h + 1) * hd]
            widest = jnp.maximum(widest, lengths(piece.astype(F32)))
            stacked[pl.ds(start * heads + h * tile, tile), :] = piece
    factor = hd ** (-0.5) * math.log2(math.e)
    small = jnp.max(widest) * jnp.max(longest) * (1.05 / hd) < SAFE * SAFE

    def weigh(at, part, shifted, mask=None, first=False):
        scores = dot_t(stacked[at, :], keys[part, :])
        if mask is not None:
            scores = jnp.where(mask, scores, MASKED)
        if shifted:
            scores = scores - high[at, :1]
        weights = jnp.exp2(scores * factor).astype(BF16)
        total[at, :] += dot(weights, values[part, :])

    def raise_high(at, part, mask=None):
        scores = dot_t(stacked[at, :], keys[part, :])
        if mask is not None:
            scores = jnp.where(mask, scores, MASKED)
        high[at, :] = jnp.maximum(high[at, :], jnp.max(scores, axis=1, keepdims=True))

    span_rows = tile * heads

    def over_keys(use, begin, end):
        blocks = [pl.ds(start * heads, span_rows) for start in range(begin, end, tile)]

        def one(i, carry):
            for at in blocks:
                use(at, pl.ds(pl.multiple_of(i * group, group), group))
            return carry

        lax.fori_loop(0, tiles, one, 0)
        to = lax.broadcasted_iota(jnp.int32, (span_rows, tile), 0) % tile
        by = lax.broadcasted_iota(jnp.int32, (span_rows, tile), 1)
        for start, at in zip(range(begin, end, tile), blocks):
            if start:
                use(at, pl.ds(cached, start))
            use(at, pl.ds(cached + start, tile), mask=by <= to)

    total[...] = jnp.zeros_like(total)
    for begin in range(0, rows, PART_ROWS):
        end = min(begin + PART_ROWS, rows)
        busy = begin < span

        @pl.when(busy & small)
        def _():
            over_keys(functools.partial(weigh, shifted=False), begin, end)

        @pl.when(busy & jnp.logical_not(small))
        def _():
            high[...] = jnp.full_like(high, MASKED)
            over_keys(raise_high, begin, end)
            over_keys(functools.partial(weigh, shifted=True), begin, end)

    for start in range(0, rows, tile):
        for h in range(heads):
            both = total[pl.ds(start * heads + h * tile, tile), :]
            out = both[:, hd:] / both[:, :hd]
            context[pl.ds(start, tile), h * hd : (h + 1) * hd] = out.astype(BF16)

    load.wait()
    cols = wout.shape[1] // 4
    for k in (3, 1, 2, 0):
        columns = pl.ds(pl.multiple_of((me ^ k) * cols, cols), cols)
        part = dot(context[...], wout[:, columns]).astype(BF16)
        if k & 1:
            far_refs[k >> 1][...] = part
        else:
            near_refs[k >> 1][...] = part


def finish_kernel(plan_ref, tokens_ref, near_ref, got_ref, crossed_ref, out_ref):
    kept = near_ref[...].astype(F32) + got_ref[...].astype(F32)
    total = tokens_ref[...].astype(F32) + (kept + crossed_ref[...].astype(F32))
    row = lax.broadcasted_iota(jnp.int32, total.shape, 0)
    out_ref[...] = jnp.where(row < plan_ref[1], total, 0.0).astype(BF16)


def call(kernel, out_shape, in_specs, args, flops, mib=51, scratch=(), exps=0, name=None):
    outs = out_shape if isinstance(out_shape, (list, tuple)) else [out_shape]
    moved = sum(a.size * a.dtype.itemsize for a in list(args) + list(outs))
    return pl.pallas_call(
        kernel,
        out_shape=out_shape,
        in_specs=in_specs,
        out_specs=jax.tree.map(lambda _: VMEM, out_shape),
        scratch_shapes=list(scratch),
        cost_estimate=pl.CostEstimate(flops=flops, bytes_accessed=moved, transcendentals=exps),
        compiler_params=pltpu.CompilerParams(vmem_limit_bytes=mib * 1024 * 1024),
        name=name,
    )(*args)


def body(
    tokens,
    norm_gain,
    w_query,
    w_keyval,
    w_out,
    span_lens,
    cached_lens,
    old_table,
    new_table,
    old_cache,
):
    tp = lax.axis_size("tp")
    groups, share, width = old_cache.shape
    block_rows = share * tp
    capacity = groups * block_rows
    rows, cols = tokens.shape
    q_cols = w_query.shape[1]
    features = w_query.shape[0]
    hd = width // 2
    most_held = capacity - rows
    piece_rows = most_held // tp

    def swap(x, bit):
        return lax.ppermute(x, "tp", [(i, i ^ bit) for i in range(tp)])

    def exchange(x):
        return lax.all_to_all(x, "seq", split_axis=0, concat_axis=0, tiled=True)

    with jax.named_scope("tokens_gather"):
        plan = jnp.concatenate([cached_lens, span_lens, old_table[0], new_table[0]])
        gain = norm_gain.reshape(tp, cols)
        gain = jnp.concatenate(
            [lax.dynamic_slice_in_dim(gain, lax.axis_index("tp") ^ j, 1) for j in range(tp)]
        ).reshape(tp, 1, cols)
        in_span = lax.broadcasted_iota(jnp.int32, (rows, 1), 0) < span_lens[0]
        own = jnp.where(in_span, tokens, jnp.zeros_like(tokens))
        across = swap(tokens, 2)
        beside = swap(tokens, 1)

    with jax.named_scope("cache_gather"):
        beside, stored, plan = lax.optimization_barrier((beside, old_cache, plan))
        arrived = exchange(stored).reshape(groups * share, width)
        arrived, across, own, gain = lax.optimization_barrier((arrived, across, own, gain))
        ordered = call(
            functools.partial(order_kernel, share),
            jax.ShapeDtypeStruct((piece_rows, width), BF16),
            [SMEM, VMEM],
            (plan, arrived),
            flops=2 * piece_rows * groups * share * width,
            name="order",
        )
        c_across = swap(ordered, 2)
        c_beside = swap(ordered, 1)

    with jax.named_scope("project"):
        corner = swap(across, 1)
        query, keyval = call(
            project_kernel,
            [
                jax.ShapeDtypeStruct((rows, q_cols), BF16),
                jax.ShapeDtypeStruct((rows, width), BF16),
            ],
            [VMEM] * 5 + [HBM] * 2,
            (
                own,
                beside,
                across,
                corner,
                gain,
                w_query.reshape(tp, cols, q_cols),
                w_keyval.reshape(tp, cols, width),
            ),
            flops=2 * rows * features * (q_cols + width),
            scratch=[
                pltpu.VMEM((rows, features), BF16),
                pltpu.VMEM((features, q_cols + width), BF16),
                pltpu.SemaphoreType.DMA((2 * tp,)),
            ],
            name="project",
        )

    with jax.named_scope("extend"):
        sent = call(
            functools.partial(extend_kernel, share, block_rows),
            jax.ShapeDtypeStruct((groups * share, width), BF16),
            [SMEM] + [VMEM] * 2,
            (plan, arrived, keyval),
            flops=4 * groups * share * groups * share * width,
            name="extend",
        )
        sent, c_across = lax.optimization_barrier((sent, c_across))
        cached = (ordered, c_beside, c_across, swap(c_across, 1))

    with jax.named_scope("attend"):
        stacked = rows * (q_cols // hd)
        far0, far1, near0, near1 = call(
            functools.partial(attend_kernel, share, block_rows),
            [jax.ShapeDtypeStruct((rows, cols), BF16)] * 4,
            [SMEM] + [VMEM] * 6 + [HBM],
            (plan, query, keyval, *cached, w_out),
            flops=4 * rows * capacity * q_cols + 2 * rows * q_cols * features,
            exps=stacked * capacity,
            mib=50,
            scratch=[
                pltpu.VMEM((capacity, hd), BF16),
                pltpu.VMEM((capacity, width), BF16),
                pltpu.VMEM((stacked, hd), BF16),
                pltpu.VMEM((stacked, width), F32),
                pltpu.VMEM((stacked, hd), F32),
                pltpu.VMEM((rows, q_cols), BF16),
                pltpu.VMEM(w_out.shape, BF16),
                pltpu.SemaphoreType.DMA,
            ],
            name="attend",
        )

    with jax.named_scope("reduce"):
        got1 = swap(far1, 1)
        pair = (near1.astype(F32) + got1.astype(F32)).astype(BF16)
        pair, sent = lax.optimization_barrier((pair, sent))
        crossed = swap(pair, 2)
        new_cache = exchange(sent.reshape(groups, share, width))

    with jax.named_scope("finish"):
        mixed = call(
            finish_kernel,
            jax.ShapeDtypeStruct((rows, cols), BF16),
            [SMEM] + [VMEM] * 4,
            (plan, own, near0, swap(far0, 1), crossed),
            flops=4 * rows * cols,
            name="finish",
        )
    return (mixed, new_cache)


def solution(mesh):
    in_specs = (
        P("seq", "tp"),
        P(),
        P(None, "tp"),
        P(),
        P("tp", None),
        P("seq"),
        P("seq"),
        P("seq", None),
        P("seq", None),
        P("seq", "tp", None),
    )
    out_specs = (P("seq", "tp"), P("seq", "tp", None))
    return jax.shard_map(body, mesh=mesh, in_specs=in_specs, out_specs=out_specs, check_vma=False)
```

```python
import functools
import math

import jax
import jax.numpy as jnp
from jax import lax
from jax.experimental import pallas as pl
from jax.experimental.pallas import tpu as pltpu
from jax.sharding import PartitionSpec as P

EPSILON = 1e-05
MASKED = -1e30
CHUNKS = 1
PART_ROWS = 256
ROW_TILE = 128
KEY_TILE = 128
NORM_ROWS = 128
MIB = 51
PROJECT_MIB = 50.375
ATTEND_MIB = 49.75
SAFE = 60.0
F32 = jnp.float32
BF16 = jnp.bfloat16

VMEM = pl.BlockSpec(memory_space=pltpu.VMEM)
SMEM = pl.BlockSpec(memory_space=pltpu.SMEM)
HBM = pl.BlockSpec(memory_space=pltpu.HBM)


def dot(a, b):
    return lax.dot_general(a, b, (((1,), (0,)), ((), ())), preferred_element_type=F32)


def dot_t(a, b):
    return lax.dot_general(a, b, (((1,), (1,)), ((), ())), preferred_element_type=F32)


def order_kernel(share, plan_ref, arrived_ref, out_ref):
    rows, count = out_ref.shape[0], arrived_ref.shape[0]
    row = lax.broadcasted_iota(jnp.int32, (rows, 128), 0)
    block = row // share
    holder = jnp.zeros_like(block)
    for b in range(rows // share):
        holder = jnp.where(block == b, plan_ref[2 + b], holder)
    index = (holder * share + row % share)[:, :1]
    column = lax.broadcasted_iota(jnp.int32, (rows, count), 1)
    pick = jnp.where(column == index, 1.0, 0.0).astype(BF16)
    out_ref[...] = dot(pick, arrived_ref[...]).astype(BF16)


def extend_kernel(share, block_rows, plan_ref, arrived_ref, kv_ref, out_ref):
    rows = arrived_ref.shape[0]
    groups = rows // share
    held, span = plan_ref[0], plan_ref[1]
    row = lax.broadcasted_iota(jnp.int32, (rows, 128), 0)
    target = row // share
    block, holder = jnp.zeros_like(row), jnp.zeros_like(row)
    for b in range(groups):
        hit = target == plan_ref[2 + groups + b]
        block = jnp.where(hit, b, block)
        holder = jnp.where(hit, plan_ref[2 + b], holder)
    position = block * block_rows + lax.axis_index("tp") * share + row % share
    old_row = jnp.where(position < held, holder * share + row % share, -1)[:, :1]
    fresh = position - held
    new_row = jnp.where((fresh >= 0) & (fresh < span), fresh, -1)[:, :1]
    column = lax.broadcasted_iota(jnp.int32, (rows, rows), 1)
    total = dot(jnp.where(column == old_row, 1.0, 0.0).astype(BF16), arrived_ref[...])
    column = lax.broadcasted_iota(jnp.int32, (rows, kv_ref.shape[0]), 1)
    total += dot(jnp.where(column == new_row, 1.0, 0.0).astype(BF16), kv_ref[...])
    out_ref[...] = total.astype(BF16)


def project_kernel(
    x0,
    x1,
    x2,
    x3,
    gain_ref,
    wq_hbm,
    wkv_hbm,
    q_ref,
    kv_ref,
    values_ref,
    limits_ref,
    normed,
    weights,
    sems,
):
    pieces = (x0, x1, x2, x3)
    me = lax.axis_index("tp")
    rows, width = x0.shape
    features = width * len(pieces)
    kv_cols = kv_ref.shape[1]
    hd = kv_cols // 2
    q_cols = weights.shape[1] - kv_cols
    heads = q_cols // hd
    loads = []
    for j in range(len(pieces)):
        at = pl.ds(j * width, width)
        for hbm, to in ((wq_hbm, pl.ds(0, q_cols)), (wkv_hbm, pl.ds(q_cols, kv_cols))):
            loads.append(
                pltpu.make_async_copy(hbm.at[me ^ j], weights.at[at, to], sems.at[len(loads)])
            )
            loads[-1].start()

    for step in range(0, rows, NORM_ROWS):
        at = pl.ds(step, NORM_ROWS)
        values = [piece[at, :].astype(F32) for piece in pieces]
        average = jnp.sum(sum(values), axis=1, keepdims=True) / features
        centred = [v - average for v in values]
        spread = jnp.sum(sum(v * v for v in centred), axis=1, keepdims=True) / features
        scale = lax.rsqrt(spread + EPSILON)
        for j, v in enumerate(centred):
            normed[at, j * width : (j + 1) * width] = (v * scale * gain_ref[j]).astype(BF16)
    for load in loads:
        load.wait()
    query = dot(normed[...], weights[:, :q_cols]).astype(BF16)
    keyval = dot(normed[...], weights[:, q_cols:]).astype(BF16)
    kv_ref[...] = keyval
    values_ref[:, hd:] = keyval[:, hd:]
    values_ref[:, :hd] = jnp.ones((rows, hd), BF16)
    limits_ref[0] = longest(keyval[:, :hd])
    for start in range(0, rows, ROW_TILE):
        for h in range(heads):
            q_ref[pl.ds(start * heads + h * ROW_TILE, ROW_TILE), :] = query[
                start : start + ROW_TILE, h * hd : (h + 1) * hd
            ]
    limits_ref[1] = longest(q_ref[...])


def longest(x):
    x = x.astype(F32)
    squares = dot((x * x).astype(BF16), jnp.ones((x.shape[1], 128), BF16))
    return jnp.max(squares.reshape(-1, 8, 128), axis=0)


def attend_kernel(share, block_rows, start_row, rows, plan_ref, q_ref, kv_ref, new_ref, *refs):
    limits_ref, pieces, wout_hbm = refs[0], refs[1:5], refs[5]
    if start_row:
        old_ref, old_limit_ref = refs[6:8]
    else:
        old_ref, old_limit_ref = refs[10:12]
    at = 8 if start_row else 6
    far_refs, near_refs = refs[at : at + 2], refs[at + 2 : at + 4]
    total, high, context, wout, sem = refs[-5:]
    me = lax.axis_index("tp")
    held, span = plan_ref[0], plan_ref[1]
    piece_rows, width = pieces[0].shape
    hd = width // 2
    heads = q_ref.shape[0] // kv_ref.shape[0]
    load = pltpu.make_async_copy(wout_hbm, wout, sem)
    load.start()

    group = KEY_TILE * len(pieces)
    most = piece_rows // KEY_TILE
    tiles = (held + group - 1) // group
    if not start_row:
        row = lax.broadcasted_iota(jnp.int32, (KEY_TILE, hd), 0)
        place = row // share * block_rows + row % share
        limit = jnp.zeros((8, 128), F32)
        for i in range(most):
            source = pl.ds(i * KEY_TILE, KEY_TILE)
            for j, piece in enumerate(pieces):
                at = pl.ds(i * group + j * KEY_TILE, KEY_TILE)
                used = place + (me ^ j) * share + i * group < held
                old_ref[at, hd:] = jnp.where(used, piece[source, hd:].astype(F32), 0.0).astype(BF16)
                old_ref[at, :hd] = jnp.where(used, 1.0, 0.0).astype(BF16)
        for piece in pieces:
            limit = jnp.maximum(limit, longest(piece[:, :hd]))
        old_limit_ref[...] = limit

    factor = hd ** (-0.5) * math.log2(math.e)
    key_limit = jnp.max(jnp.maximum(old_limit_ref[...], limits_ref[0]))
    small = key_limit * jnp.max(limits_ref[1]) * (1.05 / hd) < SAFE * SAFE

    tile_rows = ROW_TILE * heads

    def queries(t):
        return q_ref[pl.ds(start_row * heads + t * tile_rows, tile_rows), :]

    def old_keys(i):
        source = pl.ds(i * KEY_TILE, KEY_TILE)
        return jnp.concatenate([piece[source, :hd] for piece in pieces], axis=0)

    def new_scores(t):
        known = start_row + t * ROW_TILE
        scores = dot_t(queries(t), kv_ref[pl.ds(0, known + ROW_TILE), :hd])
        to = lax.broadcasted_iota(jnp.int32, (tile_rows, ROW_TILE), 0) % ROW_TILE
        by = lax.broadcasted_iota(jnp.int32, (tile_rows, ROW_TILE), 1)
        last = jnp.where(by <= to, scores[:, known:], MASKED)
        return jnp.concatenate([scores[:, :known], last], axis=1) if known else last

    def new_values(t):
        return new_ref[pl.ds(0, start_row + (t + 1) * ROW_TILE), :]

    def put(t, both):
        out = (both[:, hd:] / both[:, :hd]).astype(BF16)
        for h in range(heads):
            context[pl.ds(t * ROW_TILE, ROW_TILE), h * hd : (h + 1) * hd] = out[
                h * ROW_TILE : (h + 1) * ROW_TILE
            ]

    def fast(used, begin):
        row_tiles = range(begin // ROW_TILE, min(begin + PART_ROWS, rows) // ROW_TILE)
        steps = [(t, i) for t in row_tiles for i in range(used + 1)]

        def score(t, i):
            return new_scores(t) if i == used else dot_t(queries(t), old_keys(i))

        ahead, both = score(*steps[0]), None
        for at, (t, i) in enumerate(steps):
            scores = ahead
            if at + 1 < len(steps):
                ahead = score(*steps[at + 1])
            weights = jnp.exp2(scores * factor).astype(BF16)
            values = new_values(t) if i == used else old_ref[pl.ds(i * group, group), :]
            part = dot(weights, values)
            both = part if i == 0 else both + part
            if i == used:
                put(t, both)

    def exact(t):
        column = lax.broadcasted_iota(jnp.int32, (tile_rows, group), 1)
        within = column % KEY_TILE
        owner = me ^ (column // KEY_TILE)
        place = within // share * block_rows + within % share + owner * share

        def old_scores(i):
            scores = dot_t(queries(t), old_keys(pl.multiple_of(i, 1)))
            return jnp.where(place + i * group < held, scores, MASKED)

        def raise_high(i, carry):
            top = jnp.max(old_scores(i), axis=1, keepdims=True)
            high[...] = jnp.maximum(high[...], top)
            return carry

        def add(i, carry):
            weights = jnp.exp2((old_scores(i) - high[:, :1]) * factor).astype(BF16)
            total[...] += dot(weights, old_ref[pl.ds(pl.multiple_of(i * group, group), group), :])
            return carry

        high[...] = jnp.zeros_like(high) + jnp.max(new_scores(t), axis=1, keepdims=True)
        lax.fori_loop(0, tiles, raise_high, 0)
        weights = jnp.exp2((new_scores(t) - high[:, :1]) * factor).astype(BF16)
        total[...] = dot(weights, new_values(t))
        lax.fori_loop(0, tiles, add, 0)
        put(t, total[...])

    for begin in range(0, rows, PART_ROWS):
        busy = start_row + begin < span
        for used in range(1, most + 1):
            pl.when(busy & small & (tiles == used))(functools.partial(fast, used, begin))

        @pl.when(busy & jnp.logical_not(small))
        def _():
            for t in range(begin // ROW_TILE, min(begin + PART_ROWS, rows) // ROW_TILE):
                exact(t)

        @pl.when(jnp.logical_not(busy))
        def _():
            context[pl.ds(begin, PART_ROWS), :] = jnp.zeros((PART_ROWS, context.shape[1]), BF16)

    load.wait()
    cols = wout.shape[1] // 4
    for k in (3, 1, 2, 0):
        columns = pl.ds(pl.multiple_of((me ^ k) * cols, cols), cols)
        part = dot(context[...], wout[:, columns]).astype(BF16)
        if k & 1:
            far_refs[k >> 1][...] = part
        else:
            near_refs[k >> 1][...] = part


def finish_kernel(at, plan_ref, tokens_ref, near_ref, got_ref, crossed_ref, *refs):
    out_hbm, done, sems = refs[-3:]
    rows = near_ref.shape[0]
    half = rows // 2
    stores = []
    for i in range(2):
        here = pl.ds(i * half, half)
        there = pl.ds(at + i * half, half)
        kept = near_ref[here, :].astype(F32) + got_ref[here, :].astype(F32)
        total = tokens_ref[there, :].astype(F32) + (kept + crossed_ref[here, :].astype(F32))
        row = lax.broadcasted_iota(jnp.int32, total.shape, 0) + (at + i * half)
        done[here, :] = jnp.where(row < plan_ref[1], total, 0.0).astype(BF16)
        stores.append(pltpu.make_async_copy(done.at[here], out_hbm.at[there], sems.at[i]))
        stores[-1].start()
    for store in stores:
        store.wait()


def call(
    kernel, out_shape, in_specs, args, flops, mib=MIB, scratch=(), exps=0, name=None, into=None
):
    outs = out_shape if isinstance(out_shape, (list, tuple)) else [out_shape]
    moved = sum(a.size * a.dtype.itemsize for a in list(args) + list(outs))
    return pl.pallas_call(
        kernel,
        out_shape=out_shape,
        in_specs=in_specs,
        out_specs=jax.tree.map(lambda _: VMEM if into is None else HBM, out_shape),
        input_output_aliases=into or {},
        scratch_shapes=list(scratch),
        cost_estimate=pl.CostEstimate(flops=flops, bytes_accessed=moved, transcendentals=exps),
        compiler_params=pltpu.CompilerParams(vmem_limit_bytes=int(mib * 1024 * 1024)),
        name=name,
    )(*args)


def body(
    tokens,
    norm_gain,
    w_query,
    w_keyval,
    w_out,
    span_lens,
    cached_lens,
    old_table,
    new_table,
    old_cache,
):
    tp = lax.axis_size("tp")
    groups, share, width = old_cache.shape
    block_rows = share * tp
    capacity = groups * block_rows
    rows, cols = tokens.shape
    q_cols = w_query.shape[1]
    features = w_query.shape[0]
    hd = width // 2
    most_held = capacity - rows
    piece_rows = most_held // tp

    def swap(x, bit):
        return lax.ppermute(x, "tp", [(i, i ^ bit) for i in range(tp)])

    def exchange(x):
        return lax.all_to_all(x, "seq", split_axis=0, concat_axis=0, tiled=True)

    with jax.named_scope("tokens_gather"):
        plan = jnp.concatenate([cached_lens, span_lens, old_table[0], new_table[0]])
        gain = norm_gain.reshape(tp, cols)
        gain = jnp.concatenate(
            [lax.dynamic_slice_in_dim(gain, lax.axis_index("tp") ^ j, 1) for j in range(tp)]
        ).reshape(tp, 1, cols)
        in_span = lax.broadcasted_iota(jnp.int32, (rows, 1), 0) < span_lens[0]
        own = jnp.where(in_span, tokens, jnp.zeros_like(tokens))
        across = swap(tokens, 2)
        beside = swap(tokens, 1)

    with jax.named_scope("cache_gather"):
        beside, stored = lax.optimization_barrier((beside, old_cache))
        arrived = exchange(stored).reshape(groups * share, width)
        arrived, across, own, gain, plan = lax.optimization_barrier(
            (arrived, across, own, gain, plan)
        )
        ordered = call(
            functools.partial(order_kernel, share),
            jax.ShapeDtypeStruct((piece_rows, width), BF16),
            [SMEM, VMEM],
            (plan, arrived),
            flops=2 * piece_rows * groups * share * width,
            name="order",
        )
        c_across = swap(ordered, 2)
        c_beside = swap(ordered, 1)

    with jax.named_scope("project"):
        corner = swap(across, 1)
        stacked = rows * (q_cols // hd)
        query, keyval, values, limits = call(
            project_kernel,
            [
                jax.ShapeDtypeStruct((stacked, hd), BF16),
                jax.ShapeDtypeStruct((rows, width), BF16),
                jax.ShapeDtypeStruct((rows, width), BF16),
                jax.ShapeDtypeStruct((2, 8, 128), F32),
            ],
            [VMEM] * 5 + [HBM] * 2,
            (
                own,
                beside,
                across,
                corner,
                gain,
                w_query.reshape(tp, cols, q_cols),
                w_keyval.reshape(tp, cols, width),
            ),
            flops=2 * rows * features * (q_cols + width),
            mib=PROJECT_MIB,
            scratch=[
                pltpu.VMEM((rows, features), BF16),
                pltpu.VMEM((features, q_cols + width), BF16),
                pltpu.SemaphoreType.DMA((2 * tp,)),
            ],
            name="project",
        )

    with jax.named_scope("extend"):
        sent = call(
            functools.partial(extend_kernel, share, block_rows),
            jax.ShapeDtypeStruct((groups * share, width), BF16),
            [SMEM] + [VMEM] * 2,
            (plan, arrived, keyval),
            flops=4 * groups * share * groups * share * width,
            name="extend",
        )
        sent, c_across = lax.optimization_barrier((sent, c_across))
        cached = (ordered, c_beside, c_across, swap(c_across, 1))

    part = rows // CHUNKS
    tile_rows = ROW_TILE * (q_cols // hd)
    old = []
    mixed = None
    for c in range(CHUNKS):
        with jax.named_scope("attend"):
            outs = [jax.ShapeDtypeStruct((part, cols), BF16)] * 4
            if not old:
                outs += [
                    jax.ShapeDtypeStruct((most_held, width), BF16),
                    jax.ShapeDtypeStruct((8, 128), F32),
                ]
            seen = most_held + (c + 1) * part
            far0, far1, near0, near1, *made = call(
                functools.partial(attend_kernel, share, block_rows, c * part, part),
                outs,
                [SMEM] + [VMEM] * 8 + [HBM] + [VMEM] * len(old),
                (plan, query, keyval, values, limits, *cached, w_out, *old),
                flops=4 * part * seen * q_cols + 2 * part * q_cols * features,
                exps=part * seen * (q_cols // hd),
                mib=ATTEND_MIB,
                scratch=[
                    pltpu.VMEM((tile_rows, width), F32),
                    pltpu.VMEM((tile_rows, hd), F32),
                    pltpu.VMEM((part, q_cols), BF16),
                    pltpu.VMEM(w_out.shape, BF16),
                    pltpu.SemaphoreType.DMA,
                ],
                name="attend",
            )
            old = old or made
        with jax.named_scope("reduce"):
            got1 = swap(far1, 1)
            pair = (near1.astype(F32) + got1.astype(F32)).astype(BF16)
            query, pair = lax.optimization_barrier((query, pair))
            if c == CHUNKS - 1:
                pair, sent = lax.optimization_barrier((pair, sent))
            crossed = swap(pair, 2)
            got0 = swap(far0, 1)
        with jax.named_scope("finish"):
            mixed = call(
                functools.partial(finish_kernel, c * part),
                jax.ShapeDtypeStruct((rows, cols), BF16),
                [SMEM] + [VMEM] * 4 + [HBM] * (c > 0),
                (plan, own, near0, got0, crossed, *([mixed] if c else [])),
                flops=4 * part * cols,
                scratch=[pltpu.VMEM((part, cols), BF16), pltpu.SemaphoreType.DMA((2,))],
                name="finish",
                into={5: 0} if c else {},
            )
    with jax.named_scope("exchange"):
        new_cache = exchange(sent.reshape(groups, share, width))
    return (mixed, new_cache)


def solution(mesh):
    in_specs = (
        P("seq", "tp"),
        P(),
        P(None, "tp"),
        P(),
        P("tp", None),
        P("seq"),
        P("seq"),
        P("seq", None),
        P("seq", None),
        P("seq", "tp", None),
    )
    out_specs = (P("seq", "tp"), P("seq", "tp", None))
    return jax.shard_map(body, mesh=mesh, in_specs=in_specs, out_specs=out_specs, check_vma=False)
```

```python
import functools
import math

import jax
import jax.numpy as jnp
from jax import lax
from jax.experimental import pallas as pl
from jax.experimental.pallas import tpu as pltpu
from jax.sharding import PartitionSpec as P

EPSILON = 1e-05
MASKED = -1e30
CHUNKS = 1
PART_ROWS = 256
ROW_TILE = 128
KEY_TILE = 128
NORM_ROWS = 128
MIB = 51
SPLIT_MIB = 53.5
PROJECT_MIB = 50.375
ATTEND_MIB = 49.75
SAFE = 60.0
F32 = jnp.float32
BF16 = jnp.bfloat16

VMEM = pl.BlockSpec(memory_space=pltpu.VMEM)
SMEM = pl.BlockSpec(memory_space=pltpu.SMEM)
HBM = pl.BlockSpec(memory_space=pltpu.HBM)


def dot(a, b):
    return lax.dot_general(a, b, (((1,), (0,)), ((), ())), preferred_element_type=F32)


def dot_t(a, b):
    return lax.dot_general(a, b, (((1,), (1,)), ((), ())), preferred_element_type=F32)


def split_kernel(cache_ref, keep_ref, send_ref):
    me = lax.axis_index("seq")
    for k in range(keep_ref.shape[0]):
        keep_ref[k] = cache_ref[me ^ (2 * k)]
        send_ref[k] = cache_ref[me ^ (2 * k + 1)]


def pair_kernel(keep_ref, got_ref, *pair_refs):
    for k, pair_ref in enumerate(pair_refs):
        pair_ref[0] = keep_ref[k]
        pair_ref[1] = got_ref[k]


def place_kernel(*refs):
    me = lax.axis_index("seq")
    for k, pair_ref in enumerate(refs[:-1]):
        for j in range(2):
            refs[-1][me ^ (2 * k + j)] = pair_ref[j]


def gathered(refs):
    if len(refs) == 1:
        return refs[0][...], 0
    blocks = [ref[j] for ref in refs for j in range(ref.shape[0])]
    return jnp.concatenate(blocks, axis=0), lax.axis_index("seq")


def order_kernel(share, plan_ref, *refs):
    arrived, me = gathered(refs[:-1])
    out_ref = refs[-1]
    rows, count = out_ref.shape[0], arrived.shape[0]
    row = lax.broadcasted_iota(jnp.int32, (rows, 128), 0)
    block = row // share
    holder = jnp.zeros_like(block)
    for b in range(rows // share):
        holder = jnp.where(block == b, plan_ref[2 + b] ^ me, holder)
    index = (holder * share + row % share)[:, :1]
    column = lax.broadcasted_iota(jnp.int32, (rows, count), 1)
    pick = jnp.where(column == index, 1.0, 0.0).astype(BF16)
    out_ref[...] = dot(pick, arrived).astype(BF16)


def extend_kernel(share, block_rows, outs, plan_ref, kv_ref, *refs):
    out_refs = refs[len(refs) - outs :]
    arrived, me = gathered(refs[: len(refs) - outs])
    rows = arrived.shape[0]
    groups = rows // share
    held, span = plan_ref[0], plan_ref[1]
    row = lax.broadcasted_iota(jnp.int32, (rows, 128), 0)
    target = row // share
    block, holder = jnp.zeros_like(row), jnp.zeros_like(row)
    for b in range(groups):
        hit = target == plan_ref[2 + groups + b] ^ me
        block = jnp.where(hit, b, block)
        holder = jnp.where(hit, plan_ref[2 + b] ^ me, holder)
    position = block * block_rows + lax.axis_index("tp") * share + row % share
    old_row = jnp.where(position < held, holder * share + row % share, -1)[:, :1]
    fresh = position - held
    new_row = jnp.where((fresh >= 0) & (fresh < span), fresh, -1)[:, :1]
    column = lax.broadcasted_iota(jnp.int32, (rows, rows), 1)
    total = dot(jnp.where(column == old_row, 1.0, 0.0).astype(BF16), arrived)
    column = lax.broadcasted_iota(jnp.int32, (rows, kv_ref.shape[0]), 1)
    total += dot(jnp.where(column == new_row, 1.0, 0.0).astype(BF16), kv_ref[...])
    total = total.astype(BF16)
    if outs == 1:
        out_refs[0][...] = total
        return
    for slot in range(groups):
        out_refs[slot % outs][slot // outs] = total[slot * share : (slot + 1) * share]


def project_kernel(
    x0,
    x1,
    x2,
    x3,
    gain_ref,
    wq_hbm,
    wkv_hbm,
    q_ref,
    kv_ref,
    values_ref,
    limits_ref,
    normed,
    weights,
    sems,
):
    pieces = (x0, x1, x2, x3)
    me = lax.axis_index("tp")
    rows, width = x0.shape
    features = width * len(pieces)
    kv_cols = kv_ref.shape[1]
    hd = kv_cols // 2
    q_cols = weights.shape[1] - kv_cols
    heads = q_cols // hd
    loads = []
    for j in range(len(pieces)):
        at = pl.ds(j * width, width)
        for hbm, to in ((wq_hbm, pl.ds(0, q_cols)), (wkv_hbm, pl.ds(q_cols, kv_cols))):
            loads.append(
                pltpu.make_async_copy(hbm.at[me ^ j], weights.at[at, to], sems.at[len(loads)])
            )
            loads[-1].start()

    for step in range(0, rows, NORM_ROWS):
        at = pl.ds(step, NORM_ROWS)
        values = [piece[at, :].astype(F32) for piece in pieces]
        average = jnp.sum(sum(values), axis=1, keepdims=True) / features
        centred = [v - average for v in values]
        spread = jnp.sum(sum(v * v for v in centred), axis=1, keepdims=True) / features
        scale = lax.rsqrt(spread + EPSILON)
        for j, v in enumerate(centred):
            normed[at, j * width : (j + 1) * width] = (v * scale * gain_ref[j]).astype(BF16)
    for load in loads:
        load.wait()
    query = dot(normed[...], weights[:, :q_cols]).astype(BF16)
    keyval = dot(normed[...], weights[:, q_cols:]).astype(BF16)
    kv_ref[...] = keyval
    values_ref[:, hd:] = keyval[:, hd:]
    values_ref[:, :hd] = jnp.ones((rows, hd), BF16)
    limits_ref[0] = longest(keyval[:, :hd])
    for start in range(0, rows, ROW_TILE):
        for h in range(heads):
            q_ref[pl.ds(start * heads + h * ROW_TILE, ROW_TILE), :] = query[
                start : start + ROW_TILE, h * hd : (h + 1) * hd
            ]
    limits_ref[1] = longest(q_ref[...])


def longest(x):
    x = x.astype(F32)
    squares = dot((x * x).astype(BF16), jnp.ones((x.shape[1], 128), BF16))
    return jnp.max(squares.reshape(-1, 8, 128), axis=0)


def attend_kernel(share, block_rows, start_row, rows, plan_ref, q_ref, kv_ref, new_ref, *refs):
    limits_ref, pieces, wout_hbm = refs[0], refs[1:5], refs[5]
    if start_row:
        old_ref, old_limit_ref = refs[6:8]
    else:
        old_ref, old_limit_ref = refs[10:12]
    at = 8 if start_row else 6
    far_refs, near_refs = refs[at : at + 2], refs[at + 2 : at + 4]
    total, high, context, wout, sem = refs[-5:]
    me = lax.axis_index("tp")
    held, span = plan_ref[0], plan_ref[1]
    piece_rows, width = pieces[0].shape
    hd = width // 2
    heads = q_ref.shape[0] // kv_ref.shape[0]
    load = pltpu.make_async_copy(wout_hbm, wout, sem)
    load.start()

    group = KEY_TILE * len(pieces)
    most = piece_rows // KEY_TILE
    tiles = (held + group - 1) // group
    if not start_row:
        row = lax.broadcasted_iota(jnp.int32, (KEY_TILE, hd), 0)
        place = row // share * block_rows + row % share
        limit = jnp.zeros((8, 128), F32)
        for i in range(most):
            source = pl.ds(i * KEY_TILE, KEY_TILE)
            for j, piece in enumerate(pieces):
                at = pl.ds(i * group + j * KEY_TILE, KEY_TILE)
                used = place + (me ^ j) * share + i * group < held
                old_ref[at, hd:] = jnp.where(used, piece[source, hd:].astype(F32), 0.0).astype(BF16)
                old_ref[at, :hd] = jnp.where(used, 1.0, 0.0).astype(BF16)
        for piece in pieces:
            limit = jnp.maximum(limit, longest(piece[:, :hd]))
        old_limit_ref[...] = limit

    factor = hd ** (-0.5) * math.log2(math.e)
    key_limit = jnp.max(jnp.maximum(old_limit_ref[...], limits_ref[0]))
    small = key_limit * jnp.max(limits_ref[1]) * (1.05 / hd) < SAFE * SAFE

    tile_rows = ROW_TILE * heads

    def queries(t):
        return q_ref[pl.ds(start_row * heads + t * tile_rows, tile_rows), :]

    def old_keys(i):
        source = pl.ds(i * KEY_TILE, KEY_TILE)
        return jnp.concatenate([piece[source, :hd] for piece in pieces], axis=0)

    def new_scores(t):
        known = start_row + t * ROW_TILE
        scores = dot_t(queries(t), kv_ref[pl.ds(0, known + ROW_TILE), :hd])
        to = lax.broadcasted_iota(jnp.int32, (tile_rows, ROW_TILE), 0) % ROW_TILE
        by = lax.broadcasted_iota(jnp.int32, (tile_rows, ROW_TILE), 1)
        last = jnp.where(by <= to, scores[:, known:], MASKED)
        return jnp.concatenate([scores[:, :known], last], axis=1) if known else last

    def new_values(t):
        return new_ref[pl.ds(0, start_row + (t + 1) * ROW_TILE), :]

    def put(t, both):
        out = (both[:, hd:] / both[:, :hd]).astype(BF16)
        for h in range(heads):
            context[pl.ds(t * ROW_TILE, ROW_TILE), h * hd : (h + 1) * hd] = out[
                h * ROW_TILE : (h + 1) * ROW_TILE
            ]

    def fast(used, begin):
        row_tiles = range(begin // ROW_TILE, min(begin + PART_ROWS, rows) // ROW_TILE)
        steps = [(t, i) for t in row_tiles for i in range(used + 1)]

        def score(t, i):
            return new_scores(t) if i == used else dot_t(queries(t), old_keys(i))

        ahead, both = score(*steps[0]), None
        for at, (t, i) in enumerate(steps):
            scores = ahead
            if at + 1 < len(steps):
                ahead = score(*steps[at + 1])
            weights = jnp.exp2(scores * factor).astype(BF16)
            values = new_values(t) if i == used else old_ref[pl.ds(i * group, group), :]
            part = dot(weights, values)
            both = part if i == 0 else both + part
            if i == used:
                put(t, both)

    def exact(t):
        column = lax.broadcasted_iota(jnp.int32, (tile_rows, group), 1)
        within = column % KEY_TILE
        owner = me ^ (column // KEY_TILE)
        place = within // share * block_rows + within % share + owner * share

        def old_scores(i):
            scores = dot_t(queries(t), old_keys(pl.multiple_of(i, 1)))
            return jnp.where(place + i * group < held, scores, MASKED)

        def raise_high(i, carry):
            top = jnp.max(old_scores(i), axis=1, keepdims=True)
            high[...] = jnp.maximum(high[...], top)
            return carry

        def add(i, carry):
            weights = jnp.exp2((old_scores(i) - high[:, :1]) * factor).astype(BF16)
            total[...] += dot(weights, old_ref[pl.ds(pl.multiple_of(i * group, group), group), :])
            return carry

        high[...] = jnp.zeros_like(high) + jnp.max(new_scores(t), axis=1, keepdims=True)
        lax.fori_loop(0, tiles, raise_high, 0)
        weights = jnp.exp2((new_scores(t) - high[:, :1]) * factor).astype(BF16)
        total[...] = dot(weights, new_values(t))
        lax.fori_loop(0, tiles, add, 0)
        put(t, total[...])

    for begin in range(0, rows, PART_ROWS):
        busy = start_row + begin < span
        for used in range(1, most + 1):
            pl.when(busy & small & (tiles == used))(functools.partial(fast, used, begin))

        @pl.when(busy & jnp.logical_not(small))
        def _():
            for t in range(begin // ROW_TILE, min(begin + PART_ROWS, rows) // ROW_TILE):
                exact(t)

        @pl.when(jnp.logical_not(busy))
        def _():
            context[pl.ds(begin, PART_ROWS), :] = jnp.zeros((PART_ROWS, context.shape[1]), BF16)

    load.wait()
    cols = wout.shape[1] // 4
    for k in (3, 1, 2, 0):
        columns = pl.ds(pl.multiple_of((me ^ k) * cols, cols), cols)
        part = dot(context[...], wout[:, columns]).astype(BF16)
        if k & 1:
            far_refs[k >> 1][...] = part
        else:
            near_refs[k >> 1][...] = part


def finish_kernel(at, plan_ref, tokens_ref, near_ref, got_ref, crossed_ref, *refs):
    out_hbm, done, sems = refs[-3:]
    rows = near_ref.shape[0]
    half = rows // 2
    stores = []
    for i in range(2):
        here = pl.ds(i * half, half)
        there = pl.ds(at + i * half, half)
        kept = near_ref[here, :].astype(F32) + got_ref[here, :].astype(F32)
        total = tokens_ref[there, :].astype(F32) + (kept + crossed_ref[here, :].astype(F32))
        row = lax.broadcasted_iota(jnp.int32, total.shape, 0) + (at + i * half)
        done[here, :] = jnp.where(row < plan_ref[1], total, 0.0).astype(BF16)
        stores.append(pltpu.make_async_copy(done.at[here], out_hbm.at[there], sems.at[i]))
        stores[-1].start()
    for store in stores:
        store.wait()


def call(
    kernel, out_shape, in_specs, args, flops, mib=MIB, scratch=(), exps=0, name=None, into=None
):
    outs = out_shape if isinstance(out_shape, (list, tuple)) else [out_shape]
    moved = sum(a.size * a.dtype.itemsize for a in list(args) + list(outs))
    return pl.pallas_call(
        kernel,
        out_shape=out_shape,
        in_specs=in_specs,
        out_specs=jax.tree.map(lambda _: VMEM if into is None else HBM, out_shape),
        input_output_aliases=into or {},
        scratch_shapes=list(scratch),
        cost_estimate=pl.CostEstimate(flops=flops, bytes_accessed=moved, transcendentals=exps),
        compiler_params=pltpu.CompilerParams(vmem_limit_bytes=int(mib * 1024 * 1024)),
        name=name,
    )(*args)


def body(
    tokens,
    norm_gain,
    w_query,
    w_keyval,
    w_out,
    span_lens,
    cached_lens,
    old_table,
    new_table,
    old_cache,
):
    tp = lax.axis_size("tp")
    groups, share, width = old_cache.shape
    block_rows = share * tp
    capacity = groups * block_rows
    rows, cols = tokens.shape
    q_cols = w_query.shape[1]
    features = w_query.shape[0]
    hd = width // 2
    most_held = capacity - rows
    piece_rows = most_held // tp

    def swap(x, bit, axis="tp"):
        size = lax.axis_size(axis)
        return lax.ppermute(x, axis, [(i, i ^ bit) for i in range(size)])

    def exchange(x):
        return lax.all_to_all(x, "seq", split_axis=0, concat_axis=0, tiled=True)

    phased = groups == 8
    half = jax.ShapeDtypeStruct((groups // 2, share, width), BF16)

    def by_pairs(keep, got):
        pairs = call(
            pair_kernel,
            [jax.ShapeDtypeStruct((2, share, width), BF16)] * (groups // 2),
            [VMEM] * 2,
            (keep, got),
            flops=0,
            mib=8,
            name="pair",
        )
        return [swap(x, 2 * k, "seq") if k else x for k, x in enumerate(pairs)]

    with jax.named_scope("tokens_gather"):
        across = swap(tokens, 2)
        beside = swap(tokens, 1)

    with jax.named_scope("cache_gather"):
        beside, stored = lax.optimization_barrier((beside, old_cache))
        if phased:
            keep, send = call(
                split_kernel, [half] * 2, [VMEM], (stored,), flops=0, mib=SPLIT_MIB, name="split"
            )
            got = swap(send, 1, "seq")
            got, norm_gain, tokens_too = lax.optimization_barrier((got, norm_gain, tokens))
            arrived = by_pairs(keep, got)
        else:
            tokens_too = tokens
            arrived = [exchange(stored).reshape(groups * share, width)]
        gain = norm_gain.reshape(tp, cols)
        gain = jnp.concatenate(
            [lax.dynamic_slice_in_dim(gain, lax.axis_index("tp") ^ j, 1) for j in range(tp)]
        ).reshape(tp, 1, cols)
        plan = jnp.concatenate([cached_lens, span_lens, old_table[0], new_table[0]])
        in_span = lax.broadcasted_iota(jnp.int32, (rows, 1), 0) < span_lens[0]
        own = jnp.where(in_span, tokens_too, jnp.zeros_like(tokens))
        *arrived, across, own, gain, plan = lax.optimization_barrier(
            (*arrived, across, own, gain, plan)
        )
        ordered = call(
            functools.partial(order_kernel, share),
            jax.ShapeDtypeStruct((piece_rows, width), BF16),
            [SMEM] + [VMEM] * len(arrived),
            (plan, *arrived),
            flops=2 * piece_rows * groups * share * width,
            name="order",
        )
        c_across = swap(ordered, 2)
        c_beside = swap(ordered, 1)

    with jax.named_scope("project"):
        corner = swap(across, 1)
        stacked = rows * (q_cols // hd)
        query, keyval, values, limits = call(
            project_kernel,
            [
                jax.ShapeDtypeStruct((stacked, hd), BF16),
                jax.ShapeDtypeStruct((rows, width), BF16),
                jax.ShapeDtypeStruct((rows, width), BF16),
                jax.ShapeDtypeStruct((2, 8, 128), F32),
            ],
            [VMEM] * 5 + [HBM] * 2,
            (
                own,
                beside,
                across,
                corner,
                gain,
                w_query.reshape(tp, cols, q_cols),
                w_keyval.reshape(tp, cols, width),
            ),
            flops=2 * rows * features * (q_cols + width),
            mib=PROJECT_MIB,
            scratch=[
                pltpu.VMEM((rows, features), BF16),
                pltpu.VMEM((features, q_cols + width), BF16),
                pltpu.SemaphoreType.DMA((2 * tp,)),
            ],
            name="project",
        )

    with jax.named_scope("extend"):
        sent = call(
            functools.partial(extend_kernel, share, block_rows, 2 if phased else 1),
            [half] * 2 if phased else [jax.ShapeDtypeStruct((groups * share, width), BF16)],
            [SMEM] + [VMEM] * (1 + len(arrived)),
            (plan, keyval, *arrived),
            flops=4 * groups * share * groups * share * width,
            name="extend",
        )
        *sent, c_across = lax.optimization_barrier((*sent, c_across))
        if phased:
            keep, got = sent[0], swap(sent[1], 1, "seq")
        cached = (ordered, c_beside, c_across, swap(c_across, 1))

    part = rows // CHUNKS
    tile_rows = ROW_TILE * (q_cols // hd)
    old = []
    mixed = None
    for c in range(CHUNKS):
        with jax.named_scope("attend"):
            outs = [jax.ShapeDtypeStruct((part, cols), BF16)] * 4
            if not old:
                outs += [
                    jax.ShapeDtypeStruct((most_held, width), BF16),
                    jax.ShapeDtypeStruct((8, 128), F32),
                ]
            seen = most_held + (c + 1) * part
            far0, far1, near0, near1, *made = call(
                functools.partial(attend_kernel, share, block_rows, c * part, part),
                outs,
                [SMEM] + [VMEM] * 8 + [HBM] + [VMEM] * len(old),
                (plan, query, keyval, values, limits, *cached, w_out, *old),
                flops=4 * part * seen * q_cols + 2 * part * q_cols * features,
                exps=part * seen * (q_cols // hd),
                mib=ATTEND_MIB,
                scratch=[
                    pltpu.VMEM((tile_rows, width), F32),
                    pltpu.VMEM((tile_rows, hd), F32),
                    pltpu.VMEM((part, q_cols), BF16),
                    pltpu.VMEM(w_out.shape, BF16),
                    pltpu.SemaphoreType.DMA,
                ],
                name="attend",
            )
            old = old or made
        with jax.named_scope("reduce"):
            got1 = swap(far1, 1)
            pair = (near1.astype(F32) + got1.astype(F32)).astype(BF16)
            query, pair = lax.optimization_barrier((query, pair))
            if c == CHUNKS - 1 and phased:
                pair, got = lax.optimization_barrier((pair, got))
            elif c == CHUNKS - 1:
                pair, *sent = lax.optimization_barrier((pair, *sent))
            crossed = swap(pair, 2)
            got0 = swap(far0, 1)
        with jax.named_scope("finish"):
            mixed = call(
                functools.partial(finish_kernel, c * part),
                jax.ShapeDtypeStruct((rows, cols), BF16),
                [SMEM] + [VMEM] * 4 + [HBM] * (c > 0),
                (plan, own, near0, got0, crossed, *([mixed] if c else [])),
                flops=4 * part * cols,
                scratch=[pltpu.VMEM((part, cols), BF16), pltpu.SemaphoreType.DMA((2,))],
                name="finish",
                into={5: 0} if c else {},
            )
    with jax.named_scope("exchange"):
        if phased:
            new_cache = call(
                place_kernel,
                jax.ShapeDtypeStruct(old_cache.shape, BF16),
                [VMEM] * (groups // 2),
                by_pairs(keep, got),
                flops=0,
                mib=8,
                name="place",
            )
        else:
            new_cache = exchange(sent[0].reshape(groups, share, width))
    return (mixed, new_cache)


def solution(mesh):
    in_specs = (
        P("seq", "tp"),
        P(),
        P(None, "tp"),
        P(),
        P("tp", None),
        P("seq"),
        P("seq"),
        P("seq", None),
        P("seq", None),
        P("seq", "tp", None),
    )
    out_specs = (P("seq", "tp"), P("seq", "tp", None))
    return jax.shard_map(body, mesh=mesh, in_specs=in_specs, out_specs=out_specs, check_vma=False)
```

```python
import functools
import math

import jax
import jax.numpy as jnp
from jax import lax
from jax.experimental import pallas as pl
from jax.experimental.pallas import tpu as pltpu
from jax.sharding import PartitionSpec as P

EPSILON = 1e-05
MASKED = -1e30
CHUNKS = 1
PART_ROWS = 256
ROW_TILE = 128
KEY_TILE = 128
NORM_ROWS = 128
MIB = 51
SPLIT_MIB = 53.5
PROJECT_MIB = 50.375
ATTEND_MIB = 49.75
SAFE = 60.0
F32 = jnp.float32
BF16 = jnp.bfloat16

VMEM = pl.BlockSpec(memory_space=pltpu.VMEM)
SMEM = pl.BlockSpec(memory_space=pltpu.SMEM)
HBM = pl.BlockSpec(memory_space=pltpu.HBM)


def dot(a, b):
    return lax.dot_general(a, b, (((1,), (0,)), ((), ())), preferred_element_type=F32)


def dot_t(a, b):
    return lax.dot_general(a, b, (((1,), (1,)), ((), ())), preferred_element_type=F32)


def split_kernel(cache_ref, keep_ref, send_ref):
    me = lax.axis_index("seq")
    for k in range(keep_ref.shape[0]):
        keep_ref[k] = cache_ref[me ^ (2 * k)]
        send_ref[k] = cache_ref[me ^ (2 * k + 1)]


def pair_kernel(keep_ref, got_ref, *pair_refs):
    for k, pair_ref in enumerate(pair_refs):
        pair_ref[0] = keep_ref[k]
        pair_ref[1] = got_ref[k]


def place_kernel(*refs):
    me = lax.axis_index("seq")
    for k, pair_ref in enumerate(refs[:-1]):
        for j in range(2):
            refs[-1][me ^ (2 * k + j)] = pair_ref[j]


def gathered(refs):
    if len(refs) == 1:
        return refs[0][...], 0
    blocks = [ref[j] for ref in refs for j in range(ref.shape[0])]
    return jnp.concatenate(blocks, axis=0), lax.axis_index("seq")


def order_kernel(share, plan_ref, *refs):
    arrived, me = gathered(refs[:-1])
    out_ref = refs[-1]
    rows, count = out_ref.shape[0], arrived.shape[0]
    row = lax.broadcasted_iota(jnp.int32, (rows, 128), 0)
    block = row // share
    holder = jnp.zeros_like(block)
    for b in range(rows // share):
        holder = jnp.where(block == b, plan_ref[2 + b] ^ me, holder)
    index = (holder * share + row % share)[:, :1]
    column = lax.broadcasted_iota(jnp.int32, (rows, count), 1)
    pick = jnp.where(column == index, 1.0, 0.0).astype(BF16)
    out_ref[...] = dot(pick, arrived).astype(BF16)


def extend_kernel(share, block_rows, outs, plan_ref, kv_ref, *refs):
    out_refs = refs[len(refs) - outs :]
    arrived, me = gathered(refs[: len(refs) - outs])
    rows = arrived.shape[0]
    groups = rows // share
    held, span = plan_ref[0], plan_ref[1]
    row = lax.broadcasted_iota(jnp.int32, (rows, 128), 0)
    target = row // share
    block, holder = jnp.zeros_like(row), jnp.zeros_like(row)
    for b in range(groups):
        hit = target == plan_ref[2 + groups + b] ^ me
        block = jnp.where(hit, b, block)
        holder = jnp.where(hit, plan_ref[2 + b] ^ me, holder)
    position = block * block_rows + lax.axis_index("tp") * share + row % share
    old_row = jnp.where(position < held, holder * share + row % share, -1)[:, :1]
    fresh = position - held
    new_row = jnp.where((fresh >= 0) & (fresh < span), fresh, -1)[:, :1]
    column = lax.broadcasted_iota(jnp.int32, (rows, rows), 1)
    total = dot(jnp.where(column == old_row, 1.0, 0.0).astype(BF16), arrived)
    column = lax.broadcasted_iota(jnp.int32, (rows, kv_ref.shape[0]), 1)
    total += dot(jnp.where(column == new_row, 1.0, 0.0).astype(BF16), kv_ref[...])
    total = total.astype(BF16)
    if outs == 1:
        out_refs[0][...] = total
        return
    for slot in range(groups):
        out_refs[slot % outs][slot // outs] = total[slot * share : (slot + 1) * share]


def project_kernel(
    x0,
    x1,
    x2,
    x3,
    gain_ref,
    wq_hbm,
    wkv_hbm,
    q_ref,
    kv_ref,
    values_ref,
    limits_ref,
    normed,
    wq_ref,
    wkv_ref,
    sems,
):
    pieces = (x0, x1, x2, x3)
    me = lax.axis_index("tp")
    rows, width = x0.shape
    features = width * len(pieces)
    hd = kv_ref.shape[1] // 2
    heads = wq_ref.shape[1] // hd
    loads = []
    for hbm, to in ((wkv_hbm, wkv_ref), (wq_hbm, wq_ref)):
        for j in range(len(pieces)):
            at = pl.ds(j * width, width)
            loads.append(pltpu.make_async_copy(hbm.at[at], to.at[at], sems.at[len(loads)]))
            loads[-1].start()

    for step in range(0, rows, NORM_ROWS):
        at = pl.ds(step, NORM_ROWS)
        values = [piece[at, :].astype(F32) for piece in pieces]
        average = jnp.sum(sum(values), axis=1, keepdims=True) / features
        centred = [v - average for v in values]
        spread = jnp.sum(sum(v * v for v in centred), axis=1, keepdims=True) / features
        scale = lax.rsqrt(spread + EPSILON)
        for j, v in enumerate(centred):
            owner = me ^ j
            to = pl.ds(pl.multiple_of(owner * width, width), width)
            normed[at, to] = (v * scale * gain_ref[owner]).astype(BF16)
    for load in loads[: len(pieces)]:
        load.wait()
    keyval = dot(normed[...], wkv_ref[...]).astype(BF16)
    kv_ref[...] = keyval
    values_ref[:, hd:] = keyval[:, hd:]
    values_ref[:, :hd] = jnp.ones((rows, hd), BF16)
    limits_ref[0] = longest(keyval[:, :hd])
    for load in loads[len(pieces) :]:
        load.wait()
    query = dot(normed[...], wq_ref[...]).astype(BF16)
    for start in range(0, rows, ROW_TILE):
        for h in range(heads):
            q_ref[pl.ds(start * heads + h * ROW_TILE, ROW_TILE), :] = query[
                start : start + ROW_TILE, h * hd : (h + 1) * hd
            ]
    limits_ref[1] = longest(q_ref[...])


def longest(x):
    x = x.astype(F32)
    squares = dot((x * x).astype(BF16), jnp.ones((x.shape[1], 128), BF16))
    return jnp.max(squares.reshape(-1, 8, 128), axis=0)


def attend_kernel(share, block_rows, start_row, rows, plan_ref, q_ref, kv_ref, new_ref, *refs):
    limits_ref, pieces, wout_hbm = refs[0], refs[1:5], refs[5]
    if start_row:
        old_ref, old_limit_ref = refs[6:8]
    else:
        old_ref, old_limit_ref = refs[10:12]
    at = 8 if start_row else 6
    far_refs, near_refs = refs[at : at + 2], refs[at + 2 : at + 4]
    total, high, context, wout, sem = refs[-5:]
    me = lax.axis_index("tp")
    held, span = plan_ref[0], plan_ref[1]
    piece_rows, width = pieces[0].shape
    hd = width // 2
    heads = q_ref.shape[0] // kv_ref.shape[0]
    load = pltpu.make_async_copy(wout_hbm, wout, sem)
    load.start()

    group = KEY_TILE * len(pieces)
    most = piece_rows // KEY_TILE
    tiles = (held + group - 1) // group
    if not start_row:
        row = lax.broadcasted_iota(jnp.int32, (KEY_TILE, hd), 0)
        place = row // share * block_rows + row % share
        limit = jnp.zeros((8, 128), F32)
        for i in range(most):
            source = pl.ds(i * KEY_TILE, KEY_TILE)
            for j, piece in enumerate(pieces):
                at = pl.ds(i * group + j * KEY_TILE, KEY_TILE)
                used = place + (me ^ j) * share + i * group < held
                old_ref[at, hd:] = jnp.where(used, piece[source, hd:].astype(F32), 0.0).astype(BF16)
                old_ref[at, :hd] = jnp.where(used, 1.0, 0.0).astype(BF16)
        for piece in pieces:
            limit = jnp.maximum(limit, longest(piece[:, :hd]))
        old_limit_ref[...] = limit

    factor = hd ** (-0.5) * math.log2(math.e)
    key_limit = jnp.max(jnp.maximum(old_limit_ref[...], limits_ref[0]))
    small = key_limit * jnp.max(limits_ref[1]) * (1.05 / hd) < SAFE * SAFE

    tile_rows = ROW_TILE * heads

    def queries(t):
        return q_ref[pl.ds(start_row * heads + t * tile_rows, tile_rows), :]

    def old_keys(i):
        source = pl.ds(i * KEY_TILE, KEY_TILE)
        return jnp.concatenate([piece[source, :hd] for piece in pieces], axis=0)

    def new_scores(t):
        known = start_row + t * ROW_TILE
        scores = dot_t(queries(t), kv_ref[pl.ds(0, known + ROW_TILE), :hd])
        to = lax.broadcasted_iota(jnp.int32, (tile_rows, ROW_TILE), 0) % ROW_TILE
        by = lax.broadcasted_iota(jnp.int32, (tile_rows, ROW_TILE), 1)
        last = jnp.where(by <= to, scores[:, known:], MASKED)
        return jnp.concatenate([scores[:, :known], last], axis=1) if known else last

    def new_values(t):
        return new_ref[pl.ds(0, start_row + (t + 1) * ROW_TILE), :]

    def put(t, both):
        out = (both[:, hd:] / both[:, :hd]).astype(BF16)
        for h in range(heads):
            context[pl.ds(t * ROW_TILE, ROW_TILE), h * hd : (h + 1) * hd] = out[
                h * ROW_TILE : (h + 1) * ROW_TILE
            ]

    def fast(used, begin):
        row_tiles = range(begin // ROW_TILE, min(begin + PART_ROWS, rows) // ROW_TILE)
        steps = [(t, i) for t in row_tiles for i in range(used + 1)]

        def score(t, i):
            return new_scores(t) if i == used else dot_t(queries(t), old_keys(i))

        ahead, both = score(*steps[0]), None
        for at, (t, i) in enumerate(steps):
            scores = ahead
            if at + 1 < len(steps):
                ahead = score(*steps[at + 1])
            weights = jnp.exp2(scores * factor).astype(BF16)
            values = new_values(t) if i == used else old_ref[pl.ds(i * group, group), :]
            part = dot(weights, values)
            both = part if i == 0 else both + part
            if i == used:
                put(t, both)

    def exact(t):
        column = lax.broadcasted_iota(jnp.int32, (tile_rows, group), 1)
        within = column % KEY_TILE
        owner = me ^ (column // KEY_TILE)
        place = within // share * block_rows + within % share + owner * share

        def old_scores(i):
            scores = dot_t(queries(t), old_keys(pl.multiple_of(i, 1)))
            return jnp.where(place + i * group < held, scores, MASKED)

        def raise_high(i, carry):
            top = jnp.max(old_scores(i), axis=1, keepdims=True)
            high[...] = jnp.maximum(high[...], top)
            return carry

        def add(i, carry):
            weights = jnp.exp2((old_scores(i) - high[:, :1]) * factor).astype(BF16)
            total[...] += dot(weights, old_ref[pl.ds(pl.multiple_of(i * group, group), group), :])
            return carry

        high[...] = jnp.zeros_like(high) + jnp.max(new_scores(t), axis=1, keepdims=True)
        lax.fori_loop(0, tiles, raise_high, 0)
        weights = jnp.exp2((new_scores(t) - high[:, :1]) * factor).astype(BF16)
        total[...] = dot(weights, new_values(t))
        lax.fori_loop(0, tiles, add, 0)
        put(t, total[...])

    for begin in range(0, rows, PART_ROWS):
        busy = start_row + begin < span
        for used in range(1, most + 1):
            pl.when(busy & small & (tiles == used))(functools.partial(fast, used, begin))

        @pl.when(busy & jnp.logical_not(small))
        def _():
            for t in range(begin // ROW_TILE, min(begin + PART_ROWS, rows) // ROW_TILE):
                exact(t)

        @pl.when(jnp.logical_not(busy))
        def _():
            context[pl.ds(begin, PART_ROWS), :] = jnp.zeros((PART_ROWS, context.shape[1]), BF16)

    load.wait()
    cols = wout.shape[1] // 4
    for k in (3, 1, 2, 0):
        columns = pl.ds(pl.multiple_of((me ^ k) * cols, cols), cols)
        part = dot(context[...], wout[:, columns]).astype(BF16)
        if k & 1:
            far_refs[k >> 1][...] = part
        else:
            near_refs[k >> 1][...] = part


def finish_kernel(at, plan_ref, tokens_ref, near_ref, got_ref, crossed_ref, *refs):
    out_hbm, done, sems = refs[-3:]
    rows = near_ref.shape[0]
    half = rows // 2
    stores = []
    for i in range(2):
        here = pl.ds(i * half, half)
        there = pl.ds(at + i * half, half)
        kept = near_ref[here, :].astype(F32) + got_ref[here, :].astype(F32)
        total = tokens_ref[there, :].astype(F32) + (kept + crossed_ref[here, :].astype(F32))
        row = lax.broadcasted_iota(jnp.int32, total.shape, 0) + (at + i * half)
        done[here, :] = jnp.where(row < plan_ref[1], total, 0.0).astype(BF16)
        stores.append(pltpu.make_async_copy(done.at[here], out_hbm.at[there], sems.at[i]))
        stores[-1].start()
    for store in stores:
        store.wait()


def call(
    kernel, out_shape, in_specs, args, flops, mib=MIB, scratch=(), exps=0, name=None, into=None
):
    outs = out_shape if isinstance(out_shape, (list, tuple)) else [out_shape]
    moved = sum(a.size * a.dtype.itemsize for a in list(args) + list(outs))
    return pl.pallas_call(
        kernel,
        out_shape=out_shape,
        in_specs=in_specs,
        out_specs=jax.tree.map(lambda _: VMEM if into is None else HBM, out_shape),
        input_output_aliases=into or {},
        scratch_shapes=list(scratch),
        cost_estimate=pl.CostEstimate(flops=flops, bytes_accessed=moved, transcendentals=exps),
        compiler_params=pltpu.CompilerParams(vmem_limit_bytes=int(mib * 1024 * 1024)),
        name=name,
    )(*args)


def body(
    tokens,
    norm_gain,
    w_query,
    w_keyval,
    w_out,
    span_lens,
    cached_lens,
    old_table,
    new_table,
    old_cache,
):
    tp = lax.axis_size("tp")
    groups, share, width = old_cache.shape
    block_rows = share * tp
    capacity = groups * block_rows
    rows, cols = tokens.shape
    q_cols = w_query.shape[1]
    features = w_query.shape[0]
    hd = width // 2
    most_held = capacity - rows
    piece_rows = most_held // tp

    def swap(x, bit, axis="tp"):
        size = lax.axis_size(axis)
        return lax.ppermute(x, axis, [(i, i ^ bit) for i in range(size)])

    def exchange(x):
        return lax.all_to_all(x, "seq", split_axis=0, concat_axis=0, tiled=True)

    phased = groups == 8
    half = jax.ShapeDtypeStruct((groups // 2, share, width), BF16)

    def by_pairs(keep, got):
        pairs = call(
            pair_kernel,
            [jax.ShapeDtypeStruct((2, share, width), BF16)] * (groups // 2),
            [VMEM] * 2,
            (keep, got),
            flops=0,
            mib=8,
            name="pair",
        )
        return [swap(x, 2 * k, "seq") if k else x for k, x in enumerate(pairs)]

    with jax.named_scope("tokens_gather"):
        across = swap(tokens, 2)
        beside = swap(tokens, 1)

    with jax.named_scope("cache_gather"):
        beside, stored = lax.optimization_barrier((beside, old_cache))
        if phased:
            keep, send = call(
                split_kernel, [half] * 2, [VMEM], (stored,), flops=0, mib=SPLIT_MIB, name="split"
            )
            got = swap(send, 1, "seq")
            arrived = by_pairs(keep, got)
        else:
            arrived = [exchange(stored).reshape(groups * share, width)]
        plan = jnp.concatenate([cached_lens, span_lens, old_table[0], new_table[0]])
        in_span = lax.broadcasted_iota(jnp.int32, (rows, 1), 0) < span_lens[0]
        own = jnp.where(in_span, tokens, jnp.zeros_like(tokens))
        gain = jnp.where(span_lens[0] > 0, norm_gain, 0.0)
        *arrived, across, own, gain, plan = lax.optimization_barrier(
            (*arrived, across, own, gain, plan)
        )
        ordered = call(
            functools.partial(order_kernel, share),
            jax.ShapeDtypeStruct((piece_rows, width), BF16),
            [SMEM] + [VMEM] * len(arrived),
            (plan, *arrived),
            flops=2 * piece_rows * groups * share * width,
            name="order",
        )
        c_across = swap(ordered, 2)
        c_beside = swap(ordered, 1)

    with jax.named_scope("project"):
        corner = swap(across, 1)
        stacked = rows * (q_cols // hd)
        query, keyval, values, limits = call(
            project_kernel,
            [
                jax.ShapeDtypeStruct((stacked, hd), BF16),
                jax.ShapeDtypeStruct((rows, width), BF16),
                jax.ShapeDtypeStruct((rows, width), BF16),
                jax.ShapeDtypeStruct((2, 8, 128), F32),
            ],
            [VMEM] * 5 + [HBM] * 2,
            (
                own,
                beside,
                across,
                corner,
                gain.reshape(tp, 1, cols),
                w_query,
                w_keyval,
            ),
            flops=2 * rows * features * (q_cols + width),
            mib=PROJECT_MIB,
            scratch=[
                pltpu.VMEM((rows, features), BF16),
                pltpu.VMEM(w_query.shape, BF16),
                pltpu.VMEM(w_keyval.shape, BF16),
                pltpu.SemaphoreType.DMA((2 * tp,)),
            ],
            name="project",
        )

    with jax.named_scope("extend"):
        sent = call(
            functools.partial(extend_kernel, share, block_rows, 2 if phased else 1),
            [half] * 2 if phased else [jax.ShapeDtypeStruct((groups * share, width), BF16)],
            [SMEM] + [VMEM] * (1 + len(arrived)),
            (plan, keyval, *arrived),
            flops=4 * groups * share * groups * share * width,
            name="extend",
        )
        *sent, c_across = lax.optimization_barrier((*sent, c_across))
        if phased:
            keep, got = sent[0], swap(sent[1], 1, "seq")
        cached = (ordered, c_beside, c_across, swap(c_across, 1))

    part = rows // CHUNKS
    tile_rows = ROW_TILE * (q_cols // hd)
    old = []
    mixed = None
    for c in range(CHUNKS):
        with jax.named_scope("attend"):
            outs = [jax.ShapeDtypeStruct((part, cols), BF16)] * 4
            if not old:
                outs += [
                    jax.ShapeDtypeStruct((most_held, width), BF16),
                    jax.ShapeDtypeStruct((8, 128), F32),
                ]
            seen = most_held + (c + 1) * part
            far0, far1, near0, near1, *made = call(
                functools.partial(attend_kernel, share, block_rows, c * part, part),
                outs,
                [SMEM] + [VMEM] * 8 + [HBM] + [VMEM] * len(old),
                (plan, query, keyval, values, limits, *cached, w_out, *old),
                flops=4 * part * seen * q_cols + 2 * part * q_cols * features,
                exps=part * seen * (q_cols // hd),
                mib=ATTEND_MIB,
                scratch=[
                    pltpu.VMEM((tile_rows, width), F32),
                    pltpu.VMEM((tile_rows, hd), F32),
                    pltpu.VMEM((part, q_cols), BF16),
                    pltpu.VMEM(w_out.shape, BF16),
                    pltpu.SemaphoreType.DMA,
                ],
                name="attend",
            )
            old = old or made
        with jax.named_scope("reduce"):
            if c == CHUNKS - 1 and phased:
                far1, got = lax.optimization_barrier((far1, got))
            got1 = swap(far1, 1)
            pair = (near1.astype(F32) + got1.astype(F32)).astype(BF16)
            query, pair = lax.optimization_barrier((query, pair))
            if c == CHUNKS - 1 and phased:
                _, got = lax.optimization_barrier((pair, got))
            elif c == CHUNKS - 1:
                pair, *sent = lax.optimization_barrier((pair, *sent))
            crossed = swap(pair, 2)
            got0 = swap(far0, 1)
        with jax.named_scope("finish"):
            mixed = call(
                functools.partial(finish_kernel, c * part),
                jax.ShapeDtypeStruct((rows, cols), BF16),
                [SMEM] + [VMEM] * 4 + [HBM] * (c > 0),
                (plan, own, near0, got0, crossed, *([mixed] if c else [])),
                flops=4 * part * cols,
                scratch=[pltpu.VMEM((part, cols), BF16), pltpu.SemaphoreType.DMA((2,))],
                name="finish",
                into={5: 0} if c else {},
            )
    with jax.named_scope("exchange"):
        if phased:
            new_cache = call(
                place_kernel,
                jax.ShapeDtypeStruct(old_cache.shape, BF16),
                [VMEM] * (groups // 2),
                by_pairs(keep, got),
                flops=0,
                mib=8,
                name="place",
            )
        else:
            new_cache = exchange(sent[0].reshape(groups, share, width))
    return (mixed, new_cache)


def solution(mesh):
    in_specs = (
        P("seq", "tp"),
        P(),
        P(None, "tp"),
        P(),
        P("tp", None),
        P("seq"),
        P("seq"),
        P("seq", None),
        P("seq", None),
        P("seq", "tp", None),
    )
    out_specs = (P("seq", "tp"), P("seq", "tp", None))
    return jax.shard_map(body, mesh=mesh, in_specs=in_specs, out_specs=out_specs, check_vma=False)
```

```python
import functools
import math

import jax
import jax.numpy as jnp
from jax import lax
from jax.experimental import pallas as pl
from jax.experimental.pallas import tpu as pltpu
from jax.sharding import PartitionSpec as P

EPSILON = 1e-05
MASKED = -1e30
CHUNKS = 2
PART_ROWS = 256
ROW_TILE = 128
KEY_TILE = 128
NORM_ROWS = 128
MIB = 51
PROJECT_MIB = 50.375
ATTEND_MIB = 49.75
SAFE = 60.0
F32 = jnp.float32
BF16 = jnp.bfloat16

VMEM = pl.BlockSpec(memory_space=pltpu.VMEM)
SMEM = pl.BlockSpec(memory_space=pltpu.SMEM)
HBM = pl.BlockSpec(memory_space=pltpu.HBM)


def dot(a, b):
    return lax.dot_general(a, b, (((1,), (0,)), ((), ())), preferred_element_type=F32)


def dot_t(a, b):
    return lax.dot_general(a, b, (((1,), (1,)), ((), ())), preferred_element_type=F32)


def collect_kernel(*refs):
    for k, pair_ref in enumerate(refs[:-1]):
        refs[-1][k] = pair_ref[1]


def place_kernel(got_ref, *refs):
    me = lax.axis_index("seq")
    for k, pair_ref in enumerate(refs[:-1]):
        refs[-1][me ^ (2 * k)] = pair_ref[0]
        refs[-1][me ^ (2 * k + 1)] = got_ref[k]


def order_kernel(share, plan_ref, arrived_ref, out_ref):
    rows, count = out_ref.shape[0], arrived_ref.shape[0]
    row = lax.broadcasted_iota(jnp.int32, (rows, 128), 0)
    block = row // share
    holder = jnp.zeros_like(block)
    for b in range(rows // share):
        holder = jnp.where(block == b, plan_ref[2 + b], holder)
    index = (holder * share + row % share)[:, :1]
    column = lax.broadcasted_iota(jnp.int32, (rows, count), 1)
    pick = jnp.where(column == index, 1.0, 0.0).astype(BF16)
    out_ref[...] = dot(pick, arrived_ref[...]).astype(BF16)


def extend_kernel(share, block_rows, plan_ref, kv_ref, arrived_ref, *out_refs):
    rows = arrived_ref.shape[0]
    groups = rows // share
    held, span = plan_ref[0], plan_ref[1]
    me = lax.axis_index("seq") if len(out_refs) > 1 else 0
    row = lax.broadcasted_iota(jnp.int32, (rows, 128), 0)
    target = row // share
    block, holder = jnp.zeros_like(row), jnp.zeros_like(row)
    for b in range(groups):
        hit = target == plan_ref[2 + groups + b] ^ me
        block = jnp.where(hit, b, block)
        holder = jnp.where(hit, plan_ref[2 + b], holder)
    position = block * block_rows + lax.axis_index("tp") * share + row % share
    old_row = jnp.where(position < held, holder * share + row % share, -1)[:, :1]
    fresh = position - held
    new_row = jnp.where((fresh >= 0) & (fresh < span), fresh, -1)[:, :1]
    column = lax.broadcasted_iota(jnp.int32, (rows, rows), 1)
    total = dot(jnp.where(column == old_row, 1.0, 0.0).astype(BF16), arrived_ref[...])
    column = lax.broadcasted_iota(jnp.int32, (rows, kv_ref.shape[0]), 1)
    total += dot(jnp.where(column == new_row, 1.0, 0.0).astype(BF16), kv_ref[...])
    total = total.astype(BF16)
    if len(out_refs) == 1:
        out_refs[0][...] = total
        return
    for slot in range(groups):
        out_refs[slot // 2][slot % 2] = total[slot * share : (slot + 1) * share]


def project_kernel(
    x0,
    x1,
    x2,
    x3,
    gain_ref,
    wq_hbm,
    wkv_hbm,
    q_ref,
    kv_ref,
    values_ref,
    limits_ref,
    normed,
    wq_ref,
    wkv_ref,
    sems,
):
    pieces = (x0, x1, x2, x3)
    me = lax.axis_index("tp")
    rows, width = x0.shape
    features = width * len(pieces)
    hd = kv_ref.shape[1] // 2
    heads = wq_ref.shape[1] // hd
    loads = []
    for hbm, to in ((wkv_hbm, wkv_ref), (wq_hbm, wq_ref)):
        for j in range(len(pieces)):
            at = pl.ds(j * width, width)
            loads.append(pltpu.make_async_copy(hbm.at[at], to.at[at], sems.at[len(loads)]))
            loads[-1].start()

    for step in range(0, rows, NORM_ROWS):
        at = pl.ds(step, NORM_ROWS)
        values = [piece[at, :].astype(F32) for piece in pieces]
        average = jnp.sum(sum(values), axis=1, keepdims=True) / features
        centred = [v - average for v in values]
        spread = jnp.sum(sum(v * v for v in centred), axis=1, keepdims=True) / features
        scale = lax.rsqrt(spread + EPSILON)
        for j, v in enumerate(centred):
            owner = me ^ j
            to = pl.ds(pl.multiple_of(owner * width, width), width)
            normed[at, to] = (v * scale * gain_ref[owner]).astype(BF16)
    for load in loads[: len(pieces)]:
        load.wait()
    keyval = dot(normed[...], wkv_ref[...]).astype(BF16)
    kv_ref[...] = keyval
    values_ref[:, hd:] = keyval[:, hd:]
    values_ref[:, :hd] = jnp.ones((rows, hd), BF16)
    limits_ref[0] = longest(keyval[:, :hd])
    for load in loads[len(pieces) :]:
        load.wait()
    query = dot(normed[...], wq_ref[...]).astype(BF16)
    for start in range(0, rows, ROW_TILE):
        for h in range(heads):
            q_ref[pl.ds(start * heads + h * ROW_TILE, ROW_TILE), :] = query[
                start : start + ROW_TILE, h * hd : (h + 1) * hd
            ]
    limits_ref[1] = longest(q_ref[...])


def longest(x):
    squares = dot(x * x, jnp.ones((x.shape[1], 128), BF16))
    return jnp.max(squares.reshape(-1, 8, 128), axis=0)


def attend_kernel(share, block_rows, start_row, rows, plan_ref, q_ref, kv_ref, new_ref, *refs):
    limits_ref, pieces, wout_hbm = refs[0], refs[1:5], refs[5]
    if start_row:
        old_ref, old_limit_ref = refs[6:8]
    else:
        old_ref, old_limit_ref = refs[10:12]
    total, high, context, wout, sem = refs[-5:]
    at = 8 if start_row else 6
    count = (len(refs) - 5 - at) // 2 if start_row else 2
    far_refs, near_refs = refs[at : at + count], refs[at + count : at + 2 * count]
    me = lax.axis_index("tp")
    held, span = plan_ref[0], plan_ref[1]
    piece_rows, width = pieces[0].shape
    hd = width // 2
    heads = q_ref.shape[0] // kv_ref.shape[0]
    load = pltpu.make_async_copy(wout_hbm, wout, sem)
    load.start()

    group = KEY_TILE * len(pieces)
    most = piece_rows // KEY_TILE
    tiles = (held + group - 1) // group
    if not start_row:
        row = lax.broadcasted_iota(jnp.int32, (KEY_TILE, hd), 0)
        place = row // share * block_rows + row % share
        limit = jnp.zeros((8, 128), F32)

        def lay(i, whole):
            source = pl.ds(i * KEY_TILE, KEY_TILE)
            for j, piece in enumerate(pieces):
                at = pl.ds(i * group + j * KEY_TILE, KEY_TILE)
                if whole:
                    old_ref[at, hd:] = piece[source, hd:]
                    old_ref[at, :hd] = jnp.ones((KEY_TILE, hd), BF16)
                    continue
                used = place + (me ^ j) * share + i * group < held
                old_ref[at, hd:] = jnp.where(used, piece[source, hd:].astype(F32), 0.0).astype(BF16)
                old_ref[at, :hd] = jnp.where(used, 1.0, 0.0).astype(BF16)

        for i in range(most):
            pl.when(i < tiles - 1)(functools.partial(lay, i, True))
            pl.when(i == tiles - 1)(functools.partial(lay, i, False))
        for piece in pieces:
            limit = jnp.maximum(limit, longest(piece[:, :hd]))
        old_limit_ref[...] = limit

    factor = hd ** (-0.5) * math.log2(math.e)
    key_limit = jnp.max(jnp.maximum(old_limit_ref[...], limits_ref[0]))
    small = key_limit * jnp.max(limits_ref[1]) * (1.05 / hd) < SAFE * SAFE

    tile_rows = ROW_TILE * heads

    def queries(t):
        return q_ref[pl.ds(start_row * heads + t * tile_rows, tile_rows), :]

    def old_keys(i):
        source = pl.ds(i * KEY_TILE, KEY_TILE)
        return jnp.concatenate([piece[source, :hd] for piece in pieces], axis=0)

    def new_scores(t):
        known = start_row + t * ROW_TILE
        scores = dot_t(queries(t), kv_ref[pl.ds(0, known + ROW_TILE), :hd])
        to = lax.broadcasted_iota(jnp.int32, (tile_rows, ROW_TILE), 0) % ROW_TILE
        by = lax.broadcasted_iota(jnp.int32, (tile_rows, ROW_TILE), 1)
        last = jnp.where(by <= to, scores[:, known:], MASKED)
        return jnp.concatenate([scores[:, :known], last], axis=1) if known else last

    def new_values(t):
        return new_ref[pl.ds(0, start_row + (t + 1) * ROW_TILE), :]

    def put(t, both):
        sums = both[:, :hd]
        inverse = pl.reciprocal(sums, approx=True)
        inverse = inverse * (2.0 - sums * inverse)
        out = (both[:, hd:] * inverse).astype(BF16)
        for h in range(heads):
            context[pl.ds(t * ROW_TILE, ROW_TILE), h * hd : (h + 1) * hd] = out[
                h * ROW_TILE : (h + 1) * ROW_TILE
            ]

    def fast(used, begin):
        row_tiles = range(begin // ROW_TILE, min(begin + PART_ROWS, rows) // ROW_TILE)
        steps = [(t, i) for t in row_tiles for i in range(used + 1)]

        def score(t, i):
            return new_scores(t) if i == used else dot_t(queries(t), old_keys(i))

        ahead, both = score(*steps[0]), None
        for at, (t, i) in enumerate(steps):
            scores = ahead
            if at + 1 < len(steps):
                ahead = score(*steps[at + 1])
            weights = jnp.exp2(scores * factor).astype(BF16)
            values = new_values(t) if i == used else old_ref[pl.ds(i * group, group), :]
            part = dot(weights, values)
            both = part if i == 0 else both + part
            if i == used:
                put(t, both)

    def exact(t):
        column = lax.broadcasted_iota(jnp.int32, (tile_rows, group), 1)
        within = column % KEY_TILE
        owner = me ^ (column // KEY_TILE)
        place = within // share * block_rows + within % share + owner * share

        def old_scores(i):
            scores = dot_t(queries(t), old_keys(pl.multiple_of(i, 1)))
            return jnp.where(place + i * group < held, scores, MASKED)

        def raise_high(i, carry):
            top = jnp.max(old_scores(i), axis=1, keepdims=True)
            high[...] = jnp.maximum(high[...], top)
            return carry

        def add(i, carry):
            weights = jnp.exp2((old_scores(i) - high[:, :1]) * factor).astype(BF16)
            total[...] += dot(weights, old_ref[pl.ds(pl.multiple_of(i * group, group), group), :])
            return carry

        high[...] = jnp.zeros_like(high) + jnp.max(new_scores(t), axis=1, keepdims=True)
        lax.fori_loop(0, tiles, raise_high, 0)
        weights = jnp.exp2((new_scores(t) - high[:, :1]) * factor).astype(BF16)
        total[...] = dot(weights, new_values(t))
        lax.fori_loop(0, tiles, add, 0)
        put(t, total[...])

    for begin in range(0, rows, PART_ROWS):
        busy = start_row + begin < span
        for used in range(1, most + 1):
            pl.when(busy & small & (tiles == used))(functools.partial(fast, used, begin))

        @pl.when(busy & jnp.logical_not(small))
        def _():
            for t in range(begin // ROW_TILE, min(begin + PART_ROWS, rows) // ROW_TILE):
                exact(t)

        @pl.when(jnp.logical_not(busy))
        def _():
            context[pl.ds(begin, PART_ROWS), :] = jnp.zeros((PART_ROWS, context.shape[1]), BF16)

    load.wait()
    cols = wout.shape[1] // 4
    for k in (3, 1, 2, 0):
        columns = pl.ds(pl.multiple_of((me ^ k) * cols, cols), cols)
        part = dot(context[...], wout[:, columns]).astype(BF16)
        refs = far_refs if k & 1 else near_refs
        if k < 2:
            refs[0][...] = part
            continue
        size = rows // (len(refs) - 1)
        for i, ref in enumerate(refs[1:]):
            ref[...] = part[i * size : (i + 1) * size]


def hand_on_kernel(in_ref, out_ref):
    pass


def finish_kernel(at, plan_ref, tokens_ref, near_ref, got_ref, *refs):
    out_hbm, done, sems = refs[-3:]
    crossed_refs = refs[: sems.shape[0]]
    size = crossed_refs[0].shape[0]
    stores = []
    for i, crossed_ref in enumerate(crossed_refs):
        here = pl.ds(i * size, size)
        there = pl.ds(at + i * size, size)
        kept = near_ref[here, :].astype(F32) + got_ref[here, :].astype(F32)
        total = tokens_ref[there, :].astype(F32) + (kept + crossed_ref[...].astype(F32))
        row = lax.broadcasted_iota(jnp.int32, total.shape, 0) + (at + i * size)
        done[here, :] = jnp.where(row < plan_ref[1], total, 0.0).astype(BF16)
        stores.append(pltpu.make_async_copy(done.at[here], out_hbm.at[there], sems.at[i]))
        stores[-1].start()
    for store in stores:
        store.wait()


def call(
    kernel, out_shape, in_specs, args, flops, mib=MIB, scratch=(), exps=0, name=None, into=None
):
    outs = out_shape if isinstance(out_shape, (list, tuple)) else [out_shape]
    moved = sum(a.size * a.dtype.itemsize for a in list(args) + list(outs))
    return pl.pallas_call(
        kernel,
        out_shape=out_shape,
        in_specs=in_specs,
        out_specs=jax.tree.map(lambda _: VMEM if into is None else HBM, out_shape),
        input_output_aliases=into or {},
        scratch_shapes=list(scratch),
        cost_estimate=pl.CostEstimate(flops=flops, bytes_accessed=moved, transcendentals=exps),
        compiler_params=pltpu.CompilerParams(vmem_limit_bytes=int(mib * 1024 * 1024)),
        name=name,
    )(*args)


def body(
    tokens,
    norm_gain,
    w_query,
    w_keyval,
    w_out,
    span_lens,
    cached_lens,
    old_table,
    new_table,
    old_cache,
):
    tp = lax.axis_size("tp")
    groups, share, width = old_cache.shape
    block_rows = share * tp
    capacity = groups * block_rows
    rows, cols = tokens.shape
    q_cols = w_query.shape[1]
    features = w_query.shape[0]
    hd = width // 2
    most_held = capacity - rows
    piece_rows = most_held // tp

    def swap(x, bit, axis="tp"):
        size = lax.axis_size(axis)
        return lax.ppermute(x, axis, [(i, i ^ bit) for i in range(size)])

    def exchange(x):
        return lax.all_to_all(x, "seq", split_axis=0, concat_axis=0, tiled=True)

    phased = groups == 8
    pair_of_blocks = jax.ShapeDtypeStruct((2, share, width), BF16)

    with jax.named_scope("tokens_gather"):
        across = swap(tokens, 2)
        beside = swap(tokens, 1)

    with jax.named_scope("cache_gather"):
        beside, stored = lax.optimization_barrier((beside, old_cache))
        arrived = exchange(stored).reshape(groups * share, width)
        plan = jnp.concatenate([cached_lens, span_lens, old_table[0], new_table[0]])
        in_span = lax.broadcasted_iota(jnp.int32, (rows, 1), 0) < span_lens[0]
        own = jnp.where(in_span, tokens, jnp.zeros_like(tokens))
        gain = jnp.where(span_lens[0] > 0, norm_gain, 0.0)
        arrived, across, own, gain, plan = lax.optimization_barrier(
            (arrived, across, own, gain, plan)
        )
        ordered = call(
            functools.partial(order_kernel, share),
            jax.ShapeDtypeStruct((piece_rows, width), BF16),
            [SMEM, VMEM],
            (plan, arrived),
            flops=2 * piece_rows * groups * share * width,
            name="order",
        )
        c_across = swap(ordered, 2)
        c_beside = swap(ordered, 1)

    with jax.named_scope("project"):
        corner = swap(across, 1)
        stacked = rows * (q_cols // hd)
        query, keyval, values, limits = call(
            project_kernel,
            [
                jax.ShapeDtypeStruct((stacked, hd), BF16),
                jax.ShapeDtypeStruct((rows, width), BF16),
                jax.ShapeDtypeStruct((rows, width), BF16),
                jax.ShapeDtypeStruct((2, 8, 128), F32),
            ],
            [VMEM] * 5 + [HBM] * 2,
            (
                own,
                beside,
                across,
                corner,
                gain.reshape(tp, 1, cols),
                w_query,
                w_keyval,
            ),
            flops=2 * rows * features * (q_cols + width),
            mib=PROJECT_MIB,
            scratch=[
                pltpu.VMEM((rows, features), BF16),
                pltpu.VMEM(w_query.shape, BF16),
                pltpu.VMEM(w_keyval.shape, BF16),
                pltpu.SemaphoreType.DMA((2 * tp,)),
            ],
            name="project",
        )

    with jax.named_scope("extend"):
        sent = call(
            functools.partial(extend_kernel, share, block_rows),
            [pair_of_blocks] * (groups // 2)
            if phased
            else [jax.ShapeDtypeStruct((groups * share, width), BF16)],
            [SMEM] + [VMEM] * 2,
            (plan, keyval, arrived),
            flops=4 * groups * share * groups * share * width,
            name="extend",
        )
        *sent, c_across = lax.optimization_barrier((*sent, c_across))
        if phased:
            pairs = [swap(x, 2 * k, "seq") if k else x for k, x in enumerate(sent)]
        cached = (ordered, c_beside, c_across, swap(c_across, 1))

    part = rows // CHUNKS
    tile_rows = ROW_TILE * (q_cols // hd)
    old = []
    mixed = None
    for c in range(CHUNKS):
        last = c == CHUNKS - 1
        pieces = 2 if last else 1
        with jax.named_scope("attend"):
            outs = [jax.ShapeDtypeStruct((part, cols), BF16)]
            outs += [jax.ShapeDtypeStruct((part // pieces, cols), BF16)] * pieces
            outs += outs
            if not old:
                outs += [
                    jax.ShapeDtypeStruct((most_held, width), BF16),
                    jax.ShapeDtypeStruct((8, 128), F32),
                ]
            seen = most_held + (c + 1) * part
            sums = list(call(
                functools.partial(attend_kernel, share, block_rows, c * part, part),
                outs,
                [SMEM] + [VMEM] * 8 + [HBM] + [VMEM] * len(old),
                (plan, query, keyval, values, limits, *cached, w_out, *old),
                flops=4 * part * seen * q_cols + 2 * part * q_cols * features,
                exps=part * seen * (q_cols // hd),
                mib=ATTEND_MIB,
                scratch=[
                    pltpu.VMEM((tile_rows, width), F32),
                    pltpu.VMEM((tile_rows, hd), F32),
                    pltpu.VMEM((part, q_cols), BF16),
                    pltpu.VMEM(w_out.shape, BF16),
                    pltpu.SemaphoreType.DMA,
                ],
                name="attend",
            ))
            far0, far1 = sums[0], sums[1 : 1 + pieces]
            near0, near1 = sums[1 + pieces], sums[2 + pieces : 2 + 2 * pieces]
            old = old or sums[2 + 2 * pieces :]
        with jax.named_scope("reduce"):
            if c == 0 and phased:
                far1[0], *pairs = lax.optimization_barrier((far1[0], *pairs))
            got1 = [swap(x, 1) for x in far1]
            if c and last:
                before = pl.pallas_call(
                    hand_on_kernel,
                    out_shape=jax.ShapeDtypeStruct(before.shape, BF16),
                    in_specs=[pl.BlockSpec(memory_space=pl.ANY)],
                    out_specs=pl.BlockSpec(memory_space=pl.ANY),
                    input_output_aliases={0: 0},
                    cost_estimate=pl.CostEstimate(
                        flops=1 << 34, bytes_accessed=1024, transcendentals=0
                    ),
                    compiler_params=pltpu.CompilerParams(vmem_limit_bytes=1 << 20),
                    name="hand_on",
                )(before)
                before, *got1 = lax.optimization_barrier((before, *got1))
            both = [(x.astype(F32) + y.astype(F32)).astype(BF16) for x, y in zip(near1, got1)]
            if not last:
                query, both[0] = lax.optimization_barrier((query, both[0]))
            crossed = [swap(x, 2) for x in both]
            got0 = swap(far0, 1)
        if not last:
            before, unfinished = crossed[0], (near0, got0)
            continue
        for at, near, got, over in ((0, *unfinished, [before]), (part, near0, got0, crossed)):
            with jax.named_scope("finish"):
                mixed = call(
                    functools.partial(finish_kernel, at),
                    jax.ShapeDtypeStruct((rows, cols), BF16),
                    [SMEM] + [VMEM] * (3 + len(over)) + [HBM] * (at > 0),
                    (plan, own, near, got, *over, *([mixed] if at else [])),
                    flops=4 * part * cols,
                    scratch=[
                        pltpu.VMEM((part, cols), BF16),
                        pltpu.SemaphoreType.DMA((len(over),)),
                    ],
                    name="finish",
                    into={4 + len(over): 0} if at else {},
                )

    with jax.named_scope("exchange"):
        if phased:
            *pairs, _ = lax.optimization_barrier((*pairs, both[-1]))
            onward = call(
                collect_kernel,
                jax.ShapeDtypeStruct((groups // 2, share, width), BF16),
                [VMEM] * len(pairs),
                pairs,
                flops=0,
                mib=8,
                name="collect",
            )
            new_cache = call(
                place_kernel,
                jax.ShapeDtypeStruct(old_cache.shape, BF16),
                [VMEM] * (1 + len(pairs)),
                (swap(onward, 1, "seq"), *pairs),
                flops=0,
                mib=8,
                name="place",
            )
        else:
            new_cache = exchange(sent[0].reshape(groups, share, width))
    return (mixed, new_cache)


def solution(mesh):
    in_specs = (
        P("seq", "tp"),
        P(),
        P(None, "tp"),
        P(),
        P("tp", None),
        P("seq"),
        P("seq"),
        P("seq", None),
        P("seq", None),
        P("seq", "tp", None),
    )
    out_specs = (P("seq", "tp"), P("seq", "tp", None))
    return jax.shard_map(body, mesh=mesh, in_specs=in_specs, out_specs=out_specs, check_vma=False)
```

```python
import functools
import math

import jax
import jax.numpy as jnp
from jax import lax
from jax.experimental import pallas as pl
from jax.experimental.pallas import tpu as pltpu
from jax.sharding import PartitionSpec as P

EPSILON = 1e-05
MASKED = -1e30
CHUNKS = 2
PART_ROWS = 256
ROW_TILE = 128
KEY_TILE = 128
NORM_ROWS = 128
MIB = 51
PROJECT_MIB = 50.375
LEAST = -3e38
ATTEND_MIB = 49.75
SAFE = 60.0
F32 = jnp.float32
BF16 = jnp.bfloat16

VMEM = pl.BlockSpec(memory_space=pltpu.VMEM)
SMEM = pl.BlockSpec(memory_space=pltpu.SMEM)
HBM = pl.BlockSpec(memory_space=pltpu.HBM)


def dot(a, b):
    return lax.dot_general(a, b, (((1,), (0,)), ((), ())), preferred_element_type=F32)


def dot_t(a, b):
    return lax.dot_general(a, b, (((1,), (1,)), ((), ())), preferred_element_type=F32)


def pair_kernel(keep_ref, got_ref, *pair_refs):
    for k, pair_ref in enumerate(pair_refs):
        pair_ref[0] = keep_ref[k]
        pair_ref[1] = got_ref[k]


def place_kernel(*refs):
    me = lax.axis_index("seq")
    for k, pair_ref in enumerate(refs[:-1]):
        for j in range(2):
            refs[-1][me ^ (2 * k + j)] = pair_ref[j]


def order_kernel(share, plan_ref, arrived_ref, out_ref):
    rows, count = out_ref.shape[0], arrived_ref.shape[0]
    row = lax.broadcasted_iota(jnp.int32, (rows, 128), 0)
    block = row // share
    holder = jnp.zeros_like(block)
    for b in range(rows // share):
        holder = jnp.where(block == b, plan_ref[2 + b], holder)
    index = (holder * share + row % share)[:, :1]
    column = lax.broadcasted_iota(jnp.int32, (rows, count), 1)
    pick = jnp.where(column == index, 1.0, 0.0).astype(BF16)
    out_ref[...] = dot(pick, arrived_ref[...]).astype(BF16)


def extend_kernel(share, block_rows, plan_ref, kv_ref, arrived_ref, *out_refs):
    rows = arrived_ref.shape[0]
    groups = rows // share
    held, span = plan_ref[0], plan_ref[1]
    me = lax.axis_index("seq") if len(out_refs) > 1 else 0
    row = lax.broadcasted_iota(jnp.int32, (rows, 128), 0)
    target = row // share
    block, holder = jnp.zeros_like(row), jnp.zeros_like(row)
    for b in range(groups):
        hit = target == plan_ref[2 + groups + b] ^ me
        block = jnp.where(hit, b, block)
        holder = jnp.where(hit, plan_ref[2 + b], holder)
    position = block * block_rows + lax.axis_index("tp") * share + row % share
    old_row = jnp.where(position < held, holder * share + row % share, -1)[:, :1]
    fresh = position - held
    new_row = jnp.where((fresh >= 0) & (fresh < span), fresh, -1)[:, :1]
    column = lax.broadcasted_iota(jnp.int32, (rows, rows), 1)
    total = dot(jnp.where(column == old_row, 1.0, 0.0).astype(BF16), arrived_ref[...])
    column = lax.broadcasted_iota(jnp.int32, (rows, kv_ref.shape[0]), 1)
    total += dot(jnp.where(column == new_row, 1.0, 0.0).astype(BF16), kv_ref[...])
    total = total.astype(BF16)
    if len(out_refs) == 1:
        out_refs[0][...] = total
        return
    for slot in range(groups):
        out_refs[slot % 2][slot // 2] = total[slot * share : (slot + 1) * share]


def project_kernel(
    x0,
    x1,
    x2,
    x3,
    gain_ref,
    wq_hbm,
    wkv_hbm,
    q_ref,
    kv_ref,
    values_ref,
    limits_ref,
    normed,
    wq_ref,
    wkv_ref,
    sems,
):
    pieces = (x0, x1, x2, x3)
    me = lax.axis_index("tp")
    rows, width = x0.shape
    features = width * len(pieces)
    hd = kv_ref.shape[1] // 2
    heads = wq_ref.shape[1] // hd
    loads = []
    for hbm, to in ((wkv_hbm, wkv_ref), (wq_hbm, wq_ref)):
        for j in range(len(pieces)):
            at = pl.ds(j * width, width)
            loads.append(pltpu.make_async_copy(hbm.at[at], to.at[at], sems.at[len(loads)]))
            loads[-1].start()

    for step in range(0, rows, NORM_ROWS):
        at = pl.ds(step, NORM_ROWS)
        values = [piece[at, :].astype(F32) for piece in pieces]
        average = jnp.sum(sum(values), axis=1, keepdims=True) / features
        centred = [v - average for v in values]
        spread = jnp.sum(sum(v * v for v in centred), axis=1, keepdims=True) / features
        scale = lax.rsqrt(spread + EPSILON)
        for j, v in enumerate(centred):
            owner = me ^ j
            to = pl.ds(pl.multiple_of(owner * width, width), width)
            normed[at, to] = (v * scale * gain_ref[owner]).astype(BF16)
    for load in loads[: len(pieces)]:
        load.wait()
    keyval = dot(normed[...], wkv_ref[...]).astype(BF16)
    kv_ref[...] = keyval
    values_ref[:, hd:] = keyval[:, hd:]
    values_ref[:, :hd] = jnp.ones((rows, hd), BF16)
    limits_ref[0] = longest(keyval[:, :hd])
    for load in loads[len(pieces) :]:
        load.wait()
    query = dot(normed[...], wq_ref[...]).astype(BF16)
    for start in range(0, rows, ROW_TILE):
        for h in range(heads):
            q_ref[pl.ds(start * heads + h * ROW_TILE, ROW_TILE), :] = query[
                start : start + ROW_TILE, h * hd : (h + 1) * hd
            ]
    limits_ref[1] = longest(q_ref[...])


def longest(x):
    squares = dot(x * x, jnp.ones((x.shape[1], 128), BF16))
    return jnp.max(squares.reshape(-1, 8, 128), axis=0)


def attend_kernel(share, block_rows, start_row, rows, plan_ref, q_ref, kv_ref, new_ref, *refs):
    limits_ref, pieces, wout_hbm = refs[0], refs[1:5], refs[5]
    if start_row:
        old_ref, old_limit_ref = refs[6:8]
    else:
        old_ref, old_limit_ref = refs[10:12]
    total, high, context, wout, sem = refs[-5:]
    at = 8 if start_row else 6
    far_refs, near_refs = refs[at : at + 2], refs[at + 2 : at + 4]
    me = lax.axis_index("tp")
    held, span = plan_ref[0], plan_ref[1]
    piece_rows, width = pieces[0].shape
    hd = width // 2
    heads = q_ref.shape[0] // kv_ref.shape[0]
    load = pltpu.make_async_copy(wout_hbm, wout, sem)
    load.start()

    group = KEY_TILE * len(pieces)
    most = piece_rows // KEY_TILE
    tiles = (held + group - 1) // group
    if not start_row:
        row = lax.broadcasted_iota(jnp.int32, (KEY_TILE, hd), 0)
        place = row // share * block_rows + row % share
        limit = jnp.zeros((8, 128), F32)

        def lay(i, whole):
            source = pl.ds(i * KEY_TILE, KEY_TILE)
            for j, piece in enumerate(pieces):
                at = pl.ds(i * group + j * KEY_TILE, KEY_TILE)
                if whole:
                    old_ref[at, hd:] = piece[source, hd:]
                    old_ref[at, :hd] = jnp.ones((KEY_TILE, hd), BF16)
                    continue
                used = place + (me ^ j) * share + i * group < held
                old_ref[at, hd:] = jnp.where(used, piece[source, hd:].astype(F32), 0.0).astype(BF16)
                old_ref[at, :hd] = jnp.where(used, 1.0, 0.0).astype(BF16)

        for i in range(most):
            pl.when(i < tiles - 1)(functools.partial(lay, i, True))
            pl.when(i == tiles - 1)(functools.partial(lay, i, False))
        for piece in pieces:
            limit = jnp.maximum(limit, longest(piece[:, :hd]))
        old_limit_ref[...] = limit

    factor = hd ** (-0.5) * math.log2(math.e)
    key_limit = jnp.max(jnp.maximum(old_limit_ref[...], limits_ref[0]))
    small = key_limit * jnp.max(limits_ref[1]) * (1.05 / hd) < SAFE * SAFE

    tile_rows = ROW_TILE * heads

    def queries(t):
        return q_ref[pl.ds(start_row * heads + t * tile_rows, tile_rows), :]

    def old_keys(i):
        source = pl.ds(i * KEY_TILE, KEY_TILE)
        return jnp.concatenate([piece[source, :hd] for piece in pieces], axis=0)

    def new_scores(t):
        known = start_row + t * ROW_TILE
        scores = dot_t(queries(t), kv_ref[pl.ds(0, known + ROW_TILE), :hd])
        to = lax.broadcasted_iota(jnp.int32, (tile_rows, ROW_TILE), 0) % ROW_TILE
        by = lax.broadcasted_iota(jnp.int32, (tile_rows, ROW_TILE), 1)
        last = jnp.where(by <= to, scores[:, known:], MASKED)
        return jnp.concatenate([scores[:, :known], last], axis=1) if known else last

    def new_values(t):
        return new_ref[pl.ds(0, start_row + (t + 1) * ROW_TILE), :]

    def put(t, both):
        sums = both[:, :hd]
        inverse = pl.reciprocal(sums, approx=True)
        inverse = inverse * (2.0 - sums * inverse)
        out = (both[:, hd:] * inverse).astype(BF16)
        for h in range(heads):
            context[pl.ds(t * ROW_TILE, ROW_TILE), h * hd : (h + 1) * hd] = out[
                h * ROW_TILE : (h + 1) * ROW_TILE
            ]

    def fast(used, begin):
        row_tiles = range(begin // ROW_TILE, min(begin + PART_ROWS, rows) // ROW_TILE)
        steps = [(t, i) for t in row_tiles for i in range(used + 1)]

        def score(t, i):
            return new_scores(t) if i == used else dot_t(queries(t), old_keys(i))

        ahead, both = score(*steps[0]), None
        for at, (t, i) in enumerate(steps):
            scores = ahead
            if at + 1 < len(steps):
                ahead = score(*steps[at + 1])
            weights = jnp.exp2(scores * factor).astype(BF16)
            values = new_values(t) if i == used else old_ref[pl.ds(i * group, group), :]
            part = dot(weights, values)
            both = part if i == 0 else both + part
            if i == used:
                put(t, both)

    def exact(t):
        column = lax.broadcasted_iota(jnp.int32, (tile_rows, group), 1)
        within = column % KEY_TILE
        owner = me ^ (column // KEY_TILE)
        place = within // share * block_rows + within % share + owner * share

        def old_scores(i):
            scores = dot_t(queries(t), old_keys(pl.multiple_of(i, 1)))
            return jnp.where(place + i * group < held, scores, MASKED)

        def raise_high(i, carry):
            top = jnp.max(old_scores(i), axis=1, keepdims=True)
            high[...] = jnp.maximum(high[...], top)
            return carry

        def add(i, carry):
            weights = jnp.exp2((old_scores(i) - high[:, :1]) * factor).astype(BF16)
            total[...] += dot(weights, old_ref[pl.ds(pl.multiple_of(i * group, group), group), :])
            return carry

        high[...] = jnp.zeros_like(high) + jnp.max(new_scores(t), axis=1, keepdims=True)
        lax.fori_loop(0, tiles, raise_high, 0)
        weights = jnp.exp2((new_scores(t) - high[:, :1]) * factor).astype(BF16)
        total[...] = dot(weights, new_values(t))
        lax.fori_loop(0, tiles, add, 0)
        put(t, total[...])

    for begin in range(0, rows, PART_ROWS):
        busy = start_row + begin < span
        for used in range(1, most + 1):
            pl.when(busy & small & (tiles == used))(functools.partial(fast, used, begin))

        @pl.when(busy & jnp.logical_not(small))
        def _():
            for t in range(begin // ROW_TILE, min(begin + PART_ROWS, rows) // ROW_TILE):
                exact(t)

        @pl.when(jnp.logical_not(busy))
        def _():
            context[pl.ds(begin, PART_ROWS), :] = jnp.zeros((PART_ROWS, context.shape[1]), BF16)

    load.wait()
    cols = wout.shape[1] // 4
    for k in (3, 1, 2, 0):
        columns = pl.ds(pl.multiple_of((me ^ k) * cols, cols), cols)
        part = dot(context[...], wout[:, columns]).astype(BF16)
        if k & 1:
            far_refs[k >> 1][...] = part
        else:
            near_refs[k >> 1][...] = part


def hand_on_kernel(in_ref, out_ref):
    pass


def finish_kernel(at, plan_ref, tokens_ref, near_ref, got_ref, crossed_ref, *refs):
    out_hbm, done, sems = refs[-3:]
    half = near_ref.shape[0] // 2
    stores = []
    for i in range(2):
        here = pl.ds(i * half, half)
        there = pl.ds(at + i * half, half)
        kept = near_ref[here, :].astype(F32) + got_ref[here, :].astype(F32)
        total = tokens_ref[there, :].astype(F32) + (kept + crossed_ref[here, :].astype(F32))
        row = lax.broadcasted_iota(jnp.int32, total.shape, 0) + (at + i * half)
        done[here, :] = jnp.where(row < plan_ref[1], total, 0.0).astype(BF16)
        stores.append(pltpu.make_async_copy(done.at[here], out_hbm.at[there], sems.at[i]))
        stores[-1].start()
    for store in stores:
        store.wait()


def call(
    kernel, out_shape, in_specs, args, flops, mib=MIB, scratch=(), exps=0, name=None, into=None
):
    outs = out_shape if isinstance(out_shape, (list, tuple)) else [out_shape]
    moved = sum(a.size * a.dtype.itemsize for a in list(args) + list(outs))
    return pl.pallas_call(
        kernel,
        out_shape=out_shape,
        in_specs=in_specs,
        out_specs=jax.tree.map(lambda _: VMEM if into is None else HBM, out_shape),
        input_output_aliases=into or {},
        scratch_shapes=list(scratch),
        cost_estimate=pl.CostEstimate(flops=flops, bytes_accessed=moved, transcendentals=exps),
        compiler_params=pltpu.CompilerParams(vmem_limit_bytes=int(mib * 1024 * 1024)),
        name=name,
    )(*args)


def body(
    tokens,
    norm_gain,
    w_query,
    w_keyval,
    w_out,
    span_lens,
    cached_lens,
    old_table,
    new_table,
    old_cache,
):
    tp = lax.axis_size("tp")
    groups, share, width = old_cache.shape
    block_rows = share * tp
    capacity = groups * block_rows
    rows, cols = tokens.shape
    q_cols = w_query.shape[1]
    features = w_query.shape[0]
    hd = width // 2
    most_held = capacity - rows
    piece_rows = most_held // tp

    def swap(x, bit, axis="tp"):
        size = lax.axis_size(axis)
        return lax.ppermute(x, axis, [(i, i ^ bit) for i in range(size)])

    def exchange(x):
        return lax.all_to_all(x, "seq", split_axis=0, concat_axis=0, tiled=True)

    phased = groups == 8

    with jax.named_scope("tokens_gather"):
        across = swap(tokens, 2)
        beside = swap(tokens, 1)

    with jax.named_scope("cache_gather"):
        beside, stored = lax.optimization_barrier((beside, old_cache))
        arrived = exchange(stored).reshape(groups * share, width)
        gain = jnp.maximum(norm_gain, LEAST).reshape(tp, 1, cols)
        own = jnp.maximum(tokens, jnp.asarray(LEAST, BF16))
        across, *lens = lax.optimization_barrier(
            (across, cached_lens, span_lens, old_table[0], new_table[0])
        )
        plan = jnp.concatenate(lens)
        arrived, across, own, gain, plan = lax.optimization_barrier(
            (arrived, across, own, gain, plan)
        )
        ordered = call(
            functools.partial(order_kernel, share),
            jax.ShapeDtypeStruct((piece_rows, width), BF16),
            [SMEM, VMEM],
            (plan, arrived),
            flops=2 * piece_rows * groups * share * width,
            name="order",
        )
        c_across = swap(ordered, 2)
        c_beside = swap(ordered, 1)

    with jax.named_scope("project"):
        corner = swap(across, 1)
        stacked = rows * (q_cols // hd)
        query, keyval, values, limits = call(
            project_kernel,
            [
                jax.ShapeDtypeStruct((stacked, hd), BF16),
                jax.ShapeDtypeStruct((rows, width), BF16),
                jax.ShapeDtypeStruct((rows, width), BF16),
                jax.ShapeDtypeStruct((2, 8, 128), F32),
            ],
            [VMEM] * 5 + [HBM] * 2,
            (
                own,
                beside,
                across,
                corner,
                gain,
                w_query,
                w_keyval,
            ),
            flops=2 * rows * features * (q_cols + width),
            mib=PROJECT_MIB,
            scratch=[
                pltpu.VMEM((rows, features), BF16),
                pltpu.VMEM(w_query.shape, BF16),
                pltpu.VMEM(w_keyval.shape, BF16),
                pltpu.SemaphoreType.DMA((2 * tp,)),
            ],
            name="project",
        )

    with jax.named_scope("extend"):
        sent = call(
            functools.partial(extend_kernel, share, block_rows),
            [jax.ShapeDtypeStruct((groups // 2, share, width), BF16)] * 2
            if phased
            else [jax.ShapeDtypeStruct((groups * share, width), BF16)],
            [SMEM] + [VMEM] * 2,
            (plan, keyval, arrived),
            flops=4 * groups * share * groups * share * width,
            name="extend",
        )
        *sent, c_across = lax.optimization_barrier((*sent, c_across))
        if phased:
            keep, got = sent[0], swap(sent[1], 1, "seq")
        cached = (ordered, c_beside, c_across, swap(c_across, 1))

    part = rows // CHUNKS
    tile_rows = ROW_TILE * (q_cols // hd)
    old = []
    mixed = None
    for c in range(CHUNKS):
        last = c == CHUNKS - 1
        with jax.named_scope("attend"):
            outs = [jax.ShapeDtypeStruct((part, cols), BF16)]
            outs *= 4
            if not old:
                outs += [
                    jax.ShapeDtypeStruct((most_held, width), BF16),
                    jax.ShapeDtypeStruct((8, 128), F32),
                ]
            seen = most_held + (c + 1) * part
            sums = list(call(
                functools.partial(attend_kernel, share, block_rows, c * part, part),
                outs,
                [SMEM] + [VMEM] * 8 + [HBM] + [VMEM] * len(old),
                (plan, query, keyval, values, limits, *cached, w_out, *old),
                flops=4 * part * seen * q_cols + 2 * part * q_cols * features,
                exps=part * seen * (q_cols // hd),
                mib=ATTEND_MIB,
                scratch=[
                    pltpu.VMEM((tile_rows, width), F32),
                    pltpu.VMEM((tile_rows, hd), F32),
                    pltpu.VMEM((part, q_cols), BF16),
                    pltpu.VMEM(w_out.shape, BF16),
                    pltpu.SemaphoreType.DMA,
                ],
                name="attend",
            ))
            far0, far1, near0, near1 = sums[:4]
            old = old or sums[4:]
        with jax.named_scope("reduce"):
            if c == 0 and phased:
                far1, got = lax.optimization_barrier((far1, got))
            got1 = swap(far1, 1)
            if c and last:
                before = pl.pallas_call(
                    hand_on_kernel,
                    out_shape=jax.ShapeDtypeStruct(before.shape, BF16),
                    in_specs=[pl.BlockSpec(memory_space=pl.ANY)],
                    out_specs=pl.BlockSpec(memory_space=pl.ANY),
                    input_output_aliases={0: 0},
                    cost_estimate=pl.CostEstimate(
                        flops=1 << 34, bytes_accessed=1024, transcendentals=0
                    ),
                    compiler_params=pltpu.CompilerParams(vmem_limit_bytes=1 << 20),
                    name="hand_on",
                )(before)
                before, got1 = lax.optimization_barrier((before, got1))
            pair = (near1.astype(F32) + got1.astype(F32)).astype(BF16)
            if not last:
                query, pair = lax.optimization_barrier((query, pair))
            if last and phased:
                pair, got = lax.optimization_barrier((pair, got))
            crossed = swap(pair, 2)
            got0 = swap(far0, 1)
        if not last:
            before, unfinished = crossed, (near0, got0)
            continue
        for at, near, beside, over in ((0, *unfinished, before), (part, near0, got0, crossed)):
            with jax.named_scope("finish"):
                mixed = call(
                    functools.partial(finish_kernel, at),
                    jax.ShapeDtypeStruct((rows, cols), BF16),
                    [SMEM] + [VMEM] * 4 + [HBM] * (at > 0),
                    (plan, own, near, beside, over, *([mixed] if at else [])),
                    flops=4 * part * cols,
                    scratch=[
                        pltpu.VMEM((part, cols), BF16),
                        pltpu.SemaphoreType.DMA((2,)),
                    ],
                    name="finish",
                    into={5: 0} if at else {},
                )

    with jax.named_scope("exchange"):
        if phased:
            pairs = call(
                pair_kernel,
                [jax.ShapeDtypeStruct((2, share, width), BF16)] * (groups // 2),
                [VMEM] * 2,
                (keep, got),
                flops=0,
                mib=8,
                name="pair",
            )
            new_cache = call(
                place_kernel,
                jax.ShapeDtypeStruct(old_cache.shape, BF16),
                [VMEM] * len(pairs),
                [swap(x, 2 * k, "seq") if k else x for k, x in enumerate(pairs)],
                flops=0,
                mib=8,
                name="place",
            )
        else:
            new_cache = exchange(sent[0].reshape(groups, share, width))
    return (mixed, new_cache)


def solution(mesh):
    in_specs = (
        P("seq", "tp"),
        P(),
        P(None, "tp"),
        P(),
        P("tp", None),
        P("seq"),
        P("seq"),
        P("seq", None),
        P("seq", None),
        P("seq", "tp", None),
    )
    out_specs = (P("seq", "tp"), P("seq", "tp", None))
    return jax.shard_map(body, mesh=mesh, in_specs=in_specs, out_specs=out_specs, check_vma=False)
```

```python
import functools
import math

import jax
import jax.numpy as jnp
from jax import lax
from jax.experimental import pallas as pl
from jax.experimental.pallas import tpu as pltpu
from jax.sharding import PartitionSpec as P

EPSILON = 1e-05
MASKED = -1e30
CHUNKS = 2
PART_ROWS = 256
ROW_TILE = 128
KEY_TILE = 128
NORM_ROWS = 128
MIB = 51
PROJECT_MIB = 50.375
LEAST = -3e38
ATTEND_MIB = 49.75
SAFE = 60.0
F32 = jnp.float32
BF16 = jnp.bfloat16

VMEM = pl.BlockSpec(memory_space=pltpu.VMEM)
SMEM = pl.BlockSpec(memory_space=pltpu.SMEM)
HBM = pl.BlockSpec(memory_space=pltpu.HBM)


def dot(a, b):
    return lax.dot_general(a, b, (((1,), (0,)), ((), ())), preferred_element_type=F32)


def dot_t(a, b):
    return lax.dot_general(a, b, (((1,), (1,)), ((), ())), preferred_element_type=F32)


def pair_kernel(keep_ref, got_ref, *pair_refs):
    for k, pair_ref in enumerate(pair_refs):
        pair_ref[0] = keep_ref[k]
        pair_ref[1] = got_ref[k]


def place_kernel(*refs):
    me = lax.axis_index("seq")
    for k, pair_ref in enumerate(refs[:-1]):
        for j in range(2):
            refs[-1][me ^ (2 * k + j)] = pair_ref[j]


def order_kernel(share, plan_ref, arrived_ref, out_ref):
    rows, count = out_ref.shape[0], arrived_ref.shape[0]
    row = lax.broadcasted_iota(jnp.int32, (rows, 128), 0)
    block = row // share
    holder = jnp.zeros_like(block)
    for b in range(rows // share):
        holder = jnp.where(block == b, plan_ref[2 + b], holder)
    index = (holder * share + row % share)[:, :1]
    column = lax.broadcasted_iota(jnp.int32, (rows, count), 1)
    pick = jnp.where(column == index, 1.0, 0.0).astype(BF16)
    out_ref[...] = dot(pick, arrived_ref[...]).astype(BF16)


def extend_kernel(share, block_rows, plan_ref, kv_ref, arrived_ref, *out_refs):
    rows = arrived_ref.shape[0]
    groups = rows // share
    held, span = plan_ref[0], plan_ref[1]
    me = lax.axis_index("seq") if len(out_refs) > 1 else 0
    row = lax.broadcasted_iota(jnp.int32, (rows, 128), 0)
    target = row // share
    block, holder = jnp.zeros_like(row), jnp.zeros_like(row)
    for b in range(groups):
        hit = target == plan_ref[2 + groups + b] ^ me
        block = jnp.where(hit, b, block)
        holder = jnp.where(hit, plan_ref[2 + b], holder)
    position = block * block_rows + lax.axis_index("tp") * share + row % share
    old_row = jnp.where(position < held, holder * share + row % share, -1)[:, :1]
    fresh = position - held
    new_row = jnp.where((fresh >= 0) & (fresh < span), fresh, -1)[:, :1]
    column = lax.broadcasted_iota(jnp.int32, (rows, rows), 1)
    total = dot(jnp.where(column == old_row, 1.0, 0.0).astype(BF16), arrived_ref[...])
    column = lax.broadcasted_iota(jnp.int32, (rows, kv_ref.shape[0]), 1)
    total += dot(jnp.where(column == new_row, 1.0, 0.0).astype(BF16), kv_ref[...])
    total = total.astype(BF16)
    if len(out_refs) == 1:
        out_refs[0][...] = total
        return
    for slot in range(groups):
        out_refs[slot % 2][slot // 2] = total[slot * share : (slot + 1) * share]


def project_kernel(
    x0,
    x1,
    x2,
    x3,
    gain_ref,
    wq_hbm,
    wkv_hbm,
    q_ref,
    kv_ref,
    values_ref,
    limits_ref,
    normed,
    wq_ref,
    wkv_ref,
    sems,
):
    pieces = (x0, x1, x2, x3)
    me = lax.axis_index("tp")
    rows, width = x0.shape
    features = width * len(pieces)
    hd = kv_ref.shape[1] // 2
    heads = wq_ref.shape[1] // hd
    loads = []
    for hbm, to in ((wkv_hbm, wkv_ref), (wq_hbm, wq_ref)):
        for j in range(len(pieces)):
            at = pl.ds(j * width, width)
            loads.append(pltpu.make_async_copy(hbm.at[at], to.at[at], sems.at[len(loads)]))
            loads[-1].start()

    for step in range(0, rows, NORM_ROWS):
        at = pl.ds(step, NORM_ROWS)
        values = [piece[at, :].astype(F32) for piece in pieces]
        average = jnp.sum(sum(values), axis=1, keepdims=True) / features
        centred = [v - average for v in values]
        spread = jnp.sum(sum(v * v for v in centred), axis=1, keepdims=True) / features
        scale = lax.rsqrt(spread + EPSILON)
        for j, v in enumerate(centred):
            owner = me ^ j
            to = pl.ds(pl.multiple_of(owner * width, width), width)
            normed[at, to] = (v * scale * gain_ref[owner]).astype(BF16)
    for load in loads[: len(pieces)]:
        load.wait()
    keyval = dot(normed[...], wkv_ref[...]).astype(BF16)
    kv_ref[...] = keyval
    values_ref[:, hd:] = keyval[:, hd:]
    values_ref[:, :hd] = jnp.ones((rows, hd), BF16)
    limits_ref[0] = longest(keyval[:, :hd])
    for load in loads[len(pieces) :]:
        load.wait()
    query = dot(normed[...], wq_ref[...]).astype(BF16)
    for start in range(0, rows, ROW_TILE):
        for h in range(heads):
            q_ref[pl.ds(start * heads + h * ROW_TILE, ROW_TILE), :] = query[
                start : start + ROW_TILE, h * hd : (h + 1) * hd
            ]
    limits_ref[1] = longest(q_ref[...])


def longest(x):
    squares = dot(x * x, jnp.ones((x.shape[1], 128), BF16))
    return jnp.max(squares.reshape(-1, 8, 128), axis=0)


def attend_kernel(share, block_rows, start_row, rows, plan_ref, q_ref, kv_ref, new_ref, *refs):
    limits_ref, pieces, wout_hbm = refs[0], refs[1:5], refs[5]
    if start_row:
        old_ref, old_limit_ref = refs[6:8]
    else:
        old_ref, old_limit_ref = refs[10:12]
    total, high, context, wout, sem = refs[-5:]
    at = 8 if start_row else 6
    far_refs, near_refs = refs[at : at + 2], refs[at + 2 : at + 4]
    me = lax.axis_index("tp")
    held, span = plan_ref[0], plan_ref[1]
    piece_rows, width = pieces[0].shape
    hd = width // 2
    heads = q_ref.shape[0] // kv_ref.shape[0]
    load = pltpu.make_async_copy(wout_hbm, wout, sem)
    load.start()

    group = KEY_TILE * len(pieces)
    most = piece_rows // KEY_TILE
    tiles = (held + group - 1) // group
    if not start_row:
        row = lax.broadcasted_iota(jnp.int32, (KEY_TILE, hd), 0)
        place = row // share * block_rows + row % share
        limit = jnp.zeros((8, 128), F32)

        def lay(i, whole):
            source = pl.ds(i * KEY_TILE, KEY_TILE)
            for j, piece in enumerate(pieces):
                at = pl.ds(i * group + j * KEY_TILE, KEY_TILE)
                if whole:
                    old_ref[at, hd:] = piece[source, hd:]
                    old_ref[at, :hd] = jnp.ones((KEY_TILE, hd), BF16)
                    continue
                used = place + (me ^ j) * share + i * group < held
                old_ref[at, hd:] = jnp.where(used, piece[source, hd:].astype(F32), 0.0).astype(BF16)
                old_ref[at, :hd] = jnp.where(used, 1.0, 0.0).astype(BF16)

        for i in range(most):
            pl.when(i < tiles - 1)(functools.partial(lay, i, True))
            pl.when(i == tiles - 1)(functools.partial(lay, i, False))
        for piece in pieces:
            limit = jnp.maximum(limit, longest(piece[:, :hd]))
        old_limit_ref[...] = limit

    factor = hd ** (-0.5) * math.log2(math.e)
    key_limit = jnp.max(jnp.maximum(old_limit_ref[...], limits_ref[0]))
    small = key_limit * jnp.max(limits_ref[1]) * (1.05 / hd) < SAFE * SAFE

    tile_rows = ROW_TILE * heads

    def queries(t):
        return q_ref[pl.ds(start_row * heads + t * tile_rows, tile_rows), :]

    def old_keys(i):
        source = pl.ds(i * KEY_TILE, KEY_TILE)
        return jnp.concatenate([piece[source, :hd] for piece in pieces], axis=0)

    def new_scores(t):
        known = start_row + t * ROW_TILE
        scores = dot_t(queries(t), kv_ref[pl.ds(0, known + ROW_TILE), :hd])
        to = lax.broadcasted_iota(jnp.int32, (tile_rows, ROW_TILE), 0) % ROW_TILE
        by = lax.broadcasted_iota(jnp.int32, (tile_rows, ROW_TILE), 1)
        last = jnp.where(by <= to, scores[:, known:], MASKED)
        return jnp.concatenate([scores[:, :known], last], axis=1) if known else last

    def new_values(t):
        return new_ref[pl.ds(0, start_row + (t + 1) * ROW_TILE), :]

    def put(t, both):
        sums = both[:, :hd]
        inverse = pl.reciprocal(sums, approx=True)
        inverse = inverse * (2.0 - sums * inverse)
        out = (both[:, hd:] * inverse).astype(BF16)
        for h in range(heads):
            context[pl.ds(t * ROW_TILE, ROW_TILE), h * hd : (h + 1) * hd] = out[
                h * ROW_TILE : (h + 1) * ROW_TILE
            ]

    def fast(used, begin):
        row_tiles = range(begin // ROW_TILE, min(begin + PART_ROWS, rows) // ROW_TILE)
        steps = [(t, i) for t in row_tiles for i in range(used + 1)]

        def score(t, i):
            return new_scores(t) if i == used else dot_t(queries(t), old_keys(i))

        ahead, both = score(*steps[0]), None
        for at, (t, i) in enumerate(steps):
            scores = ahead
            if at + 1 < len(steps):
                ahead = score(*steps[at + 1])
            weights = jnp.exp2(scores * factor).astype(BF16)
            values = new_values(t) if i == used else old_ref[pl.ds(i * group, group), :]
            part = dot(weights, values)
            both = part if i == 0 else both + part
            if i == used:
                put(t, both)

    def exact(t):
        column = lax.broadcasted_iota(jnp.int32, (tile_rows, group), 1)
        within = column % KEY_TILE
        owner = me ^ (column // KEY_TILE)
        place = within // share * block_rows + within % share + owner * share

        def old_scores(i):
            scores = dot_t(queries(t), old_keys(pl.multiple_of(i, 1)))
            return jnp.where(place + i * group < held, scores, MASKED)

        def raise_high(i, carry):
            top = jnp.max(old_scores(i), axis=1, keepdims=True)
            high[...] = jnp.maximum(high[...], top)
            return carry

        def add(i, carry):
            weights = jnp.exp2((old_scores(i) - high[:, :1]) * factor).astype(BF16)
            total[...] += dot(weights, old_ref[pl.ds(pl.multiple_of(i * group, group), group), :])
            return carry

        high[...] = jnp.zeros_like(high) + jnp.max(new_scores(t), axis=1, keepdims=True)
        lax.fori_loop(0, tiles, raise_high, 0)
        weights = jnp.exp2((new_scores(t) - high[:, :1]) * factor).astype(BF16)
        total[...] = dot(weights, new_values(t))
        lax.fori_loop(0, tiles, add, 0)
        put(t, total[...])

    for begin in range(0, rows, PART_ROWS):
        busy = start_row + begin < span
        for used in range(1, most + 1):
            pl.when(busy & small & (tiles == used))(functools.partial(fast, used, begin))

        @pl.when(busy & jnp.logical_not(small))
        def _():
            for t in range(begin // ROW_TILE, min(begin + PART_ROWS, rows) // ROW_TILE):
                exact(t)

        @pl.when(jnp.logical_not(busy))
        def _():
            context[pl.ds(begin, PART_ROWS), :] = jnp.zeros((PART_ROWS, context.shape[1]), BF16)

    load.wait()
    cols = wout.shape[1] // 4
    for k in (3, 1, 2, 0):
        columns = pl.ds(pl.multiple_of((me ^ k) * cols, cols), cols)
        part = dot(context[...], wout[:, columns]).astype(BF16)
        if k & 1:
            far_refs[k >> 1][...] = part
        else:
            near_refs[k >> 1][...] = part


def hand_on_kernel(in_ref, out_ref):
    pass


def finish_kernel(at, plan_ref, tokens_ref, near_ref, got_ref, crossed_ref, *refs):
    out_hbm, done, sems = refs[-3:]
    half = near_ref.shape[0] // 2
    stores = []
    for i in range(2):
        here = pl.ds(i * half, half)
        there = pl.ds(at + i * half, half)
        kept = near_ref[here, :].astype(F32) + got_ref[here, :].astype(F32)
        total = tokens_ref[there, :].astype(F32) + (kept + crossed_ref[here, :].astype(F32))
        row = lax.broadcasted_iota(jnp.int32, total.shape, 0) + (at + i * half)
        done[here, :] = jnp.where(row < plan_ref[1], total, 0.0).astype(BF16)
        stores.append(pltpu.make_async_copy(done.at[here], out_hbm.at[there], sems.at[i]))
        stores[-1].start()
    for store in stores:
        store.wait()


def call(
    kernel, out_shape, in_specs, args, flops, mib=MIB, scratch=(), exps=0, name=None, into=None
):
    outs = out_shape if isinstance(out_shape, (list, tuple)) else [out_shape]
    moved = sum(a.size * a.dtype.itemsize for a in list(args) + list(outs))
    return pl.pallas_call(
        kernel,
        out_shape=out_shape,
        in_specs=in_specs,
        out_specs=jax.tree.map(lambda _: VMEM if into is None else HBM, out_shape),
        input_output_aliases=into or {},
        scratch_shapes=list(scratch),
        cost_estimate=pl.CostEstimate(flops=flops, bytes_accessed=moved, transcendentals=exps),
        compiler_params=pltpu.CompilerParams(vmem_limit_bytes=int(mib * 1024 * 1024)),
        name=name,
    )(*args)


def body(
    tokens,
    norm_gain,
    w_query,
    w_keyval,
    w_out,
    span_lens,
    cached_lens,
    old_table,
    new_table,
    old_cache,
):
    tp = lax.axis_size("tp")
    groups, share, width = old_cache.shape
    block_rows = share * tp
    capacity = groups * block_rows
    rows, cols = tokens.shape
    q_cols = w_query.shape[1]
    features = w_query.shape[0]
    hd = width // 2
    most_held = capacity - rows
    piece_rows = most_held // tp

    def swap(x, bit, axis="tp"):
        size = lax.axis_size(axis)
        return lax.ppermute(x, axis, [(i, i ^ bit) for i in range(size)])

    def exchange(x):
        return lax.all_to_all(x, "seq", split_axis=0, concat_axis=0, tiled=True)

    phased = groups == 8

    with jax.named_scope("tokens_gather"):
        across = swap(tokens, 2)
        beside = swap(tokens, 1)

    with jax.named_scope("cache_gather"):
        cached_lens, stored = lax.optimization_barrier((swap(cached_lens, 1), old_cache))
        arrived = exchange(stored).reshape(groups * share, width)
        gain = jnp.maximum(norm_gain, LEAST).reshape(tp, 1, cols)
        own = jnp.maximum(tokens, jnp.asarray(LEAST, BF16))
        across, *lens = lax.optimization_barrier(
            (across, cached_lens, span_lens, old_table[0], new_table[0])
        )
        plan = jnp.concatenate(lens)
        arrived, across, own, gain, plan = lax.optimization_barrier(
            (arrived, across, own, gain, plan)
        )
        ordered = call(
            functools.partial(order_kernel, share),
            jax.ShapeDtypeStruct((piece_rows, width), BF16),
            [SMEM, VMEM],
            (plan, arrived),
            flops=2 * piece_rows * groups * share * width,
            name="order",
        )
        c_across = swap(ordered, 2)
        c_beside = swap(ordered, 1)

    with jax.named_scope("project"):
        corner = swap(across, 1)
        stacked = rows * (q_cols // hd)
        query, keyval, values, limits = call(
            project_kernel,
            [
                jax.ShapeDtypeStruct((stacked, hd), BF16),
                jax.ShapeDtypeStruct((rows, width), BF16),
                jax.ShapeDtypeStruct((rows, width), BF16),
                jax.ShapeDtypeStruct((2, 8, 128), F32),
            ],
            [VMEM] * 5 + [HBM] * 2,
            (
                own,
                beside,
                across,
                corner,
                gain,
                w_query,
                w_keyval,
            ),
            flops=2 * rows * features * (q_cols + width),
            mib=PROJECT_MIB,
            scratch=[
                pltpu.VMEM((rows, features), BF16),
                pltpu.VMEM(w_query.shape, BF16),
                pltpu.VMEM(w_keyval.shape, BF16),
                pltpu.SemaphoreType.DMA((2 * tp,)),
            ],
            name="project",
        )

    with jax.named_scope("extend"):
        sent = call(
            functools.partial(extend_kernel, share, block_rows),
            [jax.ShapeDtypeStruct((groups // 2, share, width), BF16)] * 2
            if phased
            else [jax.ShapeDtypeStruct((groups * share, width), BF16)],
            [SMEM] + [VMEM] * 2,
            (plan, keyval, arrived),
            flops=4 * groups * share * groups * share * width,
            name="extend",
        )
        *sent, c_across = lax.optimization_barrier((*sent, c_across))
        if phased:
            keep, got = sent[0], swap(sent[1], 1, "seq")
        cached = (ordered, c_beside, c_across, swap(c_across, 1))

    part = rows // CHUNKS
    tile_rows = ROW_TILE * (q_cols // hd)
    old = []
    mixed = None
    for c in range(CHUNKS):
        last = c == CHUNKS - 1
        with jax.named_scope("attend"):
            outs = [jax.ShapeDtypeStruct((part, cols), BF16)]
            outs *= 4
            if not old:
                outs += [
                    jax.ShapeDtypeStruct((most_held, width), BF16),
                    jax.ShapeDtypeStruct((8, 128), F32),
                ]
            seen = most_held + (c + 1) * part
            sums = list(call(
                functools.partial(attend_kernel, share, block_rows, c * part, part),
                outs,
                [SMEM] + [VMEM] * 8 + [HBM] + [VMEM] * len(old),
                (plan, query, keyval, values, limits, *cached, w_out, *old),
                flops=4 * part * seen * q_cols + 2 * part * q_cols * features,
                exps=part * seen * (q_cols // hd),
                mib=ATTEND_MIB,
                scratch=[
                    pltpu.VMEM((tile_rows, width), F32),
                    pltpu.VMEM((tile_rows, hd), F32),
                    pltpu.VMEM((part, q_cols), BF16),
                    pltpu.VMEM(w_out.shape, BF16),
                    pltpu.SemaphoreType.DMA,
                ],
                name="attend",
            ))
            far0, far1, near0, near1 = sums[:4]
            old = old or sums[4:]
        with jax.named_scope("reduce"):
            if c == 0 and phased:
                far1, got = lax.optimization_barrier((far1, got))
            got1 = swap(far1, 1)
            if c and last:
                before = pl.pallas_call(
                    hand_on_kernel,
                    out_shape=jax.ShapeDtypeStruct(before.shape, BF16),
                    in_specs=[pl.BlockSpec(memory_space=pl.ANY)],
                    out_specs=pl.BlockSpec(memory_space=pl.ANY),
                    input_output_aliases={0: 0},
                    cost_estimate=pl.CostEstimate(
                        flops=1 << 34, bytes_accessed=1024, transcendentals=0
                    ),
                    compiler_params=pltpu.CompilerParams(vmem_limit_bytes=1 << 20),
                    name="hand_on",
                )(before)
                before, got1 = lax.optimization_barrier((before, got1))
            pair = (near1.astype(F32) + got1.astype(F32)).astype(BF16)
            if not last:
                query, pair = lax.optimization_barrier((query, pair))
            if last and phased:
                pair, got = lax.optimization_barrier((pair, got))
            crossed = swap(pair, 2)
            got0 = swap(far0, 1)
        if not last:
            before, unfinished = crossed, (near0, got0)
            continue
        for at, near, beside, over in ((0, *unfinished, before), (part, near0, got0, crossed)):
            with jax.named_scope("finish"):
                mixed = call(
                    functools.partial(finish_kernel, at),
                    jax.ShapeDtypeStruct((rows, cols), BF16),
                    [SMEM] + [VMEM] * 4 + [HBM] * (at > 0),
                    (plan, own, near, beside, over, *([mixed] if at else [])),
                    flops=4 * part * cols,
                    scratch=[
                        pltpu.VMEM((part, cols), BF16),
                        pltpu.SemaphoreType.DMA((2,)),
                    ],
                    name="finish",
                    into={5: 0} if at else {},
                )

    with jax.named_scope("exchange"):
        if phased:
            pairs = list(call(
                pair_kernel,
                [jax.ShapeDtypeStruct((2, share, width), BF16)] * (groups // 2),
                [VMEM] * 2,
                (keep, got),
                flops=0,
                mib=8,
                name="pair",
            ))
            for k in range(len(pairs) - 1, 0, -1):
                pairs[k] = swap(pairs[k], 2 * k, "seq")
            mixed, *pairs = lax.optimization_barrier((mixed, *pairs))
            new_cache = call(
                place_kernel,
                jax.ShapeDtypeStruct(old_cache.shape, BF16),
                [VMEM] * len(pairs),
                pairs,
                flops=0,
                mib=8,
                name="place",
            )
        else:
            new_cache = exchange(sent[0].reshape(groups, share, width))
    return (mixed, new_cache)


def solution(mesh):
    in_specs = (
        P("seq", "tp"),
        P(),
        P(None, "tp"),
        P(),
        P("tp", None),
        P("seq"),
        P("seq"),
        P("seq", None),
        P("seq", None),
        P("seq", "tp", None),
    )
    out_specs = (P("seq", "tp"), P("seq", "tp", None))
    return jax.shard_map(body, mesh=mesh, in_specs=in_specs, out_specs=out_specs, check_vma=False)
```

```python
import functools
import math

import jax
import jax.numpy as jnp
from jax import lax
from jax.experimental import pallas as pl
from jax.experimental.pallas import tpu as pltpu
from jax.sharding import PartitionSpec as P

EPSILON = 1e-05
MASKED = -1e30
CHUNKS = 2
PART_ROWS = 256
ROW_TILE = 128
KEY_TILE = 128
NORM_ROWS = 128
MIB = 51
PROJECT_MIB = 50.375
LEAST = -3e38
ATTEND_MIB = 49.75
SAFE = 60.0
F32 = jnp.float32
BF16 = jnp.bfloat16

VMEM = pl.BlockSpec(memory_space=pltpu.VMEM)
SMEM = pl.BlockSpec(memory_space=pltpu.SMEM)
HBM = pl.BlockSpec(memory_space=pltpu.HBM)


def dot(a, b):
    return lax.dot_general(a, b, (((1,), (0,)), ((), ())), preferred_element_type=F32)


def dot_t(a, b):
    return lax.dot_general(a, b, (((1,), (1,)), ((), ())), preferred_element_type=F32)


def pair_kernel(keep_ref, got_ref, *pair_refs):
    for k, pair_ref in enumerate(pair_refs):
        pair_ref[0] = keep_ref[k]
        pair_ref[1] = got_ref[k]


def place_kernel(*refs):
    me = lax.axis_index("seq")
    for k, pair_ref in enumerate(refs[:-1]):
        for j in range(2):
            refs[-1][me ^ (2 * k + j)] = pair_ref[j]


def order_kernel(share, plan_ref, arrived_ref, out_ref):
    rows, count = out_ref.shape[0], arrived_ref.shape[0]
    row = lax.broadcasted_iota(jnp.int32, (rows, 128), 0)
    block = row // share
    holder = jnp.zeros_like(block)
    for b in range(rows // share):
        holder = jnp.where(block == b, count // share - 1 - plan_ref[2 + b], holder)
    index = (holder * share + row % share)[:, :1]
    column = lax.broadcasted_iota(jnp.int32, (rows, count), 1)
    pick = jnp.where(column == index, 1.0, 0.0).astype(BF16)
    out_ref[...] = dot(pick, arrived_ref[...]).astype(BF16)


def extend_kernel(share, block_rows, plan_ref, kv_ref, arrived_ref, *out_refs):
    rows = arrived_ref.shape[0]
    groups = rows // share
    held, span = plan_ref[0], plan_ref[1]
    me = lax.axis_index("seq") if len(out_refs) > 1 else 0
    row = lax.broadcasted_iota(jnp.int32, (rows, 128), 0)
    target = row // share
    block, holder = jnp.zeros_like(row), jnp.zeros_like(row)
    for b in range(groups):
        hit = target == plan_ref[2 + groups + b] ^ me
        block = jnp.where(hit, b, block)
        holder = jnp.where(hit, groups - 1 - plan_ref[2 + b], holder)
    position = block * block_rows + lax.axis_index("tp") * share + row % share
    old_row = jnp.where(position < held, holder * share + row % share, -1)[:, :1]
    fresh = position - held
    new_row = jnp.where((fresh >= 0) & (fresh < span), fresh, -1)[:, :1]
    column = lax.broadcasted_iota(jnp.int32, (rows, rows), 1)
    total = dot(jnp.where(column == old_row, 1.0, 0.0).astype(BF16), arrived_ref[...])
    column = lax.broadcasted_iota(jnp.int32, (rows, kv_ref.shape[0]), 1)
    total += dot(jnp.where(column == new_row, 1.0, 0.0).astype(BF16), kv_ref[...])
    total = total.astype(BF16)
    if len(out_refs) == 1:
        out_refs[0][...] = total
        return
    for slot in range(groups):
        out_refs[slot % 2][slot // 2] = total[slot * share : (slot + 1) * share]


def project_kernel(
    x0,
    x1,
    x2,
    x3,
    gain_ref,
    wq_hbm,
    wkv_hbm,
    q_ref,
    kv_ref,
    values_ref,
    limits_ref,
    normed,
    wq_ref,
    wkv_ref,
    sems,
):
    pieces = (x0, x1, x2, x3)
    me = lax.axis_index("tp")
    rows, width = x0.shape
    features = width * len(pieces)
    hd = kv_ref.shape[1] // 2
    heads = wq_ref.shape[1] // hd
    loads = []
    for hbm, to in ((wkv_hbm, wkv_ref), (wq_hbm, wq_ref)):
        for j in range(len(pieces)):
            at = pl.ds(j * width, width)
            loads.append(pltpu.make_async_copy(hbm.at[at], to.at[at], sems.at[len(loads)]))
            loads[-1].start()

    for step in range(0, rows, NORM_ROWS):
        at = pl.ds(step, NORM_ROWS)
        values = [piece[at, :].astype(F32) for piece in pieces]
        average = jnp.sum(sum(values), axis=1, keepdims=True) / features
        centred = [v - average for v in values]
        spread = jnp.sum(sum(v * v for v in centred), axis=1, keepdims=True) / features
        scale = lax.rsqrt(spread + EPSILON)
        for j, v in enumerate(centred):
            owner = me ^ j
            to = pl.ds(pl.multiple_of(owner * width, width), width)
            normed[at, to] = (v * scale * gain_ref[owner]).astype(BF16)
    for load in loads[: len(pieces)]:
        load.wait()
    keyval = dot(normed[...], wkv_ref[...]).astype(BF16)
    kv_ref[...] = keyval
    values_ref[:, hd:] = keyval[:, hd:]
    values_ref[:, :hd] = jnp.ones((rows, hd), BF16)
    limits_ref[0] = longest(keyval[:, :hd])
    for load in loads[len(pieces) :]:
        load.wait()
    query = dot(normed[...], wq_ref[...]).astype(BF16)
    for start in range(0, rows, ROW_TILE):
        for h in range(heads):
            q_ref[pl.ds(start * heads + h * ROW_TILE, ROW_TILE), :] = query[
                start : start + ROW_TILE, h * hd : (h + 1) * hd
            ]
    limits_ref[1] = longest(q_ref[...])


def longest(x):
    squares = dot(x * x, jnp.ones((x.shape[1], 128), BF16))
    return jnp.max(squares.reshape(-1, 8, 128), axis=0)


def attend_kernel(share, block_rows, start_row, rows, plan_ref, q_ref, kv_ref, new_ref, *refs):
    limits_ref, pieces, wout_hbm = refs[0], refs[1:5], refs[5]
    if start_row:
        old_ref, old_limit_ref = refs[6:8]
    else:
        old_ref, old_limit_ref = refs[10:12]
    total, high, context, wout, sem = refs[-5:]
    at = 8 if start_row else 6
    far_refs, near_refs = refs[at : at + 2], refs[at + 2 : at + 4]
    me = lax.axis_index("tp")
    held, span = plan_ref[0], plan_ref[1]
    piece_rows, width = pieces[0].shape
    hd = width // 2
    heads = q_ref.shape[0] // kv_ref.shape[0]
    load = pltpu.make_async_copy(wout_hbm, wout, sem)
    load.start()

    group = KEY_TILE * len(pieces)
    most = piece_rows // KEY_TILE
    tiles = (held + group - 1) // group
    if not start_row:
        row = lax.broadcasted_iota(jnp.int32, (KEY_TILE, hd), 0)
        place = row // share * block_rows + row % share
        limit = jnp.zeros((8, 128), F32)

        def lay(i, whole):
            source = pl.ds(i * KEY_TILE, KEY_TILE)
            for j, piece in enumerate(pieces):
                at = pl.ds(i * group + j * KEY_TILE, KEY_TILE)
                if whole:
                    old_ref[at, hd:] = piece[source, hd:]
                    old_ref[at, :hd] = jnp.ones((KEY_TILE, hd), BF16)
                    continue
                used = place + (me ^ j) * share + i * group < held
                old_ref[at, hd:] = jnp.where(used, piece[source, hd:].astype(F32), 0.0).astype(BF16)
                old_ref[at, :hd] = jnp.where(used, 1.0, 0.0).astype(BF16)

        for i in range(most):
            pl.when(i < tiles - 1)(functools.partial(lay, i, True))
            pl.when(i == tiles - 1)(functools.partial(lay, i, False))
        for piece in pieces:
            limit = jnp.maximum(limit, longest(piece[:, :hd]))
        old_limit_ref[...] = limit

    factor = hd ** (-0.5) * math.log2(math.e)
    key_limit = jnp.max(jnp.maximum(old_limit_ref[...], limits_ref[0]))
    small = key_limit * jnp.max(limits_ref[1]) * (1.05 / hd) < SAFE * SAFE

    tile_rows = ROW_TILE * heads

    def queries(t):
        return q_ref[pl.ds(start_row * heads + t * tile_rows, tile_rows), :]

    def old_keys(i):
        source = pl.ds(i * KEY_TILE, KEY_TILE)
        return jnp.concatenate([piece[source, :hd] for piece in pieces], axis=0)

    def new_scores(t):
        known = start_row + t * ROW_TILE
        scores = dot_t(queries(t), kv_ref[pl.ds(0, known + ROW_TILE), :hd])
        to = lax.broadcasted_iota(jnp.int32, (tile_rows, ROW_TILE), 0) % ROW_TILE
        by = lax.broadcasted_iota(jnp.int32, (tile_rows, ROW_TILE), 1)
        last = jnp.where(by <= to, scores[:, known:], MASKED)
        return jnp.concatenate([scores[:, :known], last], axis=1) if known else last

    def new_values(t):
        return new_ref[pl.ds(0, start_row + (t + 1) * ROW_TILE), :]

    def put(t, both):
        sums = both[:, :hd]
        inverse = pl.reciprocal(sums, approx=True)
        inverse = inverse * (2.0 - sums * inverse)
        out = (both[:, hd:] * inverse).astype(BF16)
        for h in range(heads):
            context[pl.ds(t * ROW_TILE, ROW_TILE), h * hd : (h + 1) * hd] = out[
                h * ROW_TILE : (h + 1) * ROW_TILE
            ]

    def fast(used, begin):
        row_tiles = range(begin // ROW_TILE, min(begin + PART_ROWS, rows) // ROW_TILE)
        steps = [(t, i) for t in row_tiles for i in range(used + 1)]

        def score(t, i):
            return new_scores(t) if i == used else dot_t(queries(t), old_keys(i))

        ahead, both = score(*steps[0]), None
        for at, (t, i) in enumerate(steps):
            scores = ahead
            if at + 1 < len(steps):
                ahead = score(*steps[at + 1])
            weights = jnp.exp2(scores * factor).astype(BF16)
            values = new_values(t) if i == used else old_ref[pl.ds(i * group, group), :]
            part = dot(weights, values)
            both = part if i == 0 else both + part
            if i == used:
                put(t, both)

    def exact(t):
        column = lax.broadcasted_iota(jnp.int32, (tile_rows, group), 1)
        within = column % KEY_TILE
        owner = me ^ (column // KEY_TILE)
        place = within // share * block_rows + within % share + owner * share

        def old_scores(i):
            scores = dot_t(queries(t), old_keys(pl.multiple_of(i, 1)))
            return jnp.where(place + i * group < held, scores, MASKED)

        def raise_high(i, carry):
            top = jnp.max(old_scores(i), axis=1, keepdims=True)
            high[...] = jnp.maximum(high[...], top)
            return carry

        def add(i, carry):
            weights = jnp.exp2((old_scores(i) - high[:, :1]) * factor).astype(BF16)
            total[...] += dot(weights, old_ref[pl.ds(pl.multiple_of(i * group, group), group), :])
            return carry

        high[...] = jnp.zeros_like(high) + jnp.max(new_scores(t), axis=1, keepdims=True)
        lax.fori_loop(0, tiles, raise_high, 0)
        weights = jnp.exp2((new_scores(t) - high[:, :1]) * factor).astype(BF16)
        total[...] = dot(weights, new_values(t))
        lax.fori_loop(0, tiles, add, 0)
        put(t, total[...])

    for begin in range(0, rows, PART_ROWS):
        busy = start_row + begin < span
        for used in range(1, most + 1):
            pl.when(busy & small & (tiles == used))(functools.partial(fast, used, begin))

        @pl.when(busy & jnp.logical_not(small))
        def _():
            for t in range(begin // ROW_TILE, min(begin + PART_ROWS, rows) // ROW_TILE):
                exact(t)

        @pl.when(jnp.logical_not(busy))
        def _():
            context[pl.ds(begin, PART_ROWS), :] = jnp.zeros((PART_ROWS, context.shape[1]), BF16)

    load.wait()
    cols = wout.shape[1] // 4
    for k in (3, 1, 2, 0):
        columns = pl.ds(pl.multiple_of((me ^ k) * cols, cols), cols)
        part = dot(context[...], wout[:, columns]).astype(BF16)
        if k & 1:
            far_refs[k >> 1][...] = part
        else:
            near_refs[k >> 1][...] = part


def hand_on_kernel(in_ref, out_ref):
    pass


def finish_kernel(at, plan_ref, tokens_ref, near_ref, got_ref, crossed_ref, *refs):
    out_hbm, done, sems = refs[-3:]
    half = near_ref.shape[0] // 2
    stores = []
    for i in range(2):
        here = pl.ds(i * half, half)
        there = pl.ds(at + i * half, half)
        kept = near_ref[here, :].astype(F32) + got_ref[here, :].astype(F32)
        total = tokens_ref[there, :].astype(F32) + (kept + crossed_ref[here, :].astype(F32))
        row = lax.broadcasted_iota(jnp.int32, total.shape, 0) + (at + i * half)
        done[here, :] = jnp.where(row < plan_ref[1], total, 0.0).astype(BF16)
        stores.append(pltpu.make_async_copy(done.at[here], out_hbm.at[there], sems.at[i]))
        stores[-1].start()
    for store in stores:
        store.wait()


def call(
    kernel, out_shape, in_specs, args, flops, mib=MIB, scratch=(), exps=0, name=None, into=None
):
    outs = out_shape if isinstance(out_shape, (list, tuple)) else [out_shape]
    moved = sum(a.size * a.dtype.itemsize for a in list(args) + list(outs))
    return pl.pallas_call(
        kernel,
        out_shape=out_shape,
        in_specs=in_specs,
        out_specs=jax.tree.map(lambda _: VMEM if into is None else HBM, out_shape),
        input_output_aliases=into or {},
        scratch_shapes=list(scratch),
        cost_estimate=pl.CostEstimate(flops=flops, bytes_accessed=moved, transcendentals=exps),
        compiler_params=pltpu.CompilerParams(vmem_limit_bytes=int(mib * 1024 * 1024)),
        name=name,
    )(*args)


def body(
    tokens,
    norm_gain,
    w_query,
    w_keyval,
    w_out,
    span_lens,
    cached_lens,
    old_table,
    new_table,
    old_cache,
):
    tp = lax.axis_size("tp")
    groups, share, width = old_cache.shape
    block_rows = share * tp
    capacity = groups * block_rows
    rows, cols = tokens.shape
    q_cols = w_query.shape[1]
    features = w_query.shape[0]
    hd = width // 2
    most_held = capacity - rows
    piece_rows = most_held // tp

    def swap(x, bit, axis="tp"):
        size = lax.axis_size(axis)
        return lax.ppermute(x, axis, [(i, i ^ bit) for i in range(size)])

    def exchange(x):
        return lax.all_to_all(x, "seq", split_axis=0, concat_axis=0, tiled=True)

    phased = groups == 8

    with jax.named_scope("tokens_gather"):
        across = swap(tokens, 2)
        beside = swap(tokens, 1)

    with jax.named_scope("cache_gather"):
        beside, stored = lax.optimization_barrier((beside, jnp.flip(old_cache, 0)))
        arrived = lax.all_to_all(
            stored,
            "seq",
            split_axis=0,
            concat_axis=0,
            tiled=True,
            axis_index_groups=[list(range(groups))[::-1]],
        ).reshape(groups * share, width)
        gain = jnp.maximum(norm_gain, LEAST).reshape(tp, 1, cols)
        own = jnp.maximum(tokens, jnp.asarray(LEAST, BF16))
        across, *lens = lax.optimization_barrier(
            (across, cached_lens, span_lens, old_table[0], new_table[0])
        )
        plan = jnp.concatenate(lens)
        arrived, across, own, gain, plan = lax.optimization_barrier(
            (arrived, across, own, gain, plan)
        )
        ordered = call(
            functools.partial(order_kernel, share),
            jax.ShapeDtypeStruct((piece_rows, width), BF16),
            [SMEM, VMEM],
            (plan, arrived),
            flops=2 * piece_rows * groups * share * width,
            name="order",
        )
        c_across = swap(ordered, 2)
        c_beside = swap(ordered, 1)

    with jax.named_scope("project"):
        corner = swap(across, 1)
        stacked = rows * (q_cols // hd)
        query, keyval, values, limits = call(
            project_kernel,
            [
                jax.ShapeDtypeStruct((stacked, hd), BF16),
                jax.ShapeDtypeStruct((rows, width), BF16),
                jax.ShapeDtypeStruct((rows, width), BF16),
                jax.ShapeDtypeStruct((2, 8, 128), F32),
            ],
            [VMEM] * 5 + [HBM] * 2,
            (
                own,
                beside,
                across,
                corner,
                gain,
                w_query,
                w_keyval,
            ),
            flops=2 * rows * features * (q_cols + width),
            mib=PROJECT_MIB,
            scratch=[
                pltpu.VMEM((rows, features), BF16),
                pltpu.VMEM(w_query.shape, BF16),
                pltpu.VMEM(w_keyval.shape, BF16),
                pltpu.SemaphoreType.DMA((2 * tp,)),
            ],
            name="project",
        )

    with jax.named_scope("extend"):
        sent = call(
            functools.partial(extend_kernel, share, block_rows),
            [jax.ShapeDtypeStruct((groups // 2, share, width), BF16)] * 2
            if phased
            else [jax.ShapeDtypeStruct((groups * share, width), BF16)],
            [SMEM] + [VMEM] * 2,
            (plan, keyval, arrived),
            flops=4 * groups * share * groups * share * width,
            name="extend",
        )
        *sent, c_across = lax.optimization_barrier((*sent, c_across))
        if phased:
            keep, got = sent[0], swap(sent[1], 1, "seq")
        cached = (ordered, c_beside, c_across, swap(c_across, 1))

    part = rows // CHUNKS
    tile_rows = ROW_TILE * (q_cols // hd)
    old = []
    mixed = None
    for c in range(CHUNKS):
        last = c == CHUNKS - 1
        with jax.named_scope("attend"):
            outs = [jax.ShapeDtypeStruct((part, cols), BF16)]
            outs *= 4
            if not old:
                outs += [
                    jax.ShapeDtypeStruct((most_held, width), BF16),
                    jax.ShapeDtypeStruct((8, 128), F32),
                ]
            seen = most_held + (c + 1) * part
            sums = list(call(
                functools.partial(attend_kernel, share, block_rows, c * part, part),
                outs,
                [SMEM] + [VMEM] * 8 + [HBM] + [VMEM] * len(old),
                (plan, query, keyval, values, limits, *cached, w_out, *old),
                flops=4 * part * seen * q_cols + 2 * part * q_cols * features,
                exps=part * seen * (q_cols // hd),
                mib=ATTEND_MIB,
                scratch=[
                    pltpu.VMEM((tile_rows, width), F32),
                    pltpu.VMEM((tile_rows, hd), F32),
                    pltpu.VMEM((part, q_cols), BF16),
                    pltpu.VMEM(w_out.shape, BF16),
                    pltpu.SemaphoreType.DMA,
                ],
                name="attend",
            ))
            far0, far1, near0, near1 = sums[:4]
            old = old or sums[4:]
        with jax.named_scope("reduce"):
            if c == 0 and phased:
                far1, got = lax.optimization_barrier((far1, got))
            got1 = swap(far1, 1)
            if c and last:
                before = pl.pallas_call(
                    hand_on_kernel,
                    out_shape=jax.ShapeDtypeStruct(before.shape, BF16),
                    in_specs=[pl.BlockSpec(memory_space=pl.ANY)],
                    out_specs=pl.BlockSpec(memory_space=pl.ANY),
                    input_output_aliases={0: 0},
                    cost_estimate=pl.CostEstimate(
                        flops=1 << 34, bytes_accessed=1024, transcendentals=0
                    ),
                    compiler_params=pltpu.CompilerParams(vmem_limit_bytes=1 << 20),
                    name="hand_on",
                )(before)
                before, got1 = lax.optimization_barrier((before, got1))
            pair = (near1.astype(F32) + got1.astype(F32)).astype(BF16)
            if not last:
                query, pair = lax.optimization_barrier((query, pair))
            if last and phased:
                pair, got = lax.optimization_barrier((pair, got))
            crossed = swap(pair, 2)
            got0 = swap(far0, 1)
        if not last:
            before, unfinished = crossed, (near0, got0)
            continue
        for at, near, beside, over in ((0, *unfinished, before), (part, near0, got0, crossed)):
            with jax.named_scope("finish"):
                mixed = call(
                    functools.partial(finish_kernel, at),
                    jax.ShapeDtypeStruct((rows, cols), BF16),
                    [SMEM] + [VMEM] * 4 + [HBM] * (at > 0),
                    (plan, own, near, beside, over, *([mixed] if at else [])),
                    flops=4 * part * cols,
                    scratch=[
                        pltpu.VMEM((part, cols), BF16),
                        pltpu.SemaphoreType.DMA((2,)),
                    ],
                    name="finish",
                    into={5: 0} if at else {},
                )

    with jax.named_scope("exchange"):
        if phased:
            pairs = list(call(
                pair_kernel,
                [jax.ShapeDtypeStruct((2, share, width), BF16)] * (groups // 2),
                [VMEM] * 2,
                (keep, got),
                flops=0,
                mib=8,
                name="pair",
            ))
            for k in range(len(pairs) - 1, 0, -1):
                pairs[k] = swap(pairs[k], 2 * k, "seq")
            mixed, *pairs = lax.optimization_barrier((mixed, *pairs))
            new_cache = call(
                place_kernel,
                jax.ShapeDtypeStruct(old_cache.shape, BF16),
                [VMEM] * len(pairs),
                pairs,
                flops=0,
                mib=8,
                name="place",
            )
        else:
            new_cache = exchange(sent[0].reshape(groups, share, width))
    return (mixed, new_cache)


def solution(mesh):
    in_specs = (
        P("seq", "tp"),
        P(),
        P(None, "tp"),
        P(),
        P("tp", None),
        P("seq"),
        P("seq"),
        P("seq", None),
        P("seq", None),
        P("seq", "tp", None),
    )
    out_specs = (P("seq", "tp"), P("seq", "tp", None))
    return jax.shard_map(body, mesh=mesh, in_specs=in_specs, out_specs=out_specs, check_vma=False)
```

```python
import functools
import math

import jax
import jax.numpy as jnp
from jax import lax
from jax.experimental import pallas as pl
from jax.experimental.pallas import tpu as pltpu
from jax.sharding import PartitionSpec as P

EPSILON = 1e-05
MASKED = -1e30
CHUNKS = 2
PART_ROWS = 256
ROW_TILE = 128
KEY_TILE = 128
NORM_ROWS = 128
MIB = 51
PROJECT_MIB = 50.375
LEAST = -3e38
ATTEND_MIB = 49
SAFE = 60.0
F32 = jnp.float32
BF16 = jnp.bfloat16

VMEM = pl.BlockSpec(memory_space=pltpu.VMEM)
SMEM = pl.BlockSpec(memory_space=pltpu.SMEM)
HBM = pl.BlockSpec(memory_space=pltpu.HBM)


def dot(a, b):
    return lax.dot_general(a, b, (((1,), (0,)), ((), ())), preferred_element_type=F32)


def dot_t(a, b):
    return lax.dot_general(a, b, (((1,), (1,)), ((), ())), preferred_element_type=F32)


def pair_kernel(keep_ref, got_ref, *pair_refs):
    for k, pair_ref in enumerate(pair_refs):
        pair_ref[0] = keep_ref[k]
        pair_ref[1] = got_ref[k]


def order_kernel(share, plan_ref, arrived_ref, out_ref):
    rows, count = out_ref.shape[0], arrived_ref.shape[0]
    if share % 16 == 0:
        for b in range(rows // share):
            at = pl.ds(pl.multiple_of(plan_ref[2 + b] * share, share), share)
            out_ref[pl.ds(b * share, share), :] = arrived_ref[at, :]
        return
    row = lax.broadcasted_iota(jnp.int32, (rows, 128), 0)
    block = row // share
    holder = jnp.zeros_like(block)
    for b in range(rows // share):
        holder = jnp.where(block == b, plan_ref[2 + b], holder)
    index = (holder * share + row % share)[:, :1]
    column = lax.broadcasted_iota(jnp.int32, (rows, count), 1)
    pick = jnp.where(column == index, 1.0, 0.0).astype(BF16)
    out_ref[...] = dot(pick, arrived_ref[...]).astype(BF16)


def extend_kernel(share, block_rows, plan_ref, kv_ref, arrived_ref, *out_refs):
    rows = arrived_ref.shape[0]
    groups = rows // share
    held, span = plan_ref[0], plan_ref[1]
    me = lax.axis_index("seq") if len(out_refs) > 1 else 0
    row = lax.broadcasted_iota(jnp.int32, (rows, 128), 0)
    target = row // share
    block, holder = jnp.zeros_like(row), jnp.zeros_like(row)
    for b in range(groups):
        hit = target == plan_ref[2 + groups + b] ^ me
        block = jnp.where(hit, b, block)
        holder = jnp.where(hit, plan_ref[2 + b], holder)
    position = block * block_rows + lax.axis_index("tp") * share + row % share
    old_row = jnp.where(position < held, holder * share + row % share, -1)[:, :1]
    fresh = position - held
    new_row = jnp.where((fresh >= 0) & (fresh < span), fresh, -1)[:, :1]
    column = lax.broadcasted_iota(jnp.int32, (rows, rows), 1)
    total = dot(jnp.where(column == old_row, 1.0, 0.0).astype(BF16), arrived_ref[...])
    column = lax.broadcasted_iota(jnp.int32, (rows, kv_ref.shape[0]), 1)
    total += dot(jnp.where(column == new_row, 1.0, 0.0).astype(BF16), kv_ref[...])
    total = total.astype(BF16)
    if len(out_refs) == 1:
        out_refs[0][...] = total
        return
    for slot in range(groups):
        out_refs[slot % 2][slot // 2] = total[slot * share : (slot + 1) * share]


def project_kernel(
    x0,
    x1,
    x2,
    x3,
    gain_ref,
    wq_hbm,
    wkv_hbm,
    q_ref,
    kv_ref,
    values_ref,
    limits_ref,
    normed,
    wq_ref,
    wkv_ref,
    sems,
):
    pieces = (x0, x1, x2, x3)
    me = lax.axis_index("tp")
    rows, width = x0.shape
    features = width * len(pieces)
    hd = kv_ref.shape[1] // 2
    heads = wq_ref.shape[1] // hd
    loads = []
    for hbm, to in ((wkv_hbm, wkv_ref), (wq_hbm, wq_ref)):
        for j in range(len(pieces)):
            at = pl.ds(j * width, width)
            loads.append(pltpu.make_async_copy(hbm.at[at], to.at[at], sems.at[len(loads)]))
            loads[-1].start()

    for step in range(0, rows, NORM_ROWS):
        at = pl.ds(step, NORM_ROWS)
        values = [piece[at, :].astype(F32) for piece in pieces]
        average = jnp.sum(sum(values), axis=1, keepdims=True) / features
        centred = [v - average for v in values]
        spread = jnp.sum(sum(v * v for v in centred), axis=1, keepdims=True) / features
        scale = lax.rsqrt(spread + EPSILON)
        for j, v in enumerate(centred):
            owner = me ^ j
            to = pl.ds(pl.multiple_of(owner * width, width), width)
            normed[at, to] = (v * scale * gain_ref[owner]).astype(BF16)
    for load in loads[: len(pieces)]:
        load.wait()
    keyval = dot(normed[...], wkv_ref[...]).astype(BF16)
    kv_ref[...] = keyval
    values_ref[:, hd:] = keyval[:, hd:]
    values_ref[:, :hd] = jnp.ones((rows, hd), BF16)
    limits_ref[0] = longest(keyval[:, :hd])
    for load in loads[len(pieces) :]:
        load.wait()
    query = dot(normed[...], wq_ref[...]).astype(BF16)
    for start in range(0, rows, ROW_TILE):
        for h in range(heads):
            q_ref[pl.ds(start * heads + h * ROW_TILE, ROW_TILE), :] = query[
                start : start + ROW_TILE, h * hd : (h + 1) * hd
            ]
    limits_ref[1] = longest(q_ref[...])


def longest(x):
    squares = dot(x * x, jnp.ones((x.shape[1], 128), BF16))
    return jnp.max(squares.reshape(-1, 8, 128), axis=0)


def attend_kernel(share, block_rows, start_row, rows, plan_ref, q_ref, kv_ref, new_ref, *refs):
    limits_ref, pieces, wout_hbm = refs[0], refs[1:5], refs[5]
    total, high, context, wout, sem = refs[-5:]
    if start_row:
        old_ref, old_limit_ref, before_ref, far0_ref, far1_ref, near0_ref, near1_ref = refs[6:13]
    else:
        far1_ref, near1_ref, context_out, old_ref, old_limit_ref = refs[6:11]
    me = lax.axis_index("tp")
    held, span = plan_ref[0], plan_ref[1]
    piece_rows, width = pieces[0].shape
    hd = width // 2
    heads = q_ref.shape[0] // kv_ref.shape[0]
    load = pltpu.make_async_copy(wout_hbm, wout, sem)
    load.start()

    group = KEY_TILE * len(pieces)
    most = piece_rows // KEY_TILE
    tiles = (held + group - 1) // group
    if not start_row:
        row = lax.broadcasted_iota(jnp.int32, (KEY_TILE, hd), 0)
        place = row // share * block_rows + row % share
        limit = jnp.zeros((8, 128), F32)

        def lay(i, whole):
            source = pl.ds(i * KEY_TILE, KEY_TILE)
            for j, piece in enumerate(pieces):
                at = pl.ds(i * group + j * KEY_TILE, KEY_TILE)
                if whole:
                    old_ref[at, hd:] = piece[source, hd:]
                    old_ref[at, :hd] = jnp.ones((KEY_TILE, hd), BF16)
                    continue
                used = place + (me ^ j) * share + i * group < held
                old_ref[at, hd:] = jnp.where(used, piece[source, hd:].astype(F32), 0.0).astype(BF16)
                old_ref[at, :hd] = jnp.where(used, 1.0, 0.0).astype(BF16)

        for i in range(most):
            pl.when(i < tiles - 1)(functools.partial(lay, i, True))
            pl.when(i == tiles - 1)(functools.partial(lay, i, False))
        for piece in pieces:
            limit = jnp.maximum(limit, longest(piece[:, :hd]))
        old_limit_ref[...] = limit

    factor = hd ** (-0.5) * math.log2(math.e)
    key_limit = jnp.max(jnp.maximum(old_limit_ref[...], limits_ref[0]))
    small = key_limit * jnp.max(limits_ref[1]) * (1.05 / hd) < SAFE * SAFE

    tile_rows = ROW_TILE * heads

    def queries(t):
        return q_ref[pl.ds(start_row * heads + t * tile_rows, tile_rows), :]

    def old_keys(i):
        source = pl.ds(i * KEY_TILE, KEY_TILE)
        return jnp.concatenate([piece[source, :hd] for piece in pieces], axis=0)

    def new_scores(t):
        known = start_row + t * ROW_TILE
        scores = dot_t(queries(t), kv_ref[pl.ds(0, known + ROW_TILE), :hd])
        to = lax.broadcasted_iota(jnp.int32, (tile_rows, ROW_TILE), 0) % ROW_TILE
        by = lax.broadcasted_iota(jnp.int32, (tile_rows, ROW_TILE), 1)
        last = jnp.where(by <= to, scores[:, known:], MASKED)
        return jnp.concatenate([scores[:, :known], last], axis=1) if known else last

    def new_values(t):
        return new_ref[pl.ds(0, start_row + (t + 1) * ROW_TILE), :]

    def put(t, both):
        sums = both[:, :hd]
        inverse = pl.reciprocal(sums, approx=True)
        inverse = inverse * (2.0 - sums * inverse)
        out = (both[:, hd:] * inverse).astype(BF16)
        for h in range(heads):
            context[pl.ds(t * ROW_TILE, ROW_TILE), h * hd : (h + 1) * hd] = out[
                h * ROW_TILE : (h + 1) * ROW_TILE
            ]

    def fast(used, begin):
        row_tiles = range(begin // ROW_TILE, min(begin + PART_ROWS, rows) // ROW_TILE)
        steps = [(t, i) for t in row_tiles for i in range(used + 1)]

        def score(t, i):
            return new_scores(t) if i == used else dot_t(queries(t), old_keys(i))

        ahead, both = score(*steps[0]), None
        for at, (t, i) in enumerate(steps):
            scores = ahead
            if at + 1 < len(steps):
                ahead = score(*steps[at + 1])
            weights = jnp.exp2(scores * factor).astype(BF16)
            values = new_values(t) if i == used else old_ref[pl.ds(i * group, group), :]
            part = dot(weights, values)
            both = part if i == 0 else both + part
            if i == used:
                put(t, both)

    def exact(t):
        column = lax.broadcasted_iota(jnp.int32, (tile_rows, group), 1)
        within = column % KEY_TILE
        owner = me ^ (column // KEY_TILE)
        place = within // share * block_rows + within % share + owner * share

        def old_scores(i):
            scores = dot_t(queries(t), old_keys(pl.multiple_of(i, 1)))
            return jnp.where(place + i * group < held, scores, MASKED)

        def raise_high(i, carry):
            top = jnp.max(old_scores(i), axis=1, keepdims=True)
            high[...] = jnp.maximum(high[...], top)
            return carry

        def add(i, carry):
            weights = jnp.exp2((old_scores(i) - high[:, :1]) * factor).astype(BF16)
            total[...] += dot(weights, old_ref[pl.ds(pl.multiple_of(i * group, group), group), :])
            return carry

        high[...] = jnp.zeros_like(high) + jnp.max(new_scores(t), axis=1, keepdims=True)
        lax.fori_loop(0, tiles, raise_high, 0)
        weights = jnp.exp2((new_scores(t) - high[:, :1]) * factor).astype(BF16)
        total[...] = dot(weights, new_values(t))
        lax.fori_loop(0, tiles, add, 0)
        put(t, total[...])

    for begin in range(0, rows, PART_ROWS):
        busy = start_row + begin < span
        for used in range(1, most + 1):
            pl.when(busy & small & (tiles == used))(functools.partial(fast, used, begin))

        @pl.when(busy & jnp.logical_not(small))
        def _():
            for t in range(begin // ROW_TILE, min(begin + PART_ROWS, rows) // ROW_TILE):
                exact(t)

        @pl.when(jnp.logical_not(busy))
        def _():
            context[pl.ds(begin, PART_ROWS), :] = jnp.zeros((PART_ROWS, context.shape[1]), BF16)

    load.wait()
    cols = wout.shape[1] // 4

    def partial_sums(rows_of, k):
        columns = pl.ds(pl.multiple_of((me ^ k) * cols, cols), cols)
        return dot(rows_of[...], wout[:, columns]).astype(BF16)

    far1_ref[...] = partial_sums(context, 3)
    near1_ref[...] = partial_sums(context, 2)
    if not start_row:
        context_out[...] = context[...]
        return
    for at, rows_of in ((0, before_ref), (start_row, context)):
        far0_ref[pl.ds(at, rows), :] = partial_sums(rows_of, 1)
        near0_ref[pl.ds(at, rows), :] = partial_sums(rows_of, 0)


def hand_on_kernel(in_ref, out_ref):
    pass


def finish_kernel(at, phased, plan_ref, tokens_ref, near_ref, got_ref, crossed_ref, *refs):
    out_hbm, done, sems = refs[0 if not at else -3 - phased], refs[-2], refs[-1]
    rows = crossed_ref.shape[0]
    half = rows // 2
    stores = []
    if at and phased:
        me = lax.axis_index("seq")
        for k, pair_ref in enumerate(refs[:4]):
            for j in range(2):
                sem = sems.at[2 + len(stores)]
                slot = refs[-3].at[me ^ (2 * k + j)]
                stores.append(pltpu.make_async_copy(pair_ref.at[j], slot, sem))
                stores[-1].start()
    for i in range(2):
        here = pl.ds(i * half, half)
        there = pl.ds(at + i * half, half)
        kept = near_ref[there, :].astype(F32) + got_ref[there, :].astype(F32)
        total = tokens_ref[there, :].astype(F32) + (kept + crossed_ref[here, :].astype(F32))
        row = lax.broadcasted_iota(jnp.int32, total.shape, 0) + (at + i * half)
        done[here, :] = jnp.where(row < plan_ref[1], total, 0.0).astype(BF16)
        stores.append(pltpu.make_async_copy(done.at[here], out_hbm.at[there], sems.at[i]))
        stores[-1].start()
    for store in stores:
        store.wait()


def call(
    kernel, out_shape, in_specs, args, flops, mib=MIB, scratch=(), exps=0, name=None, into=None
):
    outs = out_shape if isinstance(out_shape, (list, tuple)) else [out_shape]
    moved = sum(a.size * a.dtype.itemsize for a in list(args) + list(outs))
    return pl.pallas_call(
        kernel,
        out_shape=out_shape,
        in_specs=in_specs,
        out_specs=jax.tree.map(lambda _: VMEM if into is None else HBM, out_shape),
        input_output_aliases=into or {},
        scratch_shapes=list(scratch),
        cost_estimate=pl.CostEstimate(flops=flops, bytes_accessed=moved, transcendentals=exps),
        compiler_params=pltpu.CompilerParams(vmem_limit_bytes=int(mib * 1024 * 1024)),
        name=name,
    )(*args)


def body(
    tokens,
    norm_gain,
    w_query,
    w_keyval,
    w_out,
    span_lens,
    cached_lens,
    old_table,
    new_table,
    old_cache,
):
    tp = lax.axis_size("tp")
    groups, share, width = old_cache.shape
    block_rows = share * tp
    capacity = groups * block_rows
    rows, cols = tokens.shape
    q_cols = w_query.shape[1]
    features = w_query.shape[0]
    hd = width // 2
    most_held = capacity - rows
    piece_rows = most_held // tp

    def swap(x, bit, axis="tp"):
        size = lax.axis_size(axis)
        return lax.ppermute(x, axis, [(i, i ^ bit) for i in range(size)])

    def exchange(x):
        return lax.all_to_all(x, "seq", split_axis=0, concat_axis=0, tiled=True)

    phased = groups == 8

    with jax.named_scope("tokens_gather"):
        across = swap(tokens, 2)
        beside = swap(tokens, 1)

    with jax.named_scope("cache_gather"):
        gain = jnp.maximum(norm_gain, LEAST).reshape(tp, 1, cols)
        gain, stored = lax.optimization_barrier((gain, old_cache))
        arrived = exchange(stored).reshape(groups * share, width)
        own = jnp.maximum(tokens, jnp.asarray(LEAST, BF16))
        across, *lens = lax.optimization_barrier(
            (across, cached_lens, span_lens, old_table[0], new_table[0])
        )
        plan = jnp.concatenate(lens)
        arrived, across, own, plan = lax.optimization_barrier((arrived, across, own, plan))
        ordered = call(
            functools.partial(order_kernel, share),
            jax.ShapeDtypeStruct((piece_rows, width), BF16),
            [SMEM, VMEM],
            (plan, arrived),
            flops=2 * piece_rows * groups * share * width,
            name="order",
        )
        c_across = swap(ordered, 2)
        c_beside = swap(ordered, 1)

    with jax.named_scope("project"):
        corner = swap(across, 1)
        stacked = rows * (q_cols // hd)
        query, keyval, values, limits = call(
            project_kernel,
            [
                jax.ShapeDtypeStruct((stacked, hd), BF16),
                jax.ShapeDtypeStruct((rows, width), BF16),
                jax.ShapeDtypeStruct((rows, width), BF16),
                jax.ShapeDtypeStruct((2, 8, 128), F32),
            ],
            [VMEM] * 5 + [HBM] * 2,
            (
                own,
                beside,
                across,
                corner,
                gain,
                w_query,
                w_keyval,
            ),
            flops=2 * rows * features * (q_cols + width),
            mib=PROJECT_MIB,
            scratch=[
                pltpu.VMEM((rows, features), BF16),
                pltpu.VMEM(w_query.shape, BF16),
                pltpu.VMEM(w_keyval.shape, BF16),
                pltpu.SemaphoreType.DMA((2 * tp,)),
            ],
            name="project",
        )

    with jax.named_scope("extend"):
        sent = call(
            functools.partial(extend_kernel, share, block_rows),
            [jax.ShapeDtypeStruct((groups // 2, share, width), BF16)] * 2
            if phased
            else [jax.ShapeDtypeStruct((groups * share, width), BF16)],
            [SMEM] + [VMEM] * 2,
            (plan, keyval, arrived),
            flops=4 * groups * share * groups * share * width,
            name="extend",
        )
        *sent, c_across = lax.optimization_barrier((*sent, c_across))
        if phased:
            keep, got = sent[0], swap(sent[1], 1, "seq")
        cached = (ordered, c_beside, c_across, swap(c_across, 1))

    part = rows // CHUNKS
    tile_rows = ROW_TILE * (q_cols // hd)
    old = []
    mixed = None
    for c in range(CHUNKS):
        last = c == CHUNKS - 1
        with jax.named_scope("attend"):
            of_part = jax.ShapeDtypeStruct((part, cols), BF16)
            of_all = jax.ShapeDtypeStruct((rows, cols), BF16)
            outs = [of_all, of_part, of_all, of_part]
            if not last:
                outs = [
                    of_part,
                    of_part,
                    jax.ShapeDtypeStruct((part, q_cols), BF16),
                    jax.ShapeDtypeStruct((most_held, width), BF16),
                    jax.ShapeDtypeStruct((8, 128), F32),
                ]
            seen = most_held + (c + 1) * part
            sums = list(call(
                functools.partial(attend_kernel, share, block_rows, c * part, part),
                outs,
                [SMEM] + [VMEM] * 8 + [HBM] + [VMEM] * len(old),
                (plan, query, keyval, values, limits, *cached, w_out, *old),
                flops=4 * part * seen * q_cols + 2 * part * q_cols * features,
                exps=part * seen * (q_cols // hd),
                mib=ATTEND_MIB,
                scratch=[
                    pltpu.VMEM((tile_rows, width), F32),
                    pltpu.VMEM((tile_rows, hd), F32),
                    pltpu.VMEM((part, q_cols), BF16),
                    pltpu.VMEM(w_out.shape, BF16),
                    pltpu.SemaphoreType.DMA,
                ],
                name="attend",
            ))
            if last:
                far0, far1, near0, near1 = sums
            else:
                far1, near1, before_rows, *old = sums
                old.append(before_rows)
        with jax.named_scope("reduce"):
            if c == 0 and phased:
                far1, got = lax.optimization_barrier((far1, got))
            got1 = swap(far1, 1)
            if c and last:
                before = pl.pallas_call(
                    hand_on_kernel,
                    out_shape=jax.ShapeDtypeStruct(before.shape, BF16),
                    in_specs=[pl.BlockSpec(memory_space=pl.ANY)],
                    out_specs=pl.BlockSpec(memory_space=pl.ANY),
                    input_output_aliases={0: 0},
                    cost_estimate=pl.CostEstimate(
                        flops=1 << 34, bytes_accessed=1024, transcendentals=0
                    ),
                    compiler_params=pltpu.CompilerParams(vmem_limit_bytes=1 << 20),
                    name="hand_on",
                )(before)
                before, got1 = lax.optimization_barrier((before, got1))
            pair = (near1.astype(F32) + got1.astype(F32)).astype(BF16)
            if not last:
                query, pair = lax.optimization_barrier((query, pair))
            if last and phased:
                pair, got = lax.optimization_barrier((pair, got))
            crossed = swap(pair, 2)
            if not last:
                before = crossed

    with jax.named_scope("exchange"):
        if phased:
            pairs = list(call(
                pair_kernel,
                [jax.ShapeDtypeStruct((2, share, width), BF16)] * (groups // 2),
                [VMEM] * 2,
                (keep, got),
                flops=0,
                mib=8,
                name="pair",
            ))
            for k in range(len(pairs) - 1, 0, -1):
                pairs[k] = swap(pairs[k], 2 * k, "seq")
        else:
            pairs = []
            new_cache = exchange(sent[0].reshape(groups, share, width))

    with jax.named_scope("finish"):
        got0 = swap(far0, 1)
        ends = (plan, own, near0, got0)
        out = jax.ShapeDtypeStruct((rows, cols), BF16)
        scratch = [pltpu.VMEM((part, cols), BF16)]
        mixed = call(
            functools.partial(finish_kernel, 0, phased),
            out,
            [SMEM] + [VMEM] * 4,
            (*ends, before),
            flops=4 * part * cols,
            scratch=scratch + [pltpu.SemaphoreType.DMA((2,))],
            name="finish",
            into={},
        )
        finished = call(
            functools.partial(finish_kernel, part, phased),
            [out, jax.ShapeDtypeStruct(old_cache.shape, BF16)] if phased else out,
            [SMEM] + [VMEM] * (4 + len(pairs)) + [HBM],
            (*ends, crossed, *pairs, mixed),
            flops=4 * part * cols,
            scratch=scratch + [pltpu.SemaphoreType.DMA((2 + groups * phased,))],
            name="finish",
            into={5 + len(pairs): 0},
        )
    return tuple(finished) if phased else (finished, new_cache)


def solution(mesh):
    in_specs = (
        P("seq", "tp"),
        P(),
        P(None, "tp"),
        P(),
        P("tp", None),
        P("seq"),
        P("seq"),
        P("seq", None),
        P("seq", None),
        P("seq", "tp", None),
    )
    out_specs = (P("seq", "tp"), P("seq", "tp", None))
    return jax.shard_map(body, mesh=mesh, in_specs=in_specs, out_specs=out_specs, check_vma=False)
```

```python
import functools
import math

import jax
import jax.numpy as jnp
from jax import lax
from jax.experimental import pallas as pl
from jax.experimental.pallas import tpu as pltpu
from jax.sharding import PartitionSpec as P

EPSILON = 1e-05
MASKED = -1e30
CHUNKS = 2
PART_ROWS = 256
ROW_TILE = 128
KEY_TILE = 128
NORM_ROWS = 128
MIB = 51
PROJECT_MIB = 50.375
LEAST = -3e38
ATTEND_MIB = 49
SAFE = 60.0
F32 = jnp.float32
BF16 = jnp.bfloat16

VMEM = pl.BlockSpec(memory_space=pltpu.VMEM)
SMEM = pl.BlockSpec(memory_space=pltpu.SMEM)
HBM = pl.BlockSpec(memory_space=pltpu.HBM)


def dot(a, b):
    return lax.dot_general(a, b, (((1,), (0,)), ((), ())), preferred_element_type=F32)


def dot_t(a, b):
    return lax.dot_general(a, b, (((1,), (1,)), ((), ())), preferred_element_type=F32)


def pair_kernel(keep_ref, got_ref, *pair_refs):
    for k, pair_ref in enumerate(pair_refs):
        pair_ref[0] = keep_ref[k]
        pair_ref[1] = got_ref[k]


def place_kernel(p0, p1, p2, p3, out_hbm, sems):
    me = lax.axis_index("seq")
    stores = []
    for k, pair_ref in enumerate((p0, p1, p2, p3)):
        for j in range(2):
            slot = out_hbm.at[me ^ (2 * k + j)]
            stores.append(pltpu.make_async_copy(pair_ref.at[j], slot, sems.at[len(stores)]))
            stores[-1].start()
    for store in stores:
        store.wait()


def order_kernel(share, plan_ref, arrived_ref, out_ref):
    rows, count = out_ref.shape[0], arrived_ref.shape[0]
    if share % 16 == 0:
        for b in range(rows // share):
            at = pl.ds(pl.multiple_of(plan_ref[2 + b] * share, share), share)
            out_ref[pl.ds(b * share, share), :] = arrived_ref[at, :]
        return
    row = lax.broadcasted_iota(jnp.int32, (rows, 128), 0)
    block = row // share
    holder = jnp.zeros_like(block)
    for b in range(rows // share):
        holder = jnp.where(block == b, plan_ref[2 + b], holder)
    index = (holder * share + row % share)[:, :1]
    column = lax.broadcasted_iota(jnp.int32, (rows, count), 1)
    pick = jnp.where(column == index, 1.0, 0.0).astype(BF16)
    out_ref[...] = dot(pick, arrived_ref[...]).astype(BF16)


def extend_kernel(share, block_rows, plan_ref, kv_ref, arrived_ref, *out_refs):
    rows = arrived_ref.shape[0]
    groups = rows // share
    held, span = plan_ref[0], plan_ref[1]
    me = lax.axis_index("seq") if len(out_refs) > 1 else 0
    row = lax.broadcasted_iota(jnp.int32, (rows, 128), 0)
    target = row // share
    block, holder = jnp.zeros_like(row), jnp.zeros_like(row)
    for b in range(groups):
        hit = target == plan_ref[2 + groups + b] ^ me
        block = jnp.where(hit, b, block)
        holder = jnp.where(hit, plan_ref[2 + b], holder)
    position = block * block_rows + lax.axis_index("tp") * share + row % share
    old_row = jnp.where(position < held, holder * share + row % share, -1)[:, :1]
    fresh = position - held
    new_row = jnp.where((fresh >= 0) & (fresh < span), fresh, -1)[:, :1]
    column = lax.broadcasted_iota(jnp.int32, (rows, rows), 1)
    total = dot(jnp.where(column == old_row, 1.0, 0.0).astype(BF16), arrived_ref[...])
    column = lax.broadcasted_iota(jnp.int32, (rows, kv_ref.shape[0]), 1)
    total += dot(jnp.where(column == new_row, 1.0, 0.0).astype(BF16), kv_ref[...])
    total = total.astype(BF16)
    if len(out_refs) == 1:
        out_refs[0][...] = total
        return
    for slot in range(groups):
        out_refs[slot % 2][slot // 2] = total[slot * share : (slot + 1) * share]


def project_kernel(
    x0,
    x1,
    x2,
    x3,
    gain_ref,
    wq_hbm,
    wkv_hbm,
    q_ref,
    kv_ref,
    values_ref,
    limits_ref,
    normed,
    wq_ref,
    wkv_ref,
    sems,
):
    pieces = (x0, x1, x2, x3)
    me = lax.axis_index("tp")
    rows, width = x0.shape
    features = width * len(pieces)
    hd = kv_ref.shape[1] // 2
    heads = wq_ref.shape[1] // hd
    loads = []
    for hbm, to in ((wkv_hbm, wkv_ref), (wq_hbm, wq_ref)):
        for j in range(len(pieces)):
            at = pl.ds(j * width, width)
            loads.append(pltpu.make_async_copy(hbm.at[at], to.at[at], sems.at[len(loads)]))
            loads[-1].start()

    for step in range(0, rows, NORM_ROWS):
        at = pl.ds(step, NORM_ROWS)
        values = [piece[at, :].astype(F32) for piece in pieces]
        average = jnp.sum(sum(values), axis=1, keepdims=True) / features
        centred = [v - average for v in values]
        spread = jnp.sum(sum(v * v for v in centred), axis=1, keepdims=True) / features
        scale = lax.rsqrt(spread + EPSILON)
        for j, v in enumerate(centred):
            owner = me ^ j
            to = pl.ds(pl.multiple_of(owner * width, width), width)
            normed[at, to] = (v * scale * gain_ref[owner]).astype(BF16)
    for load in loads[: len(pieces)]:
        load.wait()
    keyval = dot(normed[...], wkv_ref[...]).astype(BF16)
    kv_ref[...] = keyval
    values_ref[:, hd:] = keyval[:, hd:]
    values_ref[:, :hd] = jnp.ones((rows, hd), BF16)
    limits_ref[0] = longest(keyval[:, :hd])
    for load in loads[len(pieces) :]:
        load.wait()
    query = dot(normed[...], wq_ref[...]).astype(BF16)
    for start in range(0, rows, ROW_TILE):
        for h in range(heads):
            q_ref[pl.ds(start * heads + h * ROW_TILE, ROW_TILE), :] = query[
                start : start + ROW_TILE, h * hd : (h + 1) * hd
            ]
    limits_ref[1] = longest(q_ref[...])


def longest(x):
    squares = dot(x * x, jnp.ones((x.shape[1], 128), BF16))
    return jnp.max(squares.reshape(-1, 8, 128), axis=0)


def attend_kernel(share, block_rows, start_row, rows, plan_ref, q_ref, kv_ref, new_ref, *refs):
    limits_ref, pieces, wout_hbm = refs[0], refs[1:5], refs[5]
    total, high, context, wout, sem = refs[-5:]
    if start_row:
        old_ref, old_limit_ref, before_ref, far0_ref, far1_ref, near0_ref, near1_ref = refs[6:13]
    else:
        far1_ref, near1_ref, context_out, old_ref, old_limit_ref = refs[6:11]
    me = lax.axis_index("tp")
    held, span = plan_ref[0], plan_ref[1]
    piece_rows, width = pieces[0].shape
    hd = width // 2
    heads = q_ref.shape[0] // kv_ref.shape[0]
    load = pltpu.make_async_copy(wout_hbm, wout, sem)
    load.start()

    group = KEY_TILE * len(pieces)
    most = piece_rows // KEY_TILE
    tiles = (held + group - 1) // group
    if not start_row:
        row = lax.broadcasted_iota(jnp.int32, (KEY_TILE, hd), 0)
        place = row // share * block_rows + row % share
        limit = jnp.zeros((8, 128), F32)

        def lay(i, whole):
            source = pl.ds(i * KEY_TILE, KEY_TILE)
            for j, piece in enumerate(pieces):
                at = pl.ds(i * group + j * KEY_TILE, KEY_TILE)
                if whole:
                    old_ref[at, hd:] = piece[source, hd:]
                    old_ref[at, :hd] = jnp.ones((KEY_TILE, hd), BF16)
                    continue
                used = place + (me ^ j) * share + i * group < held
                old_ref[at, hd:] = jnp.where(used, piece[source, hd:].astype(F32), 0.0).astype(BF16)
                old_ref[at, :hd] = jnp.where(used, 1.0, 0.0).astype(BF16)

        for i in range(most):
            pl.when(i < tiles - 1)(functools.partial(lay, i, True))
            pl.when(i == tiles - 1)(functools.partial(lay, i, False))
        for piece in pieces:
            limit = jnp.maximum(limit, longest(piece[:, :hd]))
        old_limit_ref[...] = limit

    factor = hd ** (-0.5) * math.log2(math.e)
    key_limit = jnp.max(jnp.maximum(old_limit_ref[...], limits_ref[0]))
    small = key_limit * jnp.max(limits_ref[1]) * (1.05 / hd) < SAFE * SAFE

    tile_rows = ROW_TILE * heads

    def queries(t):
        return q_ref[pl.ds(start_row * heads + t * tile_rows, tile_rows), :]

    def old_keys(i):
        source = pl.ds(i * KEY_TILE, KEY_TILE)
        return jnp.concatenate([piece[source, :hd] for piece in pieces], axis=0)

    def new_scores(t):
        known = start_row + t * ROW_TILE
        scores = dot_t(queries(t), kv_ref[pl.ds(0, known + ROW_TILE), :hd])
        to = lax.broadcasted_iota(jnp.int32, (tile_rows, ROW_TILE), 0) % ROW_TILE
        by = lax.broadcasted_iota(jnp.int32, (tile_rows, ROW_TILE), 1)
        last = jnp.where(by <= to, scores[:, known:], MASKED)
        return jnp.concatenate([scores[:, :known], last], axis=1) if known else last

    def new_values(t):
        return new_ref[pl.ds(0, start_row + (t + 1) * ROW_TILE), :]

    def put(t, both):
        sums = both[:, :hd]
        inverse = pl.reciprocal(sums, approx=True)
        inverse = inverse * (2.0 - sums * inverse)
        out = (both[:, hd:] * inverse).astype(BF16)
        for h in range(heads):
            context[pl.ds(t * ROW_TILE, ROW_TILE), h * hd : (h + 1) * hd] = out[
                h * ROW_TILE : (h + 1) * ROW_TILE
            ]

    def fast(used, begin):
        row_tiles = range(begin // ROW_TILE, min(begin + PART_ROWS, rows) // ROW_TILE)
        steps = [(t, i) for t in row_tiles for i in range(used + 1)]

        def score(t, i):
            return new_scores(t) if i == used else dot_t(queries(t), old_keys(i))

        ahead, both = score(*steps[0]), None
        for at, (t, i) in enumerate(steps):
            scores = ahead
            if at + 1 < len(steps):
                ahead = score(*steps[at + 1])
            weights = jnp.exp2(scores * factor).astype(BF16)
            values = new_values(t) if i == used else old_ref[pl.ds(i * group, group), :]
            part = dot(weights, values)
            both = part if i == 0 else both + part
            if i == used:
                put(t, both)

    def exact(t):
        column = lax.broadcasted_iota(jnp.int32, (tile_rows, group), 1)
        within = column % KEY_TILE
        owner = me ^ (column // KEY_TILE)
        place = within // share * block_rows + within % share + owner * share

        def old_scores(i):
            scores = dot_t(queries(t), old_keys(pl.multiple_of(i, 1)))
            return jnp.where(place + i * group < held, scores, MASKED)

        def raise_high(i, carry):
            top = jnp.max(old_scores(i), axis=1, keepdims=True)
            high[...] = jnp.maximum(high[...], top)
            return carry

        def add(i, carry):
            weights = jnp.exp2((old_scores(i) - high[:, :1]) * factor).astype(BF16)
            total[...] += dot(weights, old_ref[pl.ds(pl.multiple_of(i * group, group), group), :])
            return carry

        high[...] = jnp.zeros_like(high) + jnp.max(new_scores(t), axis=1, keepdims=True)
        lax.fori_loop(0, tiles, raise_high, 0)
        weights = jnp.exp2((new_scores(t) - high[:, :1]) * factor).astype(BF16)
        total[...] = dot(weights, new_values(t))
        lax.fori_loop(0, tiles, add, 0)
        put(t, total[...])

    for begin in range(0, rows, PART_ROWS):
        busy = start_row + begin < span
        for used in range(1, most + 1):
            pl.when(busy & small & (tiles == used))(functools.partial(fast, used, begin))

        @pl.when(busy & jnp.logical_not(small))
        def _():
            for t in range(begin // ROW_TILE, min(begin + PART_ROWS, rows) // ROW_TILE):
                exact(t)

        @pl.when(jnp.logical_not(busy))
        def _():
            context[pl.ds(begin, PART_ROWS), :] = jnp.zeros((PART_ROWS, context.shape[1]), BF16)

    load.wait()
    cols = wout.shape[1] // 4

    def partial_sums(rows_of, k):
        columns = pl.ds(pl.multiple_of((me ^ k) * cols, cols), cols)
        return dot(rows_of[...], wout[:, columns]).astype(BF16)

    far1_ref[...] = partial_sums(context, 3)
    near1_ref[...] = partial_sums(context, 2)
    if not start_row:
        context_out[...] = context[...]
        return
    for at, rows_of in ((0, before_ref), (start_row, context)):
        far0_ref[pl.ds(at, rows), :] = partial_sums(rows_of, 1)
        near0_ref[pl.ds(at, rows), :] = partial_sums(rows_of, 0)


def hand_on_kernel(in_ref, out_ref):
    pass


def finish_kernel(at, plan_ref, tokens_ref, near_ref, got_ref, crossed_ref, *refs):
    out_hbm, done, sems = refs[-3:]
    rows = crossed_ref.shape[0]
    half = rows // 2
    stores = []
    for i in range(2):
        here = pl.ds(i * half, half)
        there = pl.ds(at + i * half, half)
        kept = near_ref[there, :].astype(F32) + got_ref[there, :].astype(F32)
        total = tokens_ref[there, :].astype(F32) + (kept + crossed_ref[here, :].astype(F32))
        row = lax.broadcasted_iota(jnp.int32, total.shape, 0) + (at + i * half)
        done[here, :] = jnp.where(row < plan_ref[1], total, 0.0).astype(BF16)
        stores.append(pltpu.make_async_copy(done.at[here], out_hbm.at[there], sems.at[i]))
        stores[-1].start()
    for store in stores:
        store.wait()


def call(
    kernel, out_shape, in_specs, args, flops, mib=MIB, scratch=(), exps=0, name=None, into=None
):
    outs = out_shape if isinstance(out_shape, (list, tuple)) else [out_shape]
    moved = sum(a.size * a.dtype.itemsize for a in list(args) + list(outs))
    return pl.pallas_call(
        kernel,
        out_shape=out_shape,
        in_specs=in_specs,
        out_specs=jax.tree.map(lambda _: VMEM if into is None else HBM, out_shape),
        input_output_aliases=into or {},
        scratch_shapes=list(scratch),
        cost_estimate=pl.CostEstimate(flops=flops, bytes_accessed=moved, transcendentals=exps),
        compiler_params=pltpu.CompilerParams(vmem_limit_bytes=int(mib * 1024 * 1024)),
        name=name,
    )(*args)


def hand_on(x):
    return pl.pallas_call(
        hand_on_kernel,
        out_shape=jax.ShapeDtypeStruct(x.shape, x.dtype),
        in_specs=[pl.BlockSpec(memory_space=pl.ANY)],
        out_specs=pl.BlockSpec(memory_space=pl.ANY),
        input_output_aliases={0: 0},
        cost_estimate=pl.CostEstimate(flops=1 << 34, bytes_accessed=1024, transcendentals=0),
        compiler_params=pltpu.CompilerParams(vmem_limit_bytes=1 << 20),
        name="hand_on",
    )(x)


def body(
    tokens,
    norm_gain,
    w_query,
    w_keyval,
    w_out,
    span_lens,
    cached_lens,
    old_table,
    new_table,
    old_cache,
):
    tp = lax.axis_size("tp")
    groups, share, width = old_cache.shape
    block_rows = share * tp
    capacity = groups * block_rows
    rows, cols = tokens.shape
    q_cols = w_query.shape[1]
    features = w_query.shape[0]
    hd = width // 2
    most_held = capacity - rows
    piece_rows = most_held // tp

    def swap(x, bit, axis="tp"):
        size = lax.axis_size(axis)
        return lax.ppermute(x, axis, [(i, i ^ bit) for i in range(size)])

    def exchange(x):
        return lax.all_to_all(x, "seq", split_axis=0, concat_axis=0, tiled=True)

    phased = groups == 8

    with jax.named_scope("tokens_gather"):
        across = swap(tokens, 2)
        beside = swap(tokens, 1)

    with jax.named_scope("cache_gather"):
        gain = jnp.maximum(norm_gain, LEAST).reshape(tp, 1, cols)
        gain, stored = lax.optimization_barrier((gain, old_cache))
        arrived = exchange(stored).reshape(groups * share, width)
        own = jnp.maximum(tokens, jnp.asarray(LEAST, BF16))
        across, *lens = lax.optimization_barrier(
            (across, cached_lens, span_lens, old_table[0], new_table[0])
        )
        plan = jnp.concatenate(lens)
        arrived, across, own, plan = lax.optimization_barrier((arrived, across, own, plan))
        ordered = call(
            functools.partial(order_kernel, share),
            jax.ShapeDtypeStruct((piece_rows, width), BF16),
            [SMEM, VMEM],
            (plan, arrived),
            flops=2 * piece_rows * groups * share * width,
            name="order",
        )
        c_across = swap(ordered, 2)
        c_beside = swap(ordered, 1)

    with jax.named_scope("project"):
        corner = swap(across, 1)
        stacked = rows * (q_cols // hd)
        query, keyval, values, limits = call(
            project_kernel,
            [
                jax.ShapeDtypeStruct((stacked, hd), BF16),
                jax.ShapeDtypeStruct((rows, width), BF16),
                jax.ShapeDtypeStruct((rows, width), BF16),
                jax.ShapeDtypeStruct((2, 8, 128), F32),
            ],
            [VMEM] * 5 + [HBM] * 2,
            (
                own,
                beside,
                across,
                corner,
                gain,
                w_query,
                w_keyval,
            ),
            flops=2 * rows * features * (q_cols + width),
            mib=PROJECT_MIB,
            scratch=[
                pltpu.VMEM((rows, features), BF16),
                pltpu.VMEM(w_query.shape, BF16),
                pltpu.VMEM(w_keyval.shape, BF16),
                pltpu.SemaphoreType.DMA((2 * tp,)),
            ],
            name="project",
        )

    with jax.named_scope("extend"):
        sent = call(
            functools.partial(extend_kernel, share, block_rows),
            [jax.ShapeDtypeStruct((groups // 2, share, width), BF16)] * 2
            if phased
            else [jax.ShapeDtypeStruct((groups * share, width), BF16)],
            [SMEM] + [VMEM] * 2,
            (plan, keyval, arrived),
            flops=4 * groups * share * groups * share * width,
            name="extend",
        )
        *sent, c_across = lax.optimization_barrier((*sent, c_across))
        if phased:
            keep, got = sent[0], swap(sent[1], 1, "seq")
        cached = (ordered, c_beside, c_across, swap(c_across, 1))

    part = rows // CHUNKS
    tile_rows = ROW_TILE * (q_cols // hd)
    old = []
    mixed = None
    for c in range(CHUNKS):
        last = c == CHUNKS - 1
        with jax.named_scope("attend"):
            of_part = jax.ShapeDtypeStruct((part, cols), BF16)
            of_all = jax.ShapeDtypeStruct((rows, cols), BF16)
            outs = [of_all, of_part, of_all, of_part]
            if not last:
                outs = [
                    of_part,
                    of_part,
                    jax.ShapeDtypeStruct((part, q_cols), BF16),
                    jax.ShapeDtypeStruct((most_held, width), BF16),
                    jax.ShapeDtypeStruct((8, 128), F32),
                ]
            seen = most_held + (c + 1) * part
            sums = list(call(
                functools.partial(attend_kernel, share, block_rows, c * part, part),
                outs,
                [SMEM] + [VMEM] * 8 + [HBM] + [VMEM] * len(old),
                (plan, query, keyval, values, limits, *cached, w_out, *old),
                flops=4 * part * seen * q_cols + 2 * part * q_cols * features,
                exps=part * seen * (q_cols // hd),
                mib=ATTEND_MIB,
                scratch=[
                    pltpu.VMEM((tile_rows, width), F32),
                    pltpu.VMEM((tile_rows, hd), F32),
                    pltpu.VMEM((part, q_cols), BF16),
                    pltpu.VMEM(w_out.shape, BF16),
                    pltpu.SemaphoreType.DMA,
                ],
                name="attend",
            ))
            if last:
                far0, far1, near0, near1 = sums
            else:
                far1, near1, before_rows, *old = sums
                old.append(before_rows)
        with jax.named_scope("reduce"):
            got1 = swap(far1, 1)
            if c and last:
                before = hand_on(before)
                before, got1 = lax.optimization_barrier((before, got1))
            pair = (near1.astype(F32) + got1.astype(F32)).astype(BF16)
            if not last:
                query, pair = lax.optimization_barrier((query, pair))
                if phased:
                    old[0], got = lax.optimization_barrier((old[0], got))
            if last and phased:
                pair, got = lax.optimization_barrier((pair, got))
            crossed = swap(pair, 2)
            if not last:
                before = crossed

    with jax.named_scope("exchange"):
        if phased:
            pairs = list(call(
                pair_kernel,
                [jax.ShapeDtypeStruct((2, share, width), BF16)] * (groups // 2),
                [VMEM] * 2,
                (keep, got),
                flops=0,
                mib=8,
                name="pair",
            ))
            for k in range(len(pairs) - 1, 0, -1):
                pairs[k] = swap(pairs[k], 2 * k, "seq")
        else:
            new_cache = exchange(sent[0].reshape(groups, share, width))

    with jax.named_scope("finish"):
        got0 = swap(far0, 1)
        mixed = None
        for at, over in ((0, before), (part, crossed)):
            mixed = call(
                functools.partial(finish_kernel, at),
                jax.ShapeDtypeStruct((rows, cols), BF16),
                [SMEM] + [VMEM] * 4 + [HBM] * (at > 0),
                (plan, own, near0, got0, over, *([mixed] if at else [])),
                flops=4 * part * cols,
                scratch=[pltpu.VMEM((part, cols), BF16), pltpu.SemaphoreType.DMA((2,))],
                name="finish",
                into={5: 0} if at else {},
            )
        if phased:
            mixed, *pairs = lax.optimization_barrier((mixed, *pairs))
            new_cache = call(
                place_kernel,
                jax.ShapeDtypeStruct(old_cache.shape, BF16),
                [VMEM] * len(pairs),
                pairs,
                flops=0,
                mib=8,
                scratch=[pltpu.SemaphoreType.DMA((groups,))],
                name="place",
                into={},
            )
    return (mixed, new_cache)


def solution(mesh):
    in_specs = (
        P("seq", "tp"),
        P(),
        P(None, "tp"),
        P(),
        P("tp", None),
        P("seq"),
        P("seq"),
        P("seq", None),
        P("seq", None),
        P("seq", "tp", None),
    )
    out_specs = (P("seq", "tp"), P("seq", "tp", None))
    return jax.shard_map(body, mesh=mesh, in_specs=in_specs, out_specs=out_specs, check_vma=False)
```

```python
import functools
import math

import jax
import jax.numpy as jnp
from jax import lax
from jax.experimental import pallas as pl
from jax.experimental.pallas import tpu as pltpu
from jax.sharding import PartitionSpec as P

EPSILON = 1e-05
MASKED = -1e30
CHUNKS = 2
PART_ROWS = 256
ROW_TILE = 128
KEY_TILE = 128
NORM_ROWS = 128
MIB = 51
PROJECT_MIB = 50.375
LEAST = -3e38
ATTEND_MIB = 49
EARLY_MIB = 50
SAFE = 60.0
F32 = jnp.float32
BF16 = jnp.bfloat16

VMEM = pl.BlockSpec(memory_space=pltpu.VMEM)
SMEM = pl.BlockSpec(memory_space=pltpu.SMEM)
HBM = pl.BlockSpec(memory_space=pltpu.HBM)


def dot(a, b):
    return lax.dot_general(a, b, (((1,), (0,)), ((), ())), preferred_element_type=F32)


def dot_t(a, b):
    return lax.dot_general(a, b, (((1,), (1,)), ((), ())), preferred_element_type=F32)


def pair_kernel(keep_ref, got_ref, *pair_refs):
    for k, pair_ref in enumerate(pair_refs):
        pair_ref[0] = keep_ref[k]
        pair_ref[1] = got_ref[k]


def place_kernel(p0, p1, p2, p3, out_hbm, sems):
    me = lax.axis_index("seq")
    stores = []
    for k, pair_ref in enumerate((p0, p1, p2, p3)):
        for j in range(2):
            slot = out_hbm.at[me ^ (2 * k + j)]
            stores.append(pltpu.make_async_copy(pair_ref.at[j], slot, sems.at[len(stores)]))
            stores[-1].start()
    for store in stores:
        store.wait()


def order_kernel(share, plan_ref, arrived_ref, out_ref):
    rows, count = out_ref.shape[0], arrived_ref.shape[0]
    if share % 16 == 0:
        for b in range(rows // share):
            at = pl.ds(pl.multiple_of(plan_ref[2 + b] * share, share), share)
            out_ref[pl.ds(b * share, share), :] = arrived_ref[at, :]
        return
    row = lax.broadcasted_iota(jnp.int32, (rows, 128), 0)
    block = row // share
    holder = jnp.zeros_like(block)
    for b in range(rows // share):
        holder = jnp.where(block == b, plan_ref[2 + b], holder)
    index = (holder * share + row % share)[:, :1]
    column = lax.broadcasted_iota(jnp.int32, (rows, count), 1)
    pick = jnp.where(column == index, 1.0, 0.0).astype(BF16)
    out_ref[...] = dot(pick, arrived_ref[...]).astype(BF16)


def extend_kernel(share, block_rows, plan_ref, kv_ref, arrived_ref, *out_refs):
    rows = arrived_ref.shape[0]
    groups = rows // share
    held, span = plan_ref[0], plan_ref[1]
    me = lax.axis_index("seq") if len(out_refs) > 1 else 0
    row = lax.broadcasted_iota(jnp.int32, (rows, 128), 0)
    target = row // share
    block, holder = jnp.zeros_like(row), jnp.zeros_like(row)
    for b in range(groups):
        hit = target == plan_ref[2 + groups + b] ^ me
        block = jnp.where(hit, b, block)
        holder = jnp.where(hit, plan_ref[2 + b], holder)
    position = block * block_rows + lax.axis_index("tp") * share + row % share
    old_row = jnp.where(position < held, holder * share + row % share, -1)[:, :1]
    fresh = position - held
    new_row = jnp.where((fresh >= 0) & (fresh < span), fresh, -1)[:, :1]
    column = lax.broadcasted_iota(jnp.int32, (rows, rows), 1)
    total = dot(jnp.where(column == old_row, 1.0, 0.0).astype(BF16), arrived_ref[...])
    column = lax.broadcasted_iota(jnp.int32, (rows, kv_ref.shape[0]), 1)
    total += dot(jnp.where(column == new_row, 1.0, 0.0).astype(BF16), kv_ref[...])
    total = total.astype(BF16)
    if len(out_refs) == 1:
        out_refs[0][...] = total
        return
    for slot in range(groups):
        out_refs[slot % 2][slot // 2] = total[slot * share : (slot + 1) * share]


def project_kernel(
    x0,
    x1,
    x2,
    x3,
    gain_ref,
    wq_hbm,
    wkv_hbm,
    q_ref,
    kv_ref,
    values_ref,
    limits_ref,
    normed,
    wq_ref,
    wkv_ref,
    sems,
):
    pieces = (x0, x1, x2, x3)
    me = lax.axis_index("tp")
    rows, width = x0.shape
    features = width * len(pieces)
    hd = kv_ref.shape[1] // 2
    heads = wq_ref.shape[1] // hd
    loads = []
    for hbm, to in ((wkv_hbm, wkv_ref), (wq_hbm, wq_ref)):
        for j in range(len(pieces)):
            at = pl.ds(j * width, width)
            loads.append(pltpu.make_async_copy(hbm.at[at], to.at[at], sems.at[len(loads)]))
            loads[-1].start()

    for step in range(0, rows, NORM_ROWS):
        at = pl.ds(step, NORM_ROWS)
        values = [piece[at, :].astype(F32) for piece in pieces]
        average = jnp.sum(sum(values), axis=1, keepdims=True) / features
        centred = [v - average for v in values]
        spread = jnp.sum(sum(v * v for v in centred), axis=1, keepdims=True) / features
        scale = lax.rsqrt(spread + EPSILON)
        for j, v in enumerate(centred):
            owner = me ^ j
            to = pl.ds(pl.multiple_of(owner * width, width), width)
            normed[at, to] = (v * scale * gain_ref[owner]).astype(BF16)
    for load in loads[: len(pieces)]:
        load.wait()
    keyval = dot(normed[...], wkv_ref[...]).astype(BF16)
    kv_ref[...] = keyval
    values_ref[:, hd:] = keyval[:, hd:]
    values_ref[:, :hd] = jnp.ones((rows, hd), BF16)
    limits_ref[0] = longest(keyval[:, :hd])
    for load in loads[len(pieces) :]:
        load.wait()
    query = dot(normed[...], wq_ref[...]).astype(BF16)
    for start in range(0, rows, ROW_TILE):
        for h in range(heads):
            q_ref[pl.ds(start * heads + h * ROW_TILE, ROW_TILE), :] = query[
                start : start + ROW_TILE, h * hd : (h + 1) * hd
            ]
    limits_ref[1] = longest(q_ref[...])


def longest(x):
    squares = dot(x * x, jnp.ones((x.shape[1], 128), BF16))
    return jnp.max(squares.reshape(-1, 8, 128), axis=0)


def lay_out(share, block_rows, held, owners, pieces, out_ref):
    piece_rows, width = pieces[0].shape
    hd = width // 2
    group = KEY_TILE * lax.axis_size("tp")
    tiles = (held + group - 1) // group
    row = lax.broadcasted_iota(jnp.int32, (KEY_TILE, hd), 0)
    place = row // share * block_rows + row % share

    def lay(i, whole):
        source = pl.ds(i * KEY_TILE, KEY_TILE)
        for j, (owner, piece) in enumerate(zip(owners, pieces)):
            at = pl.ds((i * len(pieces) + j) * KEY_TILE, KEY_TILE)
            if whole:
                out_ref[at, hd:] = piece[source, hd:]
                out_ref[at, :hd] = jnp.ones((KEY_TILE, hd), BF16)
                continue
            used = place + owner * share + i * group < held
            out_ref[at, hd:] = jnp.where(used, piece[source, hd:].astype(F32), 0.0).astype(BF16)
            out_ref[at, :hd] = jnp.where(used, 1.0, 0.0).astype(BF16)

    for i in range(piece_rows // KEY_TILE):
        pl.when(i < tiles - 1)(functools.partial(lay, i, True))
        pl.when(i == tiles - 1)(functools.partial(lay, i, False))


def early_kernel(share, block_rows, plan_ref, *refs):
    pieces, (out_ref, limit_ref) = refs[:-2], refs[-2:]
    me = lax.axis_index("tp")
    owners = [me ^ j for j in range(len(pieces))]
    lay_out(share, block_rows, plan_ref[0], owners, pieces, out_ref)
    limit_ref[...] = functools.reduce(
        jnp.maximum, [longest(piece[:, : piece.shape[1] // 2]) for piece in pieces]
    )


def attend_kernel(share, block_rows, start_row, rows, plan_ref, q_ref, kv_ref, new_ref, *refs):
    limits_ref, pieces, wout_hbm = refs[0], refs[1:5], refs[5]
    total, high, context, wout, sem = refs[-5:]
    most_ref, most_limit_ref = refs[6:8]
    if start_row:
        rest_ref, rest_limit_ref, before_ref, far0_ref, far1_ref, near0_ref, near1_ref = refs[8:15]
    else:
        far1_ref, near1_ref, context_out, rest_ref, rest_limit_ref = refs[8:13]
    me = lax.axis_index("tp")
    held, span = plan_ref[0], plan_ref[1]
    piece_rows, width = pieces[0].shape
    hd = width // 2
    heads = q_ref.shape[0] // kv_ref.shape[0]
    load = pltpu.make_async_copy(wout_hbm, wout, sem)
    load.start()

    group = KEY_TILE * len(pieces)
    most = piece_rows // KEY_TILE
    tiles = (held + group - 1) // group
    if not start_row:
        corner = len(pieces) - 1
        lay_out(share, block_rows, held, [me ^ corner], pieces[corner:], rest_ref)
        rest_limit_ref[...] = longest(pieces[corner][:, :hd])

    factor = hd ** (-0.5) * math.log2(math.e)
    old_limit = jnp.maximum(most_limit_ref[...], rest_limit_ref[...])
    key_limit = jnp.max(jnp.maximum(old_limit, limits_ref[0]))
    small = key_limit * jnp.max(limits_ref[1]) * (1.05 / hd) < SAFE * SAFE

    tile_rows = ROW_TILE * heads

    def queries(t):
        return q_ref[pl.ds(start_row * heads + t * tile_rows, tile_rows), :]

    def old_keys(i):
        source = pl.ds(i * KEY_TILE, KEY_TILE)
        return jnp.concatenate([piece[source, :hd] for piece in pieces], axis=0)

    def old_values(i):
        parts = []
        for ref, count in ((most_ref, len(pieces) - 1), (rest_ref, 1)):
            size = count * KEY_TILE
            at = i * size if isinstance(i, int) else pl.multiple_of(i * size, KEY_TILE)
            parts.append(ref[pl.ds(at, size), :])
        return jnp.concatenate(parts, axis=0)

    def new_scores(t):
        known = start_row + t * ROW_TILE
        scores = dot_t(queries(t), kv_ref[pl.ds(0, known + ROW_TILE), :hd])
        to = lax.broadcasted_iota(jnp.int32, (tile_rows, ROW_TILE), 0) % ROW_TILE
        by = lax.broadcasted_iota(jnp.int32, (tile_rows, ROW_TILE), 1)
        last = jnp.where(by <= to, scores[:, known:], MASKED)
        return jnp.concatenate([scores[:, :known], last], axis=1) if known else last

    def new_values(t):
        return new_ref[pl.ds(0, start_row + (t + 1) * ROW_TILE), :]

    def put(t, both):
        sums = both[:, :hd]
        inverse = pl.reciprocal(sums, approx=True)
        inverse = inverse * (2.0 - sums * inverse)
        out = (both[:, hd:] * inverse).astype(BF16)
        for h in range(heads):
            context[pl.ds(t * ROW_TILE, ROW_TILE), h * hd : (h + 1) * hd] = out[
                h * ROW_TILE : (h + 1) * ROW_TILE
            ]

    def fast(used, begin):
        row_tiles = range(begin // ROW_TILE, min(begin + PART_ROWS, rows) // ROW_TILE)
        steps = [(t, i) for t in row_tiles for i in range(used + 1)]

        def score(t, i):
            return new_scores(t) if i == used else dot_t(queries(t), old_keys(i))

        ahead, both = score(*steps[0]), None
        for at, (t, i) in enumerate(steps):
            scores = ahead
            if at + 1 < len(steps):
                ahead = score(*steps[at + 1])
            weights = jnp.exp2(scores * factor).astype(BF16)
            values = new_values(t) if i == used else old_values(i)
            part = dot(weights, values)
            both = part if i == 0 else both + part
            if i == used:
                put(t, both)

    def exact(t):
        column = lax.broadcasted_iota(jnp.int32, (tile_rows, group), 1)
        within = column % KEY_TILE
        owner = me ^ (column // KEY_TILE)
        place = within // share * block_rows + within % share + owner * share

        def old_scores(i):
            scores = dot_t(queries(t), old_keys(pl.multiple_of(i, 1)))
            return jnp.where(place + i * group < held, scores, MASKED)

        def raise_high(i, carry):
            top = jnp.max(old_scores(i), axis=1, keepdims=True)
            high[...] = jnp.maximum(high[...], top)
            return carry

        def add(i, carry):
            weights = jnp.exp2((old_scores(i) - high[:, :1]) * factor).astype(BF16)
            total[...] += dot(weights, old_values(i))
            return carry

        high[...] = jnp.zeros_like(high) + jnp.max(new_scores(t), axis=1, keepdims=True)
        lax.fori_loop(0, tiles, raise_high, 0)
        weights = jnp.exp2((new_scores(t) - high[:, :1]) * factor).astype(BF16)
        total[...] = dot(weights, new_values(t))
        lax.fori_loop(0, tiles, add, 0)
        put(t, total[...])

    for begin in range(0, rows, PART_ROWS):
        busy = start_row + begin < span
        for used in range(1, most + 1):
            pl.when(busy & small & (tiles == used))(functools.partial(fast, used, begin))

        @pl.when(busy & jnp.logical_not(small))
        def _():
            for t in range(begin // ROW_TILE, min(begin + PART_ROWS, rows) // ROW_TILE):
                exact(t)

        @pl.when(jnp.logical_not(busy))
        def _():
            context[pl.ds(begin, PART_ROWS), :] = jnp.zeros((PART_ROWS, context.shape[1]), BF16)

    load.wait()
    cols = wout.shape[1] // 4

    def partial_sums(rows_of, k):
        columns = pl.ds(pl.multiple_of((me ^ k) * cols, cols), cols)
        return dot(rows_of[...], wout[:, columns]).astype(BF16)

    far1_ref[...] = partial_sums(context, 3)
    near1_ref[...] = partial_sums(context, 2)
    if not start_row:
        context_out[...] = context[...]
        return
    for at, rows_of in ((0, before_ref), (start_row, context)):
        far0_ref[pl.ds(at, rows), :] = partial_sums(rows_of, 1)
        near0_ref[pl.ds(at, rows), :] = partial_sums(rows_of, 0)


def hand_on_kernel(in_ref, out_ref):
    pass


def finish_kernel(at, plan_ref, tokens_ref, near_ref, got_ref, crossed_ref, *refs):
    out_hbm, done, sems = refs[-3:]
    rows = crossed_ref.shape[0]
    half = rows // 2
    stores = []
    for i in range(2):
        here = pl.ds(i * half, half)
        there = pl.ds(at + i * half, half)
        kept = near_ref[there, :].astype(F32) + got_ref[there, :].astype(F32)
        total = tokens_ref[there, :].astype(F32) + (kept + crossed_ref[here, :].astype(F32))
        row = lax.broadcasted_iota(jnp.int32, total.shape, 0) + (at + i * half)
        done[here, :] = jnp.where(row < plan_ref[1], total, 0.0).astype(BF16)
        stores.append(pltpu.make_async_copy(done.at[here], out_hbm.at[there], sems.at[i]))
        stores[-1].start()
    for store in stores:
        store.wait()


def call(
    kernel, out_shape, in_specs, args, flops, mib=MIB, scratch=(), exps=0, name=None, into=None
):
    outs = out_shape if isinstance(out_shape, (list, tuple)) else [out_shape]
    moved = sum(a.size * a.dtype.itemsize for a in list(args) + list(outs))
    return pl.pallas_call(
        kernel,
        out_shape=out_shape,
        in_specs=in_specs,
        out_specs=jax.tree.map(lambda _: VMEM if into is None else HBM, out_shape),
        input_output_aliases=into or {},
        scratch_shapes=list(scratch),
        cost_estimate=pl.CostEstimate(flops=flops, bytes_accessed=moved, transcendentals=exps),
        compiler_params=pltpu.CompilerParams(vmem_limit_bytes=int(mib * 1024 * 1024)),
        name=name,
    )(*args)


def hand_on(x):
    return pl.pallas_call(
        hand_on_kernel,
        out_shape=jax.ShapeDtypeStruct(x.shape, x.dtype),
        in_specs=[pl.BlockSpec(memory_space=pl.ANY)],
        out_specs=pl.BlockSpec(memory_space=pl.ANY),
        input_output_aliases={0: 0},
        cost_estimate=pl.CostEstimate(flops=1 << 34, bytes_accessed=1024, transcendentals=0),
        compiler_params=pltpu.CompilerParams(vmem_limit_bytes=1 << 20),
        name="hand_on",
    )(x)


def body(
    tokens,
    norm_gain,
    w_query,
    w_keyval,
    w_out,
    span_lens,
    cached_lens,
    old_table,
    new_table,
    old_cache,
):
    tp = lax.axis_size("tp")
    groups, share, width = old_cache.shape
    block_rows = share * tp
    capacity = groups * block_rows
    rows, cols = tokens.shape
    q_cols = w_query.shape[1]
    features = w_query.shape[0]
    hd = width // 2
    most_held = capacity - rows
    piece_rows = most_held // tp

    def swap(x, bit, axis="tp"):
        size = lax.axis_size(axis)
        return lax.ppermute(x, axis, [(i, i ^ bit) for i in range(size)])

    def exchange(x):
        return lax.all_to_all(x, "seq", split_axis=0, concat_axis=0, tiled=True)

    phased = groups == 8

    with jax.named_scope("tokens_gather"):
        across = swap(tokens, 2)
        beside = swap(tokens, 1)

    with jax.named_scope("cache_gather"):
        gain = jnp.maximum(norm_gain, LEAST).reshape(tp, 1, cols)
        gain, stored = lax.optimization_barrier((gain, old_cache))
        arrived = exchange(stored).reshape(groups * share, width)
        own = jnp.maximum(tokens, jnp.asarray(LEAST, BF16))
        across, *lens = lax.optimization_barrier(
            (across, cached_lens, span_lens, old_table[0], new_table[0])
        )
        plan = jnp.concatenate(lens)
        arrived, across, own, plan = lax.optimization_barrier((arrived, across, own, plan))
        ordered = call(
            functools.partial(order_kernel, share),
            jax.ShapeDtypeStruct((piece_rows, width), BF16),
            [SMEM, VMEM],
            (plan, arrived),
            flops=2 * piece_rows * groups * share * width,
            name="order",
        )
        c_across = swap(ordered, 2)
        c_beside = swap(ordered, 1)

    with jax.named_scope("project"):
        corner = swap(across, 1)
        stacked = rows * (q_cols // hd)
        query, keyval, values, limits = call(
            project_kernel,
            [
                jax.ShapeDtypeStruct((stacked, hd), BF16),
                jax.ShapeDtypeStruct((rows, width), BF16),
                jax.ShapeDtypeStruct((rows, width), BF16),
                jax.ShapeDtypeStruct((2, 8, 128), F32),
            ],
            [VMEM] * 5 + [HBM] * 2,
            (
                own,
                beside,
                across,
                corner,
                gain,
                w_query,
                w_keyval,
            ),
            flops=2 * rows * features * (q_cols + width),
            mib=PROJECT_MIB,
            scratch=[
                pltpu.VMEM((rows, features), BF16),
                pltpu.VMEM(w_query.shape, BF16),
                pltpu.VMEM(w_keyval.shape, BF16),
                pltpu.SemaphoreType.DMA((2 * tp,)),
            ],
            name="project",
        )

    with jax.named_scope("extend"):
        sent = call(
            functools.partial(extend_kernel, share, block_rows),
            [jax.ShapeDtypeStruct((groups // 2, share, width), BF16)] * 2
            if phased
            else [jax.ShapeDtypeStruct((groups * share, width), BF16)],
            [SMEM] + [VMEM] * 2,
            (plan, keyval, arrived),
            flops=4 * groups * share * groups * share * width,
            name="extend",
        )
        *sent, c_across = lax.optimization_barrier((*sent, c_across))
        if phased:
            keep, got = sent[0], swap(sent[1], 1, "seq")
        cached = (ordered, c_beside, c_across, swap(c_across, 1))

    with jax.named_scope("early"):
        early = call(
            functools.partial(early_kernel, share, block_rows),
            [
                jax.ShapeDtypeStruct(((tp - 1) * piece_rows, width), BF16),
                jax.ShapeDtypeStruct((8, 128), F32),
            ],
            [SMEM] + [VMEM] * (tp - 1),
            (plan, *cached[:-1]),
            flops=1 << 30,
            mib=EARLY_MIB,
            name="early",
        )

    part = rows // CHUNKS
    tile_rows = ROW_TILE * (q_cols // hd)
    old = list(early)
    mixed = None
    for c in range(CHUNKS):
        last = c == CHUNKS - 1
        with jax.named_scope("attend"):
            of_part = jax.ShapeDtypeStruct((part, cols), BF16)
            of_all = jax.ShapeDtypeStruct((rows, cols), BF16)
            outs = [of_all, of_part, of_all, of_part]
            if not last:
                outs = [
                    of_part,
                    of_part,
                    jax.ShapeDtypeStruct((part, q_cols), BF16),
                    jax.ShapeDtypeStruct((piece_rows, width), BF16),
                    jax.ShapeDtypeStruct((8, 128), F32),
                ]
            seen = most_held + (c + 1) * part
            sums = list(call(
                functools.partial(attend_kernel, share, block_rows, c * part, part),
                outs,
                [SMEM] + [VMEM] * 8 + [HBM] + [VMEM] * len(old),
                (plan, query, keyval, values, limits, *cached, w_out, *old),
                flops=4 * part * seen * q_cols + 2 * part * q_cols * features,
                exps=part * seen * (q_cols // hd),
                mib=ATTEND_MIB,
                scratch=[
                    pltpu.VMEM((tile_rows, width), F32),
                    pltpu.VMEM((tile_rows, hd), F32),
                    pltpu.VMEM((part, q_cols), BF16),
                    pltpu.VMEM(w_out.shape, BF16),
                    pltpu.SemaphoreType.DMA,
                ],
                name="attend",
            ))
            if last:
                far0, far1, near0, near1 = sums
            else:
                far1, near1, before_rows, *rest = sums
                old += [*rest, before_rows]
        with jax.named_scope("reduce"):
            if last and phased:
                far1, got = lax.optimization_barrier((far1, got))
            got1 = swap(far1, 1)
            if c and last:
                before = hand_on(before)
                before, got1 = lax.optimization_barrier((before, got1))
            pair = (near1.astype(F32) + got1.astype(F32)).astype(BF16)
            if not last:
                query, pair = lax.optimization_barrier((query, pair))
            if last and phased:
                pair, got = lax.optimization_barrier((pair, got))
            crossed = swap(pair, 2)
            if not last:
                before = crossed

    with jax.named_scope("exchange"):
        if phased:
            pairs = list(call(
                pair_kernel,
                [jax.ShapeDtypeStruct((2, share, width), BF16)] * (groups // 2),
                [VMEM] * 2,
                (keep, got),
                flops=0,
                mib=8,
                name="pair",
            ))
            for k in range(len(pairs) - 1, 0, -1):
                pairs[k] = swap(pairs[k], 2 * k, "seq")
        else:
            new_cache = exchange(sent[0].reshape(groups, share, width))

    with jax.named_scope("finish"):
        got0 = swap(far0, 1)
        mixed = None
        for at, over in ((0, before), (part, crossed)):
            mixed = call(
                functools.partial(finish_kernel, at),
                jax.ShapeDtypeStruct((rows, cols), BF16),
                [SMEM] + [VMEM] * 4 + [HBM] * (at > 0),
                (plan, own, near0, got0, over, *([mixed] if at else [])),
                flops=4 * part * cols,
                scratch=[pltpu.VMEM((part, cols), BF16), pltpu.SemaphoreType.DMA((2,))],
                name="finish",
                into={5: 0} if at else {},
            )
        if phased:
            mixed, *pairs = lax.optimization_barrier((mixed, *pairs))
            new_cache = call(
                place_kernel,
                jax.ShapeDtypeStruct(old_cache.shape, BF16),
                [VMEM] * len(pairs),
                pairs,
                flops=0,
                mib=8,
                scratch=[pltpu.SemaphoreType.DMA((groups,))],
                name="place",
                into={},
            )
    return (mixed, new_cache)


def solution(mesh):
    in_specs = (
        P("seq", "tp"),
        P(),
        P(None, "tp"),
        P(),
        P("tp", None),
        P("seq"),
        P("seq"),
        P("seq", None),
        P("seq", None),
        P("seq", "tp", None),
    )
    out_specs = (P("seq", "tp"), P("seq", "tp", None))
    return jax.shard_map(body, mesh=mesh, in_specs=in_specs, out_specs=out_specs, check_vma=False)
```

```python
import functools
import math

import jax
import jax.numpy as jnp
from jax import lax
from jax.experimental import pallas as pl
from jax.experimental.pallas import tpu as pltpu
from jax.sharding import PartitionSpec as P

EPSILON = 1e-05
MASKED = -1e30
CHUNKS = 2
PART_ROWS = 256
ROW_TILE = 128
KEY_TILE = 128
NORM_ROWS = 128
MIB = 51
PROJECT_MIB = 50.375
LEAST = -3e38
ATTEND_MIB = 49
EARLY_MIB = 50
SAFE = 60.0
F32 = jnp.float32
BF16 = jnp.bfloat16

VMEM = pl.BlockSpec(memory_space=pltpu.VMEM)
SMEM = pl.BlockSpec(memory_space=pltpu.SMEM)
HBM = pl.BlockSpec(memory_space=pltpu.HBM)


def dot(a, b):
    return lax.dot_general(a, b, (((1,), (0,)), ((), ())), preferred_element_type=F32)


def dot_t(a, b):
    return lax.dot_general(a, b, (((1,), (1,)), ((), ())), preferred_element_type=F32)


def pair_kernel(keep_ref, got_ref, *pair_refs):
    for k, pair_ref in enumerate(pair_refs):
        pair_ref[0] = keep_ref[k]
        pair_ref[1] = got_ref[k]


def place_kernel(p3, p2, p1, p0, out_hbm, sems):
    me = lax.axis_index("seq")
    stores = []
    for k, pair_ref in enumerate((p0, p1, p2, p3)):
        for j in range(2):
            slot = out_hbm.at[me ^ (2 * k + j)]
            stores.append(pltpu.make_async_copy(pair_ref.at[j], slot, sems.at[len(stores)]))
            stores[-1].start()
    for store in stores:
        store.wait()


def order_kernel(share, plan_ref, arrived_ref, out_ref):
    rows, count = out_ref.shape[0], arrived_ref.shape[0]
    if share % 16 == 0:
        for b in range(rows // share):
            at = pl.ds(pl.multiple_of(plan_ref[2 + b] * share, share), share)
            out_ref[pl.ds(b * share, share), :] = arrived_ref[at, :]
        return
    row = lax.broadcasted_iota(jnp.int32, (rows, 128), 0)
    block = row // share
    holder = jnp.zeros_like(block)
    for b in range(rows // share):
        holder = jnp.where(block == b, plan_ref[2 + b], holder)
    index = (holder * share + row % share)[:, :1]
    column = lax.broadcasted_iota(jnp.int32, (rows, count), 1)
    pick = jnp.where(column == index, 1.0, 0.0).astype(BF16)
    out_ref[...] = dot(pick, arrived_ref[...]).astype(BF16)


def extend_kernel(share, block_rows, plan_ref, kv_ref, arrived_ref, *out_refs):
    rows = arrived_ref.shape[0]
    groups = rows // share
    held, span = plan_ref[0], plan_ref[1]
    me = lax.axis_index("seq") if len(out_refs) > 1 else 0
    row = lax.broadcasted_iota(jnp.int32, (rows, 128), 0)
    target = row // share
    block, holder = jnp.zeros_like(row), jnp.zeros_like(row)
    for b in range(groups):
        hit = target == plan_ref[2 + groups + b] ^ me
        block = jnp.where(hit, b, block)
        holder = jnp.where(hit, plan_ref[2 + b], holder)
    position = block * block_rows + lax.axis_index("tp") * share + row % share
    old_row = jnp.where(position < held, holder * share + row % share, -1)[:, :1]
    fresh = position - held
    new_row = jnp.where((fresh >= 0) & (fresh < span), fresh, -1)[:, :1]
    column = lax.broadcasted_iota(jnp.int32, (rows, rows), 1)
    total = dot(jnp.where(column == old_row, 1.0, 0.0).astype(BF16), arrived_ref[...])
    column = lax.broadcasted_iota(jnp.int32, (rows, kv_ref.shape[0]), 1)
    total += dot(jnp.where(column == new_row, 1.0, 0.0).astype(BF16), kv_ref[...])
    total = total.astype(BF16)
    if len(out_refs) == 1:
        out_refs[0][...] = total
        return
    for slot in range(groups):
        out_refs[slot % 2][slot // 2] = total[slot * share : (slot + 1) * share]


def project_kernel(
    x0,
    x1,
    x2,
    x3,
    gain_ref,
    wq_hbm,
    wkv_hbm,
    q_ref,
    kv_ref,
    values_ref,
    limits_ref,
    normed,
    wq_ref,
    wkv_ref,
    sems,
):
    pieces = (x0, x1, x2, x3)
    me = lax.axis_index("tp")
    rows, width = x0.shape
    features = width * len(pieces)
    hd = kv_ref.shape[1] // 2
    heads = wq_ref.shape[1] // hd
    loads = []
    for hbm, to in ((wkv_hbm, wkv_ref), (wq_hbm, wq_ref)):
        for j in range(len(pieces)):
            at = pl.ds(j * width, width)
            loads.append(pltpu.make_async_copy(hbm.at[at], to.at[at], sems.at[len(loads)]))
            loads[-1].start()

    for step in range(0, rows, NORM_ROWS):
        at = pl.ds(step, NORM_ROWS)
        values = [piece[at, :].astype(F32) for piece in pieces]
        average = jnp.sum(sum(values), axis=1, keepdims=True) / features
        centred = [v - average for v in values]
        spread = jnp.sum(sum(v * v for v in centred), axis=1, keepdims=True) / features
        scale = lax.rsqrt(spread + EPSILON)
        for j, v in enumerate(centred):
            owner = me ^ j
            to = pl.ds(pl.multiple_of(owner * width, width), width)
            normed[at, to] = (v * scale * gain_ref[owner]).astype(BF16)
    for load in loads[: len(pieces)]:
        load.wait()
    keyval = dot(normed[...], wkv_ref[...]).astype(BF16)
    kv_ref[...] = keyval
    values_ref[:, hd:] = keyval[:, hd:]
    values_ref[:, :hd] = jnp.ones((rows, hd), BF16)
    limits_ref[0] = longest(keyval[:, :hd])
    for load in loads[len(pieces) :]:
        load.wait()
    query = dot(normed[...], wq_ref[...]).astype(BF16)
    for start in range(0, rows, ROW_TILE):
        for h in range(heads):
            q_ref[pl.ds(start * heads + h * ROW_TILE, ROW_TILE), :] = query[
                start : start + ROW_TILE, h * hd : (h + 1) * hd
            ]
    limits_ref[1] = longest(q_ref[...])


def longest(x):
    squares = dot(x * x, jnp.ones((x.shape[1], 128), BF16))
    return jnp.max(squares.reshape(-1, 8, 128), axis=0)


def lay_out(share, block_rows, held, owners, pieces, out_ref):
    piece_rows, width = pieces[0].shape
    hd = width // 2
    group = KEY_TILE * lax.axis_size("tp")
    tiles = (held + group - 1) // group
    row = lax.broadcasted_iota(jnp.int32, (KEY_TILE, hd), 0)
    place = row // share * block_rows + row % share

    def lay(i, whole):
        source = pl.ds(i * KEY_TILE, KEY_TILE)
        for j, (owner, piece) in enumerate(zip(owners, pieces)):
            at = pl.ds((i * len(pieces) + j) * KEY_TILE, KEY_TILE)
            if whole:
                out_ref[at, hd:] = piece[source, hd:]
                out_ref[at, :hd] = jnp.ones((KEY_TILE, hd), BF16)
                continue
            used = place + owner * share + i * group < held
            out_ref[at, hd:] = jnp.where(used, piece[source, hd:].astype(F32), 0.0).astype(BF16)
            out_ref[at, :hd] = jnp.where(used, 1.0, 0.0).astype(BF16)

    for i in range(piece_rows // KEY_TILE):
        pl.when(i < tiles - 1)(functools.partial(lay, i, True))
        pl.when(i == tiles - 1)(functools.partial(lay, i, False))


def early_kernel(share, block_rows, plan_ref, *refs):
    pieces, (out_ref, limit_ref) = refs[:-2], refs[-2:]
    me = lax.axis_index("tp")
    owners = [me ^ j for j in range(len(pieces))]
    lay_out(share, block_rows, plan_ref[0], owners, pieces, out_ref)
    limit_ref[...] = functools.reduce(
        jnp.maximum, [longest(piece[:, : piece.shape[1] // 2]) for piece in pieces]
    )


def attend_kernel(share, block_rows, start_row, rows, plan_ref, q_ref, kv_ref, new_ref, *refs):
    limits_ref, pieces, wout_hbm = refs[0], refs[1:5], refs[5]
    total, high, context, wout, sem = refs[-5:]
    most_ref, most_limit_ref = refs[6:8]
    if start_row:
        rest_ref, rest_limit_ref, before_ref, far0_ref, far1_ref, near0_ref, near1_ref = refs[8:15]
    else:
        far1_ref, near1_ref, context_out, rest_ref, rest_limit_ref = refs[8:13]
    me = lax.axis_index("tp")
    held, span = plan_ref[0], plan_ref[1]
    piece_rows, width = pieces[0].shape
    hd = width // 2
    heads = q_ref.shape[0] // kv_ref.shape[0]
    load = pltpu.make_async_copy(wout_hbm, wout, sem)
    load.start()

    group = KEY_TILE * len(pieces)
    most = piece_rows // KEY_TILE
    tiles = (held + group - 1) // group
    if not start_row:
        corner = len(pieces) - 1
        lay_out(share, block_rows, held, [me ^ corner], pieces[corner:], rest_ref)
        rest_limit_ref[...] = longest(pieces[corner][:, :hd])

    factor = hd ** (-0.5) * math.log2(math.e)
    old_limit = jnp.maximum(most_limit_ref[...], rest_limit_ref[...])
    key_limit = jnp.max(jnp.maximum(old_limit, limits_ref[0]))
    small = key_limit * jnp.max(limits_ref[1]) * (1.05 / hd) < SAFE * SAFE

    tile_rows = ROW_TILE * heads

    def queries(t):
        return q_ref[pl.ds(start_row * heads + t * tile_rows, tile_rows), :]

    def old_keys(i):
        source = pl.ds(i * KEY_TILE, KEY_TILE)
        return jnp.concatenate([piece[source, :hd] for piece in pieces], axis=0)

    def old_values(i):
        parts = []
        for ref, count in ((most_ref, len(pieces) - 1), (rest_ref, 1)):
            size = count * KEY_TILE
            at = i * size if isinstance(i, int) else pl.multiple_of(i * size, KEY_TILE)
            parts.append(ref[pl.ds(at, size), :])
        return jnp.concatenate(parts, axis=0)

    def new_scores(t):
        known = start_row + t * ROW_TILE
        scores = dot_t(queries(t), kv_ref[pl.ds(0, known + ROW_TILE), :hd])
        to = lax.broadcasted_iota(jnp.int32, (tile_rows, ROW_TILE), 0) % ROW_TILE
        by = lax.broadcasted_iota(jnp.int32, (tile_rows, ROW_TILE), 1)
        last = jnp.where(by <= to, scores[:, known:], MASKED)
        return jnp.concatenate([scores[:, :known], last], axis=1) if known else last

    def new_values(t):
        return new_ref[pl.ds(0, start_row + (t + 1) * ROW_TILE), :]

    def put(t, both):
        sums = both[:, :hd]
        inverse = pl.reciprocal(sums, approx=True)
        inverse = inverse * (2.0 - sums * inverse)
        out = (both[:, hd:] * inverse).astype(BF16)
        for h in range(heads):
            context[pl.ds(t * ROW_TILE, ROW_TILE), h * hd : (h + 1) * hd] = out[
                h * ROW_TILE : (h + 1) * ROW_TILE
            ]

    def fast(used, begin):
        row_tiles = range(begin // ROW_TILE, min(begin + PART_ROWS, rows) // ROW_TILE)
        steps = [(t, i) for t in row_tiles for i in range(used + 1)]

        def score(t, i):
            return new_scores(t) if i == used else dot_t(queries(t), old_keys(i))

        ahead, both = score(*steps[0]), None
        for at, (t, i) in enumerate(steps):
            scores = ahead
            if at + 1 < len(steps):
                ahead = score(*steps[at + 1])
            weights = jnp.exp2(scores * factor).astype(BF16)
            values = new_values(t) if i == used else old_values(i)
            part = dot(weights, values)
            both = part if i == 0 else both + part
            if i == used:
                put(t, both)

    def exact(t):
        column = lax.broadcasted_iota(jnp.int32, (tile_rows, group), 1)
        within = column % KEY_TILE
        owner = me ^ (column // KEY_TILE)
        place = within // share * block_rows + within % share + owner * share

        def old_scores(i):
            scores = dot_t(queries(t), old_keys(pl.multiple_of(i, 1)))
            return jnp.where(place + i * group < held, scores, MASKED)

        def raise_high(i, carry):
            top = jnp.max(old_scores(i), axis=1, keepdims=True)
            high[...] = jnp.maximum(high[...], top)
            return carry

        def add(i, carry):
            weights = jnp.exp2((old_scores(i) - high[:, :1]) * factor).astype(BF16)
            total[...] += dot(weights, old_values(i))
            return carry

        high[...] = jnp.zeros_like(high) + jnp.max(new_scores(t), axis=1, keepdims=True)
        lax.fori_loop(0, tiles, raise_high, 0)
        weights = jnp.exp2((new_scores(t) - high[:, :1]) * factor).astype(BF16)
        total[...] = dot(weights, new_values(t))
        lax.fori_loop(0, tiles, add, 0)
        put(t, total[...])

    for begin in range(0, rows, PART_ROWS):
        busy = start_row + begin < span
        for used in range(1, most + 1):
            pl.when(busy & small & (tiles == used))(functools.partial(fast, used, begin))

        @pl.when(busy & jnp.logical_not(small))
        def _():
            for t in range(begin // ROW_TILE, min(begin + PART_ROWS, rows) // ROW_TILE):
                exact(t)

        @pl.when(jnp.logical_not(busy))
        def _():
            context[pl.ds(begin, PART_ROWS), :] = jnp.zeros((PART_ROWS, context.shape[1]), BF16)

    load.wait()
    cols = wout.shape[1] // 4

    def partial_sums(rows_of, k):
        columns = pl.ds(pl.multiple_of((me ^ k) * cols, cols), cols)
        return dot(rows_of[...], wout[:, columns]).astype(BF16)

    far1_ref[...] = partial_sums(context, 3)
    near1_ref[...] = partial_sums(context, 2)
    if not start_row:
        context_out[...] = context[...]
        return
    for at, rows_of in ((0, before_ref), (start_row, context)):
        far0_ref[pl.ds(at, rows), :] = partial_sums(rows_of, 1)
        near0_ref[pl.ds(at, rows), :] = partial_sums(rows_of, 0)


def hand_on_kernel(in_ref, out_ref):
    pass


def finish_kernel(at, plan_ref, tokens_ref, near_ref, got_ref, crossed_ref, *refs):
    out_hbm, done, sems = refs[-3:]
    rows = crossed_ref.shape[0]
    half = rows // 2
    stores = []
    for i in range(2):
        here = pl.ds(i * half, half)
        there = pl.ds(at + i * half, half)
        kept = near_ref[there, :].astype(F32) + got_ref[there, :].astype(F32)
        total = tokens_ref[there, :].astype(F32) + (kept + crossed_ref[here, :].astype(F32))
        row = lax.broadcasted_iota(jnp.int32, total.shape, 0) + (at + i * half)
        done[here, :] = jnp.where(row < plan_ref[1], total, 0.0).astype(BF16)
        stores.append(pltpu.make_async_copy(done.at[here], out_hbm.at[there], sems.at[i]))
        stores[-1].start()
    for store in stores:
        store.wait()


def call(
    kernel, out_shape, in_specs, args, flops, mib=MIB, scratch=(), exps=0, name=None, into=None
):
    outs = out_shape if isinstance(out_shape, (list, tuple)) else [out_shape]
    moved = sum(a.size * a.dtype.itemsize for a in list(args) + list(outs))
    return pl.pallas_call(
        kernel,
        out_shape=out_shape,
        in_specs=in_specs,
        out_specs=jax.tree.map(lambda _: VMEM if into is None else HBM, out_shape),
        input_output_aliases=into or {},
        scratch_shapes=list(scratch),
        cost_estimate=pl.CostEstimate(flops=flops, bytes_accessed=moved, transcendentals=exps),
        compiler_params=pltpu.CompilerParams(vmem_limit_bytes=int(mib * 1024 * 1024)),
        name=name,
    )(*args)


def hand_on(x):
    return pl.pallas_call(
        hand_on_kernel,
        out_shape=jax.ShapeDtypeStruct(x.shape, x.dtype),
        in_specs=[pl.BlockSpec(memory_space=pl.ANY)],
        out_specs=pl.BlockSpec(memory_space=pl.ANY),
        input_output_aliases={0: 0},
        cost_estimate=pl.CostEstimate(flops=1 << 34, bytes_accessed=1024, transcendentals=0),
        compiler_params=pltpu.CompilerParams(vmem_limit_bytes=1 << 20),
        name="hand_on",
    )(x)


def body(
    tokens,
    norm_gain,
    w_query,
    w_keyval,
    w_out,
    span_lens,
    cached_lens,
    old_table,
    new_table,
    old_cache,
):
    tp = lax.axis_size("tp")
    groups, share, width = old_cache.shape
    block_rows = share * tp
    capacity = groups * block_rows
    rows, cols = tokens.shape
    q_cols = w_query.shape[1]
    features = w_query.shape[0]
    hd = width // 2
    most_held = capacity - rows
    piece_rows = most_held // tp

    def swap(x, bit, axis="tp"):
        size = lax.axis_size(axis)
        return lax.ppermute(x, axis, [(i, i ^ bit) for i in range(size)])

    def exchange(x):
        return lax.all_to_all(x, "seq", split_axis=0, concat_axis=0, tiled=True)

    phased = groups == 8

    with jax.named_scope("tokens_gather"):
        across = swap(tokens, 2)
        beside = swap(tokens, 1)

    with jax.named_scope("cache_gather"):
        gain = jnp.maximum(norm_gain, LEAST).reshape(tp, 1, cols)
        gain, stored = lax.optimization_barrier((gain, old_cache))
        arrived = exchange(stored).reshape(groups * share, width)
        own = jnp.maximum(tokens, jnp.asarray(LEAST, BF16))
        across, *lens = lax.optimization_barrier(
            (across, cached_lens, span_lens, old_table[0], new_table[0])
        )
        plan = jnp.concatenate(lens)
        arrived, across, own, plan = lax.optimization_barrier((arrived, across, own, plan))
        ordered = call(
            functools.partial(order_kernel, share),
            jax.ShapeDtypeStruct((piece_rows, width), BF16),
            [SMEM, VMEM],
            (plan, arrived),
            flops=2 * piece_rows * groups * share * width,
            name="order",
        )
        c_across = swap(ordered, 2)
        c_beside = swap(ordered, 1)

    with jax.named_scope("project"):
        corner = swap(across, 1)
        stacked = rows * (q_cols // hd)
        query, keyval, values, limits = call(
            project_kernel,
            [
                jax.ShapeDtypeStruct((stacked, hd), BF16),
                jax.ShapeDtypeStruct((rows, width), BF16),
                jax.ShapeDtypeStruct((rows, width), BF16),
                jax.ShapeDtypeStruct((2, 8, 128), F32),
            ],
            [VMEM] * 5 + [HBM] * 2,
            (
                own,
                beside,
                across,
                corner,
                gain,
                w_query,
                w_keyval,
            ),
            flops=2 * rows * features * (q_cols + width),
            mib=PROJECT_MIB,
            scratch=[
                pltpu.VMEM((rows, features), BF16),
                pltpu.VMEM(w_query.shape, BF16),
                pltpu.VMEM(w_keyval.shape, BF16),
                pltpu.SemaphoreType.DMA((2 * tp,)),
            ],
            name="project",
        )

    with jax.named_scope("extend"):
        sent = call(
            functools.partial(extend_kernel, share, block_rows),
            [jax.ShapeDtypeStruct((groups // 2, share, width), BF16)] * 2
            if phased
            else [jax.ShapeDtypeStruct((groups * share, width), BF16)],
            [SMEM] + [VMEM] * 2,
            (plan, keyval, arrived),
            flops=4 * groups * share * groups * share * width,
            name="extend",
        )
        *sent, c_across = lax.optimization_barrier((*sent, c_across))
        if phased:
            keep, got = sent[0], swap(sent[1], 1, "seq")
        cached = (ordered, c_beside, c_across, swap(c_across, 1))

    with jax.named_scope("early"):
        early = call(
            functools.partial(early_kernel, share, block_rows),
            [
                jax.ShapeDtypeStruct(((tp - 1) * piece_rows, width), BF16),
                jax.ShapeDtypeStruct((8, 128), F32),
            ],
            [SMEM] + [VMEM] * (tp - 1),
            (plan, *cached[:-1]),
            flops=1 << 30,
            mib=EARLY_MIB,
            name="early",
        )

    part = rows // CHUNKS
    tile_rows = ROW_TILE * (q_cols // hd)
    old = list(early)
    mixed = None
    for c in range(CHUNKS):
        last = c == CHUNKS - 1
        with jax.named_scope("attend"):
            of_part = jax.ShapeDtypeStruct((part, cols), BF16)
            of_all = jax.ShapeDtypeStruct((rows, cols), BF16)
            outs = [of_all, of_part, of_all, of_part]
            if not last:
                outs = [
                    of_part,
                    of_part,
                    jax.ShapeDtypeStruct((part, q_cols), BF16),
                    jax.ShapeDtypeStruct((piece_rows, width), BF16),
                    jax.ShapeDtypeStruct((8, 128), F32),
                ]
            seen = most_held + (c + 1) * part
            sums = list(call(
                functools.partial(attend_kernel, share, block_rows, c * part, part),
                outs,
                [SMEM] + [VMEM] * 8 + [HBM] + [VMEM] * len(old),
                (plan, query, keyval, values, limits, *cached, w_out, *old),
                flops=4 * part * seen * q_cols + 2 * part * q_cols * features,
                exps=part * seen * (q_cols // hd),
                mib=ATTEND_MIB,
                scratch=[
                    pltpu.VMEM((tile_rows, width), F32),
                    pltpu.VMEM((tile_rows, hd), F32),
                    pltpu.VMEM((part, q_cols), BF16),
                    pltpu.VMEM(w_out.shape, BF16),
                    pltpu.SemaphoreType.DMA,
                ],
                name="attend",
            ))
            if last:
                far0, far1, near0, near1 = sums
            else:
                far1, near1, before_rows, *rest = sums
                old += [*rest, before_rows]
        with jax.named_scope("reduce"):
            if last and phased:
                far1, got = lax.optimization_barrier((far1, got))
            got1 = swap(far1, 1)
            if c and last:
                before = hand_on(before)
                before, got1 = lax.optimization_barrier((before, got1))
            pair = (near1.astype(F32) + got1.astype(F32)).astype(BF16)
            if not last:
                query, pair = lax.optimization_barrier((query, pair))
            if last and phased:
                pair, got = lax.optimization_barrier((pair, got))
            crossed = swap(pair, 2)
            if not last:
                before = crossed

    with jax.named_scope("exchange"):
        if phased:
            pairs = list(call(
                pair_kernel,
                [jax.ShapeDtypeStruct((2, share, width), BF16)] * (groups // 2),
                [VMEM] * 2,
                (keep, got),
                flops=0,
                mib=8,
                name="pair",
            ))
            for k in range(len(pairs) - 1, 1, -1):
                pairs[k] = swap(pairs[k], 2 * k, "seq")
        else:
            new_cache = exchange(sent[0].reshape(groups, share, width))

    with jax.named_scope("finish"):
        got0 = swap(far0, 1)
        mixed = None
        for at, over in ((0, before), (part, crossed)):
            mixed = call(
                functools.partial(finish_kernel, at),
                jax.ShapeDtypeStruct((rows, cols), BF16),
                [SMEM] + [VMEM] * 4 + [HBM] * (at > 0),
                (plan, own, near0, got0, over, *([mixed] if at else [])),
                flops=4 * part * cols,
                scratch=[pltpu.VMEM((part, cols), BF16), pltpu.SemaphoreType.DMA((2,))],
                name="finish",
                into={5: 0} if at else {},
            )
            if phased and not at:
                mixed, pairs[1] = lax.optimization_barrier((mixed, pairs[1]))
                pairs[1] = swap(pairs[1], 2, "seq")
        if phased:
            mixed, *pairs = lax.optimization_barrier((mixed, *pairs))
            new_cache = call(
                place_kernel,
                jax.ShapeDtypeStruct(old_cache.shape, BF16),
                [VMEM] * len(pairs),
                pairs[::-1],
                flops=0,
                mib=8,
                scratch=[pltpu.SemaphoreType.DMA((groups,))],
                name="place",
                into={},
            )
    return (mixed, new_cache)


def solution(mesh):
    in_specs = (
        P("seq", "tp"),
        P(),
        P(None, "tp"),
        P(),
        P("tp", None),
        P("seq"),
        P("seq"),
        P("seq", None),
        P("seq", None),
        P("seq", "tp", None),
    )
    out_specs = (P("seq", "tp"), P("seq", "tp", None))
    return jax.shard_map(body, mesh=mesh, in_specs=in_specs, out_specs=out_specs, check_vma=False)
```

```python
import functools
import math

import jax
import jax.numpy as jnp
from jax import lax
from jax.experimental import pallas as pl
from jax.experimental.pallas import tpu as pltpu
from jax.sharding import PartitionSpec as P

EPSILON = 1e-05
MASKED = -1e30
CHUNKS = 2
PART_ROWS = 256
ROW_TILE = 128
KEY_TILE = 128
NORM_ROWS = 128
MIB = 51
PROJECT_MIB = 50.375
LEAST = -3e38
ATTEND_MIB = 49
EARLY_MIB = 50
SAFE = 60.0
F32 = jnp.float32
BF16 = jnp.bfloat16

VMEM = pl.BlockSpec(memory_space=pltpu.VMEM)
SMEM = pl.BlockSpec(memory_space=pltpu.SMEM)
HBM = pl.BlockSpec(memory_space=pltpu.HBM)


def dot(a, b):
    return lax.dot_general(a, b, (((1,), (0,)), ((), ())), preferred_element_type=F32)


def dot_t(a, b):
    return lax.dot_general(a, b, (((1,), (1,)), ((), ())), preferred_element_type=F32)


def pair_kernel(keep_ref, got_ref, *pair_refs):
    for k, pair_ref in enumerate(pair_refs):
        pair_ref[0] = keep_ref[k]
        pair_ref[1] = got_ref[k]


def place_kernel(p0, p1, p2, p3, out_hbm, sems):
    me = lax.axis_index("seq")
    stores = []
    for k, pair_ref in enumerate((p0, p1, p2, p3)):
        for j in range(2):
            slot = out_hbm.at[me ^ (2 * k + j)]
            stores.append(pltpu.make_async_copy(pair_ref.at[j], slot, sems.at[len(stores)]))
            stores[-1].start()
    for store in stores:
        store.wait()


def order_kernel(share, plan_ref, arrived_ref, out_ref):
    rows, count = out_ref.shape[0], arrived_ref.shape[0]
    if share % 16 == 0:
        for b in range(rows // share):
            at = pl.ds(pl.multiple_of(plan_ref[2 + b] * share, share), share)
            out_ref[pl.ds(b * share, share), :] = arrived_ref[at, :]
        return
    row = lax.broadcasted_iota(jnp.int32, (rows, 128), 0)
    block = row // share
    holder = jnp.zeros_like(block)
    for b in range(rows // share):
        holder = jnp.where(block == b, plan_ref[2 + b], holder)
    index = (holder * share + row % share)[:, :1]
    column = lax.broadcasted_iota(jnp.int32, (rows, count), 1)
    pick = jnp.where(column == index, 1.0, 0.0).astype(BF16)
    out_ref[...] = dot(pick, arrived_ref[...]).astype(BF16)


def extend_kernel(share, block_rows, plan_ref, kv_ref, arrived_ref, *out_refs):
    rows = arrived_ref.shape[0]
    groups = rows // share
    held, span = plan_ref[0], plan_ref[1]
    me = lax.axis_index("seq") if len(out_refs) > 1 else 0
    row = lax.broadcasted_iota(jnp.int32, (rows, 128), 0)
    target = row // share
    block, holder = jnp.zeros_like(row), jnp.zeros_like(row)
    for b in range(groups):
        hit = target == plan_ref[2 + groups + b] ^ me
        block = jnp.where(hit, b, block)
        holder = jnp.where(hit, plan_ref[2 + b], holder)
    position = block * block_rows + lax.axis_index("tp") * share + row % share
    old_row = jnp.where(position < held, holder * share + row % share, -1)[:, :1]
    fresh = position - held
    new_row = jnp.where((fresh >= 0) & (fresh < span), fresh, -1)[:, :1]
    column = lax.broadcasted_iota(jnp.int32, (rows, rows), 1)
    total = dot(jnp.where(column == old_row, 1.0, 0.0).astype(BF16), arrived_ref[...])
    column = lax.broadcasted_iota(jnp.int32, (rows, kv_ref.shape[0]), 1)
    total += dot(jnp.where(column == new_row, 1.0, 0.0).astype(BF16), kv_ref[...])
    total = total.astype(BF16)
    if len(out_refs) == 1:
        out_refs[0][...] = total
        return
    for slot in range(groups):
        out_refs[slot % 2][slot // 2] = total[slot * share : (slot + 1) * share]


def project_kernel(
    x0,
    x1,
    x2,
    x3,
    gain_ref,
    wq_hbm,
    wkv_hbm,
    q_ref,
    kv_ref,
    values_ref,
    limits_ref,
    normed,
    wq_ref,
    wkv_ref,
    sems,
):
    pieces = (x0, x1, x2, x3)
    me = lax.axis_index("tp")
    rows, width = x0.shape
    features = width * len(pieces)
    hd = kv_ref.shape[1] // 2
    heads = wq_ref.shape[1] // hd
    loads = []
    for hbm, to in ((wkv_hbm, wkv_ref), (wq_hbm, wq_ref)):
        for j in range(len(pieces)):
            at = pl.ds(j * width, width)
            loads.append(pltpu.make_async_copy(hbm.at[at], to.at[at], sems.at[len(loads)]))
            loads[-1].start()

    for step in range(0, rows, NORM_ROWS):
        at = pl.ds(step, NORM_ROWS)
        values = [piece[at, :].astype(F32) for piece in pieces]
        average = jnp.sum(sum(values), axis=1, keepdims=True) / features
        centred = [v - average for v in values]
        spread = jnp.sum(sum(v * v for v in centred), axis=1, keepdims=True) / features
        scale = lax.rsqrt(spread + EPSILON)
        for j, v in enumerate(centred):
            owner = me ^ j
            to = pl.ds(pl.multiple_of(owner * width, width), width)
            normed[at, to] = (v * scale * gain_ref[owner]).astype(BF16)
    for load in loads[: len(pieces)]:
        load.wait()
    keyval = dot(normed[...], wkv_ref[...]).astype(BF16)
    kv_ref[...] = keyval
    values_ref[:, hd:] = keyval[:, hd:]
    values_ref[:, :hd] = jnp.ones((rows, hd), BF16)
    limits_ref[0] = longest(keyval[:, :hd])
    for load in loads[len(pieces) :]:
        load.wait()
    query = dot(normed[...], wq_ref[...]).astype(BF16)
    for start in range(0, rows, ROW_TILE):
        for h in range(heads):
            q_ref[pl.ds(start * heads + h * ROW_TILE, ROW_TILE), :] = query[
                start : start + ROW_TILE, h * hd : (h + 1) * hd
            ]
    limits_ref[1] = longest(q_ref[...])


def longest(x):
    squares = dot(x * x, jnp.ones((x.shape[1], 128), BF16))
    return jnp.max(squares.reshape(-1, 8, 128), axis=0)


def lay_out(share, block_rows, held, owners, pieces, out_ref):
    piece_rows, width = pieces[0].shape
    hd = width // 2
    group = KEY_TILE * lax.axis_size("tp")
    tiles = (held + group - 1) // group
    row = lax.broadcasted_iota(jnp.int32, (KEY_TILE, hd), 0)
    place = row // share * block_rows + row % share

    def lay(i, whole):
        source = pl.ds(i * KEY_TILE, KEY_TILE)
        for j, (owner, piece) in enumerate(zip(owners, pieces)):
            at = pl.ds((i * len(pieces) + j) * KEY_TILE, KEY_TILE)
            if whole:
                out_ref[at, hd:] = piece[source, hd:]
                out_ref[at, :hd] = jnp.ones((KEY_TILE, hd), BF16)
                continue
            used = place + owner * share + i * group < held
            out_ref[at, hd:] = jnp.where(used, piece[source, hd:].astype(F32), 0.0).astype(BF16)
            out_ref[at, :hd] = jnp.where(used, 1.0, 0.0).astype(BF16)

    for i in range(piece_rows // KEY_TILE):
        pl.when(i < tiles - 1)(functools.partial(lay, i, True))
        pl.when(i == tiles - 1)(functools.partial(lay, i, False))


def early_kernel(share, block_rows, plan_ref, *refs):
    pieces, (out_ref, limit_ref) = refs[:-2], refs[-2:]
    me = lax.axis_index("tp")
    owners = [me ^ j for j in range(len(pieces))]
    lay_out(share, block_rows, plan_ref[0], owners, pieces, out_ref)
    limit_ref[...] = functools.reduce(
        jnp.maximum, [longest(piece[:, : piece.shape[1] // 2]) for piece in pieces]
    )


def attend_kernel(share, block_rows, start_row, rows, plan_ref, q_ref, kv_ref, new_ref, *refs):
    limits_ref, pieces, wout_hbm = refs[0], refs[1:5], refs[5]
    total, high, context, wout, sem = refs[-5:]
    most_ref, most_limit_ref = refs[6:8]
    if start_row:
        rest_ref, rest_limit_ref, before_ref, far0_ref, far1_ref, near0_ref, near1_ref = refs[8:15]
    else:
        far1_ref, near1_ref, context_out, rest_ref, rest_limit_ref = refs[8:13]
    me = lax.axis_index("tp")
    held, span = plan_ref[0], plan_ref[1]
    piece_rows, width = pieces[0].shape
    hd = width // 2
    heads = q_ref.shape[0] // kv_ref.shape[0]
    load = pltpu.make_async_copy(wout_hbm, wout, sem)
    load.start()

    group = KEY_TILE * len(pieces)
    most = piece_rows // KEY_TILE
    tiles = (held + group - 1) // group
    if not start_row:
        corner = len(pieces) - 1
        lay_out(share, block_rows, held, [me ^ corner], pieces[corner:], rest_ref)
        rest_limit_ref[...] = longest(pieces[corner][:, :hd])

    factor = hd ** (-0.5) * math.log2(math.e)
    old_limit = jnp.maximum(most_limit_ref[...], rest_limit_ref[...])
    key_limit = jnp.max(jnp.maximum(old_limit, limits_ref[0]))
    small = key_limit * jnp.max(limits_ref[1]) * (1.05 / hd) < SAFE * SAFE

    tile_rows = ROW_TILE * heads

    def queries(t):
        return q_ref[pl.ds(start_row * heads + t * tile_rows, tile_rows), :]

    def old_keys(i):
        source = pl.ds(i * KEY_TILE, KEY_TILE)
        return jnp.concatenate([piece[source, :hd] for piece in pieces], axis=0)

    def old_values(i):
        parts = []
        for ref, count in ((most_ref, len(pieces) - 1), (rest_ref, 1)):
            size = count * KEY_TILE
            at = i * size if isinstance(i, int) else pl.multiple_of(i * size, KEY_TILE)
            parts.append(ref[pl.ds(at, size), :])
        return jnp.concatenate(parts, axis=0)

    def new_scores(t):
        known = start_row + t * ROW_TILE
        scores = dot_t(queries(t), kv_ref[pl.ds(0, known + ROW_TILE), :hd])
        to = lax.broadcasted_iota(jnp.int32, (tile_rows, ROW_TILE), 0) % ROW_TILE
        by = lax.broadcasted_iota(jnp.int32, (tile_rows, ROW_TILE), 1)
        last = jnp.where(by <= to, scores[:, known:], MASKED)
        return jnp.concatenate([scores[:, :known], last], axis=1) if known else last

    def new_values(t):
        return new_ref[pl.ds(0, start_row + (t + 1) * ROW_TILE), :]

    def put(t, both):
        sums = both[:, :hd]
        inverse = pl.reciprocal(sums, approx=True)
        inverse = inverse * (2.0 - sums * inverse)
        out = (both[:, hd:] * inverse).astype(BF16)
        for h in range(heads):
            context[pl.ds(t * ROW_TILE, ROW_TILE), h * hd : (h + 1) * hd] = out[
                h * ROW_TILE : (h + 1) * ROW_TILE
            ]

    def fast(used, begin):
        row_tiles = range(begin // ROW_TILE, min(begin + PART_ROWS, rows) // ROW_TILE)
        steps = [(t, i) for t in row_tiles for i in range(used + 1)]

        def score(t, i):
            return new_scores(t) if i == used else dot_t(queries(t), old_keys(i))

        ahead, both = score(*steps[0]), None
        for at, (t, i) in enumerate(steps):
            scores = ahead
            if at + 1 < len(steps):
                ahead = score(*steps[at + 1])
            weights = jnp.exp2(scores * factor).astype(BF16)
            values = new_values(t) if i == used else old_values(i)
            part = dot(weights, values)
            both = part if i == 0 else both + part
            if i == used:
                put(t, both)

    def exact(t):
        column = lax.broadcasted_iota(jnp.int32, (tile_rows, group), 1)
        within = column % KEY_TILE
        owner = me ^ (column // KEY_TILE)
        place = within // share * block_rows + within % share + owner * share

        def old_scores(i):
            scores = dot_t(queries(t), old_keys(pl.multiple_of(i, 1)))
            return jnp.where(place + i * group < held, scores, MASKED)

        def raise_high(i, carry):
            top = jnp.max(old_scores(i), axis=1, keepdims=True)
            high[...] = jnp.maximum(high[...], top)
            return carry

        def add(i, carry):
            weights = jnp.exp2((old_scores(i) - high[:, :1]) * factor).astype(BF16)
            total[...] += dot(weights, old_values(i))
            return carry

        high[...] = jnp.zeros_like(high) + jnp.max(new_scores(t), axis=1, keepdims=True)
        lax.fori_loop(0, tiles, raise_high, 0)
        weights = jnp.exp2((new_scores(t) - high[:, :1]) * factor).astype(BF16)
        total[...] = dot(weights, new_values(t))
        lax.fori_loop(0, tiles, add, 0)
        put(t, total[...])

    for begin in range(0, rows, PART_ROWS):
        busy = start_row + begin < span
        for used in range(1, most + 1):
            pl.when(busy & small & (tiles == used))(functools.partial(fast, used, begin))

        @pl.when(busy & jnp.logical_not(small))
        def _():
            for t in range(begin // ROW_TILE, min(begin + PART_ROWS, rows) // ROW_TILE):
                exact(t)

        @pl.when(jnp.logical_not(busy))
        def _():
            context[pl.ds(begin, PART_ROWS), :] = jnp.zeros((PART_ROWS, context.shape[1]), BF16)

    load.wait()
    cols = wout.shape[1] // 4

    def partial_sums(rows_of, k):
        columns = pl.ds(pl.multiple_of((me ^ k) * cols, cols), cols)
        return dot(rows_of[...], wout[:, columns]).astype(BF16)

    far1_ref[...] = partial_sums(context, 3)
    near1_ref[...] = partial_sums(context, 2)
    if not start_row:
        context_out[...] = context[...]
        return
    for at, rows_of in ((0, before_ref), (start_row, context)):
        far0_ref[pl.ds(at, rows), :] = partial_sums(rows_of, 1)
        near0_ref[pl.ds(at, rows), :] = partial_sums(rows_of, 0)


def hand_on_kernel(in_ref, out_ref):
    pass


def finish_kernel(at, plan_ref, tokens_ref, near_ref, got_ref, crossed_ref, *refs):
    out_hbm, done, sems = refs[-3:]
    rows = crossed_ref.shape[0]
    half = rows // 2
    stores = []
    for i in range(2):
        here = pl.ds(i * half, half)
        there = pl.ds(at + i * half, half)
        kept = near_ref[there, :].astype(F32) + got_ref[there, :].astype(F32)
        total = tokens_ref[there, :].astype(F32) + (kept + crossed_ref[here, :].astype(F32))
        row = lax.broadcasted_iota(jnp.int32, total.shape, 0) + (at + i * half)
        done[here, :] = jnp.where(row < plan_ref[1], total, 0.0).astype(BF16)
        stores.append(pltpu.make_async_copy(done.at[here], out_hbm.at[there], sems.at[i]))
        stores[-1].start()
    for store in stores:
        store.wait()


def call(
    kernel, out_shape, in_specs, args, flops, mib=MIB, scratch=(), exps=0, name=None, into=None
):
    outs = out_shape if isinstance(out_shape, (list, tuple)) else [out_shape]
    moved = sum(a.size * a.dtype.itemsize for a in list(args) + list(outs))
    return pl.pallas_call(
        kernel,
        out_shape=out_shape,
        in_specs=in_specs,
        out_specs=jax.tree.map(lambda _: VMEM if into is None else HBM, out_shape),
        input_output_aliases=into or {},
        scratch_shapes=list(scratch),
        cost_estimate=pl.CostEstimate(flops=flops, bytes_accessed=moved, transcendentals=exps),
        compiler_params=pltpu.CompilerParams(vmem_limit_bytes=int(mib * 1024 * 1024)),
        name=name,
    )(*args)


def hand_on(x):
    return pl.pallas_call(
        hand_on_kernel,
        out_shape=jax.ShapeDtypeStruct(x.shape, x.dtype),
        in_specs=[pl.BlockSpec(memory_space=pl.ANY)],
        out_specs=pl.BlockSpec(memory_space=pl.ANY),
        input_output_aliases={0: 0},
        cost_estimate=pl.CostEstimate(flops=1 << 34, bytes_accessed=1024, transcendentals=0),
        compiler_params=pltpu.CompilerParams(vmem_limit_bytes=1 << 20),
        name="hand_on",
    )(x)


def body(
    tokens,
    norm_gain,
    w_query,
    w_keyval,
    w_out,
    span_lens,
    cached_lens,
    old_table,
    new_table,
    old_cache,
):
    tp = lax.axis_size("tp")
    groups, share, width = old_cache.shape
    block_rows = share * tp
    capacity = groups * block_rows
    rows, cols = tokens.shape
    q_cols = w_query.shape[1]
    features = w_query.shape[0]
    hd = width // 2
    most_held = capacity - rows
    piece_rows = most_held // tp

    def swap(x, bit, axis="tp"):
        size = lax.axis_size(axis)
        return lax.ppermute(x, axis, [(i, i ^ bit) for i in range(size)])

    def exchange(x):
        return lax.all_to_all(x, "seq", split_axis=0, concat_axis=0, tiled=True)

    phased = groups == 8

    with jax.named_scope("tokens_gather"):
        across = swap(tokens, 2)
        beside = swap(tokens, 1)

    with jax.named_scope("cache_gather"):
        number, stored = lax.optimization_barrier((lax.axis_index("seq"), old_cache))
        gain = jnp.maximum(norm_gain, jnp.where(number < groups, LEAST, 0.0)).reshape(tp, 1, cols)
        arrived = exchange(stored).reshape(groups * share, width)
        own = jnp.maximum(tokens, jnp.asarray(LEAST, BF16))
        across, *lens = lax.optimization_barrier(
            (across, cached_lens, span_lens, old_table[0], new_table[0])
        )
        plan = jnp.concatenate(lens)
        arrived, across, own, gain, plan = lax.optimization_barrier(
            (arrived, across, own, gain, plan)
        )
        ordered = call(
            functools.partial(order_kernel, share),
            jax.ShapeDtypeStruct((piece_rows, width), BF16),
            [SMEM, VMEM],
            (plan, arrived),
            flops=2 * piece_rows * groups * share * width,
            name="order",
        )
        c_across = swap(ordered, 2)
        c_beside = swap(ordered, 1)

    with jax.named_scope("project"):
        corner = swap(across, 1)
        stacked = rows * (q_cols // hd)
        query, keyval, values, limits = call(
            project_kernel,
            [
                jax.ShapeDtypeStruct((stacked, hd), BF16),
                jax.ShapeDtypeStruct((rows, width), BF16),
                jax.ShapeDtypeStruct((rows, width), BF16),
                jax.ShapeDtypeStruct((2, 8, 128), F32),
            ],
            [VMEM] * 5 + [HBM] * 2,
            (
                own,
                beside,
                across,
                corner,
                gain,
                w_query,
                w_keyval,
            ),
            flops=2 * rows * features * (q_cols + width),
            mib=PROJECT_MIB,
            scratch=[
                pltpu.VMEM((rows, features), BF16),
                pltpu.VMEM(w_query.shape, BF16),
                pltpu.VMEM(w_keyval.shape, BF16),
                pltpu.SemaphoreType.DMA((2 * tp,)),
            ],
            name="project",
        )

    with jax.named_scope("extend"):
        sent = call(
            functools.partial(extend_kernel, share, block_rows),
            [jax.ShapeDtypeStruct((groups // 2, share, width), BF16)] * 2
            if phased
            else [jax.ShapeDtypeStruct((groups * share, width), BF16)],
            [SMEM] + [VMEM] * 2,
            (plan, keyval, arrived),
            flops=4 * groups * share * groups * share * width,
            name="extend",
        )
        *sent, c_across = lax.optimization_barrier((*sent, c_across))
        if phased:
            keep, got = sent[0], swap(sent[1], 1, "seq")
        cached = (ordered, c_beside, c_across, swap(c_across, 1))

    with jax.named_scope("early"):
        early = call(
            functools.partial(early_kernel, share, block_rows),
            [
                jax.ShapeDtypeStruct(((tp - 1) * piece_rows, width), BF16),
                jax.ShapeDtypeStruct((8, 128), F32),
            ],
            [SMEM] + [VMEM] * (tp - 1),
            (plan, *cached[:-1]),
            flops=1 << 30,
            mib=EARLY_MIB,
            name="early",
        )

    part = rows // CHUNKS
    tile_rows = ROW_TILE * (q_cols // hd)
    old = list(early)
    mixed = None
    for c in range(CHUNKS):
        last = c == CHUNKS - 1
        with jax.named_scope("attend"):
            of_part = jax.ShapeDtypeStruct((part, cols), BF16)
            of_all = jax.ShapeDtypeStruct((rows, cols), BF16)
            outs = [of_all, of_part, of_all, of_part]
            if not last:
                outs = [
                    of_part,
                    of_part,
                    jax.ShapeDtypeStruct((part, q_cols), BF16),
                    jax.ShapeDtypeStruct((piece_rows, width), BF16),
                    jax.ShapeDtypeStruct((8, 128), F32),
                ]
            seen = most_held + (c + 1) * part
            sums = list(call(
                functools.partial(attend_kernel, share, block_rows, c * part, part),
                outs,
                [SMEM] + [VMEM] * 8 + [HBM] + [VMEM] * len(old),
                (plan, query, keyval, values, limits, *cached, w_out, *old),
                flops=4 * part * seen * q_cols + 2 * part * q_cols * features,
                exps=part * seen * (q_cols // hd),
                mib=ATTEND_MIB,
                scratch=[
                    pltpu.VMEM((tile_rows, width), F32),
                    pltpu.VMEM((tile_rows, hd), F32),
                    pltpu.VMEM((part, q_cols), BF16),
                    pltpu.VMEM(w_out.shape, BF16),
                    pltpu.SemaphoreType.DMA,
                ],
                name="attend",
            ))
            if last:
                far0, far1, near0, near1 = sums
            else:
                far1, near1, before_rows, *rest = sums
                old += [*rest, before_rows]
        with jax.named_scope("reduce"):
            if last and phased:
                far1, got = lax.optimization_barrier((far1, got))
            got1 = swap(far1, 1)
            if c and last:
                before = hand_on(before)
                before, got1 = lax.optimization_barrier((before, got1))
            pair = (near1.astype(F32) + got1.astype(F32)).astype(BF16)
            if not last:
                query, pair = lax.optimization_barrier((query, pair))
            if last and phased:
                pair, got = lax.optimization_barrier((pair, got))
            crossed = swap(pair, 2)
            if not last:
                before = crossed

    with jax.named_scope("exchange"):
        if phased:
            pairs = list(call(
                pair_kernel,
                [jax.ShapeDtypeStruct((2, share, width), BF16)] * (groups // 2),
                [VMEM] * 2,
                (keep, got),
                flops=0,
                mib=8,
                name="pair",
            ))
            for k in range(len(pairs) - 1, 0, -1):
                pairs[k] = swap(pairs[k], 2 * k, "seq")
        else:
            new_cache = exchange(sent[0].reshape(groups, share, width))

    with jax.named_scope("finish"):
        got0 = swap(far0, 1)
        mixed = None
        for at, over in ((0, before), (part, crossed)):
            mixed = call(
                functools.partial(finish_kernel, at),
                jax.ShapeDtypeStruct((rows, cols), BF16),
                [SMEM] + [VMEM] * 4 + [HBM] * (at > 0),
                (plan, own, near0, got0, over, *([mixed] if at else [])),
                flops=4 * part * cols,
                scratch=[pltpu.VMEM((part, cols), BF16), pltpu.SemaphoreType.DMA((2,))],
                name="finish",
                into={5: 0} if at else {},
            )
        if phased:
            mixed, *pairs = lax.optimization_barrier((mixed, *pairs))
            new_cache = call(
                place_kernel,
                jax.ShapeDtypeStruct(old_cache.shape, BF16),
                [VMEM] * len(pairs),
                pairs,
                flops=0,
                mib=8,
                scratch=[pltpu.SemaphoreType.DMA((groups,))],
                name="place",
                into={},
            )
    return (mixed, new_cache)


def solution(mesh):
    in_specs = (
        P("seq", "tp"),
        P(),
        P(None, "tp"),
        P(),
        P("tp", None),
        P("seq"),
        P("seq"),
        P("seq", None),
        P("seq", None),
        P("seq", "tp", None),
    )
    out_specs = (P("seq", "tp"), P("seq", "tp", None))
    return jax.shard_map(body, mesh=mesh, in_specs=in_specs, out_specs=out_specs, check_vma=False)
```

```python
import functools
import math

import jax
import jax.numpy as jnp
from jax import lax
from jax.experimental import pallas as pl
from jax.experimental.pallas import tpu as pltpu
from jax.sharding import PartitionSpec as P

EPSILON = 1e-05
MASKED = -1e30
CHUNKS = 2
PART_ROWS = 256
ROW_TILE = 128
KEY_TILE = 128
NORM_ROWS = 128
MIB = 51
PROJECT_MIB = 50.375
LEAST = -3e38
ATTEND_MIB = 49
EARLY_MIB = 50
SAFE = 60.0
F32 = jnp.float32
BF16 = jnp.bfloat16

VMEM = pl.BlockSpec(memory_space=pltpu.VMEM)
SMEM = pl.BlockSpec(memory_space=pltpu.SMEM)
HBM = pl.BlockSpec(memory_space=pltpu.HBM)


def dot(a, b):
    return lax.dot_general(a, b, (((1,), (0,)), ((), ())), preferred_element_type=F32)


def dot_t(a, b):
    return lax.dot_general(a, b, (((1,), (1,)), ((), ())), preferred_element_type=F32)


def pair_kernel(keep_ref, got_ref, *pair_refs):
    for k, pair_ref in enumerate(pair_refs):
        pair_ref[0] = keep_ref[k]
        pair_ref[1] = got_ref[k]


def place_kernel(p0, p1, p2, p3, out_hbm, sems):
    me = lax.axis_index("seq")
    stores = []
    for k, pair_ref in enumerate((p0, p1, p2, p3)):
        for j in range(2):
            slot = out_hbm.at[me ^ (2 * k + j)]
            stores.append(pltpu.make_async_copy(pair_ref.at[j], slot, sems.at[len(stores)]))
            stores[-1].start()
    for store in stores:
        store.wait()


def order_kernel(share, plan_ref, arrived_ref, out_ref):
    rows, count = out_ref.shape[0], arrived_ref.shape[0]
    if share % 16 == 0:
        for b in range(rows // share):
            at = pl.ds(pl.multiple_of(plan_ref[2 + b] * share, share), share)
            out_ref[pl.ds(b * share, share), :] = arrived_ref[at, :]
        return
    row = lax.broadcasted_iota(jnp.int32, (rows, 128), 0)
    block = row // share
    holder = jnp.zeros_like(block)
    for b in range(rows // share):
        holder = jnp.where(block == b, plan_ref[2 + b], holder)
    index = (holder * share + row % share)[:, :1]
    column = lax.broadcasted_iota(jnp.int32, (rows, count), 1)
    pick = jnp.where(column == index, 1.0, 0.0).astype(BF16)
    out_ref[...] = dot(pick, arrived_ref[...]).astype(BF16)


def extend_kernel(share, block_rows, plan_ref, kv_ref, arrived_ref, *out_refs):
    rows = arrived_ref.shape[0]
    groups = rows // share
    held, span = plan_ref[0], plan_ref[1]
    me = lax.axis_index("seq") if len(out_refs) > 1 else 0
    row = lax.broadcasted_iota(jnp.int32, (rows, 128), 0)
    target = row // share
    block, holder = jnp.zeros_like(row), jnp.zeros_like(row)
    for b in range(groups):
        hit = target == plan_ref[2 + groups + b] ^ me
        block = jnp.where(hit, b, block)
        holder = jnp.where(hit, plan_ref[2 + b], holder)
    position = block * block_rows + lax.axis_index("tp") * share + row % share
    old_row = jnp.where(position < held, holder * share + row % share, -1)[:, :1]
    fresh = position - held
    new_row = jnp.where((fresh >= 0) & (fresh < span), fresh, -1)[:, :1]
    column = lax.broadcasted_iota(jnp.int32, (rows, rows), 1)
    total = dot(jnp.where(column == old_row, 1.0, 0.0).astype(BF16), arrived_ref[...])
    column = lax.broadcasted_iota(jnp.int32, (rows, kv_ref.shape[0]), 1)
    total += dot(jnp.where(column == new_row, 1.0, 0.0).astype(BF16), kv_ref[...])
    total = total.astype(BF16)
    if len(out_refs) == 1:
        out_refs[0][...] = total
        return
    for slot in range(groups):
        out_refs[slot % 2][slot // 2] = total[slot * share : (slot + 1) * share]


def project_kernel(
    x0,
    x1,
    x2,
    x3,
    gain_ref,
    wq_hbm,
    wkv_hbm,
    q_ref,
    kv_ref,
    values_ref,
    limits_ref,
    normed,
    wq_ref,
    wkv_ref,
    sems,
):
    pieces = (x0, x1, x2, x3)
    me = lax.axis_index("tp")
    rows, width = x0.shape
    features = width * len(pieces)
    hd = kv_ref.shape[1] // 2
    heads = wq_ref.shape[1] // hd
    loads = []
    for hbm, to in ((wkv_hbm, wkv_ref), (wq_hbm, wq_ref)):
        for j in range(len(pieces)):
            at = pl.ds(j * width, width)
            loads.append(pltpu.make_async_copy(hbm.at[at], to.at[at], sems.at[len(loads)]))
            loads[-1].start()

    for step in range(0, rows, NORM_ROWS):
        at = pl.ds(step, NORM_ROWS)
        values = [piece[at, :].astype(F32) for piece in pieces]
        average = jnp.sum(sum(values), axis=1, keepdims=True) / features
        centred = [v - average for v in values]
        spread = jnp.sum(sum(v * v for v in centred), axis=1, keepdims=True) / features
        scale = lax.rsqrt(spread + EPSILON)
        for j, v in enumerate(centred):
            owner = me ^ j
            to = pl.ds(pl.multiple_of(owner * width, width), width)
            normed[at, to] = (v * scale * gain_ref[owner]).astype(BF16)
    for load in loads[: len(pieces)]:
        load.wait()
    keyval = dot(normed[...], wkv_ref[...]).astype(BF16)
    kv_ref[...] = keyval
    values_ref[:, hd:] = keyval[:, hd:]
    values_ref[:, :hd] = jnp.ones((rows, hd), BF16)
    limits_ref[0] = longest(keyval[:, :hd])
    for load in loads[len(pieces) :]:
        load.wait()
    query = dot(normed[...], wq_ref[...]).astype(BF16)
    for start in range(0, rows, ROW_TILE):
        for h in range(heads):
            q_ref[pl.ds(start * heads + h * ROW_TILE, ROW_TILE), :] = query[
                start : start + ROW_TILE, h * hd : (h + 1) * hd
            ]
    limits_ref[1] = longest(q_ref[...])


def longest(x):
    squares = dot(x * x, jnp.ones((x.shape[1], 128), BF16))
    return jnp.max(squares.reshape(-1, 8, 128), axis=0)


def lay_out(share, block_rows, held, owners, pieces, out_ref):
    piece_rows, width = pieces[0].shape
    hd = width // 2
    group = KEY_TILE * lax.axis_size("tp")
    tiles = (held + group - 1) // group
    row = lax.broadcasted_iota(jnp.int32, (KEY_TILE, hd), 0)
    place = row // share * block_rows + row % share

    def lay(i, whole):
        source = pl.ds(i * KEY_TILE, KEY_TILE)
        for j, (owner, piece) in enumerate(zip(owners, pieces)):
            at = pl.ds((i * len(pieces) + j) * KEY_TILE, KEY_TILE)
            if whole:
                out_ref[at, hd:] = piece[source, hd:]
                out_ref[at, :hd] = jnp.ones((KEY_TILE, hd), BF16)
                continue
            used = place + owner * share + i * group < held
            out_ref[at, hd:] = jnp.where(used, piece[source, hd:].astype(F32), 0.0).astype(BF16)
            out_ref[at, :hd] = jnp.where(used, 1.0, 0.0).astype(BF16)

    for i in range(piece_rows // KEY_TILE):
        pl.when(i < tiles - 1)(functools.partial(lay, i, True))
        pl.when(i == tiles - 1)(functools.partial(lay, i, False))


def early_kernel(share, block_rows, plan_ref, *refs):
    pieces, (out_ref, limit_ref) = refs[:-2], refs[-2:]
    me = lax.axis_index("tp")
    owners = [me ^ j for j in range(len(pieces))]
    lay_out(share, block_rows, plan_ref[0], owners, pieces, out_ref)
    limit_ref[...] = functools.reduce(
        jnp.maximum, [longest(piece[:, : piece.shape[1] // 2]) for piece in pieces]
    )


def attend_kernel(share, block_rows, start_row, rows, plan_ref, q_ref, kv_ref, new_ref, *refs):
    limits_ref, pieces, wout_hbm = refs[0], refs[1:5], refs[5]
    total, high, context, wout, sem = refs[-5:]
    most_ref, most_limit_ref = refs[6:8]
    if start_row:
        rest_ref, rest_limit_ref, before_ref, far0_ref, far1_ref, near0_ref, near1_ref = refs[8:15]
    else:
        far1_ref, near1_ref, context_out, rest_ref, rest_limit_ref = refs[8:13]
    me = lax.axis_index("tp")
    held, span = plan_ref[0], plan_ref[1]
    piece_rows, width = pieces[0].shape
    hd = width // 2
    heads = q_ref.shape[0] // kv_ref.shape[0]
    load = pltpu.make_async_copy(wout_hbm, wout, sem)
    load.start()

    group = KEY_TILE * len(pieces)
    most = piece_rows // KEY_TILE
    tiles = (held + group - 1) // group
    if not start_row:
        corner = len(pieces) - 1
        lay_out(share, block_rows, held, [me ^ corner], pieces[corner:], rest_ref)
        rest_limit_ref[...] = longest(pieces[corner][:, :hd])

    factor = hd ** (-0.5) * math.log2(math.e)
    old_limit = jnp.maximum(most_limit_ref[...], rest_limit_ref[...])
    key_limit = jnp.max(jnp.maximum(old_limit, limits_ref[0]))
    small = key_limit * jnp.max(limits_ref[1]) * (1.05 / hd) < SAFE * SAFE

    tile_rows = ROW_TILE * heads

    def queries(t):
        return q_ref[pl.ds(start_row * heads + t * tile_rows, tile_rows), :]

    def old_keys(i):
        source = pl.ds(i * KEY_TILE, KEY_TILE)
        return jnp.concatenate([piece[source, :hd] for piece in pieces], axis=0)

    def old_values(i):
        parts = []
        for ref, count in ((most_ref, len(pieces) - 1), (rest_ref, 1)):
            size = count * KEY_TILE
            at = i * size if isinstance(i, int) else pl.multiple_of(i * size, KEY_TILE)
            parts.append(ref[pl.ds(at, size), :])
        return jnp.concatenate(parts, axis=0)

    def new_scores(t):
        known = start_row + t * ROW_TILE
        scores = dot_t(queries(t), kv_ref[pl.ds(0, known + ROW_TILE), :hd])
        to = lax.broadcasted_iota(jnp.int32, (tile_rows, ROW_TILE), 0) % ROW_TILE
        by = lax.broadcasted_iota(jnp.int32, (tile_rows, ROW_TILE), 1)
        last = jnp.where(by <= to, scores[:, known:], MASKED)
        return jnp.concatenate([scores[:, :known], last], axis=1) if known else last

    def new_values(t):
        return new_ref[pl.ds(0, start_row + (t + 1) * ROW_TILE), :]

    def put(t, both):
        sums = both[:, :hd]
        inverse = pl.reciprocal(sums, approx=True)
        inverse = inverse * (2.0 - sums * inverse)
        out = (both[:, hd:] * inverse).astype(BF16)
        for h in range(heads):
            context[pl.ds(t * ROW_TILE, ROW_TILE), h * hd : (h + 1) * hd] = out[
                h * ROW_TILE : (h + 1) * ROW_TILE
            ]

    def fast(used, begin):
        row_tiles = range(begin // ROW_TILE, min(begin + PART_ROWS, rows) // ROW_TILE)
        steps = [(t, i) for t in row_tiles for i in range(used + 1)]

        def score(t, i):
            return new_scores(t) if i == used else dot_t(queries(t), old_keys(i))

        ahead, both = score(*steps[0]), None
        for at, (t, i) in enumerate(steps):
            scores = ahead
            if at + 1 < len(steps):
                ahead = score(*steps[at + 1])
            weights = jnp.exp2(scores * factor).astype(BF16)
            values = new_values(t) if i == used else old_values(i)
            part = dot(weights, values)
            both = part if i == 0 else both + part
            if i == used:
                put(t, both)

    def exact(t):
        column = lax.broadcasted_iota(jnp.int32, (tile_rows, group), 1)
        within = column % KEY_TILE
        owner = me ^ (column // KEY_TILE)
        place = within // share * block_rows + within % share + owner * share

        def old_scores(i):
            scores = dot_t(queries(t), old_keys(pl.multiple_of(i, 1)))
            return jnp.where(place + i * group < held, scores, MASKED)

        def raise_high(i, carry):
            top = jnp.max(old_scores(i), axis=1, keepdims=True)
            high[...] = jnp.maximum(high[...], top)
            return carry

        def add(i, carry):
            weights = jnp.exp2((old_scores(i) - high[:, :1]) * factor).astype(BF16)
            total[...] += dot(weights, old_values(i))
            return carry

        high[...] = jnp.zeros_like(high) + jnp.max(new_scores(t), axis=1, keepdims=True)
        lax.fori_loop(0, tiles, raise_high, 0)
        weights = jnp.exp2((new_scores(t) - high[:, :1]) * factor).astype(BF16)
        total[...] = dot(weights, new_values(t))
        lax.fori_loop(0, tiles, add, 0)
        put(t, total[...])

    for begin in range(0, rows, PART_ROWS):
        busy = start_row + begin < span
        for used in range(1, most + 1):
            pl.when(busy & small & (tiles == used))(functools.partial(fast, used, begin))

        @pl.when(busy & jnp.logical_not(small))
        def _():
            for t in range(begin // ROW_TILE, min(begin + PART_ROWS, rows) // ROW_TILE):
                exact(t)

        @pl.when(jnp.logical_not(busy))
        def _():
            context[pl.ds(begin, PART_ROWS), :] = jnp.zeros((PART_ROWS, context.shape[1]), BF16)

    load.wait()
    cols = wout.shape[1] // 4

    def partial_sums(rows_of, k):
        columns = pl.ds(pl.multiple_of((me ^ k) * cols, cols), cols)
        return dot(rows_of[...], wout[:, columns]).astype(BF16)

    far1_ref[...] = partial_sums(context, 3)
    near1_ref[...] = partial_sums(context, 2)
    if not start_row:
        context_out[...] = context[...]
        return
    for at, rows_of in ((0, before_ref), (start_row, context)):
        far0_ref[pl.ds(at, rows), :] = partial_sums(rows_of, 1)
        near0_ref[pl.ds(at, rows), :] = partial_sums(rows_of, 0)


def hand_on_kernel(in_ref, out_ref):
    pass


def finish_kernel(at, plan_ref, tokens_ref, near_ref, got_ref, crossed_ref, *refs):
    out_hbm, done, sems = refs[-3:]
    rows = crossed_ref.shape[0]
    half = rows // 2
    stores = []
    for i in range(2):
        here = pl.ds(i * half, half)
        there = pl.ds(at + i * half, half)
        kept = near_ref[there, :].astype(F32) + got_ref[there, :].astype(F32)
        total = tokens_ref[there, :].astype(F32) + (kept + crossed_ref[here, :].astype(F32))
        row = lax.broadcasted_iota(jnp.int32, total.shape, 0) + (at + i * half)
        done[here, :] = jnp.where(row < plan_ref[1], total, 0.0).astype(BF16)
        stores.append(pltpu.make_async_copy(done.at[here], out_hbm.at[there], sems.at[i]))
        stores[-1].start()
    for store in stores:
        store.wait()


def call(
    kernel, out_shape, in_specs, args, flops, mib=MIB, scratch=(), exps=0, name=None, into=None
):
    outs = out_shape if isinstance(out_shape, (list, tuple)) else [out_shape]
    moved = sum(a.size * a.dtype.itemsize for a in list(args) + list(outs))
    return pl.pallas_call(
        kernel,
        out_shape=out_shape,
        in_specs=in_specs,
        out_specs=jax.tree.map(lambda _: VMEM if into is None else HBM, out_shape),
        input_output_aliases=into or {},
        scratch_shapes=list(scratch),
        cost_estimate=pl.CostEstimate(flops=flops, bytes_accessed=moved, transcendentals=exps),
        compiler_params=pltpu.CompilerParams(vmem_limit_bytes=int(mib * 1024 * 1024)),
        name=name,
    )(*args)


def hand_on(x):
    return pl.pallas_call(
        hand_on_kernel,
        out_shape=jax.ShapeDtypeStruct(x.shape, x.dtype),
        in_specs=[pl.BlockSpec(memory_space=pl.ANY)],
        out_specs=pl.BlockSpec(memory_space=pl.ANY),
        input_output_aliases={0: 0},
        cost_estimate=pl.CostEstimate(flops=1 << 34, bytes_accessed=1024, transcendentals=0),
        compiler_params=pltpu.CompilerParams(vmem_limit_bytes=1 << 20),
        name="hand_on",
    )(x)


def body(
    tokens,
    norm_gain,
    w_query,
    w_keyval,
    w_out,
    span_lens,
    cached_lens,
    old_table,
    new_table,
    old_cache,
):
    tp = lax.axis_size("tp")
    groups, share, width = old_cache.shape
    block_rows = share * tp
    capacity = groups * block_rows
    rows, cols = tokens.shape
    q_cols = w_query.shape[1]
    features = w_query.shape[0]
    hd = width // 2
    most_held = capacity - rows
    piece_rows = most_held // tp

    def swap(x, bit, axis="tp"):
        size = lax.axis_size(axis)
        return lax.ppermute(x, axis, [(i, i ^ bit) for i in range(size)])

    def exchange(x):
        return lax.all_to_all(x, "seq", split_axis=0, concat_axis=0, tiled=True)

    phased = groups == 8

    with jax.named_scope("tokens_gather"):
        across = swap(tokens, 2)
        beside = swap(tokens, 1)

    with jax.named_scope("cache_gather"):
        gain = jnp.maximum(norm_gain, LEAST).reshape(tp, 1, cols)
        gain, stored = lax.optimization_barrier((gain, old_cache))
        arrived = exchange(stored).reshape(groups * share, width)
        own = jnp.maximum(tokens, jnp.asarray(LEAST, BF16))
        across, *lens = lax.optimization_barrier(
            (across, cached_lens, span_lens, old_table[0], new_table[0])
        )
        plan = jnp.concatenate(lens)
        arrived, across, own, plan = lax.optimization_barrier((arrived, across, own, plan))
        ordered = call(
            functools.partial(order_kernel, share),
            jax.ShapeDtypeStruct((piece_rows, width), BF16),
            [SMEM, VMEM],
            (plan, arrived),
            flops=2 * piece_rows * groups * share * width,
            name="order",
        )
        c_across = swap(ordered, 2)
        c_beside = swap(ordered, 1)

    with jax.named_scope("project"):
        corner = swap(across, 1)
        stacked = rows * (q_cols // hd)
        query, keyval, values, limits = call(
            project_kernel,
            [
                jax.ShapeDtypeStruct((stacked, hd), BF16),
                jax.ShapeDtypeStruct((rows, width), BF16),
                jax.ShapeDtypeStruct((rows, width), BF16),
                jax.ShapeDtypeStruct((2, 8, 128), F32),
            ],
            [VMEM] * 5 + [HBM] * 2,
            (
                own,
                beside,
                across,
                corner,
                gain,
                w_query,
                w_keyval,
            ),
            flops=2 * rows * features * (q_cols + width),
            mib=PROJECT_MIB,
            scratch=[
                pltpu.VMEM((rows, features), BF16),
                pltpu.VMEM(w_query.shape, BF16),
                pltpu.VMEM(w_keyval.shape, BF16),
                pltpu.SemaphoreType.DMA((2 * tp,)),
            ],
            name="project",
        )

    with jax.named_scope("extend"):
        sent = call(
            functools.partial(extend_kernel, share, block_rows),
            [jax.ShapeDtypeStruct((groups // 2, share, width), BF16)] * 2
            if phased
            else [jax.ShapeDtypeStruct((groups * share, width), BF16)],
            [SMEM] + [VMEM] * 2,
            (plan, keyval, arrived),
            flops=4 * groups * share * groups * share * width,
            name="extend",
        )
        *sent, c_across = lax.optimization_barrier((*sent, c_across))
        if phased:
            keep, got = sent[0], swap(sent[1], 1, "seq")
        cached = (ordered, c_beside, c_across, swap(c_across, 1))

    with jax.named_scope("early"):
        early = call(
            functools.partial(early_kernel, share, block_rows),
            [
                jax.ShapeDtypeStruct(((tp - 1) * piece_rows, width), BF16),
                jax.ShapeDtypeStruct((8, 128), F32),
            ],
            [SMEM] + [VMEM] * (tp - 1),
            (plan, *cached[:-1]),
            flops=1 << 30,
            mib=EARLY_MIB,
            name="early",
        )

    part = rows // CHUNKS
    tile_rows = ROW_TILE * (q_cols // hd)
    old = list(early)
    mixed = None
    for c in range(CHUNKS):
        last = c == CHUNKS - 1
        with jax.named_scope("attend"):
            of_part = jax.ShapeDtypeStruct((part, cols), BF16)
            of_all = jax.ShapeDtypeStruct((rows, cols), BF16)
            outs = [of_all, of_part, of_all, of_part]
            if not last:
                outs = [
                    of_part,
                    of_part,
                    jax.ShapeDtypeStruct((part, q_cols), BF16),
                    jax.ShapeDtypeStruct((piece_rows, width), BF16),
                    jax.ShapeDtypeStruct((8, 128), F32),
                ]
            seen = most_held + (c + 1) * part
            sums = list(call(
                functools.partial(attend_kernel, share, block_rows, c * part, part),
                outs,
                [SMEM] + [VMEM] * 8 + [HBM] + [VMEM] * len(old),
                (plan, query, keyval, values, limits, *cached, w_out, *old),
                flops=4 * part * seen * q_cols + 2 * part * q_cols * features,
                exps=part * seen * (q_cols // hd),
                mib=ATTEND_MIB,
                scratch=[
                    pltpu.VMEM((tile_rows, width), F32),
                    pltpu.VMEM((tile_rows, hd), F32),
                    pltpu.VMEM((part, q_cols), BF16),
                    pltpu.VMEM(w_out.shape, BF16),
                    pltpu.SemaphoreType.DMA,
                ],
                name="attend",
            ))
            if last:
                far0, far1, near0, near1 = sums
            else:
                far1, near1, before_rows, *rest = sums
                old += [*rest, before_rows]
        with jax.named_scope("reduce"):
            if last and phased:
                far1, got = lax.optimization_barrier((far1, got))
            got1 = swap(far1, 1)
            if c and last:
                before = hand_on(before)
                before, got1 = lax.optimization_barrier((before, got1))
            pair = (near1.astype(F32) + got1.astype(F32)).astype(BF16)
            if not last:
                query, pair = lax.optimization_barrier((query, pair))
            if last and phased:
                pair, got = lax.optimization_barrier((pair, got))
            crossed = swap(pair, 2)
            if not last:
                before = crossed

    with jax.named_scope("exchange"):
        if phased:
            pairs = list(call(
                pair_kernel,
                [jax.ShapeDtypeStruct((2, share, width), BF16)] * (groups // 2),
                [VMEM] * 2,
                (keep, got),
                flops=0,
                mib=8,
                name="pair",
            ))
            for k in range(len(pairs) - 1, 1, -1):
                pairs[k] = swap(pairs[k], 2 * k, "seq")
        else:
            new_cache = exchange(sent[0].reshape(groups, share, width))

    with jax.named_scope("finish"):
        got0 = swap(far0, 1)
        if phased:
            got0, pairs[1] = lax.optimization_barrier((got0, pairs[1]))
            pairs[1] = swap(pairs[1], 2, "seq")
        mixed = None
        for at, over in ((0, before), (part, crossed)):
            mixed = call(
                functools.partial(finish_kernel, at),
                jax.ShapeDtypeStruct((rows, cols), BF16),
                [SMEM] + [VMEM] * 4 + [HBM] * (at > 0),
                (plan, own, near0, got0, over, *([mixed] if at else [])),
                flops=4 * part * cols,
                scratch=[pltpu.VMEM((part, cols), BF16), pltpu.SemaphoreType.DMA((2,))],
                name="finish",
                into={5: 0} if at else {},
            )
        if phased:
            mixed, *pairs = lax.optimization_barrier((mixed, *pairs))
            new_cache = call(
                place_kernel,
                jax.ShapeDtypeStruct(old_cache.shape, BF16),
                [VMEM] * len(pairs),
                pairs,
                flops=0,
                mib=8,
                scratch=[pltpu.SemaphoreType.DMA((groups,))],
                name="place",
                into={},
            )
    return (mixed, new_cache)


def solution(mesh):
    in_specs = (
        P("seq", "tp"),
        P(),
        P(None, "tp"),
        P(),
        P("tp", None),
        P("seq"),
        P("seq"),
        P("seq", None),
        P("seq", None),
        P("seq", "tp", None),
    )
    out_specs = (P("seq", "tp"), P("seq", "tp", None))
    return jax.shard_map(body, mesh=mesh, in_specs=in_specs, out_specs=out_specs, check_vma=False)
```

```python
import functools
import math

import jax
import jax.numpy as jnp
from jax import lax
from jax.experimental import pallas as pl
from jax.experimental.pallas import tpu as pltpu
from jax.sharding import PartitionSpec as P

EPSILON = 1e-05
MASKED = -1e30
CHUNKS = 2
PART_ROWS = 256
ROW_TILE = 128
KEY_TILE = 128
NORM_ROWS = 128
MIB = 51
PROJECT_MIB = 50.375
LEAST = -3e38
ATTEND_MIB = 49
EARLY_MIB = 50
SAFE = 60.0
F32 = jnp.float32
BF16 = jnp.bfloat16

VMEM = pl.BlockSpec(memory_space=pltpu.VMEM)
SMEM = pl.BlockSpec(memory_space=pltpu.SMEM)
HBM = pl.BlockSpec(memory_space=pltpu.HBM)


def dot(a, b):
    return lax.dot_general(a, b, (((1,), (0,)), ((), ())), preferred_element_type=F32)


def dot_t(a, b):
    return lax.dot_general(a, b, (((1,), (1,)), ((), ())), preferred_element_type=F32)


def pair_kernel(keep_ref, got_ref, *pair_refs):
    for k, pair_ref in enumerate(pair_refs):
        pair_ref[0] = keep_ref[k]
        pair_ref[1] = got_ref[k]


def place_kernel(p0, p1, p2, p3, out_hbm, sems):
    me = lax.axis_index("seq")
    stores = []
    for k, pair_ref in enumerate((p0, p1, p2, p3)):
        for j in range(2):
            slot = out_hbm.at[me ^ (2 * k + j)]
            stores.append(pltpu.make_async_copy(pair_ref.at[j], slot, sems.at[len(stores)]))
            stores[-1].start()
    for store in stores:
        store.wait()


def order_kernel(share, plan_ref, arrived_ref, out_ref):
    rows, count = out_ref.shape[0], arrived_ref.shape[0]
    if share % 16 == 0:
        for b in range(rows // share):
            at = pl.ds(pl.multiple_of(plan_ref[2 + b] * share, share), share)
            out_ref[pl.ds(b * share, share), :] = arrived_ref[at, :]
        return
    row = lax.broadcasted_iota(jnp.int32, (rows, 128), 0)
    block = row // share
    holder = jnp.zeros_like(block)
    for b in range(rows // share):
        holder = jnp.where(block == b, plan_ref[2 + b], holder)
    index = (holder * share + row % share)[:, :1]
    column = lax.broadcasted_iota(jnp.int32, (rows, count), 1)
    pick = jnp.where(column == index, 1.0, 0.0).astype(BF16)
    out_ref[...] = dot(pick, arrived_ref[...]).astype(BF16)


def extend_kernel(share, block_rows, plan_ref, kv_ref, arrived_ref, *out_refs):
    rows = arrived_ref.shape[0]
    groups = rows // share
    held, span = plan_ref[0], plan_ref[1]
    me = lax.axis_index("seq") if len(out_refs) > 1 else 0
    row = lax.broadcasted_iota(jnp.int32, (rows, 128), 0)
    target = row // share
    block, holder = jnp.zeros_like(row), jnp.zeros_like(row)
    for b in range(groups):
        hit = target == plan_ref[2 + groups + b] ^ me
        block = jnp.where(hit, b, block)
        holder = jnp.where(hit, plan_ref[2 + b], holder)
    position = block * block_rows + lax.axis_index("tp") * share + row % share
    old_row = jnp.where(position < held, holder * share + row % share, -1)[:, :1]
    fresh = position - held
    new_row = jnp.where((fresh >= 0) & (fresh < span), fresh, -1)[:, :1]
    column = lax.broadcasted_iota(jnp.int32, (rows, rows), 1)
    total = dot(jnp.where(column == old_row, 1.0, 0.0).astype(BF16), arrived_ref[...])
    column = lax.broadcasted_iota(jnp.int32, (rows, kv_ref.shape[0]), 1)
    total += dot(jnp.where(column == new_row, 1.0, 0.0).astype(BF16), kv_ref[...])
    total = total.astype(BF16)
    if len(out_refs) == 1:
        out_refs[0][...] = total
        return
    for slot in range(groups):
        out_refs[slot % 2][slot // 2] = total[slot * share : (slot + 1) * share]


def project_kernel(
    x0,
    x1,
    x2,
    x3,
    gain_ref,
    wq_hbm,
    wkv_hbm,
    q_ref,
    kv_ref,
    values_ref,
    limits_ref,
    normed,
    wq_ref,
    wkv_ref,
    sems,
):
    pieces = (x0, x1, x2, x3)
    me = lax.axis_index("tp")
    rows, width = x0.shape
    features = width * len(pieces)
    hd = kv_ref.shape[1] // 2
    heads = wq_ref.shape[1] // hd
    loads = []
    for hbm, to in ((wkv_hbm, wkv_ref), (wq_hbm, wq_ref)):
        for j in range(len(pieces)):
            at = pl.ds(j * width, width)
            loads.append(pltpu.make_async_copy(hbm.at[at], to.at[at], sems.at[len(loads)]))
            loads[-1].start()

    for step in range(0, rows, NORM_ROWS):
        at = pl.ds(step, NORM_ROWS)
        values = [piece[at, :].astype(F32) for piece in pieces]
        average = jnp.sum(sum(values), axis=1, keepdims=True) / features
        centred = [v - average for v in values]
        spread = jnp.sum(sum(v * v for v in centred), axis=1, keepdims=True) / features
        scale = lax.rsqrt(spread + EPSILON)
        for j, v in enumerate(centred):
            owner = me ^ j
            to = pl.ds(pl.multiple_of(owner * width, width), width)
            normed[at, to] = (v * scale * gain_ref[owner]).astype(BF16)
    for load in loads[: len(pieces)]:
        load.wait()
    keyval = dot(normed[...], wkv_ref[...]).astype(BF16)
    kv_ref[...] = keyval
    values_ref[:, hd:] = keyval[:, hd:]
    values_ref[:, :hd] = jnp.ones((rows, hd), BF16)
    limits_ref[0] = longest(keyval[:, :hd])
    for load in loads[len(pieces) :]:
        load.wait()
    query = dot(normed[...], wq_ref[...]).astype(BF16)
    for start in range(0, rows, ROW_TILE):
        for h in range(heads):
            q_ref[pl.ds(start * heads + h * ROW_TILE, ROW_TILE), :] = query[
                start : start + ROW_TILE, h * hd : (h + 1) * hd
            ]
    limits_ref[1] = longest(q_ref[...])


def longest(x):
    squares = dot(x * x, jnp.ones((x.shape[1], 128), BF16))
    return jnp.max(squares.reshape(-1, 8, 128), axis=0)


def lay_out(share, block_rows, held, owners, pieces, out_ref):
    piece_rows, width = pieces[0].shape
    hd = width // 2
    group = KEY_TILE * lax.axis_size("tp")
    tiles = (held + group - 1) // group
    row = lax.broadcasted_iota(jnp.int32, (KEY_TILE, hd), 0)
    place = row // share * block_rows + row % share

    def lay(i, whole):
        source = pl.ds(i * KEY_TILE, KEY_TILE)
        for j, (owner, piece) in enumerate(zip(owners, pieces)):
            at = pl.ds((i * len(pieces) + j) * KEY_TILE, KEY_TILE)
            if whole:
                out_ref[at, hd:] = piece[source, hd:]
                out_ref[at, :hd] = jnp.ones((KEY_TILE, hd), BF16)
                continue
            used = place + owner * share + i * group < held
            out_ref[at, hd:] = jnp.where(used, piece[source, hd:].astype(F32), 0.0).astype(BF16)
            out_ref[at, :hd] = jnp.where(used, 1.0, 0.0).astype(BF16)

    for i in range(piece_rows // KEY_TILE):
        pl.when(i < tiles - 1)(functools.partial(lay, i, True))
        pl.when(i == tiles - 1)(functools.partial(lay, i, False))


def early_kernel(share, block_rows, plan_ref, *refs):
    pieces, (out_ref, limit_ref) = refs[:-2], refs[-2:]
    me = lax.axis_index("tp")
    owners = [me ^ j for j in range(len(pieces))]
    lay_out(share, block_rows, plan_ref[0], owners, pieces, out_ref)
    limit_ref[...] = functools.reduce(
        jnp.maximum, [longest(piece[:, : piece.shape[1] // 2]) for piece in pieces]
    )


def attend_kernel(share, block_rows, start_row, rows, plan_ref, q_ref, kv_ref, new_ref, *refs):
    limits_ref, pieces, wout_hbm = refs[0], refs[1:5], refs[5]
    total, high, context, wout, sem = refs[-5:]
    most_ref, most_limit_ref = refs[6:8]
    if start_row:
        rest_ref, rest_limit_ref, before_ref, far0_ref, far1_ref, near0_ref, near1_ref = refs[8:15]
    else:
        far1_ref, near1_ref, context_out, rest_ref, rest_limit_ref = refs[8:13]
    me = lax.axis_index("tp")
    held, span = plan_ref[0], plan_ref[1]
    piece_rows, width = pieces[0].shape
    hd = width // 2
    heads = q_ref.shape[0] // kv_ref.shape[0]
    load = pltpu.make_async_copy(wout_hbm, wout, sem)
    load.start()

    group = KEY_TILE * len(pieces)
    most = piece_rows // KEY_TILE
    tiles = (held + group - 1) // group
    if not start_row:
        corner = len(pieces) - 1
        lay_out(share, block_rows, held, [me ^ corner], pieces[corner:], rest_ref)
        rest_limit_ref[...] = longest(pieces[corner][:, :hd])

    factor = hd ** (-0.5) * math.log2(math.e)
    old_limit = jnp.maximum(most_limit_ref[...], rest_limit_ref[...])
    key_limit = jnp.max(jnp.maximum(old_limit, limits_ref[0]))
    small = key_limit * jnp.max(limits_ref[1]) * (1.05 / hd) < SAFE * SAFE

    tile_rows = ROW_TILE * heads

    def queries(t):
        return q_ref[pl.ds(start_row * heads + t * tile_rows, tile_rows), :]

    def old_keys(i):
        source = pl.ds(i * KEY_TILE, KEY_TILE)
        return jnp.concatenate([piece[source, :hd] for piece in pieces], axis=0)

    def old_values(i):
        parts = []
        for ref, count in ((most_ref, len(pieces) - 1), (rest_ref, 1)):
            size = count * KEY_TILE
            at = i * size if isinstance(i, int) else pl.multiple_of(i * size, KEY_TILE)
            parts.append(ref[pl.ds(at, size), :])
        return jnp.concatenate(parts, axis=0)

    def new_scores(t):
        known = start_row + t * ROW_TILE
        scores = dot_t(queries(t), kv_ref[pl.ds(0, known + ROW_TILE), :hd])
        to = lax.broadcasted_iota(jnp.int32, (tile_rows, ROW_TILE), 0) % ROW_TILE
        by = lax.broadcasted_iota(jnp.int32, (tile_rows, ROW_TILE), 1)
        last = jnp.where(by <= to, scores[:, known:], MASKED)
        return jnp.concatenate([scores[:, :known], last], axis=1) if known else last

    def new_values(t):
        return new_ref[pl.ds(0, start_row + (t + 1) * ROW_TILE), :]

    def put(t, both):
        sums = both[:, :hd]
        inverse = pl.reciprocal(sums, approx=True)
        inverse = inverse * (2.0 - sums * inverse)
        out = (both[:, hd:] * inverse).astype(BF16)
        for h in range(heads):
            context[pl.ds(t * ROW_TILE, ROW_TILE), h * hd : (h + 1) * hd] = out[
                h * ROW_TILE : (h + 1) * ROW_TILE
            ]

    def fast(used, begin):
        first = begin // ROW_TILE
        tiles_of = range(first, min(begin + PART_ROWS, rows) // ROW_TILE)
        at_all = pl.ds((start_row + begin) * heads, len(tiles_of) * tile_rows)
        steps = [(None, i) for i in range(used)] + [(t, used) for t in tiles_of]

        def score(t, i):
            return new_scores(t) if i == used else dot_t(q_ref[at_all, :], old_keys(i))

        ahead, both = score(*steps[0]), None
        for at, (t, i) in enumerate(steps):
            scores = ahead
            if at + 1 < len(steps):
                ahead = score(*steps[at + 1])
            weights = jnp.exp2(scores * factor).astype(BF16)
            if i < used:
                part = dot(weights, old_values(i))
                both = part if i == 0 else both + part
            else:
                here = (t - first) * tile_rows
                put(t, both[here : here + tile_rows] + dot(weights, new_values(t)))

    def exact(t):
        column = lax.broadcasted_iota(jnp.int32, (tile_rows, group), 1)
        within = column % KEY_TILE
        owner = me ^ (column // KEY_TILE)
        place = within // share * block_rows + within % share + owner * share

        def old_scores(i):
            scores = dot_t(queries(t), old_keys(pl.multiple_of(i, 1)))
            return jnp.where(place + i * group < held, scores, MASKED)

        def raise_high(i, carry):
            top = jnp.max(old_scores(i), axis=1, keepdims=True)
            high[...] = jnp.maximum(high[...], top)
            return carry

        def add(i, carry):
            weights = jnp.exp2((old_scores(i) - high[:, :1]) * factor).astype(BF16)
            total[...] += dot(weights, old_values(i))
            return carry

        high[...] = jnp.zeros_like(high) + jnp.max(new_scores(t), axis=1, keepdims=True)
        lax.fori_loop(0, tiles, raise_high, 0)
        weights = jnp.exp2((new_scores(t) - high[:, :1]) * factor).astype(BF16)
        total[...] = dot(weights, new_values(t))
        lax.fori_loop(0, tiles, add, 0)
        put(t, total[...])

    for begin in range(0, rows, PART_ROWS):
        busy = start_row + begin < span
        for used in range(1, most + 1):
            pl.when(busy & small & (tiles == used))(functools.partial(fast, used, begin))

        @pl.when(busy & jnp.logical_not(small))
        def _():
            for t in range(begin // ROW_TILE, min(begin + PART_ROWS, rows) // ROW_TILE):
                exact(t)

        @pl.when(jnp.logical_not(busy))
        def _():
            context[pl.ds(begin, PART_ROWS), :] = jnp.zeros((PART_ROWS, context.shape[1]), BF16)

    load.wait()
    cols = wout.shape[1] // 4

    def partial_sums(rows_of, k):
        columns = pl.ds(pl.multiple_of((me ^ k) * cols, cols), cols)
        return dot(rows_of[...], wout[:, columns]).astype(BF16)

    far1_ref[...] = partial_sums(context, 3)
    near1_ref[...] = partial_sums(context, 2)
    if not start_row:
        context_out[...] = context[...]
        return
    for at, rows_of in ((0, before_ref), (start_row, context)):
        far0_ref[pl.ds(at, rows), :] = partial_sums(rows_of, 1)
        near0_ref[pl.ds(at, rows), :] = partial_sums(rows_of, 0)


def hand_on_kernel(in_ref, out_ref):
    pass


def finish_kernel(at, plan_ref, tokens_ref, near_ref, got_ref, crossed_ref, *refs):
    out_hbm, done, sems = refs[-3:]
    rows = crossed_ref.shape[0]
    half = rows // 2
    stores = []
    for i in range(2):
        here = pl.ds(i * half, half)
        there = pl.ds(at + i * half, half)
        kept = near_ref[there, :].astype(F32) + got_ref[there, :].astype(F32)
        total = tokens_ref[there, :].astype(F32) + (kept + crossed_ref[here, :].astype(F32))
        row = lax.broadcasted_iota(jnp.int32, total.shape, 0) + (at + i * half)
        done[here, :] = jnp.where(row < plan_ref[1], total, 0.0).astype(BF16)
        stores.append(pltpu.make_async_copy(done.at[here], out_hbm.at[there], sems.at[i]))
        stores[-1].start()
    for store in stores:
        store.wait()


def call(
    kernel, out_shape, in_specs, args, flops, mib=MIB, scratch=(), exps=0, name=None, into=None
):
    outs = out_shape if isinstance(out_shape, (list, tuple)) else [out_shape]
    moved = sum(a.size * a.dtype.itemsize for a in list(args) + list(outs))
    return pl.pallas_call(
        kernel,
        out_shape=out_shape,
        in_specs=in_specs,
        out_specs=jax.tree.map(lambda _: VMEM if into is None else HBM, out_shape),
        input_output_aliases=into or {},
        scratch_shapes=list(scratch),
        cost_estimate=pl.CostEstimate(flops=flops, bytes_accessed=moved, transcendentals=exps),
        compiler_params=pltpu.CompilerParams(vmem_limit_bytes=int(mib * 1024 * 1024)),
        name=name,
    )(*args)


def hand_on(x):
    return pl.pallas_call(
        hand_on_kernel,
        out_shape=jax.ShapeDtypeStruct(x.shape, x.dtype),
        in_specs=[pl.BlockSpec(memory_space=pl.ANY)],
        out_specs=pl.BlockSpec(memory_space=pl.ANY),
        input_output_aliases={0: 0},
        cost_estimate=pl.CostEstimate(flops=1 << 34, bytes_accessed=1024, transcendentals=0),
        compiler_params=pltpu.CompilerParams(vmem_limit_bytes=1 << 20),
        name="hand_on",
    )(x)


def body(
    tokens,
    norm_gain,
    w_query,
    w_keyval,
    w_out,
    span_lens,
    cached_lens,
    old_table,
    new_table,
    old_cache,
):
    tp = lax.axis_size("tp")
    groups, share, width = old_cache.shape
    block_rows = share * tp
    capacity = groups * block_rows
    rows, cols = tokens.shape
    q_cols = w_query.shape[1]
    features = w_query.shape[0]
    hd = width // 2
    most_held = capacity - rows
    piece_rows = most_held // tp

    def swap(x, bit, axis="tp"):
        size = lax.axis_size(axis)
        return lax.ppermute(x, axis, [(i, i ^ bit) for i in range(size)])

    def exchange(x):
        return lax.all_to_all(x, "seq", split_axis=0, concat_axis=0, tiled=True)

    phased = groups == 8

    with jax.named_scope("tokens_gather"):
        across = swap(tokens, 2)
        beside = swap(tokens, 1)

    with jax.named_scope("cache_gather"):
        gain = jnp.maximum(norm_gain, LEAST).reshape(tp, 1, cols)
        gain, stored = lax.optimization_barrier((gain, old_cache))
        arrived = exchange(stored).reshape(groups * share, width)
        own = jnp.maximum(tokens, jnp.asarray(LEAST, BF16))
        across, *lens = lax.optimization_barrier(
            (across, cached_lens, span_lens, old_table[0], new_table[0])
        )
        plan = jnp.concatenate(lens)
        arrived, across, own, plan = lax.optimization_barrier((arrived, across, own, plan))
        ordered = call(
            functools.partial(order_kernel, share),
            jax.ShapeDtypeStruct((piece_rows, width), BF16),
            [SMEM, VMEM],
            (plan, arrived),
            flops=2 * piece_rows * groups * share * width,
            name="order",
        )
        c_across = swap(ordered, 2)
        c_beside = swap(ordered, 1)

    with jax.named_scope("project"):
        corner = swap(across, 1)
        stacked = rows * (q_cols // hd)
        query, keyval, values, limits = call(
            project_kernel,
            [
                jax.ShapeDtypeStruct((stacked, hd), BF16),
                jax.ShapeDtypeStruct((rows, width), BF16),
                jax.ShapeDtypeStruct((rows, width), BF16),
                jax.ShapeDtypeStruct((2, 8, 128), F32),
            ],
            [VMEM] * 5 + [HBM] * 2,
            (
                own,
                beside,
                across,
                corner,
                gain,
                w_query,
                w_keyval,
            ),
            flops=2 * rows * features * (q_cols + width),
            mib=PROJECT_MIB,
            scratch=[
                pltpu.VMEM((rows, features), BF16),
                pltpu.VMEM(w_query.shape, BF16),
                pltpu.VMEM(w_keyval.shape, BF16),
                pltpu.SemaphoreType.DMA((2 * tp,)),
            ],
            name="project",
        )

    with jax.named_scope("extend"):
        sent = call(
            functools.partial(extend_kernel, share, block_rows),
            [jax.ShapeDtypeStruct((groups // 2, share, width), BF16)] * 2
            if phased
            else [jax.ShapeDtypeStruct((groups * share, width), BF16)],
            [SMEM] + [VMEM] * 2,
            (plan, keyval, arrived),
            flops=4 * groups * share * groups * share * width,
            name="extend",
        )
        *sent, c_across = lax.optimization_barrier((*sent, c_across))
        if phased:
            keep, got = sent[0], swap(sent[1], 1, "seq")
        cached = (ordered, c_beside, c_across, swap(c_across, 1))

    with jax.named_scope("early"):
        early = call(
            functools.partial(early_kernel, share, block_rows),
            [
                jax.ShapeDtypeStruct(((tp - 1) * piece_rows, width), BF16),
                jax.ShapeDtypeStruct((8, 128), F32),
            ],
            [SMEM] + [VMEM] * (tp - 1),
            (plan, *cached[:-1]),
            flops=1 << 30,
            mib=EARLY_MIB,
            name="early",
        )

    part = rows // CHUNKS
    tile_rows = ROW_TILE * (q_cols // hd)
    old = list(early)
    mixed = None
    for c in range(CHUNKS):
        last = c == CHUNKS - 1
        with jax.named_scope("attend"):
            of_part = jax.ShapeDtypeStruct((part, cols), BF16)
            of_all = jax.ShapeDtypeStruct((rows, cols), BF16)
            outs = [of_all, of_part, of_all, of_part]
            if not last:
                outs = [
                    of_part,
                    of_part,
                    jax.ShapeDtypeStruct((part, q_cols), BF16),
                    jax.ShapeDtypeStruct((piece_rows, width), BF16),
                    jax.ShapeDtypeStruct((8, 128), F32),
                ]
            seen = most_held + (c + 1) * part
            sums = list(call(
                functools.partial(attend_kernel, share, block_rows, c * part, part),
                outs,
                [SMEM] + [VMEM] * 8 + [HBM] + [VMEM] * len(old),
                (plan, query, keyval, values, limits, *cached, w_out, *old),
                flops=4 * part * seen * q_cols + 2 * part * q_cols * features,
                exps=part * seen * (q_cols // hd),
                mib=ATTEND_MIB,
                scratch=[
                    pltpu.VMEM((tile_rows, width), F32),
                    pltpu.VMEM((tile_rows, hd), F32),
                    pltpu.VMEM((part, q_cols), BF16),
                    pltpu.VMEM(w_out.shape, BF16),
                    pltpu.SemaphoreType.DMA,
                ],
                name="attend",
            ))
            if last:
                far0, far1, near0, near1 = sums
            else:
                far1, near1, before_rows, *rest = sums
                old += [*rest, before_rows]
        with jax.named_scope("reduce"):
            if last and phased:
                far1, got = lax.optimization_barrier((far1, got))
            got1 = swap(far1, 1)
            if c and last:
                before = hand_on(before)
                before, got1 = lax.optimization_barrier((before, got1))
            pair = (near1.astype(F32) + got1.astype(F32)).astype(BF16)
            if not last:
                query, pair = lax.optimization_barrier((query, pair))
            if last and phased:
                pair, got = lax.optimization_barrier((pair, got))
            crossed = swap(pair, 2)
            if not last:
                before = crossed

    with jax.named_scope("exchange"):
        if phased:
            pairs = list(call(
                pair_kernel,
                [jax.ShapeDtypeStruct((2, share, width), BF16)] * (groups // 2),
                [VMEM] * 2,
                (keep, got),
                flops=0,
                mib=8,
                name="pair",
            ))
            for k in range(len(pairs) - 1, 1, -1):
                pairs[k] = swap(pairs[k], 2 * k, "seq")
        else:
            new_cache = exchange(sent[0].reshape(groups, share, width))

    with jax.named_scope("finish"):
        got0 = swap(far0, 1)
        if phased:
            got0, pairs[1] = lax.optimization_barrier((got0, pairs[1]))
            pairs[1] = swap(pairs[1], 2, "seq")
        mixed = None
        for at, over in ((0, before), (part, crossed)):
            mixed = call(
                functools.partial(finish_kernel, at),
                jax.ShapeDtypeStruct((rows, cols), BF16),
                [SMEM] + [VMEM] * 4 + [HBM] * (at > 0),
                (plan, own, near0, got0, over, *([mixed] if at else [])),
                flops=4 * part * cols,
                scratch=[pltpu.VMEM((part, cols), BF16), pltpu.SemaphoreType.DMA((2,))],
                name="finish",
                into={5: 0} if at else {},
            )
        if phased:
            mixed, *pairs = lax.optimization_barrier((mixed, *pairs))
            new_cache = call(
                place_kernel,
                jax.ShapeDtypeStruct(old_cache.shape, BF16),
                [VMEM] * len(pairs),
                pairs,
                flops=0,
                mib=8,
                scratch=[pltpu.SemaphoreType.DMA((groups,))],
                name="place",
                into={},
            )
    return (mixed, new_cache)


def solution(mesh):
    in_specs = (
        P("seq", "tp"),
        P(),
        P(None, "tp"),
        P(),
        P("tp", None),
        P("seq"),
        P("seq"),
        P("seq", None),
        P("seq", None),
        P("seq", "tp", None),
    )
    out_specs = (P("seq", "tp"), P("seq", "tp", None))
    return jax.shard_map(body, mesh=mesh, in_specs=in_specs, out_specs=out_specs, check_vma=False)
```

```python
import functools
import math

import jax
import jax.numpy as jnp
from jax import lax
from jax.experimental import pallas as pl
from jax.experimental.pallas import tpu as pltpu
from jax.sharding import PartitionSpec as P

EPSILON = 1e-05
MASKED = -1e30
CHUNKS = 2
PART_ROWS = 256
ROW_TILE = 128
KEY_TILE = 128
NORM_ROWS = 128
MIB = 51
PROJECT_MIB = 50.375
LEAST = -3e38
ATTEND_MIB = 49
EARLY_MIB = 50
SAFE = 60.0
F32 = jnp.float32
BF16 = jnp.bfloat16

VMEM = pl.BlockSpec(memory_space=pltpu.VMEM)
SMEM = pl.BlockSpec(memory_space=pltpu.SMEM)
HBM = pl.BlockSpec(memory_space=pltpu.HBM)


def dot(a, b):
    return lax.dot_general(a, b, (((1,), (0,)), ((), ())), preferred_element_type=F32)


def dot_t(a, b):
    return lax.dot_general(a, b, (((1,), (1,)), ((), ())), preferred_element_type=F32)


def pair_kernel(keep_ref, got_ref, *pair_refs):
    for k, pair_ref in enumerate(pair_refs):
        pair_ref[0] = keep_ref[k]
        pair_ref[1] = got_ref[k]


def place_kernel(p0, p1, p2, p3, out_hbm, sems):
    me = lax.axis_index("seq")
    stores = []
    for k, pair_ref in enumerate((p0, p1, p2, p3)):
        for j in range(2):
            slot = out_hbm.at[me ^ (2 * k + j)]
            stores.append(pltpu.make_async_copy(pair_ref.at[j], slot, sems.at[len(stores)]))
            stores[-1].start()
    for store in stores:
        store.wait()


def order_kernel(share, plan_ref, arrived_ref, out_ref):
    rows, count = out_ref.shape[0], arrived_ref.shape[0]
    if share % 16 == 0:
        for b in range(rows // share):
            at = pl.ds(pl.multiple_of(plan_ref[2 + b] * share, share), share)
            out_ref[pl.ds(b * share, share), :] = arrived_ref[at, :]
        return
    row = lax.broadcasted_iota(jnp.int32, (rows, 128), 0)
    block = row // share
    holder = jnp.zeros_like(block)
    for b in range(rows // share):
        holder = jnp.where(block == b, plan_ref[2 + b], holder)
    index = (holder * share + row % share)[:, :1]
    column = lax.broadcasted_iota(jnp.int32, (rows, count), 1)
    pick = jnp.where(column == index, 1.0, 0.0).astype(BF16)
    out_ref[...] = dot(pick, arrived_ref[...]).astype(BF16)


def extend_kernel(share, block_rows, plan_ref, kv_ref, arrived_ref, *out_refs):
    rows = arrived_ref.shape[0]
    groups = rows // share
    held, span = plan_ref[0], plan_ref[1]
    me = lax.axis_index("seq") if len(out_refs) > 1 else 0
    row = lax.broadcasted_iota(jnp.int32, (rows, 128), 0)
    target = row // share
    block, holder = jnp.zeros_like(row), jnp.zeros_like(row)
    for b in range(groups):
        hit = target == plan_ref[2 + groups + b] ^ me
        block = jnp.where(hit, b, block)
        holder = jnp.where(hit, plan_ref[2 + b], holder)
    position = block * block_rows + lax.axis_index("tp") * share + row % share
    old_row = jnp.where(position < held, holder * share + row % share, -1)[:, :1]
    fresh = position - held
    new_row = jnp.where((fresh >= 0) & (fresh < span), fresh, -1)[:, :1]
    column = lax.broadcasted_iota(jnp.int32, (rows, rows), 1)
    total = dot(jnp.where(column == old_row, 1.0, 0.0).astype(BF16), arrived_ref[...])
    column = lax.broadcasted_iota(jnp.int32, (rows, kv_ref.shape[0]), 1)
    total += dot(jnp.where(column == new_row, 1.0, 0.0).astype(BF16), kv_ref[...])
    total = total.astype(BF16)
    if len(out_refs) == 1:
        out_refs[0][...] = total
        return
    for slot in range(groups):
        out_refs[slot % 2][slot // 2] = total[slot * share : (slot + 1) * share]


def project_kernel(
    x0,
    x1,
    x2,
    x3,
    gain_ref,
    wq_hbm,
    wkv_hbm,
    q_ref,
    kv_ref,
    values_ref,
    limits_ref,
    normed,
    wq_ref,
    wkv_ref,
    sems,
):
    pieces = (x0, x1, x2, x3)
    me = lax.axis_index("tp")
    rows, width = x0.shape
    features = width * len(pieces)
    hd = kv_ref.shape[1] // 2
    heads = wq_ref.shape[1] // hd
    loads = []
    for hbm, to in ((wkv_hbm, wkv_ref), (wq_hbm, wq_ref)):
        for j in range(len(pieces)):
            at = pl.ds(j * width, width)
            loads.append(pltpu.make_async_copy(hbm.at[at], to.at[at], sems.at[len(loads)]))
            loads[-1].start()

    for step in range(0, rows, NORM_ROWS):
        at = pl.ds(step, NORM_ROWS)
        values = [piece[at, :].astype(F32) for piece in pieces]
        average = jnp.sum(sum(values), axis=1, keepdims=True) / features
        centred = [v - average for v in values]
        spread = jnp.sum(sum(v * v for v in centred), axis=1, keepdims=True) / features
        scale = lax.rsqrt(spread + EPSILON)
        for j, v in enumerate(centred):
            owner = me ^ j
            to = pl.ds(pl.multiple_of(owner * width, width), width)
            normed[at, to] = (v * scale * gain_ref[owner]).astype(BF16)
    for load in loads[: len(pieces)]:
        load.wait()
    keyval = dot(normed[...], wkv_ref[...]).astype(BF16)
    kv_ref[...] = keyval
    values_ref[:, hd:] = keyval[:, hd:]
    values_ref[:, :hd] = jnp.ones((rows, hd), BF16)
    limits_ref[0] = longest(keyval[:, :hd])
    for load in loads[len(pieces) :]:
        load.wait()
    query = dot(normed[...], wq_ref[...]).astype(BF16)
    for start in range(0, rows, ROW_TILE):
        for h in range(heads):
            q_ref[pl.ds(start * heads + h * ROW_TILE, ROW_TILE), :] = query[
                start : start + ROW_TILE, h * hd : (h + 1) * hd
            ]
    limits_ref[1] = longest(q_ref[...])


def longest(x):
    squares = dot(x * x, jnp.ones((x.shape[1], 128), BF16))
    return jnp.max(squares.reshape(-1, 8, 128), axis=0)


def lay_out(share, block_rows, held, owners, pieces, out_ref):
    piece_rows, width = pieces[0].shape
    hd = width // 2
    group = KEY_TILE * lax.axis_size("tp")
    tiles = (held + group - 1) // group
    row = lax.broadcasted_iota(jnp.int32, (KEY_TILE, hd), 0)
    place = row // share * block_rows + row % share

    def lay(i, whole):
        source = pl.ds(i * KEY_TILE, KEY_TILE)
        for j, (owner, piece) in enumerate(zip(owners, pieces)):
            at = pl.ds((i * len(pieces) + j) * KEY_TILE, KEY_TILE)
            if whole:
                out_ref[at, hd:] = piece[source, hd:]
                out_ref[at, :hd] = jnp.ones((KEY_TILE, hd), BF16)
                continue
            used = place + owner * share + i * group < held
            out_ref[at, hd:] = jnp.where(used, piece[source, hd:].astype(F32), 0.0).astype(BF16)
            out_ref[at, :hd] = jnp.where(used, 1.0, 0.0).astype(BF16)

    for i in range(piece_rows // KEY_TILE):
        pl.when(i < tiles - 1)(functools.partial(lay, i, True))
        pl.when(i == tiles - 1)(functools.partial(lay, i, False))


def early_kernel(share, block_rows, plan_ref, *refs):
    pieces, (out_ref, limit_ref) = refs[:-2], refs[-2:]
    me = lax.axis_index("tp")
    owners = [me ^ j for j in range(len(pieces))]
    lay_out(share, block_rows, plan_ref[0], owners, pieces, out_ref)
    limit_ref[...] = functools.reduce(
        jnp.maximum, [longest(piece[:, : piece.shape[1] // 2]) for piece in pieces]
    )


def attend_kernel(share, block_rows, start_row, rows, plan_ref, q_ref, kv_ref, new_ref, *refs):
    limits_ref, pieces, wout_hbm = refs[0], refs[1:5], refs[5]
    total, high, context, wout, sem = refs[-5:]
    most_ref, most_limit_ref = refs[6:8]
    if start_row:
        rest_ref, rest_limit_ref, before_ref, far0_ref, far1_ref, near0_ref, near1_ref = refs[8:15]
    else:
        far1_ref, near1_ref, context_out, rest_ref, rest_limit_ref = refs[8:13]
    me = lax.axis_index("tp")
    held, span = plan_ref[0], plan_ref[1]
    piece_rows, width = pieces[0].shape
    hd = width // 2
    heads = q_ref.shape[0] // kv_ref.shape[0]
    load = pltpu.make_async_copy(wout_hbm, wout, sem)
    load.start()

    group = KEY_TILE * len(pieces)
    most = piece_rows // KEY_TILE
    tiles = (held + group - 1) // group
    if not start_row:
        corner = len(pieces) - 1
        lay_out(share, block_rows, held, [me ^ corner], pieces[corner:], rest_ref)
        rest_limit_ref[...] = longest(pieces[corner][:, :hd])

    factor = hd ** (-0.5) * math.log2(math.e)
    old_limit = jnp.maximum(most_limit_ref[...], rest_limit_ref[...])
    key_limit = jnp.max(jnp.maximum(old_limit, limits_ref[0]))
    small = key_limit * jnp.max(limits_ref[1]) * (1.05 / hd) < SAFE * SAFE

    tile_rows = ROW_TILE * heads

    def queries(t, first=0, count=heads):
        at = start_row * heads + t * tile_rows + first * ROW_TILE
        return q_ref[pl.ds(at, count * ROW_TILE), :]

    def old_keys(i):
        source = pl.ds(i * KEY_TILE, KEY_TILE)
        return jnp.concatenate([piece[source, :hd] for piece in pieces], axis=0)

    def old_values(i):
        parts = []
        for ref, count in ((most_ref, len(pieces) - 1), (rest_ref, 1)):
            size = count * KEY_TILE
            at = i * size if isinstance(i, int) else pl.multiple_of(i * size, KEY_TILE)
            parts.append(ref[pl.ds(at, size), :])
        return jnp.concatenate(parts, axis=0)

    def new_scores(t, first=0, count=heads):
        known = start_row + t * ROW_TILE
        scores = dot_t(queries(t, first, count), kv_ref[pl.ds(0, known + ROW_TILE), :hd])
        to = lax.broadcasted_iota(jnp.int32, (count * ROW_TILE, ROW_TILE), 0) % ROW_TILE
        by = lax.broadcasted_iota(jnp.int32, (count * ROW_TILE, ROW_TILE), 1)
        last = jnp.where(by <= to, scores[:, known:], MASKED)
        return jnp.concatenate([scores[:, :known], last], axis=1) if known else last

    def new_values(t):
        return new_ref[pl.ds(0, start_row + (t + 1) * ROW_TILE), :]

    def put(t, both, first=0, count=heads):
        sums = both[:, :hd]
        inverse = pl.reciprocal(sums, approx=True)
        inverse = inverse * (2.0 - sums * inverse)
        out = (both[:, hd:] * inverse).astype(BF16)
        for h in range(count):
            to = slice((first + h) * hd, (first + h + 1) * hd)
            context[pl.ds(t * ROW_TILE, ROW_TILE), to] = out[h * ROW_TILE : (h + 1) * ROW_TILE]

    def fast(used, begin):
        row_tiles = range(begin // ROW_TILE, min(begin + PART_ROWS, rows) // ROW_TILE)
        count = max(heads // 2, 1)
        groups = range(0, heads, count)
        steps = [(t, g, i) for t in row_tiles for g in groups for i in range(used + 1)]

        def score(t, g, i):
            if i == used:
                return new_scores(t, g, count)
            return dot_t(queries(t, g, count), old_keys(i))

        ahead, both = score(*steps[0]), None
        for at, (t, g, i) in enumerate(steps):
            scores = ahead
            if at + 1 < len(steps):
                ahead = score(*steps[at + 1])
            weights = jnp.exp2(scores * factor).astype(BF16)
            values = new_values(t) if i == used else old_values(i)
            part = dot(weights, values)
            both = part if i == 0 else both + part
            if i == used:
                put(t, both, g, count)

    def exact(t):
        column = lax.broadcasted_iota(jnp.int32, (tile_rows, group), 1)
        within = column % KEY_TILE
        owner = me ^ (column // KEY_TILE)
        place = within // share * block_rows + within % share + owner * share

        def old_scores(i):
            scores = dot_t(queries(t), old_keys(pl.multiple_of(i, 1)))
            return jnp.where(place + i * group < held, scores, MASKED)

        def raise_high(i, carry):
            top = jnp.max(old_scores(i), axis=1, keepdims=True)
            high[...] = jnp.maximum(high[...], top)
            return carry

        def add(i, carry):
            weights = jnp.exp2((old_scores(i) - high[:, :1]) * factor).astype(BF16)
            total[...] += dot(weights, old_values(i))
            return carry

        high[...] = jnp.zeros_like(high) + jnp.max(new_scores(t), axis=1, keepdims=True)
        lax.fori_loop(0, tiles, raise_high, 0)
        weights = jnp.exp2((new_scores(t) - high[:, :1]) * factor).astype(BF16)
        total[...] = dot(weights, new_values(t))
        lax.fori_loop(0, tiles, add, 0)
        put(t, total[...])

    for begin in range(0, rows, PART_ROWS):
        busy = start_row + begin < span
        for used in range(1, most + 1):
            pl.when(busy & small & (tiles == used))(functools.partial(fast, used, begin))

        @pl.when(busy & jnp.logical_not(small))
        def _():
            for t in range(begin // ROW_TILE, min(begin + PART_ROWS, rows) // ROW_TILE):
                exact(t)

        @pl.when(jnp.logical_not(busy))
        def _():
            context[pl.ds(begin, PART_ROWS), :] = jnp.zeros((PART_ROWS, context.shape[1]), BF16)

    load.wait()
    cols = wout.shape[1] // 4

    def partial_sums(rows_of, k):
        columns = pl.ds(pl.multiple_of((me ^ k) * cols, cols), cols)
        return dot(rows_of[...], wout[:, columns]).astype(BF16)

    far1_ref[...] = partial_sums(context, 3)
    near1_ref[...] = partial_sums(context, 2)
    if not start_row:
        context_out[...] = context[...]
        return
    for at, rows_of in ((0, before_ref), (start_row, context)):
        far0_ref[pl.ds(at, rows), :] = partial_sums(rows_of, 1)
        near0_ref[pl.ds(at, rows), :] = partial_sums(rows_of, 0)


def hand_on_kernel(in_ref, out_ref):
    pass


def finish_kernel(at, plan_ref, tokens_ref, near_ref, got_ref, crossed_ref, *refs):
    out_hbm, done, sems = refs[-3:]
    rows = crossed_ref.shape[0]
    half = rows // 2
    stores = []
    for i in range(2):
        here = pl.ds(i * half, half)
        there = pl.ds(at + i * half, half)
        kept = near_ref[there, :].astype(F32) + got_ref[there, :].astype(F32)
        total = tokens_ref[there, :].astype(F32) + (kept + crossed_ref[here, :].astype(F32))
        row = lax.broadcasted_iota(jnp.int32, total.shape, 0) + (at + i * half)
        done[here, :] = jnp.where(row < plan_ref[1], total, 0.0).astype(BF16)
        stores.append(pltpu.make_async_copy(done.at[here], out_hbm.at[there], sems.at[i]))
        stores[-1].start()
    for store in stores:
        store.wait()


def call(
    kernel, out_shape, in_specs, args, flops, mib=MIB, scratch=(), exps=0, name=None, into=None
):
    outs = out_shape if isinstance(out_shape, (list, tuple)) else [out_shape]
    moved = sum(a.size * a.dtype.itemsize for a in list(args) + list(outs))
    return pl.pallas_call(
        kernel,
        out_shape=out_shape,
        in_specs=in_specs,
        out_specs=jax.tree.map(lambda _: VMEM if into is None else HBM, out_shape),
        input_output_aliases=into or {},
        scratch_shapes=list(scratch),
        cost_estimate=pl.CostEstimate(flops=flops, bytes_accessed=moved, transcendentals=exps),
        compiler_params=pltpu.CompilerParams(vmem_limit_bytes=int(mib * 1024 * 1024)),
        name=name,
    )(*args)


def hand_on(x):
    return pl.pallas_call(
        hand_on_kernel,
        out_shape=jax.ShapeDtypeStruct(x.shape, x.dtype),
        in_specs=[pl.BlockSpec(memory_space=pl.ANY)],
        out_specs=pl.BlockSpec(memory_space=pl.ANY),
        input_output_aliases={0: 0},
        cost_estimate=pl.CostEstimate(flops=1 << 34, bytes_accessed=1024, transcendentals=0),
        compiler_params=pltpu.CompilerParams(vmem_limit_bytes=1 << 20),
        name="hand_on",
    )(x)


def body(
    tokens,
    norm_gain,
    w_query,
    w_keyval,
    w_out,
    span_lens,
    cached_lens,
    old_table,
    new_table,
    old_cache,
):
    tp = lax.axis_size("tp")
    groups, share, width = old_cache.shape
    block_rows = share * tp
    capacity = groups * block_rows
    rows, cols = tokens.shape
    q_cols = w_query.shape[1]
    features = w_query.shape[0]
    hd = width // 2
    most_held = capacity - rows
    piece_rows = most_held // tp

    def swap(x, bit, axis="tp"):
        size = lax.axis_size(axis)
        return lax.ppermute(x, axis, [(i, i ^ bit) for i in range(size)])

    def exchange(x):
        return lax.all_to_all(x, "seq", split_axis=0, concat_axis=0, tiled=True)

    phased = groups == 8

    with jax.named_scope("tokens_gather"):
        across = swap(tokens, 2)
        beside = swap(tokens, 1)

    with jax.named_scope("cache_gather"):
        gain = jnp.maximum(norm_gain, LEAST).reshape(tp, 1, cols)
        gain, stored = lax.optimization_barrier((gain, old_cache))
        arrived = exchange(stored).reshape(groups * share, width)
        own = jnp.maximum(tokens, jnp.asarray(LEAST, BF16))
        across, *lens = lax.optimization_barrier(
            (across, cached_lens, span_lens, old_table[0], new_table[0])
        )
        plan = jnp.concatenate(lens)
        arrived, across, own, plan = lax.optimization_barrier((arrived, across, own, plan))
        ordered = call(
            functools.partial(order_kernel, share),
            jax.ShapeDtypeStruct((piece_rows, width), BF16),
            [SMEM, VMEM],
            (plan, arrived),
            flops=2 * piece_rows * groups * share * width,
            name="order",
        )
        c_across = swap(ordered, 2)
        c_beside = swap(ordered, 1)

    with jax.named_scope("project"):
        corner = swap(across, 1)
        stacked = rows * (q_cols // hd)
        query, keyval, values, limits = call(
            project_kernel,
            [
                jax.ShapeDtypeStruct((stacked, hd), BF16),
                jax.ShapeDtypeStruct((rows, width), BF16),
                jax.ShapeDtypeStruct((rows, width), BF16),
                jax.ShapeDtypeStruct((2, 8, 128), F32),
            ],
            [VMEM] * 5 + [HBM] * 2,
            (
                own,
                beside,
                across,
                corner,
                gain,
                w_query,
                w_keyval,
            ),
            flops=2 * rows * features * (q_cols + width),
            mib=PROJECT_MIB,
            scratch=[
                pltpu.VMEM((rows, features), BF16),
                pltpu.VMEM(w_query.shape, BF16),
                pltpu.VMEM(w_keyval.shape, BF16),
                pltpu.SemaphoreType.DMA((2 * tp,)),
            ],
            name="project",
        )

    with jax.named_scope("extend"):
        sent = call(
            functools.partial(extend_kernel, share, block_rows),
            [jax.ShapeDtypeStruct((groups // 2, share, width), BF16)] * 2
            if phased
            else [jax.ShapeDtypeStruct((groups * share, width), BF16)],
            [SMEM] + [VMEM] * 2,
            (plan, keyval, arrived),
            flops=4 * groups * share * groups * share * width,
            name="extend",
        )
        *sent, c_across = lax.optimization_barrier((*sent, c_across))
        if phased:
            keep, got = sent[0], swap(sent[1], 1, "seq")
        cached = (ordered, c_beside, c_across, swap(c_across, 1))

    with jax.named_scope("early"):
        early = call(
            functools.partial(early_kernel, share, block_rows),
            [
                jax.ShapeDtypeStruct(((tp - 1) * piece_rows, width), BF16),
                jax.ShapeDtypeStruct((8, 128), F32),
            ],
            [SMEM] + [VMEM] * (tp - 1),
            (plan, *cached[:-1]),
            flops=1 << 30,
            mib=EARLY_MIB,
            name="early",
        )

    part = rows // CHUNKS
    tile_rows = ROW_TILE * (q_cols // hd)
    old = list(early)
    mixed = None
    for c in range(CHUNKS):
        last = c == CHUNKS - 1
        with jax.named_scope("attend"):
            of_part = jax.ShapeDtypeStruct((part, cols), BF16)
            of_all = jax.ShapeDtypeStruct((rows, cols), BF16)
            outs = [of_all, of_part, of_all, of_part]
            if not last:
                outs = [
                    of_part,
                    of_part,
                    jax.ShapeDtypeStruct((part, q_cols), BF16),
                    jax.ShapeDtypeStruct((piece_rows, width), BF16),
                    jax.ShapeDtypeStruct((8, 128), F32),
                ]
            seen = most_held + (c + 1) * part
            sums = list(call(
                functools.partial(attend_kernel, share, block_rows, c * part, part),
                outs,
                [SMEM] + [VMEM] * 8 + [HBM] + [VMEM] * len(old),
                (plan, query, keyval, values, limits, *cached, w_out, *old),
                flops=4 * part * seen * q_cols + 2 * part * q_cols * features,
                exps=part * seen * (q_cols // hd),
                mib=ATTEND_MIB,
                scratch=[
                    pltpu.VMEM((tile_rows, width), F32),
                    pltpu.VMEM((tile_rows, hd), F32),
                    pltpu.VMEM((part, q_cols), BF16),
                    pltpu.VMEM(w_out.shape, BF16),
                    pltpu.SemaphoreType.DMA,
                ],
                name="attend",
            ))
            if last:
                far0, far1, near0, near1 = sums
            else:
                far1, near1, before_rows, *rest = sums
                old += [*rest, before_rows]
        with jax.named_scope("reduce"):
            if last and phased:
                far1, got = lax.optimization_barrier((far1, got))
            got1 = swap(far1, 1)
            if c and last:
                before = hand_on(before)
                before, got1 = lax.optimization_barrier((before, got1))
            pair = (near1.astype(F32) + got1.astype(F32)).astype(BF16)
            if not last:
                query, pair = lax.optimization_barrier((query, pair))
            if last and phased:
                pair, got = lax.optimization_barrier((pair, got))
            crossed = swap(pair, 2)
            if not last:
                before = crossed

    with jax.named_scope("exchange"):
        if phased:
            pairs = list(call(
                pair_kernel,
                [jax.ShapeDtypeStruct((2, share, width), BF16)] * (groups // 2),
                [VMEM] * 2,
                (keep, got),
                flops=0,
                mib=8,
                name="pair",
            ))
            for k in range(len(pairs) - 1, 1, -1):
                pairs[k] = swap(pairs[k], 2 * k, "seq")
        else:
            new_cache = exchange(sent[0].reshape(groups, share, width))

    with jax.named_scope("finish"):
        got0 = swap(far0, 1)
        if phased:
            got0, pairs[1] = lax.optimization_barrier((got0, pairs[1]))
            pairs[1] = swap(pairs[1], 2, "seq")
        mixed = None
        for at, over in ((0, before), (part, crossed)):
            mixed = call(
                functools.partial(finish_kernel, at),
                jax.ShapeDtypeStruct((rows, cols), BF16),
                [SMEM] + [VMEM] * 4 + [HBM] * (at > 0),
                (plan, own, near0, got0, over, *([mixed] if at else [])),
                flops=4 * part * cols,
                scratch=[pltpu.VMEM((part, cols), BF16), pltpu.SemaphoreType.DMA((2,))],
                name="finish",
                into={5: 0} if at else {},
            )
        if phased:
            mixed, *pairs = lax.optimization_barrier((mixed, *pairs))
            new_cache = call(
                place_kernel,
                jax.ShapeDtypeStruct(old_cache.shape, BF16),
                [VMEM] * len(pairs),
                pairs,
                flops=0,
                mib=8,
                scratch=[pltpu.SemaphoreType.DMA((groups,))],
                name="place",
                into={},
            )
    return (mixed, new_cache)


def solution(mesh):
    in_specs = (
        P("seq", "tp"),
        P(),
        P(None, "tp"),
        P(),
        P("tp", None),
        P("seq"),
        P("seq"),
        P("seq", None),
        P("seq", None),
        P("seq", "tp", None),
    )
    out_specs = (P("seq", "tp"), P("seq", "tp", None))
    return jax.shard_map(body, mesh=mesh, in_specs=in_specs, out_specs=out_specs, check_vma=False)
```

```python
import functools
import math

import jax
import jax.numpy as jnp
from jax import lax
from jax.experimental import pallas as pl
from jax.experimental.pallas import tpu as pltpu
from jax.sharding import PartitionSpec as P

EPSILON = 1e-05
MASKED = -1e30
CHUNKS = 2
PART_ROWS = 256
ROW_TILE = 128
KEY_TILE = 128
NORM_ROWS = 128
MIB = 51
PROJECT_MIB = 50.375
LEAST = -3e38
ATTEND_MIB = 49
EARLY_MIB = 50
SAFE = 60.0
F32 = jnp.float32
BF16 = jnp.bfloat16

VMEM = pl.BlockSpec(memory_space=pltpu.VMEM)
SMEM = pl.BlockSpec(memory_space=pltpu.SMEM)
HBM = pl.BlockSpec(memory_space=pltpu.HBM)


def dot(a, b):
    return lax.dot_general(a, b, (((1,), (0,)), ((), ())), preferred_element_type=F32)


def dot_t(a, b):
    return lax.dot_general(a, b, (((1,), (1,)), ((), ())), preferred_element_type=F32)


def pair_kernel(keep_ref, got_ref, *pair_refs):
    for k, pair_ref in enumerate(pair_refs):
        pair_ref[0] = keep_ref[k]
        pair_ref[1] = got_ref[k]


def place_kernel(p0, p1, p2, p3, out_hbm, sems):
    me = lax.axis_index("seq")
    stores = []
    for k, pair_ref in enumerate((p0, p1, p2, p3)):
        for j in range(2):
            slot = out_hbm.at[me ^ (2 * k + j)]
            stores.append(pltpu.make_async_copy(pair_ref.at[j], slot, sems.at[len(stores)]))
            stores[-1].start()
    for store in stores:
        store.wait()


def order_kernel(share, plan_ref, arrived_ref, out_ref):
    rows, count = out_ref.shape[0], arrived_ref.shape[0]
    if share % 16 == 0:
        for b in range(rows // share):
            at = pl.ds(pl.multiple_of(plan_ref[2 + b] * share, share), share)
            out_ref[pl.ds(b * share, share), :] = arrived_ref[at, :]
        return
    row = lax.broadcasted_iota(jnp.int32, (rows, 128), 0)
    block = row // share
    holder = jnp.zeros_like(block)
    for b in range(rows // share):
        holder = jnp.where(block == b, plan_ref[2 + b], holder)
    index = (holder * share + row % share)[:, :1]
    column = lax.broadcasted_iota(jnp.int32, (rows, count), 1)
    pick = jnp.where(column == index, 1.0, 0.0).astype(BF16)
    out_ref[...] = dot(pick, arrived_ref[...]).astype(BF16)


def extend_kernel(share, block_rows, plan_ref, kv_ref, arrived_ref, *out_refs):
    rows = arrived_ref.shape[0]
    groups = rows // share
    held, span = plan_ref[0], plan_ref[1]
    me = lax.axis_index("seq") if len(out_refs) > 1 else 0
    row = lax.broadcasted_iota(jnp.int32, (rows, 128), 0)
    target = row // share
    block, holder = jnp.zeros_like(row), jnp.zeros_like(row)
    for b in range(groups):
        hit = target == plan_ref[2 + groups + b] ^ me
        block = jnp.where(hit, b, block)
        holder = jnp.where(hit, plan_ref[2 + b], holder)
    position = block * block_rows + lax.axis_index("tp") * share + row % share
    old_row = jnp.where(position < held, holder * share + row % share, -1)[:, :1]
    fresh = position - held
    new_row = jnp.where((fresh >= 0) & (fresh < span), fresh, -1)[:, :1]
    column = lax.broadcasted_iota(jnp.int32, (rows, rows), 1)
    total = dot(jnp.where(column == old_row, 1.0, 0.0).astype(BF16), arrived_ref[...])
    column = lax.broadcasted_iota(jnp.int32, (rows, kv_ref.shape[0]), 1)
    total += dot(jnp.where(column == new_row, 1.0, 0.0).astype(BF16), kv_ref[...])
    total = total.astype(BF16)
    if len(out_refs) == 1:
        out_refs[0][...] = total
        return
    for slot in range(groups):
        out_refs[slot % 2][slot // 2] = total[slot * share : (slot + 1) * share]


def project_kernel(
    x0,
    x1,
    x2,
    x3,
    gain_ref,
    wq_hbm,
    wkv_hbm,
    q_ref,
    kv_ref,
    values_ref,
    limits_ref,
    normed,
    wq_ref,
    wkv_ref,
    sems,
):
    pieces = (x0, x1, x2, x3)
    me = lax.axis_index("tp")
    rows, width = x0.shape
    features = width * len(pieces)
    hd = kv_ref.shape[1] // 2
    heads = wq_ref.shape[1] // hd
    loads = []
    for hbm, to in ((wkv_hbm, wkv_ref), (wq_hbm, wq_ref)):
        for j in range(len(pieces)):
            at = pl.ds(j * width, width)
            loads.append(pltpu.make_async_copy(hbm.at[at], to.at[at], sems.at[len(loads)]))
            loads[-1].start()

    for step in range(0, rows, NORM_ROWS):
        at = pl.ds(step, NORM_ROWS)
        values = [piece[at, :].astype(F32) for piece in pieces]
        average = jnp.sum(sum(values), axis=1, keepdims=True) / features
        centred = [v - average for v in values]
        spread = jnp.sum(sum(v * v for v in centred), axis=1, keepdims=True) / features
        scale = lax.rsqrt(spread + EPSILON)
        for j, v in enumerate(centred):
            owner = me ^ j
            to = pl.ds(pl.multiple_of(owner * width, width), width)
            normed[at, to] = (v * scale * gain_ref[owner]).astype(BF16)
    for load in loads[: len(pieces)]:
        load.wait()
    keyval = dot(normed[...], wkv_ref[...]).astype(BF16)
    kv_ref[...] = keyval
    values_ref[:, hd:] = keyval[:, hd:]
    values_ref[:, :hd] = jnp.ones((rows, hd), BF16)
    limits_ref[0] = longest(keyval[:, :hd])
    for load in loads[len(pieces) :]:
        load.wait()
    query = dot(normed[...], wq_ref[...]).astype(BF16)
    for start in range(0, rows, ROW_TILE):
        for h in range(heads):
            q_ref[pl.ds(start * heads + h * ROW_TILE, ROW_TILE), :] = query[
                start : start + ROW_TILE, h * hd : (h + 1) * hd
            ]
    limits_ref[1] = longest(q_ref[...])


def longest(x):
    squares = dot(x * x, jnp.ones((x.shape[1], 128), BF16))
    return jnp.max(squares.reshape(-1, 8, 128), axis=0)


def lay_out(share, block_rows, held, owners, pieces, out_ref):
    piece_rows, width = pieces[0].shape
    hd = width // 2
    group = KEY_TILE * lax.axis_size("tp")
    tiles = (held + group - 1) // group
    row = lax.broadcasted_iota(jnp.int32, (KEY_TILE, hd), 0)
    place = row // share * block_rows + row % share

    def lay(i, whole):
        source = pl.ds(i * KEY_TILE, KEY_TILE)
        for j, (owner, piece) in enumerate(zip(owners, pieces)):
            at = pl.ds((i * len(pieces) + j) * KEY_TILE, KEY_TILE)
            if whole:
                out_ref[at, hd:] = piece[source, hd:]
                out_ref[at, :hd] = jnp.ones((KEY_TILE, hd), BF16)
                continue
            used = place + owner * share + i * group < held
            out_ref[at, hd:] = jnp.where(used, piece[source, hd:].astype(F32), 0.0).astype(BF16)
            out_ref[at, :hd] = jnp.where(used, 1.0, 0.0).astype(BF16)

    for i in range(piece_rows // KEY_TILE):
        pl.when(i < tiles - 1)(functools.partial(lay, i, True))
        pl.when(i == tiles - 1)(functools.partial(lay, i, False))


def early_kernel(share, block_rows, plan_ref, *refs):
    pieces, (out_ref, limit_ref) = refs[:-2], refs[-2:]
    me = lax.axis_index("tp")
    owners = [me ^ j for j in range(len(pieces))]
    lay_out(share, block_rows, plan_ref[0], owners, pieces, out_ref)
    limit_ref[...] = functools.reduce(
        jnp.maximum, [longest(piece[:, : piece.shape[1] // 2]) for piece in pieces]
    )


def attend_kernel(share, block_rows, start_row, rows, plan_ref, q_ref, kv_ref, new_ref, *refs):
    limits_ref, pieces, wout_hbm = refs[0], refs[1:5], refs[5]
    total, high, context, wout, sem = refs[-5:]
    most_ref, most_limit_ref = refs[6:8]
    if start_row:
        rest_ref, rest_limit_ref, before_ref, far0_ref, far1_ref, near0_ref, near1_ref = refs[8:15]
    else:
        far1_ref, near1_ref, context_out, rest_ref, rest_limit_ref = refs[8:13]
    me = lax.axis_index("tp")
    held, span = plan_ref[0], plan_ref[1]
    piece_rows, width = pieces[0].shape
    hd = width // 2
    heads = q_ref.shape[0] // kv_ref.shape[0]
    load = pltpu.make_async_copy(wout_hbm, wout, sem)
    load.start()

    group = KEY_TILE * len(pieces)
    most = piece_rows // KEY_TILE
    tiles = (held + group - 1) // group
    if not start_row:
        corner = len(pieces) - 1
        lay_out(share, block_rows, held, [me ^ corner], pieces[corner:], rest_ref)
        rest_limit_ref[...] = longest(pieces[corner][:, :hd])

    factor = hd ** (-0.5) * math.log2(math.e)
    old_limit = jnp.maximum(most_limit_ref[...], rest_limit_ref[...])
    key_limit = jnp.max(jnp.maximum(old_limit, limits_ref[0]))
    small = key_limit * jnp.max(limits_ref[1]) * (1.05 / hd) < SAFE * SAFE

    tile_rows = ROW_TILE * heads

    def queries(t, first=0, count=heads):
        at = start_row * heads + t * tile_rows + first * ROW_TILE
        return q_ref[pl.ds(at, count * ROW_TILE), :]

    def old_keys(i):
        source = pl.ds(i * KEY_TILE, KEY_TILE)
        return jnp.concatenate([piece[source, :hd] for piece in pieces], axis=0)

    def old_values(i):
        parts = []
        for ref, count in ((most_ref, len(pieces) - 1), (rest_ref, 1)):
            size = count * KEY_TILE
            at = i * size if isinstance(i, int) else pl.multiple_of(i * size, KEY_TILE)
            parts.append(ref[pl.ds(at, size), :])
        return jnp.concatenate(parts, axis=0)

    def new_scores(t, first=0, count=heads):
        known = start_row + t * ROW_TILE
        scores = dot_t(queries(t, first, count), kv_ref[pl.ds(0, known + ROW_TILE), :hd])
        to = lax.broadcasted_iota(jnp.int32, (count * ROW_TILE, ROW_TILE), 0) % ROW_TILE
        by = lax.broadcasted_iota(jnp.int32, (count * ROW_TILE, ROW_TILE), 1)
        last = jnp.where(by <= to, scores[:, known:], MASKED)
        return jnp.concatenate([scores[:, :known], last], axis=1) if known else last

    def new_values(t):
        return new_ref[pl.ds(0, start_row + (t + 1) * ROW_TILE), :]

    def put(t, both, first=0, count=heads):
        sums = both[:, :hd]
        inverse = pl.reciprocal(sums, approx=True)
        inverse = inverse * (2.0 - sums * inverse)
        out = (both[:, hd:] * inverse).astype(BF16)
        for h in range(count):
            to = slice((first + h) * hd, (first + h + 1) * hd)
            context[pl.ds(t * ROW_TILE, ROW_TILE), to] = out[h * ROW_TILE : (h + 1) * ROW_TILE]

    def fast(used, begin):
        row_tiles = range(begin // ROW_TILE, min(begin + PART_ROWS, rows) // ROW_TILE)
        count = max(heads // 2, 1)
        groups = range(0, heads, count)
        steps = [(t, g, i) for t in row_tiles for g in groups for i in range(used + 1)]

        def score(t, g, i):
            if i == used:
                return new_scores(t, g, count)
            return dot_t(queries(t, g, count), old_keys(i))

        ahead, both = score(*steps[0]), None
        for at, (t, g, i) in enumerate(steps):
            scores = ahead
            if at + 1 < len(steps):
                ahead = score(*steps[at + 1])
            weights = jnp.exp2(scores * factor).astype(BF16)
            values = new_values(t) if i == used else old_values(i)
            part = dot(weights, values)
            both = part if i == 0 else both + part
            if i == used:
                put(t, both, g, count)

    def exact(t):
        column = lax.broadcasted_iota(jnp.int32, (tile_rows, group), 1)
        within = column % KEY_TILE
        owner = me ^ (column // KEY_TILE)
        place = within // share * block_rows + within % share + owner * share

        def old_scores(i):
            scores = dot_t(queries(t), old_keys(pl.multiple_of(i, 1)))
            return jnp.where(place + i * group < held, scores, MASKED)

        def raise_high(i, carry):
            top = jnp.max(old_scores(i), axis=1, keepdims=True)
            high[...] = jnp.maximum(high[...], top)
            return carry

        def add(i, carry):
            weights = jnp.exp2((old_scores(i) - high[:, :1]) * factor).astype(BF16)
            total[...] += dot(weights, old_values(i))
            return carry

        high[...] = jnp.zeros_like(high) + jnp.max(new_scores(t), axis=1, keepdims=True)
        lax.fori_loop(0, tiles, raise_high, 0)
        weights = jnp.exp2((new_scores(t) - high[:, :1]) * factor).astype(BF16)
        total[...] = dot(weights, new_values(t))
        lax.fori_loop(0, tiles, add, 0)
        put(t, total[...])

    for begin in range(0, rows, PART_ROWS):
        busy = start_row + begin < span
        for used in range(1, most + 1):
            pl.when(busy & small & (tiles == used))(functools.partial(fast, used, begin))

        @pl.when(busy & jnp.logical_not(small))
        def _():
            for t in range(begin // ROW_TILE, min(begin + PART_ROWS, rows) // ROW_TILE):
                exact(t)

        @pl.when(jnp.logical_not(busy))
        def _():
            context[pl.ds(begin, PART_ROWS), :] = jnp.zeros((PART_ROWS, context.shape[1]), BF16)

    load.wait()
    cols = wout.shape[1] // 4

    def partial_sums(rows_of, k):
        columns = pl.ds(pl.multiple_of((me ^ k) * cols, cols), cols)
        return dot(rows_of[...], wout[:, columns]).astype(BF16)

    far1_ref[...] = partial_sums(context, 3)
    near1_ref[...] = partial_sums(context, 2)
    if not start_row:
        context_out[...] = context[...]
        return
    for at, rows_of in ((0, before_ref), (start_row, context)):
        far0_ref[pl.ds(at, rows), :] = partial_sums(rows_of, 1)
        near0_ref[pl.ds(at, rows), :] = partial_sums(rows_of, 0)


def hand_on_kernel(in_ref, out_ref):
    pass


def finish_kernel(at, plan_ref, tokens_ref, near_ref, got_ref, crossed_ref, *refs):
    out_hbm, done, sems = refs[-3:]
    rows = crossed_ref.shape[0]
    size = rows // 4
    stores = []
    for i in range(4):
        here = pl.ds(i * size, size)
        there = pl.ds(at + i * size, size)
        kept = near_ref[there, :].astype(F32) + got_ref[there, :].astype(F32)
        total = tokens_ref[there, :].astype(F32) + (kept + crossed_ref[here, :].astype(F32))
        row = lax.broadcasted_iota(jnp.int32, total.shape, 0) + (at + i * size)
        done[here, :] = jnp.where(row < plan_ref[1], total, 0.0).astype(BF16)
        stores.append(pltpu.make_async_copy(done.at[here], out_hbm.at[there], sems.at[i]))
        stores[-1].start()
    for store in stores:
        store.wait()


def call(
    kernel, out_shape, in_specs, args, flops, mib=MIB, scratch=(), exps=0, name=None, into=None
):
    outs = out_shape if isinstance(out_shape, (list, tuple)) else [out_shape]
    moved = sum(a.size * a.dtype.itemsize for a in list(args) + list(outs))
    return pl.pallas_call(
        kernel,
        out_shape=out_shape,
        in_specs=in_specs,
        out_specs=jax.tree.map(lambda _: VMEM if into is None else HBM, out_shape),
        input_output_aliases=into or {},
        scratch_shapes=list(scratch),
        cost_estimate=pl.CostEstimate(flops=flops, bytes_accessed=moved, transcendentals=exps),
        compiler_params=pltpu.CompilerParams(vmem_limit_bytes=int(mib * 1024 * 1024)),
        name=name,
    )(*args)


def hand_on(x):
    return pl.pallas_call(
        hand_on_kernel,
        out_shape=jax.ShapeDtypeStruct(x.shape, x.dtype),
        in_specs=[pl.BlockSpec(memory_space=pl.ANY)],
        out_specs=pl.BlockSpec(memory_space=pl.ANY),
        input_output_aliases={0: 0},
        cost_estimate=pl.CostEstimate(flops=1 << 34, bytes_accessed=1024, transcendentals=0),
        compiler_params=pltpu.CompilerParams(vmem_limit_bytes=1 << 20),
        name="hand_on",
    )(x)


def body(
    tokens,
    norm_gain,
    w_query,
    w_keyval,
    w_out,
    span_lens,
    cached_lens,
    old_table,
    new_table,
    old_cache,
):
    tp = lax.axis_size("tp")
    groups, share, width = old_cache.shape
    block_rows = share * tp
    capacity = groups * block_rows
    rows, cols = tokens.shape
    q_cols = w_query.shape[1]
    features = w_query.shape[0]
    hd = width // 2
    most_held = capacity - rows
    piece_rows = most_held // tp

    def swap(x, bit, axis="tp"):
        size = lax.axis_size(axis)
        return lax.ppermute(x, axis, [(i, i ^ bit) for i in range(size)])

    def exchange(x):
        return lax.all_to_all(x, "seq", split_axis=0, concat_axis=0, tiled=True)

    phased = groups == 8

    with jax.named_scope("tokens_gather"):
        across = swap(tokens, 2)
        beside = swap(tokens, 1)

    with jax.named_scope("cache_gather"):
        gain = jnp.maximum(norm_gain, LEAST).reshape(tp, 1, cols)
        gain, stored = lax.optimization_barrier((gain, old_cache))
        arrived = exchange(stored).reshape(groups * share, width)
        own = jnp.maximum(tokens, jnp.asarray(LEAST, BF16))
        across, *lens = lax.optimization_barrier(
            (across, cached_lens, span_lens, old_table[0], new_table[0])
        )
        plan = jnp.concatenate(lens)
        arrived, across, own, plan = lax.optimization_barrier((arrived, across, own, plan))
        ordered = call(
            functools.partial(order_kernel, share),
            jax.ShapeDtypeStruct((piece_rows, width), BF16),
            [SMEM, VMEM],
            (plan, arrived),
            flops=2 * piece_rows * groups * share * width,
            name="order",
        )
        c_across = swap(ordered, 2)
        c_beside = swap(ordered, 1)

    with jax.named_scope("project"):
        corner = swap(across, 1)
        stacked = rows * (q_cols // hd)
        query, keyval, values, limits = call(
            project_kernel,
            [
                jax.ShapeDtypeStruct((stacked, hd), BF16),
                jax.ShapeDtypeStruct((rows, width), BF16),
                jax.ShapeDtypeStruct((rows, width), BF16),
                jax.ShapeDtypeStruct((2, 8, 128), F32),
            ],
            [VMEM] * 5 + [HBM] * 2,
            (
                own,
                beside,
                across,
                corner,
                gain,
                w_query,
                w_keyval,
            ),
            flops=2 * rows * features * (q_cols + width),
            mib=PROJECT_MIB,
            scratch=[
                pltpu.VMEM((rows, features), BF16),
                pltpu.VMEM(w_query.shape, BF16),
                pltpu.VMEM(w_keyval.shape, BF16),
                pltpu.SemaphoreType.DMA((2 * tp,)),
            ],
            name="project",
        )

    with jax.named_scope("extend"):
        sent = call(
            functools.partial(extend_kernel, share, block_rows),
            [jax.ShapeDtypeStruct((groups // 2, share, width), BF16)] * 2
            if phased
            else [jax.ShapeDtypeStruct((groups * share, width), BF16)],
            [SMEM] + [VMEM] * 2,
            (plan, keyval, arrived),
            flops=4 * groups * share * groups * share * width,
            name="extend",
        )
        *sent, c_across = lax.optimization_barrier((*sent, c_across))
        if phased:
            keep, got = sent[0], swap(sent[1], 1, "seq")
        cached = (ordered, c_beside, c_across, swap(c_across, 1))

    with jax.named_scope("early"):
        early = call(
            functools.partial(early_kernel, share, block_rows),
            [
                jax.ShapeDtypeStruct(((tp - 1) * piece_rows, width), BF16),
                jax.ShapeDtypeStruct((8, 128), F32),
            ],
            [SMEM] + [VMEM] * (tp - 1),
            (plan, *cached[:-1]),
            flops=1 << 30,
            mib=EARLY_MIB,
            name="early",
        )

    part = rows // CHUNKS
    tile_rows = ROW_TILE * (q_cols // hd)
    old = list(early)
    mixed = None
    for c in range(CHUNKS):
        last = c == CHUNKS - 1
        with jax.named_scope("attend"):
            of_part = jax.ShapeDtypeStruct((part, cols), BF16)
            of_all = jax.ShapeDtypeStruct((rows, cols), BF16)
            outs = [of_all, of_part, of_all, of_part]
            if not last:
                outs = [
                    of_part,
                    of_part,
                    jax.ShapeDtypeStruct((part, q_cols), BF16),
                    jax.ShapeDtypeStruct((piece_rows, width), BF16),
                    jax.ShapeDtypeStruct((8, 128), F32),
                ]
            seen = most_held + (c + 1) * part
            sums = list(call(
                functools.partial(attend_kernel, share, block_rows, c * part, part),
                outs,
                [SMEM] + [VMEM] * 8 + [HBM] + [VMEM] * len(old),
                (plan, query, keyval, values, limits, *cached, w_out, *old),
                flops=4 * part * seen * q_cols + 2 * part * q_cols * features,
                exps=part * seen * (q_cols // hd),
                mib=ATTEND_MIB,
                scratch=[
                    pltpu.VMEM((tile_rows, width), F32),
                    pltpu.VMEM((tile_rows, hd), F32),
                    pltpu.VMEM((part, q_cols), BF16),
                    pltpu.VMEM(w_out.shape, BF16),
                    pltpu.SemaphoreType.DMA,
                ],
                name="attend",
            ))
            if last:
                far0, far1, near0, near1 = sums
            else:
                far1, near1, before_rows, *rest = sums
                old += [*rest, before_rows]
        with jax.named_scope("reduce"):
            if last and phased:
                far1, got = lax.optimization_barrier((far1, got))
            got1 = swap(far1, 1)
            if c and last:
                before = hand_on(before)
                before, got1 = lax.optimization_barrier((before, got1))
            pair = (near1.astype(F32) + got1.astype(F32)).astype(BF16)
            if not last:
                query, pair = lax.optimization_barrier((query, pair))
            if last and phased:
                pair, got = lax.optimization_barrier((pair, got))
            crossed = swap(pair, 2)
            if not last:
                before = crossed

    with jax.named_scope("exchange"):
        if phased:
            pairs = list(call(
                pair_kernel,
                [jax.ShapeDtypeStruct((2, share, width), BF16)] * (groups // 2),
                [VMEM] * 2,
                (keep, got),
                flops=0,
                mib=8,
                name="pair",
            ))
            for k in range(len(pairs) - 1, 1, -1):
                pairs[k] = swap(pairs[k], 2 * k, "seq")
        else:
            new_cache = exchange(sent[0].reshape(groups, share, width))

    with jax.named_scope("finish"):
        got0 = swap(far0, 1)
        if phased:
            got0, pairs[1] = lax.optimization_barrier((got0, pairs[1]))
            pairs[1] = swap(pairs[1], 2, "seq")
        mixed = None
        for at, over in ((0, before), (part, crossed)):
            mixed = call(
                functools.partial(finish_kernel, at),
                jax.ShapeDtypeStruct((rows, cols), BF16),
                [SMEM] + [VMEM] * 4 + [HBM] * (at > 0),
                (plan, own, near0, got0, over, *([mixed] if at else [])),
                flops=4 * part * cols,
                scratch=[pltpu.VMEM((part, cols), BF16), pltpu.SemaphoreType.DMA((4,))],
                name="finish",
                into={5: 0} if at else {},
            )
        if phased:
            mixed, *pairs = lax.optimization_barrier((mixed, *pairs))
            new_cache = call(
                place_kernel,
                jax.ShapeDtypeStruct(old_cache.shape, BF16),
                [VMEM] * len(pairs),
                pairs,
                flops=0,
                mib=8,
                scratch=[pltpu.SemaphoreType.DMA((groups,))],
                name="place",
                into={},
            )
    return (mixed, new_cache)


def solution(mesh):
    in_specs = (
        P("seq", "tp"),
        P(),
        P(None, "tp"),
        P(),
        P("tp", None),
        P("seq"),
        P("seq"),
        P("seq", None),
        P("seq", None),
        P("seq", "tp", None),
    )
    out_specs = (P("seq", "tp"), P("seq", "tp", None))
    return jax.shard_map(body, mesh=mesh, in_specs=in_specs, out_specs=out_specs, check_vma=False)
```
